32 devices in a mesh: orb: 8 (over z, x), wall: 4 (over y, core).
Axes of the slice: x: 2, y: 2, z: 4, core: 2. Of those that a mesh axis runs over, the one named last changes fastest.
Arguments:
- fluid_state: float32 [8, 98304], P(None, ('orb', 'wall')), may hold values from -4 to 4, as said below
- ghost_list: int32 [7, 192], P(None, ('orb', 'wall')), may hold values from 0 to 23, as said below
- pair_list: int32 [768, 14], P(('orb', 'wall')), may hold values from 0 to 65, as said below
- wall_state: float32 [4, 24576], P(None, ('orb', 'wall')), may hold values from 0 to 0.6, as said below
- wall_count: int32 [192], P(('orb', 'wall')), may hold values from 1 to 128, as said below
- wall_pairs: int32 [768, 4], P(('orb', 'wall')), may hold values from 0 to 7, as said below
Outputs:
- density_rate: float32 [98304], P(('orb', 'wall'))
- acceleration: float32 [3, 98304], P(None, ('orb', 'wall'))
- time_step: float32 [], replicated
The draws below stay inside these ranges and needn't reach their ends.
Inputs may be any that keep to these rules, and one draw needn't show every extreme that they name: `fluid_state`: rows: position from 0 to 0.6, velocity from -4 to 4, density from 0.97 to 1.03, mass from 0.001 to 0.003. `ghost_list`: the 6 entries of one mask and one domain are distinct. `pair_list`: the 14 entries of one block are distinct, and every candidate index is named by some block of each domain. `wall_state`: rows: x and y from 0 to 0.6, z from 0 to 0.15, mass from 0.001 to 0.003. `wall_count`: the live particles fill the first columns of their wall block. `wall_pairs`: the 4 entries of one block are distinct, and every wall candidate index is named by some block of each domain.
All inputs are finite; a program needn't handle non-finite values.
Results may differ from the reference program's by a relative error of at most 0.0003.
Values sent between devices are 32-bit elements; how exact they have to be, the bound alone decides.
No kernel may reach another device: no remote copies, remote signals or barrier semaphores. Data moves between devices by JAX's collectives and lax.ppermute only.
A program may use at most 64 MiB of HBM per device.

```python
import jax
import jax.numpy as jnp
from jax import lax

NB = 24
K = 14
KW = 4
GH = 6
WB = 6
EB = 1
DOMAINS = 32
PARTICLES = 98304
WALLS = 24576
N_ORB = 8
N_WALL = 4


def draw_fluid_state(key, part):
    keys = jax.random.split(key, 5)
    position = jax.random.uniform(keys[0], (3, PARTICLES), jnp.float32, 0.0, 0.6)
    velocity = jnp.clip(jax.random.normal(keys[2], (3, PARTICLES), jnp.float32), -4.0, 4.0)
    density = jax.random.uniform(keys[3], (1, PARTICLES), jnp.float32, 0.97, 1.03)
    masses = jax.random.uniform(keys[4], (1, PARTICLES), jnp.float32, 0.001, 0.003)
    return jnp.concatenate([position, velocity, density, masses], axis=0).astype(jnp.float32)


def draw_wall_state(key, part):
    keys = jax.random.split(key, 3)
    plane = jax.random.uniform(keys[0], (2, WALLS), jnp.float32, 0.0, 0.6)
    height = jax.random.uniform(keys[1], (1, WALLS), jnp.float32, 0.0, 0.15)
    masses = jax.random.uniform(keys[2], (1, WALLS), jnp.float32, 0.001, 0.003)
    return jnp.concatenate([plane, height, masses], axis=0).astype(jnp.float32)


def draw_ghost_list(key, part):
    keys = jax.random.split(key, 7 * DOMAINS)

    def pick_rows(single):
        return jax.random.permutation(single, NB)[:GH]
    rows = jax.vmap(pick_rows)(keys)
    return rows.reshape(7, DOMAINS * GH).astype(jnp.int32)


def spread_lists(key, blocks_per, listed, choices_total):
    keys = jax.random.split(key, DOMAINS)
    picks = (jnp.arange(blocks_per)[:, None] * listed + jnp.arange(listed)[None, :]) % choices_total

    def pick_rows(single):
        return jax.random.permutation(single, choices_total)[picks]
    rows = jax.vmap(pick_rows)(keys)
    return rows.reshape(DOMAINS * blocks_per, listed).astype(jnp.int32)


def draw_pair_list(key, part):
    return spread_lists(jax.random.fold_in(key, 11), NB, K, NB + 7 * GH)


def draw_wall_pairs(key, part):
    return spread_lists(jax.random.fold_in(key, 23), NB, KW, WB + 2 * EB)


def draw_wall_count(key, part):
    keys = jax.random.split(key, 3)
    pillar = jax.random.randint(keys[0], (DOMAINS * WB,), 0, 4) == 0
    sparse = jax.random.randint(keys[1], (DOMAINS * WB,), 1, 65)
    counts = jnp.where(pillar, 128, sparse)
    forced = jax.random.randint(keys[2], (), 0, DOMAINS * WB)
    return counts.at[forced].set(128).astype(jnp.int32)


def setup_inputs(seed: int = 0) -> dict:
    key_of = jax.random.split(jax.random.key(seed), 7)
    fluid_state = draw_fluid_state(jax.random.fold_in(key_of[6], 71), 0)
    ghost_list = draw_ghost_list(jax.random.fold_in(key_of[6], 71), 0)
    pair_list = draw_pair_list(jax.random.fold_in(key_of[6], 71), 0)
    wall_state = draw_wall_state(jax.random.fold_in(key_of[6], 71), 0)
    wall_count = draw_wall_count(jax.random.fold_in(key_of[6], 71), 0)
    wall_pairs = draw_wall_pairs(jax.random.fold_in(key_of[6], 71), 0)
    return {"fluid_state": fluid_state, "ghost_list": ghost_list, "pair_list": pair_list, "wall_state": wall_state, "wall_count": wall_count, "wall_pairs": wall_pairs}


smoothing = 0.1
support = 0.3
kernel_norm = 21.0 / (2.0 * 3.141592653589793 * support ** 3)
grad_coeff = -20.0 / support ** 2 * kernel_norm
tait_coeff = 25.0 / 7.0
visc_coeff = 0.05
cohesion = 2000.0
adhesion = 2000.0
gravity = 9.81
courant = 0.25

def kernel_parts(target_pos, source_pos):
    offset = target_pos[None, :, :, None] - source_pos[:, :, None, :]
    dist_sq = lax.optimization_barrier(jnp.sum(offset * offset, axis=1))
    radius = jnp.sqrt(dist_sq)
    scaled = radius / support
    falloff = jnp.maximum(1.0 - scaled, 0.0)
    cubed = falloff * falloff * falloff
    return (offset, dist_sq, grad_coeff * cubed, cubed * (4.0 * scaled - 1.0))

def pressure_of(density):
    return tait_coeff * (density ** 7 - 1.0)

def block_terms(target, sources, walls):
    target_pos = target[0:3]
    target_vel = target[3:6]
    target_rho = target[6]
    target_press = pressure_of(target_rho)
    source_rho = sources[:, 6]
    offset, dist_sq, grad_scale, pull = kernel_parts(target_pos, sources[:, 0:3])
    vel_diff = target_vel[None, :, :, None] - sources[:, 3:6][:, :, None, :]
    approach = lax.optimization_barrier(jnp.sum(vel_diff * offset, axis=1))
    mass_row = sources[:, 7][:, None, :]
    fluid_rate = lax.optimization_barrier(jnp.sum(mass_row * approach * grad_scale, axis=(0, 2)))
    mean_rho = 0.5 * (target_rho[None, :, None] + source_rho[:, None, :])
    viscous = -visc_coeff * jnp.minimum(approach, 0.0) / ((dist_sq + 0.0001) * mean_rho)
    press_term = (target_press / target_rho ** 2)[None, :, None] + (pressure_of(source_rho) / source_rho ** 2)[:, None, :] + viscous
    weight = mass_row * (press_term * grad_scale + cohesion * pull)
    fluid_force = -lax.optimization_barrier(jnp.sum(weight[:, None] * offset, axis=(0, 3)))
    wall_offset, wall_dist, wall_grad, wall_pull = kernel_parts(target_pos, walls[:, 0:3])
    wall_masses = walls[:, 3][:, None, :]
    wall_approach = lax.optimization_barrier(jnp.sum(target_vel[None, :, :, None] * wall_offset, axis=1))
    wall_rate = lax.optimization_barrier(jnp.sum(wall_masses * wall_approach * wall_grad, axis=(0, 2)))
    own_press = (2.0 * target_press / target_rho ** 2)[None, :, None]
    wall_weight = wall_masses * (own_press * wall_grad + adhesion * wall_pull)
    wall_force = -lax.optimization_barrier(jnp.sum(wall_weight[:, None] * wall_offset, axis=(0, 3)))
    downward = jnp.array([0.0, 0.0, -gravity], jnp.float32)[:, None]
    return (fluid_rate + wall_rate, fluid_force + wall_force + downward)

def reference(fluid_state, ghost_list, pair_list, wall_state, wall_count, wall_pairs):
    domains = N_ORB * N_WALL
    blocks = jnp.transpose(fluid_state.reshape(8, domains * NB, 128), (1, 0, 2))
    ghost_table = ghost_list.reshape(7, domains, GH)
    alive = (jnp.arange(128, dtype=jnp.int32)[None, :] < wall_count[:, None]).astype(jnp.float32).reshape(-1)
    wall_live = jnp.concatenate([wall_state[0:3], wall_state[3:4] * alive[None, :]], axis=0)
    wall_blocks = jnp.transpose(wall_live.reshape(4, domains * WB, 128), (1, 0, 2))
    pair_table = pair_list.reshape(domains, NB, K)
    wall_table = wall_pairs.reshape(domains, NB, KW)
    patterns = jnp.arange(1, 8, dtype=jnp.int32)
    local_ids = jnp.arange(NB, dtype=jnp.int32)
    edge_ids = jnp.arange(EB, dtype=jnp.int32)

    def one_domain(domain):
        orb_place = domain // N_WALL
        wall_place = domain % N_WALL
        partners = jnp.bitwise_xor(orb_place, patterns) * N_WALL + wall_place
        chosen = ghost_table[patterns - 1, partners]
        ghost_ids = (partners[:, None] * NB + chosen).reshape(-1)
        candidates = blocks[jnp.concatenate([domain * NB + local_ids, ghost_ids])]
        below = wall_blocks[jnp.maximum(domain - 1, 0) * WB + WB - EB + edge_ids]
        below = jnp.where(wall_place > 0, below, jnp.zeros_like(below))
        above = wall_blocks[jnp.minimum(domain + 1, domains - 1) * WB + edge_ids]
        above = jnp.where(wall_place < N_WALL - 1, above, jnp.zeros_like(above))
        own_walls = wall_blocks[domain * WB + jnp.arange(WB, dtype=jnp.int32)]
        wall_cands = jnp.concatenate([below, own_walls, above], axis=0)

        def per_block(inputs):
            return block_terms(inputs[0], candidates[inputs[1]], wall_cands[inputs[2]])
        return lax.map(per_block, (candidates[0:NB], pair_table[domain], wall_table[domain]))
    rates, forces = lax.map(one_domain, jnp.arange(domains, dtype=jnp.int32))
    density_rate = rates.reshape(-1)
    acceleration = jnp.transpose(forces, (2, 0, 1, 3)).reshape(3, -1)
    peak = jnp.max(jnp.sqrt(lax.optimization_barrier(jnp.sum(acceleration * acceleration, axis=0))))
    time_step = courant * jnp.sqrt(smoothing / (peak + 1e-06))
    return (density_rate, acceleration, time_step)
```

```python
import jax
import jax.numpy as jnp
from jax import lax
from jax.sharding import PartitionSpec as P

EB = 1


smoothing = 0.1
support = 0.3
kernel_norm = 21.0 / (2.0 * 3.141592653589793 * support**3)
grad_coeff = -20.0 / support**2 * kernel_norm
tait_coeff = 25.0 / 7.0
visc_coeff = 0.05
cohesion = 2000.0
adhesion = 2000.0
gravity = 9.81
courant = 0.25


def swapped(shard, axis, bit):
    return lax.ppermute(shard, axis, [(i, i ^ 1 << bit) for i in range(lax.axis_size(axis))])


def padded(block, sides, width):
    for axis, dim in sides:
        count = lax.axis_size(axis)
        forward = [(i, i + 1) for i in range(count - 1)]
        backward = [(target, source) for source, target in forward]
        low = lax.ppermute(
            lax.slice_in_dim(block, block.shape[dim] - width, None, axis=dim), axis, forward
        )
        high = lax.ppermute(lax.slice_in_dim(block, 0, width, axis=dim), axis, backward)
        block = jnp.concatenate([low, block, high], axis=dim)
    return block


def kernel_parts(target_pos, source_pos):
    offset = target_pos[None, :, :, None] - source_pos[:, :, None, :]
    dist_sq = jnp.sum(offset * offset, axis=1)
    radius = jnp.sqrt(dist_sq)
    scaled = radius / support
    falloff = jnp.maximum(1.0 - scaled, 0.0)
    cubed = falloff * falloff * falloff
    return (offset, dist_sq, grad_coeff * cubed, cubed * (4.0 * scaled - 1.0))


def pressure_of(density):
    return tait_coeff * (density**7 - 1.0)


def block_terms(target, sources, walls):
    target_pos = target[0:3]
    target_vel = target[3:6]
    target_rho = target[6]
    target_press = pressure_of(target_rho)
    source_rho = sources[:, 6]
    offset, dist_sq, grad_scale, pull = kernel_parts(target_pos, sources[:, 0:3])
    vel_diff = target_vel[None, :, :, None] - sources[:, 3:6][:, :, None, :]
    approach = jnp.sum(vel_diff * offset, axis=1)
    mass_row = sources[:, 7][:, None, :]
    fluid_rate = jnp.sum(mass_row * approach * grad_scale, axis=(0, 2))
    mean_rho = 0.5 * (target_rho[None, :, None] + source_rho[:, None, :])
    viscous = -visc_coeff * jnp.minimum(approach, 0.0) / ((dist_sq + 0.0001) * mean_rho)
    press_term = (
        (target_press / target_rho**2)[None, :, None]
        + (pressure_of(source_rho) / source_rho**2)[:, None, :]
        + viscous
    )
    weight = mass_row * (press_term * grad_scale + cohesion * pull)
    fluid_force = -jnp.sum(weight[:, None] * offset, axis=(0, 3))
    wall_offset, wall_dist, wall_grad, wall_pull = kernel_parts(target_pos, walls[:, 0:3])
    wall_masses = walls[:, 3][:, None, :]
    wall_approach = jnp.sum(target_vel[None, :, :, None] * wall_offset, axis=1)
    wall_rate = jnp.sum(wall_masses * wall_approach * wall_grad, axis=(0, 2))
    own_press = (2.0 * target_press / target_rho**2)[None, :, None]
    wall_weight = wall_masses * (own_press * wall_grad + adhesion * wall_pull)
    wall_force = -jnp.sum(wall_weight[:, None] * wall_offset, axis=(0, 3))
    downward = jnp.array([0.0, 0.0, -gravity], jnp.float32)[:, None]
    return (fluid_rate + wall_rate, fluid_force + wall_force + downward)


def grouped(array):
    return array.reshape((-1, 2) + array.shape[1:])


def per_device(fluid_state, ghost_list, pair_list, wall_state, wall_count, wall_pairs):
    block_total = fluid_state.shape[1] // 128
    own_blocks = jnp.transpose(fluid_state.reshape(8, block_total, 128), (1, 0, 2))
    place = lax.axis_index("orb")
    members = jnp.arange(8, dtype=jnp.int32)
    slots = jnp.bitwise_xor(members, place % 8)
    own_slot = jnp.zeros((1, ghost_list.shape[1]), jnp.int32)
    sent = own_blocks[jnp.concatenate([own_slot, ghost_list], axis=0)[slots]]
    groups = [list(range(g, g + 8)) for g in range(0, lax.axis_size("orb"), 8)]
    landed = lax.all_to_all(
        sent, "orb", 0, 0, axis_index_groups=groups if len(groups) > 1 else None
    )
    ghosts = landed[jnp.bitwise_xor(members[1:], place % 8)]
    candidates = jnp.concatenate([own_blocks, ghosts.reshape(-1, 8, 128)], axis=0)
    alive = (
        (jnp.arange(128, dtype=jnp.int32)[None, :] < wall_count[:, None])
        .astype(jnp.float32)
        .reshape(-1)
    )
    wall_live = jnp.concatenate([wall_state[0:3], wall_state[3:4] * alive[None, :]], axis=0)
    rim_width = EB * 128
    extended = padded(wall_live, (("wall", 1),), rim_width)
    wall_cands = jnp.transpose(extended.reshape(4, -1, 128), (1, 0, 2))

    def per_block(target, pair_row, wall_row):
        return block_terms(target, candidates[pair_row], wall_cands[wall_row])

    def per_group(inputs):
        return jax.vmap(per_block)(inputs[0], inputs[1], inputs[2])

    rates, forces = lax.map(
        per_group, (grouped(own_blocks), grouped(pair_list), grouped(wall_pairs))
    )
    density_rate = rates.reshape(-1)
    acceleration = jnp.transpose(forces.reshape(-1, 3, 128), (1, 0, 2)).reshape(3, -1)
    local_peak = jnp.max(jnp.sqrt(jnp.sum(acceleration * acceleration, axis=0)))
    peak = local_peak
    for axis in ("wall", "orb"):
        for bit in range((lax.axis_size(axis) - 1).bit_length()):
            peak = jnp.maximum(peak, swapped(peak, axis, bit))
    time_step = courant * jnp.sqrt(smoothing / (peak + 1e-06))
    return (density_rate, acceleration, time_step)


def solution(mesh):
    return jax.shard_map(
        per_device,
        mesh=mesh,
        in_specs=(
            P(None, ("orb", "wall")),
            P(None, ("orb", "wall")),
            P(("orb", "wall"), None),
            P(None, ("orb", "wall")),
            P(("orb", "wall")),
            P(("orb", "wall"), None),
        ),
        out_specs=(P(("orb", "wall")), P(None, ("orb", "wall")), P()),
        check_vma=False,
    )
```

```python
import functools

import jax
import jax.numpy as jnp
from jax import lax
from jax.experimental import pallas as pl
from jax.experimental.pallas import tpu as pltpu
from jax.sharding import PartitionSpec as P

EB = 1
LANES = 128
FEATURES = 64
MOMENTS = 16

smoothing = 0.1
support = 0.3
kernel_norm = 21.0 / (2.0 * 3.141592653589793 * support**3)
grad_coeff = -20.0 / support**2 * kernel_norm
tait_coeff = 25.0 / 7.0
visc_coeff = 0.05
cohesion = 2000.0
adhesion = 2000.0
gravity = 9.81
courant = 0.25

center = 0.3
shift = 0.0001 / support**2
approach_coeff = grad_coeff * visc_coeff * 2.0 / (support * 4.0 * cohesion)

SPLITS = ((0, 0), (0, 1), (1, 0), (0, 2), (2, 0), (1, 1), (1, 2), (2, 1))


def rounded(value):
    return value.astype(jnp.bfloat16).astype(jnp.float32)


def split(value):
    first = rounded(value)
    rest = value - first
    second = rounded(rest)
    return (first, second, rest - second)


def dotted(left, right):
    return left[0] * right[0] + left[1] * right[1] + left[2] * right[2]


def pressure_ratio(density):
    square = density * density
    return tait_coeff * (square * square * square * density - 1.0) / square


def loaded(ref, row, count, stride):
    return ref[pl.ds(row, count, stride=stride), :]


def scaled_position(ref, count, stride):
    return [(loaded(ref, d, count, stride) - center) * (1.0 / support) for d in range(3)]


def source_rows(pos, vel, density):
    one = jnp.ones_like(pos[0])
    rows = [one, one, one]
    rows += split(dotted(pos, pos))
    if vel is not None:
        rows += split(approach_coeff * dotted(pos, vel))
    else:
        rows += [one * 0.0] * 3
    for d in range(3):
        pieces = split(pos[d])
        rows += [pieces[t] for _, t in SPLITS]
    if vel is not None:
        for d in range(3):
            pieces = split(vel[d])
            rows += [pieces[t] for _, t in SPLITS]
    zero = one * 0.0
    rows += [zero] * (FEATURES - len(rows))
    if density is not None:
        rows[FEATURES - 1] = density
    return rows


def target_rows(pos, vel):
    one = jnp.ones_like(pos[0])
    zero = one * 0.0
    near = list(split(dotted(pos, pos))) + [one] * 3 + [zero] * 3
    along = list(split(approach_coeff * dotted(pos, vel))) + [zero] * 3 + [one] * 3
    for d in range(3):
        pieces = split(-2.0 * pos[d])
        near += [pieces[p] for p, _ in SPLITS]
        pieces = split(-approach_coeff * vel[d])
        along += [pieces[p] for p, _ in SPLITS]
    for d in range(3):
        pieces = split(-approach_coeff * pos[d])
        along += [pieces[p] for p, _ in SPLITS]
    near += [zero] * (FEATURES - len(near))
    along += [zero] * (FEATURES - len(along))
    return near, along


def moment_rows(pos, vel, mass, own, other):
    columns = [other] + [other * p for p in pos]
    columns += [own] + [own * p for p in pos]
    columns += [mass] + [mass * p for p in pos]
    if vel is not None:
        columns += [mass * v for v in vel] + [mass * dotted(pos, vel)]
    else:
        columns += [mass * 0.0] * 4
    pieces = [split(column) for column in columns]
    return [pieces[c][p] for p in range(3) for c in range(MOMENTS)]


def put_sources(rows, moments, count, base, stage, src, mom, rho):
    for k, row in enumerate(rows):
        stage[pl.ds(k, count, stride=FEATURES), :] = row

    def turn(b, carry):
        block = stage[pl.ds(pl.multiple_of(b * FEATURES, FEATURES), FEATURES), :]
        turned = block.T
        src[base + b] = turned.astype(jnp.bfloat16)
        if rho is not None:
            rho[base + b] = jnp.broadcast_to(turned[:, FEATURES - 1 :], (LANES, LANES))
        return carry

    lax.fori_loop(0, count, turn, 0)
    depth = 3 * MOMENTS
    for k, row in enumerate(moments):
        stage[pl.ds(k, count, stride=depth), :] = row

    def place(b, carry):
        block = stage[pl.ds(pl.multiple_of(b * depth, depth), depth), :].astype(jnp.bfloat16)
        mom[base + b] = jnp.concatenate([block, block], axis=1)
        return carry

    lax.fori_loop(0, count, place, 0)


def fluid_sources(ref, count, base, stage, src, mom, rho):
    pos = scaled_position(ref, count, 8)
    vel = [loaded(ref, 3 + d, count, 8) for d in range(3)]
    density = loaded(ref, 6, count, 8)
    mass = loaded(ref, 7, count, 8)
    other = mass * (3.0 * cohesion + grad_coeff * pressure_ratio(density))
    rows = source_rows(pos, vel, density)
    put_sources(rows, moment_rows(pos, vel, mass, mass, other), count, base, stage, src, mom, rho)


def wall_sources(ref, count, stage, src, mom):
    pos = scaled_position(ref, count, 4)
    mass = loaded(ref, 3, count, 4)
    rows = source_rows(pos, None, None)
    moments = moment_rows(pos, None, mass, 2.0 * mass, (3.0 * adhesion) * mass)
    put_sources(rows, moments, count, 0, stage, src, mom, None)


def put_targets(ref, count, stage, tgt):
    pos = scaled_position(ref, count, 8)
    vel = [loaded(ref, 3 + d, count, 8) for d in range(3)]
    for half, rows in enumerate(target_rows(pos, vel)):
        for k, row in enumerate(rows):
            stage[pl.ds(k, count, stride=FEATURES), :] = row

        def place(b, carry):
            block = stage[pl.ds(pl.multiple_of(b * FEATURES, FEATURES), FEATURES), :]
            tgt[b, :, half * LANES : (half + 1) * LANES] = block.astype(jnp.bfloat16)
            return carry

        lax.fori_loop(0, count, place, 0)


def in_two(value):
    high = value.astype(jnp.bfloat16)
    return high, (value - high.astype(jnp.float32)).astype(jnp.bfloat16)


def falloff_of(dist_sq):
    guarded = jnp.maximum(dist_sq, 1e-30)
    root = guarded * lax.rsqrt(guarded)
    falloff = jnp.maximum(1.0 - root, 0.0)
    return guarded, falloff, falloff * falloff * falloff


def weighted(moments, cubed, blend):
    cubed_high, cubed_low = in_two(cubed)
    blend_high, blend_low = in_two(blend)
    weights = jnp.concatenate(
        [
            jnp.concatenate([cubed_high, blend_high], axis=1),
            jnp.concatenate([cubed_low, blend_low], axis=1),
        ],
        axis=0,
    )
    return jnp.dot(moments, weights, preferred_element_type=jnp.float32)


def pair_kernel(
    blocks, walls, own_ref, ghost_ref, wall_ref, pair_ref, wpair_ref, place_ref,
    rate_ref, accel_ref, peak_ref, stage, src, mom, rho, wsrc, wmom, tgt,
    acc_cubed, acc_blend, table,
):
    ghosts = ghost_ref.shape[0] // 8
    per_mask = ghosts // 8
    place = place_ref[0]
    for c in range(blocks):
        table[c] = c
    for mask in range(1, 8):
        for g in range(per_mask):
            table[blocks + (mask - 1) * per_mask + g] = (
                blocks + jnp.bitwise_xor(place, mask) * per_mask + g
            )
    fluid_sources(own_ref, blocks, 0, stage, src, mom, rho)
    fluid_sources(ghost_ref, ghosts, blocks, stage, src, mom, rho)
    wall_sources(wall_ref, walls, stage, wsrc, wmom)
    put_targets(own_ref, blocks, stage, tgt)

    def per_target(b, carry):
        target = tgt[b]
        target_rho = own_ref[pl.ds(b * 8 + 6, 1), :]
        total = jnp.zeros((3 * MOMENTS, 2 * LANES), jnp.float32)
        for k in range(pair_ref.shape[1]):
            s = table[pair_ref[b, k]]
            product = jnp.dot(src[s], target, preferred_element_type=jnp.float32)
            guarded, falloff, cubed = falloff_of(product[:, :LANES])
            approach = product[:, LANES:]
            spread = (guarded + shift) * (rho[s] + target_rho)
            viscous = jnp.maximum(approach, 0.0) / spread
            total += weighted(mom[s], cubed, cubed * (falloff + viscous))
        for k in range(wpair_ref.shape[1]):
            s = wpair_ref[b, k]
            product = jnp.dot(wsrc[s], target[:, :LANES], preferred_element_type=jnp.float32)
            _, falloff, cubed = falloff_of(product)
            total += weighted(wmom[s], cubed, cubed * falloff)
        folded = total[:MOMENTS] + total[MOMENTS : 2 * MOMENTS] + total[2 * MOMENTS :]
        rows = pl.ds(pl.multiple_of(b * MOMENTS, MOMENTS), MOMENTS)
        acc_cubed[rows, :] = folded[:, :LANES]
        acc_blend[rows, :] = folded[:, LANES:]
        return carry

    lax.fori_loop(0, blocks, per_target, 0)

    pos = scaled_position(own_ref, blocks, 8)
    vel = [loaded(own_ref, 3 + d, blocks, 8) for d in range(3)]
    own_press = grad_coeff * pressure_ratio(loaded(own_ref, 6, blocks, 8))

    def summed(row, ref=acc_cubed):
        return loaded(ref, row, blocks, MOMENTS)

    mass_sum = summed(8)
    mass_pos = [summed(9 + d) for d in range(3)]
    mass_vel = [summed(12 + d) for d in range(3)]
    rate = dotted(pos, vel) * mass_sum - dotted(vel, mass_pos) - dotted(pos, mass_vel) + summed(15)
    rate_ref[...] = (support * grad_coeff) * rate
    square = jnp.zeros_like(rate)
    for d in range(3):
        force = pos[d] * summed(0) - summed(1 + d)
        force += own_press * (pos[d] * summed(4) - summed(5 + d))
        force -= (4.0 * cohesion) * (pos[d] * summed(8, acc_blend) - summed(9 + d, acc_blend))
        force = -support * force
        if d == 2:
            force -= gravity
        square += force * force
        stage[pl.ds(d, blocks, stride=8), :] = force
    for b in range(blocks):
        accel_ref[:, b * LANES : (b + 1) * LANES] = stage[b * 8 : b * 8 + 3, :]
    peak_ref[...] = jnp.full(peak_ref.shape, jnp.sqrt(jnp.max(square)), jnp.float32)


def pair_pass(own, ghosts, walls, pair_list, wall_pairs, place):
    blocks = own.shape[0] // 8
    ghost_blocks = ghosts.shape[0] // 8
    wall_blocks = walls.shape[0] // 4
    total = blocks + ghost_blocks
    depth = 3 * MOMENTS
    smem = pl.BlockSpec(memory_space=pltpu.SMEM)
    vmem = pl.BlockSpec(memory_space=pltpu.VMEM)
    return pl.pallas_call(
        functools.partial(pair_kernel, blocks, wall_blocks),
        out_shape=(
            jax.ShapeDtypeStruct((blocks, LANES), jnp.float32),
            jax.ShapeDtypeStruct((3, blocks * LANES), jnp.float32),
            jax.ShapeDtypeStruct((8, LANES), jnp.float32),
        ),
        in_specs=[vmem, vmem, vmem, smem, smem, smem],
        out_specs=(vmem, vmem, vmem),
        scratch_shapes=[
            pltpu.VMEM((ghost_blocks * FEATURES, LANES), jnp.float32),
            pltpu.VMEM((total, LANES, FEATURES), jnp.bfloat16),
            pltpu.VMEM((total, depth, 2 * LANES), jnp.bfloat16),
            pltpu.VMEM((total, LANES, LANES), jnp.float32),
            pltpu.VMEM((wall_blocks, LANES, FEATURES), jnp.bfloat16),
            pltpu.VMEM((wall_blocks, depth, 2 * LANES), jnp.bfloat16),
            pltpu.VMEM((blocks, FEATURES, 2 * LANES), jnp.bfloat16),
            pltpu.VMEM((blocks * MOMENTS, LANES), jnp.float32),
            pltpu.VMEM((blocks * MOMENTS, LANES), jnp.float32),
            pltpu.SMEM((total,), jnp.int32),
        ],
        compiler_params=pltpu.CompilerParams(vmem_limit_bytes=40 * 1024 * 1024),
        name="pair_pass",
    )(own, ghosts, walls, pair_list, wall_pairs, place)


def swapped(shard, axis, bit):
    return lax.ppermute(shard, axis, [(i, i ^ 1 << bit) for i in range(lax.axis_size(axis))])


def padded(block, sides, width):
    for axis, dim in sides:
        count = lax.axis_size(axis)
        forward = [(i, i + 1) for i in range(count - 1)]
        backward = [(target, source) for source, target in forward]
        low = lax.ppermute(
            lax.slice_in_dim(block, block.shape[dim] - width, None, axis=dim), axis, forward
        )
        high = lax.ppermute(lax.slice_in_dim(block, 0, width, axis=dim), axis, backward)
        block = jnp.concatenate([low, block, high], axis=dim)
    return block


def per_device(fluid_state, ghost_list, pair_list, wall_state, wall_count, wall_pairs):
    block_total = fluid_state.shape[1] // LANES
    own_blocks = jnp.transpose(fluid_state.reshape(8, block_total, LANES), (1, 0, 2))
    place = lax.axis_index("orb") % 8
    slots = jnp.bitwise_xor(jnp.arange(8, dtype=jnp.int32), place)
    own_slot = jnp.zeros((1, ghost_list.shape[1]), jnp.int32)
    sent = own_blocks[jnp.concatenate([own_slot, ghost_list], axis=0)[slots]]
    groups = [list(range(g, g + 8)) for g in range(0, lax.axis_size("orb"), 8)]
    landed = lax.all_to_all(
        sent, "orb", 0, 0, axis_index_groups=groups if len(groups) > 1 else None
    )
    alive = (
        (jnp.arange(LANES, dtype=jnp.int32)[None, :] < wall_count[:, None])
        .astype(jnp.float32)
        .reshape(-1)
    )
    wall_live = jnp.concatenate([wall_state[0:3], wall_state[3:4] * alive[None, :]], axis=0)
    extended = padded(wall_live, (("wall", 1),), EB * LANES)
    wall_cands = jnp.transpose(extended.reshape(4, -1, LANES), (1, 0, 2))
    rate, acceleration, local_peak = pair_pass(
        own_blocks.reshape(-1, LANES),
        landed.reshape(-1, LANES),
        wall_cands.reshape(-1, LANES),
        pair_list,
        wall_pairs,
        place.reshape(1),
    )
    peak = local_peak[0, 0]
    for axis in ("wall", "orb"):
        for bit in range((lax.axis_size(axis) - 1).bit_length()):
            peak = jnp.maximum(peak, swapped(peak, axis, bit))
    time_step = courant * jnp.sqrt(smoothing / (peak + 1e-06))
    return (rate.reshape(-1), acceleration, time_step)


def solution(mesh):
    return jax.shard_map(
        per_device,
        mesh=mesh,
        in_specs=(
            P(None, ("orb", "wall")),
            P(None, ("orb", "wall")),
            P(("orb", "wall"), None),
            P(None, ("orb", "wall")),
            P(("orb", "wall")),
            P(("orb", "wall"), None),
        ),
        out_specs=(P(("orb", "wall")), P(None, ("orb", "wall")), P()),
        check_vma=False,
    )
```

```python
import functools

import jax
import jax.numpy as jnp
from jax import lax
from jax.experimental import pallas as pl
from jax.experimental.pallas import tpu as pltpu
from jax.sharding import PartitionSpec as P

EB = 1
LANES = 128
FEATURES = 64
MOMENTS = 16

smoothing = 0.1
support = 0.3
kernel_norm = 21.0 / (2.0 * 3.141592653589793 * support**3)
grad_coeff = -20.0 / support**2 * kernel_norm
tait_coeff = 25.0 / 7.0
visc_coeff = 0.05
cohesion = 2000.0
adhesion = 2000.0
gravity = 9.81
courant = 0.25

center = 0.3
shift = 0.0001 / support**2
approach_coeff = grad_coeff * visc_coeff * 2.0 / (support * 4.0 * cohesion)

SPLITS = ((0, 0), (0, 1), (1, 0), (0, 2), (2, 0), (1, 1), (1, 2), (2, 1))


def rounded(value):
    return value.astype(jnp.bfloat16).astype(jnp.float32)


def split(value):
    first = rounded(value)
    rest = value - first
    second = rounded(rest)
    return (first, second, rest - second)


def dotted(left, right):
    return left[0] * right[0] + left[1] * right[1] + left[2] * right[2]


def pressure_ratio(density):
    square = density * density
    return tait_coeff * (square * square * square * density - 1.0) / square


def loaded(ref, row, count, stride):
    return ref[pl.ds(row, count, stride=stride), :]


def scaled_position(ref, count, stride):
    return [(loaded(ref, d, count, stride) - center) * (1.0 / support) for d in range(3)]


def source_rows(pos, vel, density):
    one = jnp.ones_like(pos[0])
    rows = [one, one, one]
    rows += split(dotted(pos, pos))
    if vel is not None:
        rows += split(approach_coeff * dotted(pos, vel))
    else:
        rows += [one * 0.0] * 3
    for d in range(3):
        pieces = split(pos[d])
        rows += [pieces[t] for _, t in SPLITS]
    if vel is not None:
        for d in range(3):
            pieces = split(vel[d])
            rows += [pieces[t] for _, t in SPLITS]
    zero = one * 0.0
    rows += [zero] * (FEATURES - len(rows))
    if density is not None:
        rows[FEATURES - 1] = density
    return rows


def target_rows(pos, vel):
    one = jnp.ones_like(pos[0])
    zero = one * 0.0
    near = list(split(dotted(pos, pos))) + [one] * 3 + [zero] * 3
    along = list(split(approach_coeff * dotted(pos, vel))) + [zero] * 3 + [one] * 3
    for d in range(3):
        pieces = split(-2.0 * pos[d])
        near += [pieces[p] for p, _ in SPLITS]
        pieces = split(-approach_coeff * vel[d])
        along += [pieces[p] for p, _ in SPLITS]
    for d in range(3):
        pieces = split(-approach_coeff * pos[d])
        along += [pieces[p] for p, _ in SPLITS]
    near += [zero] * (FEATURES - len(near))
    along += [zero] * (FEATURES - len(along))
    return near, along


def moment_rows(pos, vel, mass, own, other):
    columns = [other] + [other * p for p in pos]
    columns += [own] + [own * p for p in pos]
    columns += [mass] + [mass * p for p in pos]
    if vel is not None:
        columns += [mass * v for v in vel] + [mass * dotted(pos, vel)]
    else:
        columns += [mass * 0.0] * 4
    pieces = [split(column) for column in columns]
    return [pieces[c][p] for p in range(3) for c in range(MOMENTS)]


def put_sources(rows, moments, count, base, stage, src, mom, rho):
    for k, row in enumerate(rows):
        stage[pl.ds(k, count, stride=FEATURES), :] = row

    def turn(b, carry):
        block = stage[pl.ds(pl.multiple_of(b * FEATURES, FEATURES), FEATURES), :]
        turned = block.T
        src[base + b] = turned.astype(jnp.bfloat16)
        if rho is not None:
            rho[base + b] = jnp.broadcast_to(turned[:, FEATURES - 1 :], (LANES, LANES))
        return carry

    lax.fori_loop(0, count, turn, 0)
    depth = 3 * MOMENTS
    for k, row in enumerate(moments):
        stage[pl.ds(k, count, stride=depth), :] = row

    def place(b, carry):
        block = stage[pl.ds(pl.multiple_of(b * depth, depth), depth), :].astype(jnp.bfloat16)
        mom[base + b] = jnp.concatenate([block, block], axis=1)
        return carry

    lax.fori_loop(0, count, place, 0)


def fluid_sources(ref, count, base, stage, src, mom, rho):
    pos = scaled_position(ref, count, 8)
    vel = [loaded(ref, 3 + d, count, 8) for d in range(3)]
    density = loaded(ref, 6, count, 8)
    mass = loaded(ref, 7, count, 8)
    other = mass * (3.0 * cohesion + grad_coeff * pressure_ratio(density))
    rows = source_rows(pos, vel, density)
    put_sources(rows, moment_rows(pos, vel, mass, mass, other), count, base, stage, src, mom, rho)


def wall_sources(ref, count, stage, src, mom):
    pos = scaled_position(ref, count, 4)
    mass = loaded(ref, 3, count, 4)
    rows = source_rows(pos, None, None)
    moments = moment_rows(pos, None, mass, 2.0 * mass, (3.0 * adhesion) * mass)
    put_sources(rows, moments, count, 0, stage, src, mom, None)


def put_targets(ref, count, stage, tgt):
    pos = scaled_position(ref, count, 8)
    vel = [loaded(ref, 3 + d, count, 8) for d in range(3)]
    for half, rows in enumerate(target_rows(pos, vel)):
        for k, row in enumerate(rows):
            stage[pl.ds(k, count, stride=FEATURES), :] = row

        def place(b, carry):
            block = stage[pl.ds(pl.multiple_of(b * FEATURES, FEATURES), FEATURES), :]
            tgt[b, :, half * LANES : (half + 1) * LANES] = block.astype(jnp.bfloat16)
            return carry

        lax.fori_loop(0, count, place, 0)


def in_two(value):
    high = value.astype(jnp.bfloat16)
    return high, (value - high.astype(jnp.float32)).astype(jnp.bfloat16)


def falloff_of(dist_sq):
    guarded = jnp.maximum(dist_sq, 1e-30)
    root = guarded * lax.rsqrt(guarded)
    falloff = jnp.maximum(1.0 - root, 0.0)
    return guarded, falloff, falloff * falloff * falloff


def weighted(moments, cubed, blend):
    cubed_high, cubed_low = in_two(cubed)
    blend_high, blend_low = in_two(blend)
    weights = jnp.concatenate(
        [
            jnp.concatenate([cubed_high, blend_high], axis=1),
            jnp.concatenate([cubed_low, blend_low], axis=1),
        ],
        axis=0,
    )
    return jnp.dot(moments, weights, preferred_element_type=jnp.float32)


def pair_kernel(
    blocks, walls, own_ref, ghost_ref, wall_ref, pair_ref, wpair_ref,
    rate_ref, accel_ref, peak_ref, stage, src, mom, rho, wsrc, wmom, tgt,
    acc_cubed, acc_blend,
):
    ghosts = ghost_ref.shape[0] // 8
    fluid_sources(own_ref, blocks, 0, stage, src, mom, rho)
    fluid_sources(ghost_ref, ghosts, blocks, stage, src, mom, rho)
    wall_sources(wall_ref, walls, stage, wsrc, wmom)
    put_targets(own_ref, blocks, stage, tgt)

    def per_target(b, carry):
        target = tgt[b]
        target_rho = own_ref[pl.ds(b * 8 + 6, 1), :]
        total = jnp.zeros((3 * MOMENTS, 2 * LANES), jnp.float32)
        for k in range(pair_ref.shape[1]):
            s = pair_ref[b, k]
            product = jnp.dot(src[s], target, preferred_element_type=jnp.float32)
            guarded, falloff, cubed = falloff_of(product[:, :LANES])
            approach = product[:, LANES:]
            spread = (guarded + shift) * (rho[s] + target_rho)
            viscous = jnp.maximum(approach, 0.0) * pl.reciprocal(spread, approx=True)
            total += weighted(mom[s], cubed, cubed * (falloff + viscous))
        for k in range(wpair_ref.shape[1]):
            s = wpair_ref[b, k]
            product = jnp.dot(wsrc[s], target[:, :LANES], preferred_element_type=jnp.float32)
            _, falloff, cubed = falloff_of(product)
            total += weighted(wmom[s], cubed, cubed * falloff)
        folded = total[:MOMENTS] + total[MOMENTS : 2 * MOMENTS] + total[2 * MOMENTS :]
        rows = pl.ds(pl.multiple_of(b * MOMENTS, MOMENTS), MOMENTS)
        acc_cubed[rows, :] = folded[:, :LANES]
        acc_blend[rows, :] = folded[:, LANES:]
        return carry

    lax.fori_loop(0, blocks, per_target, 0)

    pos = scaled_position(own_ref, blocks, 8)
    vel = [loaded(own_ref, 3 + d, blocks, 8) for d in range(3)]
    own_press = grad_coeff * pressure_ratio(loaded(own_ref, 6, blocks, 8))

    def summed(row, ref=acc_cubed):
        return loaded(ref, row, blocks, MOMENTS)

    mass_sum = summed(8)
    mass_pos = [summed(9 + d) for d in range(3)]
    mass_vel = [summed(12 + d) for d in range(3)]
    rate = dotted(pos, vel) * mass_sum - dotted(vel, mass_pos) - dotted(pos, mass_vel) + summed(15)
    rate_ref[...] = (support * grad_coeff) * rate
    square = jnp.zeros_like(rate)
    for d in range(3):
        force = pos[d] * summed(0) - summed(1 + d)
        force += own_press * (pos[d] * summed(4) - summed(5 + d))
        force -= (4.0 * cohesion) * (pos[d] * summed(8, acc_blend) - summed(9 + d, acc_blend))
        force = -support * force
        if d == 2:
            force -= gravity
        square += force * force
        stage[pl.ds(d, blocks, stride=8), :] = force
    for b in range(blocks):
        accel_ref[:, b * LANES : (b + 1) * LANES] = stage[b * 8 : b * 8 + 3, :]
    peak_ref[...] = jnp.full(peak_ref.shape, jnp.sqrt(jnp.max(square)), jnp.float32)


def pair_pass(own, ghosts, walls, pair_list, wall_pairs):
    blocks = own.shape[0] // 8
    ghost_blocks = ghosts.shape[0] // 8
    wall_blocks = walls.shape[0] // 4
    total = blocks + ghost_blocks
    depth = 3 * MOMENTS
    smem = pl.BlockSpec(memory_space=pltpu.SMEM)
    vmem = pl.BlockSpec(memory_space=pltpu.VMEM)
    return pl.pallas_call(
        functools.partial(pair_kernel, blocks, wall_blocks),
        out_shape=(
            jax.ShapeDtypeStruct((blocks, LANES), jnp.float32),
            jax.ShapeDtypeStruct((3, blocks * LANES), jnp.float32),
            jax.ShapeDtypeStruct((8, LANES), jnp.float32),
        ),
        in_specs=[vmem, vmem, vmem, smem, smem],
        out_specs=(vmem, vmem, vmem),
        scratch_shapes=[
            pltpu.VMEM((ghost_blocks * FEATURES, LANES), jnp.float32),
            pltpu.VMEM((total, LANES, FEATURES), jnp.bfloat16),
            pltpu.VMEM((total, depth, 2 * LANES), jnp.bfloat16),
            pltpu.VMEM((total, LANES, LANES), jnp.float32),
            pltpu.VMEM((wall_blocks, LANES, FEATURES), jnp.bfloat16),
            pltpu.VMEM((wall_blocks, depth, 2 * LANES), jnp.bfloat16),
            pltpu.VMEM((blocks, FEATURES, 2 * LANES), jnp.bfloat16),
            pltpu.VMEM((blocks * MOMENTS, LANES), jnp.float32),
            pltpu.VMEM((blocks * MOMENTS, LANES), jnp.float32),
        ],
        compiler_params=pltpu.CompilerParams(vmem_limit_bytes=40 * 1024 * 1024),
        name="pair_pass",
    )(own, ghosts, walls, pair_list, wall_pairs)


def swapped(shard, axis, bit):
    return lax.ppermute(shard, axis, [(i, i ^ 1 << bit) for i in range(lax.axis_size(axis))])


def padded(block, sides, width):
    for axis, dim in sides:
        count = lax.axis_size(axis)
        forward = [(i, i + 1) for i in range(count - 1)]
        backward = [(target, source) for source, target in forward]
        low = lax.ppermute(
            lax.slice_in_dim(block, block.shape[dim] - width, None, axis=dim), axis, forward
        )
        high = lax.ppermute(lax.slice_in_dim(block, 0, width, axis=dim), axis, backward)
        block = jnp.concatenate([low, block, high], axis=dim)
    return block


def per_device(fluid_state, ghost_list, pair_list, wall_state, wall_count, wall_pairs):
    block_total = fluid_state.shape[1] // LANES
    own_blocks = jnp.transpose(fluid_state.reshape(8, block_total, LANES), (1, 0, 2))
    place = lax.axis_index("orb") % 8
    groups = [list(range(g, g + 8)) for g in range(0, lax.axis_size("orb"), 8)]
    groups = groups if len(groups) > 1 else None
    everyone = lax.all_gather(own_blocks, "orb", axis_index_groups=groups)
    lists = lax.all_gather(ghost_list, "orb", axis_index_groups=groups)
    partners = jnp.bitwise_xor(jnp.arange(8, dtype=jnp.int32), place)
    chosen = lists[partners[1:], jnp.arange(7, dtype=jnp.int32)]
    landed = everyone[partners[1:, None], chosen]
    alive = (
        (jnp.arange(LANES, dtype=jnp.int32)[None, :] < wall_count[:, None])
        .astype(jnp.float32)
        .reshape(-1)
    )
    wall_live = jnp.concatenate([wall_state[0:3], wall_state[3:4] * alive[None, :]], axis=0)
    extended = padded(wall_live, (("wall", 1),), EB * LANES)
    wall_cands = jnp.transpose(extended.reshape(4, -1, LANES), (1, 0, 2))
    rate, acceleration, local_peak = pair_pass(
        own_blocks.reshape(-1, LANES),
        landed.reshape(-1, LANES),
        wall_cands.reshape(-1, LANES),
        pair_list,
        wall_pairs,
    )
    peak = jnp.max(lax.all_gather(local_peak[:1], ("orb", "wall")))
    time_step = courant * jnp.sqrt(smoothing / (peak + 1e-06))
    return (rate.reshape(-1), acceleration, time_step)


def solution(mesh):
    return jax.shard_map(
        per_device,
        mesh=mesh,
        in_specs=(
            P(None, ("orb", "wall")),
            P(None, ("orb", "wall")),
            P(("orb", "wall"), None),
            P(None, ("orb", "wall")),
            P(("orb", "wall")),
            P(("orb", "wall"), None),
        ),
        out_specs=(P(("orb", "wall")), P(None, ("orb", "wall")), P()),
        check_vma=False,
    )
```

```python
import functools

import jax
import jax.numpy as jnp
from jax import lax
from jax.experimental import pallas as pl
from jax.experimental.pallas import tpu as pltpu
from jax.sharding import PartitionSpec as P

EB = 1
LANES = 128
FEATURES = 64
MOMENTS = 16
CHUNK = 16

smoothing = 0.1
support = 0.3
kernel_norm = 21.0 / (2.0 * 3.141592653589793 * support**3)
grad_coeff = -20.0 / support**2 * kernel_norm
tait_coeff = 25.0 / 7.0
visc_coeff = 0.05
cohesion = 2000.0
adhesion = 2000.0
gravity = 9.81
courant = 0.25

center = 0.3
shift = 0.0001 / support**2
approach_coeff = grad_coeff * visc_coeff * 2.0 / (support * 4.0 * cohesion)

SPLITS = ((0, 0), (0, 1), (1, 0), (0, 2), (2, 0), (1, 1), (1, 2), (2, 1))


def rounded(value):
    return value.astype(jnp.bfloat16).astype(jnp.float32)


def split(value):
    first = rounded(value)
    rest = value - first
    second = rounded(rest)
    return (first, second, rest - second)


def dotted(left, right):
    return left[0] * right[0] + left[1] * right[1] + left[2] * right[2]


def pressure_ratio(density):
    square = density * density
    return tait_coeff * (square * square * square * density - 1.0) / square


def loaded(ref, row, count, stride):
    return ref[pl.ds(row, count, stride=stride), :]


def scaled_position(ref, count, stride):
    return [(loaded(ref, d, count, stride) - center) * (1.0 / support) for d in range(3)]


def source_rows(pos, vel, density):
    one = jnp.ones_like(pos[0])
    rows = [one, one, one]
    rows += split(dotted(pos, pos))
    if vel is not None:
        rows += split(approach_coeff * dotted(pos, vel))
    else:
        rows += [one * 0.0] * 3
    for d in range(3):
        pieces = split(pos[d])
        rows += [pieces[t] for _, t in SPLITS]
    if vel is not None:
        for d in range(3):
            pieces = split(vel[d])
            rows += [pieces[t] for _, t in SPLITS]
    zero = one * 0.0
    rows += [zero] * (FEATURES - len(rows))
    if density is not None:
        rows[FEATURES - 1] = density
    return rows


def target_rows(pos, vel):
    one = jnp.ones_like(pos[0])
    zero = one * 0.0
    near = list(split(dotted(pos, pos))) + [one] * 3 + [zero] * 3
    along = list(split(approach_coeff * dotted(pos, vel))) + [zero] * 3 + [one] * 3
    for d in range(3):
        pieces = split(-2.0 * pos[d])
        near += [pieces[p] for p, _ in SPLITS]
        pieces = split(-approach_coeff * vel[d])
        along += [pieces[p] for p, _ in SPLITS]
    for d in range(3):
        pieces = split(-approach_coeff * pos[d])
        along += [pieces[p] for p, _ in SPLITS]
    near += [zero] * (FEATURES - len(near))
    along += [zero] * (FEATURES - len(along))
    return near, along


def moment_rows(pos, vel, mass, own, other):
    columns = [other] + [other * p for p in pos]
    columns += [own] + [own * p for p in pos]
    columns += [mass] + [mass * p for p in pos]
    if vel is not None:
        columns += [mass * v for v in vel] + [mass * dotted(pos, vel)]
    else:
        columns += [mass * 0.0] * 4
    pieces = [split(column) for column in columns]
    return [pieces[c][p] for p in range(3) for c in range(MOMENTS)]


def put_sources(rows, moments, count, base, stage, src, mom, rho):
    for k, row in enumerate(rows):
        stage[pl.ds(k, count, stride=FEATURES), :] = row

    def turn(b, carry):
        block = stage[pl.ds(pl.multiple_of(b * FEATURES, FEATURES), FEATURES), :]
        turned = block.T
        src[base + b] = turned.astype(jnp.bfloat16)
        if rho is not None:
            rho[base + b] = jnp.broadcast_to(turned[:, FEATURES - 1 :], (LANES, LANES))
        return carry

    lax.fori_loop(0, count, turn, 0)
    depth = 3 * MOMENTS
    for k, row in enumerate(moments):
        stage[pl.ds(k, count, stride=depth), :] = row

    def place(b, carry):
        block = stage[pl.ds(pl.multiple_of(b * depth, depth), depth), :].astype(jnp.bfloat16)
        mom[base + b] = jnp.concatenate([block, block], axis=1)
        return carry

    lax.fori_loop(0, count, place, 0)


def fluid_sources(ref, count, base, stage, src, mom, rho):
    pos = scaled_position(ref, count, 8)
    vel = [loaded(ref, 3 + d, count, 8) for d in range(3)]
    density = loaded(ref, 6, count, 8)
    mass = loaded(ref, 7, count, 8)
    other = mass * (3.0 * cohesion + grad_coeff * pressure_ratio(density))
    rows = source_rows(pos, vel, density)
    put_sources(rows, moment_rows(pos, vel, mass, mass, other), count, base, stage, src, mom, rho)


def wall_sources(ref, count, stage, src, mom):
    pos = scaled_position(ref, count, 4)
    mass = loaded(ref, 3, count, 4)
    rows = source_rows(pos, None, None)
    moments = moment_rows(pos, None, mass, 2.0 * mass, (3.0 * adhesion) * mass)
    put_sources(rows, moments, count, 0, stage, src, mom, None)


def put_targets(ref, count, stage, tgt):
    pos = scaled_position(ref, count, 8)
    vel = [loaded(ref, 3 + d, count, 8) for d in range(3)]
    for half, rows in enumerate(target_rows(pos, vel)):
        for k, row in enumerate(rows):
            stage[pl.ds(k, count, stride=FEATURES), :] = row

        def place(b, carry):
            block = stage[pl.ds(pl.multiple_of(b * FEATURES, FEATURES), FEATURES), :]
            tgt[b, :, half * LANES : (half + 1) * LANES] = block.astype(jnp.bfloat16)
            return carry

        lax.fori_loop(0, count, place, 0)


def in_two(value):
    high = value.astype(jnp.bfloat16)
    return high, (value - high.astype(jnp.float32)).astype(jnp.bfloat16)


def falloff_of(dist_sq):
    guarded = jnp.maximum(dist_sq, 1e-30)
    root = guarded * lax.rsqrt(guarded)
    falloff = jnp.maximum(1.0 - root, 0.0)
    return guarded, falloff, falloff * falloff * falloff


def put_weights(weights, first, cubed, blend):
    rows = cubed.shape[0]
    for half, value in enumerate((cubed, blend)):
        lanes = slice(half * LANES, (half + 1) * LANES)
        high, low = in_two(value)
        weights[first : first + rows, lanes] = high
        weights[LANES + first : LANES + first + rows, lanes] = low


def fluid_weights(product, weights, rho_j, rho_i):
    for first in range(0, LANES, CHUNK):
        rows = slice(first, first + CHUNK)
        guarded, falloff, cubed = falloff_of(product[rows, :LANES])
        spread = (guarded + shift) * (rho_j[rows, :] + rho_i)
        viscous = jnp.maximum(product[rows, LANES:], 0.0) * pl.reciprocal(spread, approx=True)
        put_weights(weights, first, cubed, cubed * (falloff + viscous))


def wall_weights(product, weights):
    for first in range(0, LANES, CHUNK):
        _, falloff, cubed = falloff_of(product[first : first + CHUNK, :LANES])
        put_weights(weights, first, cubed, cubed * falloff)


def listed(pair_ref, keep, source_of, sources, targets, trash):
    blocks, width = pair_ref.shape

    def put(at, source, target):
        sources[at] = source
        targets[at] = target

    put(0, 0, trash)

    def row(b, count):
        for k in range(width):
            candidate = pair_ref[b, k]
            put(count + 1, source_of(candidate), b)
            count += keep(candidate)
        return count

    count = lax.fori_loop(0, blocks, row, 0)
    for extra in range(1, 4):
        put(count + extra, 0, trash)
    return count


def run_pairs(count, sources, targets, blocks, first, second, third):
    def at(t):
        target = targets[t + 1]
        return sources[t + 1], jnp.minimum(target, blocks - 1), target

    first(0, *at(0)[:2])

    def steps(i, carry):
        for slot in range(2):
            t = 2 * i + slot
            first(1 - slot, *at(t + 1)[:2])
            second(slot, *at(t)[:2])
            source, _, target = at(t - 1)
            third(1 - slot, source, target)
        return carry

    pairs = (count + 1) // 2
    lax.fori_loop(0, pairs, steps, 0)
    source, _, target = at(2 * pairs - 1)
    third(1, source, target)


def stages(own_ref, src, mom, rho, tgt, acc, products, weights):
    def first(slot, s, b):
        if rho is not None:
            products[slot][...] = jnp.dot(src[s], tgt[b], preferred_element_type=jnp.float32)
        else:
            products[slot][:, :LANES] = jnp.dot(
                src[s], tgt[b, :, :LANES], preferred_element_type=jnp.float32
            )

    def second(slot, s, b):
        if rho is not None:
            rho_i = own_ref[pl.ds(b * 8 + 6, 1), :]
            fluid_weights(products[slot], weights[slot], rho.at[s], rho_i)
        else:
            wall_weights(products[slot], weights[slot])

    def third(slot, s, b):
        acc[b] += jnp.dot(mom[s], weights[slot][...], preferred_element_type=jnp.float32)

    return first, second, third


def folded(acc, b):
    total = acc[b]
    return total[:MOMENTS] + total[MOMENTS : 2 * MOMENTS] + total[2 * MOMENTS :]


def own_kernel(
    blocks, own_ref, pair_ref, tgt, sum_cubed, sum_blend,
    stage, src, mom, rho, acc, product0, product1, weight0, weight1, sources, targets,
):
    count = listed(
        pair_ref, lambda c: (c < blocks).astype(jnp.int32), lambda c: jnp.minimum(c, blocks - 1),
        sources, targets, blocks,
    )
    fluid_sources(own_ref, blocks, 0, stage, src, mom, rho)
    put_targets(own_ref, blocks, stage, tgt)
    acc[...] = jnp.zeros_like(acc)
    parts = stages(
        own_ref, src, mom, rho, tgt, acc, (product0, product1), (weight0, weight1)
    )
    run_pairs(count, sources, targets, blocks, *parts)

    def fold(b, carry):
        total = folded(acc, b)
        rows = pl.ds(pl.multiple_of(b * MOMENTS, MOMENTS), MOMENTS)
        sum_cubed[rows, :] = total[:, :LANES]
        sum_blend[rows, :] = total[:, LANES:]
        return carry

    lax.fori_loop(0, blocks, fold, 0)


def ghost_kernel(
    blocks, walls, own_ref, ghost_ref, wall_ref, pair_ref, wpair_ref, place_ref, tgt, own_cubed,
    own_blend, rate_ref, accel_ref, peak_ref, stage, src, mom, rho, wsrc, wmom, acc,
    acc_cubed, acc_blend, product0, product1, weight0, weight1, sources, targets, wsources,
    wtargets, table,
):
    ghosts = ghost_ref.shape[0] // 8
    per_mask = ghosts // 8
    for c in range(blocks):
        table[c] = 0
    for mask in range(1, 8):
        for g in range(per_mask):
            table[blocks + (mask - 1) * per_mask + g] = (
                jnp.bitwise_xor(place_ref[0], mask) * per_mask + g
            )
    count = listed(
        pair_ref, lambda c: (c >= blocks).astype(jnp.int32), lambda c: table[c],
        sources, targets, blocks,
    )
    wcount = listed(wpair_ref, lambda c: 1, lambda c: c, wsources, wtargets, blocks)
    fluid_sources(ghost_ref, ghosts, 0, stage, src, mom, rho)
    wall_sources(wall_ref, walls, stage, wsrc, wmom)
    acc[...] = jnp.zeros_like(acc)
    buffers = ((product0, product1), (weight0, weight1))
    parts = stages(own_ref, src, mom, rho, tgt, acc, *buffers)
    run_pairs(count, sources, targets, blocks, *parts)
    parts = stages(own_ref, wsrc, wmom, None, tgt, acc, *buffers)
    run_pairs(wcount, wsources, wtargets, blocks, *parts)

    def fold(b, carry):
        total = folded(acc, b)
        rows = pl.ds(pl.multiple_of(b * MOMENTS, MOMENTS), MOMENTS)
        acc_cubed[rows, :] = own_cubed[rows, :] + total[:, :LANES]
        acc_blend[rows, :] = own_blend[rows, :] + total[:, LANES:]
        return carry

    lax.fori_loop(0, blocks, fold, 0)
    finish(blocks, own_ref, acc_cubed, acc_blend, stage, rate_ref, accel_ref, peak_ref)


def finish(blocks, own_ref, acc_cubed, acc_blend, stage, rate_ref, accel_ref, peak_ref):
    pos = scaled_position(own_ref, blocks, 8)
    vel = [loaded(own_ref, 3 + d, blocks, 8) for d in range(3)]
    own_press = grad_coeff * pressure_ratio(loaded(own_ref, 6, blocks, 8))

    def summed(row, ref=acc_cubed):
        return loaded(ref, row, blocks, MOMENTS)

    mass_sum = summed(8)
    mass_pos = [summed(9 + d) for d in range(3)]
    mass_vel = [summed(12 + d) for d in range(3)]
    rate = dotted(pos, vel) * mass_sum - dotted(vel, mass_pos) - dotted(pos, mass_vel) + summed(15)
    rate_ref[...] = (support * grad_coeff) * rate
    square = jnp.zeros_like(rate)
    for d in range(3):
        force = pos[d] * summed(0) - summed(1 + d)
        force += own_press * (pos[d] * summed(4) - summed(5 + d))
        force -= (4.0 * cohesion) * (pos[d] * summed(8, acc_blend) - summed(9 + d, acc_blend))
        force = -support * force
        if d == 2:
            force -= gravity
        square += force * force
        stage[pl.ds(d, blocks, stride=8), :] = force
    for b in range(blocks):
        accel_ref[:, b * LANES : (b + 1) * LANES] = stage[b * 8 : b * 8 + 3, :]
    peak_ref[...] = jnp.full(peak_ref.shape, jnp.sqrt(jnp.max(square)), jnp.float32)


def buffers_for(sources, blocks):
    depth = 3 * MOMENTS
    wide = pltpu.VMEM((LANES, 2 * LANES), jnp.float32)
    square = pltpu.VMEM((2 * LANES, 2 * LANES), jnp.bfloat16)
    return (
        [
            pltpu.VMEM((max(sources, blocks) * FEATURES, LANES), jnp.float32),
            pltpu.VMEM((sources, LANES, FEATURES), jnp.bfloat16),
            pltpu.VMEM((sources, depth, 2 * LANES), jnp.bfloat16),
            pltpu.VMEM((sources, LANES, LANES), jnp.float32),
        ],
        pltpu.VMEM((blocks + 1, depth, 2 * LANES), jnp.float32),
        [wide, wide, square, square],
    )


def tile_cost(tiles):
    return pl.CostEstimate(
        flops=tiles * LANES * LANES * 1000, bytes_accessed=0, transcendentals=0
    )


SMEM = pl.BlockSpec(memory_space=pltpu.SMEM)
VMEM = pl.BlockSpec(memory_space=pltpu.VMEM)
PARAMS = pltpu.CompilerParams(vmem_limit_bytes=40 * 1024 * 1024)


def own_pass(own, pair_list):
    blocks = own.shape[0] // 8
    entries = pair_list.size + 4
    sums = jax.ShapeDtypeStruct((blocks * MOMENTS, LANES), jnp.float32)
    features, acc, buffers = buffers_for(blocks, blocks)
    return pl.pallas_call(
        functools.partial(own_kernel, blocks),
        out_shape=(
            jax.ShapeDtypeStruct((blocks, FEATURES, 2 * LANES), jnp.bfloat16), sums, sums,
        ),
        in_specs=[VMEM, SMEM],
        out_specs=(VMEM, VMEM, VMEM),
        scratch_shapes=features + [acc] + buffers + [pltpu.SMEM((entries,), jnp.int32)] * 2,
        compiler_params=PARAMS,
        cost_estimate=tile_cost(pair_list.size),
        name="own_pass",
    )(own, pair_list)


def ghost_pass(own, ghosts, walls, pair_list, wall_pairs, place, tgt, cubed, blend):
    blocks = own.shape[0] // 8
    ghost_blocks = ghosts.shape[0] // 8
    wall_blocks = walls.shape[0] // 4
    depth = 3 * MOMENTS
    features, acc, buffers = buffers_for(ghost_blocks, blocks)
    sums = pltpu.VMEM((blocks * MOMENTS, LANES), jnp.float32)
    return pl.pallas_call(
        functools.partial(ghost_kernel, blocks, wall_blocks),
        out_shape=(
            jax.ShapeDtypeStruct((blocks, LANES), jnp.float32),
            jax.ShapeDtypeStruct((3, blocks * LANES), jnp.float32),
            jax.ShapeDtypeStruct((8, LANES), jnp.float32),
        ),
        in_specs=[VMEM, VMEM, VMEM, SMEM, SMEM, SMEM, VMEM, VMEM, VMEM],
        out_specs=(VMEM, VMEM, VMEM),
        scratch_shapes=features
        + [
            pltpu.VMEM((wall_blocks, LANES, FEATURES), jnp.bfloat16),
            pltpu.VMEM((wall_blocks, depth, 2 * LANES), jnp.bfloat16),
            acc,
            sums,
            sums,
        ]
        + buffers
        + [pltpu.SMEM((pair_list.size + 4,), jnp.int32)] * 2
        + [pltpu.SMEM((wall_pairs.size + 4,), jnp.int32)] * 2
        + [pltpu.SMEM((blocks + ghost_blocks,), jnp.int32)],
        compiler_params=PARAMS,
        cost_estimate=tile_cost(pair_list.size),
        name="ghost_pass",
    )(own, ghosts, walls, pair_list, wall_pairs, place, tgt, cubed, blend)


def padded(block, sides, width):
    for axis, dim in sides:
        count = lax.axis_size(axis)
        forward = [(i, i + 1) for i in range(count - 1)]
        backward = [(target, source) for source, target in forward]
        low = lax.ppermute(
            lax.slice_in_dim(block, block.shape[dim] - width, None, axis=dim), axis, forward
        )
        high = lax.ppermute(lax.slice_in_dim(block, 0, width, axis=dim), axis, backward)
        block = jnp.concatenate([low, block, high], axis=dim)
    return block


def per_device(fluid_state, ghost_list, pair_list, wall_state, wall_count, wall_pairs):
    block_total = fluid_state.shape[1] // LANES
    own_blocks = jnp.transpose(fluid_state.reshape(8, block_total, LANES), (1, 0, 2))
    place = lax.axis_index("orb") % 8
    masks = jnp.bitwise_xor(jnp.arange(8, dtype=jnp.int32), place)
    sent = own_blocks[ghost_list[jnp.maximum(masks - 1, 0)]]
    groups = [list(range(g, g + 8)) for g in range(0, lax.axis_size("orb"), 8)]
    landed = lax.all_to_all(
        sent, "orb", 0, 0, axis_index_groups=groups if len(groups) > 1 else None
    )
    alive = (
        (jnp.arange(LANES, dtype=jnp.int32)[None, :] < wall_count[:, None])
        .astype(jnp.float32)
        .reshape(-1)
    )
    wall_live = jnp.concatenate([wall_state[0:3], wall_state[3:4] * alive[None, :]], axis=0)
    extended = padded(wall_live, (("wall", 1),), EB * LANES)
    wall_cands = jnp.transpose(extended.reshape(4, -1, LANES), (1, 0, 2))
    own = own_blocks.reshape(-1, LANES)
    own_sums = own_pass(own, pair_list)
    rate, acceleration, local_peak = ghost_pass(
        own,
        landed.reshape(-1, LANES),
        wall_cands.reshape(-1, LANES),
        pair_list,
        wall_pairs,
        place.reshape(1),
        *own_sums,
    )
    peak = local_peak[:1]
    for axis in ("wall", "orb"):
        copies = jnp.broadcast_to(peak, (lax.axis_size(axis), 1, LANES))
        peak = jnp.max(lax.all_to_all(copies, axis, 0, 0), axis=0)
    peak = peak[0, 0]
    time_step = courant * jnp.sqrt(smoothing / (peak + 1e-06))
    return (rate.reshape(-1), acceleration, time_step)


def solution(mesh):
    return jax.shard_map(
        per_device,
        mesh=mesh,
        in_specs=(
            P(None, ("orb", "wall")),
            P(None, ("orb", "wall")),
            P(("orb", "wall"), None),
            P(None, ("orb", "wall")),
            P(("orb", "wall")),
            P(("orb", "wall"), None),
        ),
        out_specs=(P(("orb", "wall")), P(None, ("orb", "wall")), P()),
        check_vma=False,
    )
```

```python
import functools

import jax
import jax.numpy as jnp
from jax import lax
from jax.experimental import pallas as pl
from jax.experimental.pallas import tpu as pltpu
from jax.sharding import PartitionSpec as P

EB = 1
LANES = 128
FEATURES = 64
MOMENTS = 16
CHUNK = 16

smoothing = 0.1
support = 0.3
kernel_norm = 21.0 / (2.0 * 3.141592653589793 * support**3)
grad_coeff = -20.0 / support**2 * kernel_norm
tait_coeff = 25.0 / 7.0
visc_coeff = 0.05
cohesion = 2000.0
adhesion = 2000.0
gravity = 9.81
courant = 0.25

center = 0.3
shift = 0.0001 / support**2
approach_coeff = grad_coeff * visc_coeff * 2.0 / (support * 4.0 * cohesion)
press_coeff = -grad_coeff / (4.0 * cohesion)

SPLITS = ((0, 0), (0, 1), (1, 0), (0, 2), (2, 0), (1, 1), (1, 2), (2, 1))


def rounded(value):
    return value.astype(jnp.bfloat16).astype(jnp.float32)


def split(value):
    first = rounded(value)
    rest = value - first
    second = rounded(rest)
    return (first, second, rest - second)


def dotted(left, right):
    return left[0] * right[0] + left[1] * right[1] + left[2] * right[2]


def pressure_ratio(density):
    square = density * density
    return tait_coeff * (square * square * square * density - 1.0) / square


def loaded(ref, row, count, stride):
    return ref[pl.ds(row, count, stride=stride), :]


def scaled_position(ref, count, stride):
    return [(loaded(ref, d, count, stride) - center) * (1.0 / support) for d in range(3)]


def source_rows(pos, vel, extras):
    one = jnp.ones_like(pos[0])
    zero = one * 0.0
    rows = [one, one, one]
    rows += split(dotted(pos, pos))
    rows += split(approach_coeff * dotted(pos, vel)) if vel is not None else [zero] * 3
    for part in (pos, vel) if vel is not None else (pos,):
        for value in part:
            pieces = split(value)
            rows += [pieces[t] for _, t in SPLITS]
    return rows + [zero] * (FEATURES - len(rows) - len(extras)) + extras


def target_rows(pos, vel):
    one = jnp.ones_like(pos[0])
    zero = one * 0.0
    near = list(split(dotted(pos, pos))) + [one] * 3 + [zero] * 3
    along = list(split(approach_coeff * dotted(pos, vel))) + [zero] * 3 + [one] * 3
    for d in range(3):
        pieces = split(-2.0 * pos[d])
        near += [pieces[p] for p, _ in SPLITS]
        pieces = split(-approach_coeff * vel[d])
        along += [pieces[p] for p, _ in SPLITS]
    for d in range(3):
        pieces = split(-approach_coeff * pos[d])
        along += [pieces[p] for p, _ in SPLITS]
    near += [zero] * (FEATURES - len(near))
    along += [zero] * (FEATURES - len(along))
    return near, along


def moment_rows(pos, mass):
    pieces = [split(column) for column in [mass] + [mass * p for p in pos]]
    rows = [piece[p] for p in range(3) for piece in pieces]
    return rows + [mass * 0.0] * (MOMENTS - len(rows))


def put_sources(rows, moments, count, base, extras, stage, src, mom, wide):
    for k, row in enumerate(rows):
        stage[pl.ds(k, count, stride=FEATURES), :] = row

    def turn(b, carry):
        block = stage[pl.ds(pl.multiple_of(b * FEATURES, FEATURES), FEATURES), :]
        turned = block.T
        src[base + b] = turned.astype(jnp.bfloat16)
        for n in range(extras):
            lane = FEATURES - extras + n
            wide[base + b, n] = jnp.broadcast_to(turned[:, lane : lane + 1], (LANES, LANES))
        return carry

    lax.fori_loop(0, count, turn, 0)
    for k, row in enumerate(moments):
        stage[pl.ds(k, count, stride=MOMENTS), :] = row

    def place(b, carry):
        block = stage[pl.ds(pl.multiple_of(b * MOMENTS, MOMENTS), MOMENTS), :]
        mom[base + b] = block.astype(jnp.bfloat16)
        return carry

    lax.fori_loop(0, count, place, 0)


def fluid_sources(ref, count, base, stage, src, mom, wide):
    pos = scaled_position(ref, count, 8)
    vel = [loaded(ref, 3 + d, count, 8) for d in range(3)]
    density = loaded(ref, 6, count, 8)
    mass = loaded(ref, 7, count, 8)
    extras = [mass, density, press_coeff * pressure_ratio(density) - 0.75]
    rows = source_rows(pos, vel, extras)
    put_sources(rows, moment_rows(pos, mass), count, base, 3, stage, src, mom, wide)


def wall_sources(ref, count, stage, src, mom, wide):
    pos = scaled_position(ref, count, 4)
    mass = loaded(ref, 3, count, 4)
    rows = source_rows(pos, None, [mass])
    moments = moment_rows(pos, (adhesion / cohesion) * mass)
    put_sources(rows, moments, count, 0, 1, stage, src, mom, wide)


def put_targets(ref, count, stage, tgt):
    pos = scaled_position(ref, count, 8)
    vel = [loaded(ref, 3 + d, count, 8) for d in range(3)]
    for half, rows in enumerate(target_rows(pos, vel)):
        for k, row in enumerate(rows):
            stage[pl.ds(k, count, stride=FEATURES), :] = row

        def place(b, carry):
            block = stage[pl.ds(pl.multiple_of(b * FEATURES, FEATURES), FEATURES), :]
            tgt[b, :, half * LANES : (half + 1) * LANES] = block.astype(jnp.bfloat16)
            return carry

        lax.fori_loop(0, count, place, 0)


def in_two(value):
    high = value.astype(jnp.bfloat16)
    return high, (value - high.astype(jnp.float32)).astype(jnp.bfloat16)


def falloff_of(dist_sq):
    guarded = jnp.maximum(dist_sq, 1e-30)
    root = guarded * lax.rsqrt(guarded)
    falloff = jnp.maximum(1.0 - root, 0.0)
    return guarded, falloff, falloff * falloff * falloff


def weights_of(product, press_i, rho_i, wide):
    highs, lows = [], []
    rate = jnp.zeros((8, LANES), jnp.float32)
    for first in range(0, LANES, CHUNK):
        rows = slice(first, first + CHUNK)
        approach = product[rows, LANES:]
        guarded, falloff, cubed = falloff_of(product[rows, :LANES])
        blend = falloff + press_i
        if rho_i is not None:
            spread = (guarded + shift) * (wide[1, rows, :] + rho_i)
            blend += wide[2, rows, :]
            blend += jnp.maximum(approach, 0.0) * pl.reciprocal(spread, approx=True)
        high, low = in_two(cubed * blend)
        highs.append(high)
        lows.append(low)
        part = (cubed * approach) * wide[0, rows, :]
        for n in range(0, CHUNK, 8):
            rate += part[n : n + 8]
    halves = [jnp.concatenate(pieces, axis=0) for pieces in (highs, lows)]
    return jnp.concatenate(halves, axis=1), rate


def pair_kernel(
    blocks, walls, own_ref, ghost_ref, wall_ref, pair_ref, wpair_ref, place_ref,
    rate_ref, accel_ref, peak_ref, stage, src, mom, wide, wsrc, wmom, wwide, tgt, press, sums,
    rates, table,
):
    ghosts = ghost_ref.shape[0] // 8
    per_mask = ghosts // 8
    for c in range(blocks):
        table[c] = c
    for mask in range(1, 8):
        for g in range(per_mask):
            table[blocks + (mask - 1) * per_mask + g] = (
                blocks + jnp.bitwise_xor(place_ref[0], mask) * per_mask + g
            )
    fluid_sources(own_ref, blocks, 0, stage, src, mom, wide)
    fluid_sources(ghost_ref, ghosts, blocks, stage, src, mom, wide)
    wall_sources(wall_ref, walls, stage, wsrc, wmom, wwide)
    put_targets(own_ref, blocks, stage, tgt)
    press[...] = press_coeff * pressure_ratio(loaded(own_ref, 6, blocks, 8))

    def per_target(b, carry):
        target = tgt[b]
        rho_i = own_ref[pl.ds(b * 8 + 6, 1), :]
        press_i = press[pl.ds(b, 1), :]
        wall_press = (2.0 * cohesion / adhesion) * press_i - 0.75
        tiles = []
        for k in range(pair_ref.shape[1]):
            s = table[pair_ref[b, k]]
            tiles.append((src.at[s], mom.at[s], wide.at[s], press_i, rho_i))
        for k in range(wpair_ref.shape[1]):
            s = wpair_ref[b, k]
            tiles.append((wsrc.at[s], wmom.at[s], wwide.at[s], wall_press, None))

        def product_of(tile):
            return jnp.dot(tile[0][...], target, preferred_element_type=jnp.float32)

        total = jnp.zeros((MOMENTS, 2 * LANES), jnp.float32)
        rate = jnp.zeros((8, LANES), jnp.float32)
        ahead = product_of(tiles[0])
        waiting = None
        for n, (_, moments, spread, tile_press, tile_rho) in enumerate(tiles):
            product = ahead
            if n + 1 < len(tiles):
                ahead = product_of(tiles[n + 1])
            weights, part = weights_of(product, tile_press, tile_rho, spread)
            rate += part
            if waiting is not None:
                total += jnp.dot(*waiting, preferred_element_type=jnp.float32)
            waiting = (moments[...], weights)
        total += jnp.dot(*waiting, preferred_element_type=jnp.float32)
        rows = pl.ds(pl.multiple_of(b * MOMENTS, MOMENTS), MOMENTS)
        sums[rows, :] = total[:, :LANES] + total[:, LANES:]
        rates[pl.ds(pl.multiple_of(b * 8, 8), 8), :] = rate
        return carry

    lax.fori_loop(0, blocks, per_target, 0)

    pos = scaled_position(own_ref, blocks, 8)
    rate = loaded(rates, 0, blocks, 8)
    for n in range(1, 8):
        rate += loaded(rates, n, blocks, 8)
    rate_ref[...] = (support * grad_coeff / approach_coeff) * rate

    def summed(column):
        parts = [loaded(sums, p * 4 + column, blocks, MOMENTS) for p in range(3)]
        return parts[0] + parts[1] + parts[2]

    mass_sum = summed(0)
    square = jnp.zeros_like(rate)
    for d in range(3):
        force = (4.0 * cohesion * support) * (pos[d] * mass_sum - summed(1 + d))
        if d == 2:
            force -= gravity
        square += force * force
        stage[pl.ds(d, blocks, stride=8), :] = force
    for b in range(blocks):
        accel_ref[:, b * LANES : (b + 1) * LANES] = stage[b * 8 : b * 8 + 3, :]
    peak_ref[...] = jnp.full(peak_ref.shape, jnp.sqrt(jnp.max(square)), jnp.float32)


def pair_pass(own, ghosts, walls, pair_list, wall_pairs, place):
    blocks = own.shape[0] // 8
    ghost_blocks = ghosts.shape[0] // 8
    wall_blocks = walls.shape[0] // 4
    total = blocks + ghost_blocks
    smem = pl.BlockSpec(memory_space=pltpu.SMEM)
    vmem = pl.BlockSpec(memory_space=pltpu.VMEM)
    return pl.pallas_call(
        functools.partial(pair_kernel, blocks, wall_blocks),
        out_shape=(
            jax.ShapeDtypeStruct((blocks, LANES), jnp.float32),
            jax.ShapeDtypeStruct((3, blocks * LANES), jnp.float32),
            jax.ShapeDtypeStruct((8, LANES), jnp.float32),
        ),
        in_specs=[vmem, vmem, vmem, smem, smem, smem],
        out_specs=(vmem, vmem, vmem),
        scratch_shapes=[
            pltpu.VMEM((ghost_blocks * FEATURES, LANES), jnp.float32),
            pltpu.VMEM((total, LANES, FEATURES), jnp.bfloat16),
            pltpu.VMEM((total, MOMENTS, LANES), jnp.bfloat16),
            pltpu.VMEM((total, 3, LANES, LANES), jnp.float32),
            pltpu.VMEM((wall_blocks, LANES, FEATURES), jnp.bfloat16),
            pltpu.VMEM((wall_blocks, MOMENTS, LANES), jnp.bfloat16),
            pltpu.VMEM((wall_blocks, 1, LANES, LANES), jnp.float32),
            pltpu.VMEM((blocks, FEATURES, 2 * LANES), jnp.bfloat16),
            pltpu.VMEM((blocks, LANES), jnp.float32),
            pltpu.VMEM((blocks * MOMENTS, LANES), jnp.float32),
            pltpu.VMEM((blocks * 8, LANES), jnp.float32),
            pltpu.SMEM((total,), jnp.int32),
        ],
        compiler_params=pltpu.CompilerParams(vmem_limit_bytes=40 * 1024 * 1024),
        name="pair_pass",
    )(own, ghosts, walls, pair_list, wall_pairs, place)


def swapped(shard, axis, bit):
    return lax.ppermute(shard, axis, [(i, i ^ 1 << bit) for i in range(lax.axis_size(axis))])


def padded(block, sides, width):
    for axis, dim in sides:
        count = lax.axis_size(axis)
        forward = [(i, i + 1) for i in range(count - 1)]
        backward = [(target, source) for source, target in forward]
        low = lax.ppermute(
            lax.slice_in_dim(block, block.shape[dim] - width, None, axis=dim), axis, forward
        )
        high = lax.ppermute(lax.slice_in_dim(block, 0, width, axis=dim), axis, backward)
        block = jnp.concatenate([low, block, high], axis=dim)
    return block


def per_device(fluid_state, ghost_list, pair_list, wall_state, wall_count, wall_pairs):
    block_total = fluid_state.shape[1] // LANES
    own_blocks = jnp.transpose(fluid_state.reshape(8, block_total, LANES), (1, 0, 2))
    place = lax.axis_index("orb") % 8
    masks = jnp.bitwise_xor(jnp.arange(8, dtype=jnp.int32), place)
    sent = own_blocks[ghost_list[jnp.maximum(masks - 1, 0)]]
    groups = [list(range(g, g + 8)) for g in range(0, lax.axis_size("orb"), 8)]
    landed = lax.all_to_all(
        sent, "orb", 0, 0, axis_index_groups=groups if len(groups) > 1 else None
    )
    alive = (
        (jnp.arange(LANES, dtype=jnp.int32)[None, :] < wall_count[:, None])
        .astype(jnp.float32)
        .reshape(-1)
    )
    wall_live = jnp.concatenate([wall_state[0:3], wall_state[3:4] * alive[None, :]], axis=0)
    extended = padded(wall_live, (("wall", 1),), EB * LANES)
    wall_cands = jnp.transpose(extended.reshape(4, -1, LANES), (1, 0, 2))
    rate, acceleration, local_peak = pair_pass(
        own_blocks.reshape(-1, LANES),
        landed.reshape(-1, LANES),
        wall_cands.reshape(-1, LANES),
        pair_list,
        wall_pairs,
        place.reshape(1),
    )
    peak = local_peak
    for axis in ("wall", "orb"):
        for bit in range((lax.axis_size(axis) - 1).bit_length()):
            peak = jnp.maximum(peak, swapped(peak, axis, bit))
    peak = peak[0, 0]
    time_step = courant * jnp.sqrt(smoothing / (peak + 1e-06))
    return (rate.reshape(-1), acceleration, time_step)


def solution(mesh):
    return jax.shard_map(
        per_device,
        mesh=mesh,
        in_specs=(
            P(None, ("orb", "wall")),
            P(None, ("orb", "wall")),
            P(("orb", "wall"), None),
            P(None, ("orb", "wall")),
            P(("orb", "wall")),
            P(("orb", "wall"), None),
        ),
        out_specs=(P(("orb", "wall")), P(None, ("orb", "wall")), P()),
        check_vma=False,
    )
```

```python
import functools

import jax
import jax.numpy as jnp
from jax import lax
from jax.experimental import pallas as pl
from jax.experimental.pallas import tpu as pltpu
from jax.sharding import PartitionSpec as P

EB = 1
LANES = 128
FEATURES = 64
MOMENTS = 16
CHUNK = 128

smoothing = 0.1
support = 0.3
kernel_norm = 21.0 / (2.0 * 3.141592653589793 * support**3)
grad_coeff = -20.0 / support**2 * kernel_norm
tait_coeff = 25.0 / 7.0
visc_coeff = 0.05
cohesion = 2000.0
adhesion = 2000.0
gravity = 9.81
courant = 0.25

center = 0.3
shift = 0.0001 / support**2
approach_coeff = grad_coeff * visc_coeff * 2.0 / (support * 4.0 * cohesion)
press_coeff = -grad_coeff / (4.0 * cohesion)

SPLITS = ((0, 0), (0, 1), (1, 0), (0, 2), (2, 0), (1, 1), (1, 2), (2, 1))


def rounded(value):
    return value.astype(jnp.bfloat16).astype(jnp.float32)


def split(value):
    first = rounded(value)
    rest = value - first
    second = rounded(rest)
    return (first, second, rest - second)


def dotted(left, right):
    return left[0] * right[0] + left[1] * right[1] + left[2] * right[2]


def pressure_ratio(density):
    square = density * density
    return tait_coeff * (square * square * square * density - 1.0) / square


def loaded(ref, row, count, stride):
    return ref[pl.ds(row, count, stride=stride), :]


def scaled_position(ref, count, stride):
    return [(loaded(ref, d, count, stride) - center) * (1.0 / support) for d in range(3)]


def source_rows(pos, vel, extras):
    one = jnp.ones_like(pos[0])
    zero = one * 0.0
    rows = [one, one, one]
    rows += split(dotted(pos, pos))
    rows += split(approach_coeff * dotted(pos, vel)) if vel is not None else [zero] * 3
    for part in (pos, vel) if vel is not None else (pos,):
        for value in part:
            pieces = split(value)
            rows += [pieces[t] for _, t in SPLITS]
    return rows + [zero] * (FEATURES - len(rows) - len(extras)) + extras


def target_rows(pos, vel):
    one = jnp.ones_like(pos[0])
    zero = one * 0.0
    near = list(split(dotted(pos, pos))) + [one] * 3 + [zero] * 3
    along = list(split(approach_coeff * dotted(pos, vel))) + [zero] * 3 + [one] * 3
    for d in range(3):
        pieces = split(-2.0 * pos[d])
        near += [pieces[p] for p, _ in SPLITS]
        pieces = split(-approach_coeff * vel[d])
        along += [pieces[p] for p, _ in SPLITS]
    for d in range(3):
        pieces = split(-approach_coeff * pos[d])
        along += [pieces[p] for p, _ in SPLITS]
    near += [zero] * (FEATURES - len(near))
    along += [zero] * (FEATURES - len(along))
    return near, along


def moment_rows(pos, mass):
    pieces = [split(column) for column in [mass] + [mass * p for p in pos]]
    rows = [piece[p] for p in range(3) for piece in pieces]
    return rows + [mass * 0.0] * (MOMENTS - len(rows))


def put_sources(rows, moments, count, base, extras, stage, src, mom, wide):
    for k, row in enumerate(rows):
        stage[pl.ds(k, count, stride=FEATURES), :] = row

    def turn(b, carry):
        block = stage[pl.ds(pl.multiple_of(b * FEATURES, FEATURES), FEATURES), :]
        turned = block.T
        src[base + b] = turned.astype(jnp.bfloat16)
        for n in range(extras):
            lane = FEATURES - extras + n
            wide[base + b, n] = jnp.broadcast_to(turned[:, lane : lane + 1], (LANES, LANES))
        return carry

    lax.fori_loop(0, count, turn, 0)
    for k, row in enumerate(moments):
        stage[pl.ds(k, count, stride=MOMENTS), :] = row

    def place(b, carry):
        block = stage[pl.ds(pl.multiple_of(b * MOMENTS, MOMENTS), MOMENTS), :]
        mom[base + b] = block.astype(jnp.bfloat16)
        return carry

    lax.fori_loop(0, count, place, 0)


def fluid_sources(ref, count, base, stage, src, mom, wide):
    pos = scaled_position(ref, count, 8)
    vel = [loaded(ref, 3 + d, count, 8) for d in range(3)]
    density = loaded(ref, 6, count, 8)
    mass = loaded(ref, 7, count, 8)
    extras = [mass, density, press_coeff * pressure_ratio(density) - 0.75]
    rows = source_rows(pos, vel, extras)
    put_sources(rows, moment_rows(pos, mass), count, base, 3, stage, src, mom, wide)


def wall_sources(ref, count, stage, src, mom, wide):
    pos = scaled_position(ref, count, 4)
    mass = loaded(ref, 3, count, 4)
    rows = source_rows(pos, None, [mass])
    moments = moment_rows(pos, (adhesion / cohesion) * mass)
    put_sources(rows, moments, count, 0, 1, stage, src, mom, wide)


def put_targets(ref, count, stage, tgt):
    pos = scaled_position(ref, count, 8)
    vel = [loaded(ref, 3 + d, count, 8) for d in range(3)]
    for half, rows in enumerate(target_rows(pos, vel)):
        for k, row in enumerate(rows):
            stage[pl.ds(k, count, stride=FEATURES), :] = row

        def place(b, carry):
            block = stage[pl.ds(pl.multiple_of(b * FEATURES, FEATURES), FEATURES), :]
            tgt[b, :, half * LANES : (half + 1) * LANES] = block.astype(jnp.bfloat16)
            return carry

        lax.fori_loop(0, count, place, 0)


def in_two(value):
    high = value.astype(jnp.bfloat16)
    return high, (value - high.astype(jnp.float32)).astype(jnp.bfloat16)


def falloff_of(dist_sq):
    guarded = jnp.maximum(dist_sq, 1e-30)
    root = guarded * lax.rsqrt(guarded)
    falloff = jnp.maximum(1.0 - root, 0.0)
    return guarded, falloff, falloff * falloff * falloff


def weights_of(product, press_i, rho_i, wide):
    highs, lows = [], []
    rate = jnp.zeros((8, LANES), jnp.float32)
    for first in range(0, LANES, CHUNK):
        rows = slice(first, first + CHUNK)
        approach = product[rows, LANES:]
        guarded, falloff, cubed = falloff_of(product[rows, :LANES])
        blend = falloff + press_i
        if rho_i is not None:
            spread = (guarded + shift) * (wide[1, rows, :] + rho_i)
            blend += wide[2, rows, :]
            blend += jnp.maximum(approach, 0.0) * pl.reciprocal(spread, approx=True)
        high, low = in_two(cubed * blend)
        highs.append(high)
        lows.append(low)
        part = (cubed * approach) * wide[0, rows, :]
        for n in range(0, CHUNK, 8):
            rate += part[n : n + 8]
    halves = [jnp.concatenate(pieces, axis=0) for pieces in (highs, lows)]
    return jnp.concatenate(halves, axis=1), rate


def pair_kernel(
    blocks, walls, own_ref, ghost_ref, wall_ref, pair_ref, wpair_ref, place_ref,
    rate_ref, accel_ref, peak_ref, stage, src, mom, wide, wsrc, wmom, wwide, tgt, press, sums,
    rates, table,
):
    ghosts = ghost_ref.shape[0] // 8
    per_mask = ghosts // 8
    for c in range(blocks):
        table[c] = c
    for mask in range(1, 8):
        for g in range(per_mask):
            table[blocks + (mask - 1) * per_mask + g] = (
                blocks + jnp.bitwise_xor(place_ref[0], mask) * per_mask + g
            )
    fluid_sources(own_ref, blocks, 0, stage, src, mom, wide)
    fluid_sources(ghost_ref, ghosts, blocks, stage, src, mom, wide)
    wall_sources(wall_ref, walls, stage, wsrc, wmom, wwide)
    put_targets(own_ref, blocks, stage, tgt)
    press[...] = press_coeff * pressure_ratio(loaded(own_ref, 6, blocks, 8))

    def per_target(b, carry):
        target = tgt[b]
        rho_i = own_ref[pl.ds(b * 8 + 6, 1), :]
        press_i = press[pl.ds(b, 1), :]
        wall_press = (2.0 * cohesion / adhesion) * press_i - 0.75
        tiles = []
        for k in range(pair_ref.shape[1]):
            s = table[pair_ref[b, k]]
            tiles.append((src.at[s], mom.at[s], wide.at[s], press_i, rho_i))
        for k in range(wpair_ref.shape[1]):
            s = wpair_ref[b, k]
            tiles.append((wsrc.at[s], wmom.at[s], wwide.at[s], wall_press, None))

        def product_of(tile):
            return jnp.dot(tile[0][...], target, preferred_element_type=jnp.float32)

        total = jnp.zeros((MOMENTS, 2 * LANES), jnp.float32)
        rate = jnp.zeros((8, LANES), jnp.float32)
        ahead = product_of(tiles[0])
        waiting = None
        for n, (_, moments, spread, tile_press, tile_rho) in enumerate(tiles):
            product = ahead
            if n + 1 < len(tiles):
                ahead = product_of(tiles[n + 1])
            weights, part = weights_of(product, tile_press, tile_rho, spread)
            rate += part
            if waiting is not None:
                total += jnp.dot(*waiting, preferred_element_type=jnp.float32)
            waiting = (moments[...], weights)
        total += jnp.dot(*waiting, preferred_element_type=jnp.float32)
        rows = pl.ds(pl.multiple_of(b * MOMENTS, MOMENTS), MOMENTS)
        sums[rows, :] = total[:, :LANES] + total[:, LANES:]
        rates[pl.ds(pl.multiple_of(b * 8, 8), 8), :] = rate
        return carry

    lax.fori_loop(0, blocks, per_target, 0)

    pos = scaled_position(own_ref, blocks, 8)
    rate = loaded(rates, 0, blocks, 8)
    for n in range(1, 8):
        rate += loaded(rates, n, blocks, 8)
    rate_ref[...] = (support * grad_coeff / approach_coeff) * rate

    def summed(column):
        parts = [loaded(sums, p * 4 + column, blocks, MOMENTS) for p in range(3)]
        return parts[0] + parts[1] + parts[2]

    mass_sum = summed(0)
    square = jnp.zeros_like(rate)
    for d in range(3):
        force = (4.0 * cohesion * support) * (pos[d] * mass_sum - summed(1 + d))
        if d == 2:
            force -= gravity
        square += force * force
        stage[pl.ds(d, blocks, stride=8), :] = force
    for b in range(blocks):
        accel_ref[:, b * LANES : (b + 1) * LANES] = stage[b * 8 : b * 8 + 3, :]
    peak_ref[...] = jnp.full(peak_ref.shape, jnp.sqrt(jnp.max(square)), jnp.float32)


def pair_pass(own, ghosts, walls, pair_list, wall_pairs, place):
    blocks = own.shape[0] // 8
    ghost_blocks = ghosts.shape[0] // 8
    wall_blocks = walls.shape[0] // 4
    total = blocks + ghost_blocks
    smem = pl.BlockSpec(memory_space=pltpu.SMEM)
    vmem = pl.BlockSpec(memory_space=pltpu.VMEM)
    return pl.pallas_call(
        functools.partial(pair_kernel, blocks, wall_blocks),
        out_shape=(
            jax.ShapeDtypeStruct((blocks, LANES), jnp.float32),
            jax.ShapeDtypeStruct((3, blocks * LANES), jnp.float32),
            jax.ShapeDtypeStruct((8, LANES), jnp.float32),
        ),
        in_specs=[vmem, vmem, vmem, smem, smem, smem],
        out_specs=(vmem, vmem, vmem),
        scratch_shapes=[
            pltpu.VMEM((ghost_blocks * FEATURES, LANES), jnp.float32),
            pltpu.VMEM((total, LANES, FEATURES), jnp.bfloat16),
            pltpu.VMEM((total, MOMENTS, LANES), jnp.bfloat16),
            pltpu.VMEM((total, 3, LANES, LANES), jnp.float32),
            pltpu.VMEM((wall_blocks, LANES, FEATURES), jnp.bfloat16),
            pltpu.VMEM((wall_blocks, MOMENTS, LANES), jnp.bfloat16),
            pltpu.VMEM((wall_blocks, 1, LANES, LANES), jnp.float32),
            pltpu.VMEM((blocks, FEATURES, 2 * LANES), jnp.bfloat16),
            pltpu.VMEM((blocks, LANES), jnp.float32),
            pltpu.VMEM((blocks * MOMENTS, LANES), jnp.float32),
            pltpu.VMEM((blocks * 8, LANES), jnp.float32),
            pltpu.SMEM((total,), jnp.int32),
        ],
        compiler_params=pltpu.CompilerParams(vmem_limit_bytes=40 * 1024 * 1024),
        name="pair_pass",
    )(own, ghosts, walls, pair_list, wall_pairs, place)


def swapped(shard, axis, bit):
    return lax.ppermute(shard, axis, [(i, i ^ 1 << bit) for i in range(lax.axis_size(axis))])


def padded(block, sides, width):
    for axis, dim in sides:
        count = lax.axis_size(axis)
        forward = [(i, i + 1) for i in range(count - 1)]
        backward = [(target, source) for source, target in forward]
        low = lax.ppermute(
            lax.slice_in_dim(block, block.shape[dim] - width, None, axis=dim), axis, forward
        )
        high = lax.ppermute(lax.slice_in_dim(block, 0, width, axis=dim), axis, backward)
        block = jnp.concatenate([low, block, high], axis=dim)
    return block


def per_device(fluid_state, ghost_list, pair_list, wall_state, wall_count, wall_pairs):
    block_total = fluid_state.shape[1] // LANES
    own_blocks = jnp.transpose(fluid_state.reshape(8, block_total, LANES), (1, 0, 2))
    place = lax.axis_index("orb") % 8
    masks = jnp.bitwise_xor(jnp.arange(8, dtype=jnp.int32), place)
    sent = own_blocks[ghost_list[jnp.maximum(masks - 1, 0)]]
    groups = [list(range(g, g + 8)) for g in range(0, lax.axis_size("orb"), 8)]
    landed = lax.all_to_all(
        sent, "orb", 0, 0, axis_index_groups=groups if len(groups) > 1 else None
    )
    alive = (
        (jnp.arange(LANES, dtype=jnp.int32)[None, :] < wall_count[:, None])
        .astype(jnp.float32)
        .reshape(-1)
    )
    wall_live = jnp.concatenate([wall_state[0:3], wall_state[3:4] * alive[None, :]], axis=0)
    extended = padded(wall_live, (("wall", 1),), EB * LANES)
    wall_cands = jnp.transpose(extended.reshape(4, -1, LANES), (1, 0, 2))
    rate, acceleration, local_peak = pair_pass(
        own_blocks.reshape(-1, LANES),
        landed.reshape(-1, LANES),
        wall_cands.reshape(-1, LANES),
        pair_list,
        wall_pairs,
        place.reshape(1),
    )
    peak = local_peak
    for axis in ("wall", "orb"):
        for bit in range((lax.axis_size(axis) - 1).bit_length()):
            peak = jnp.maximum(peak, swapped(peak, axis, bit))
    peak = peak[0, 0]
    time_step = courant * jnp.sqrt(smoothing / (peak + 1e-06))
    return (rate.reshape(-1), acceleration, time_step)


def solution(mesh):
    return jax.shard_map(
        per_device,
        mesh=mesh,
        in_specs=(
            P(None, ("orb", "wall")),
            P(None, ("orb", "wall")),
            P(("orb", "wall"), None),
            P(None, ("orb", "wall")),
            P(("orb", "wall")),
            P(("orb", "wall"), None),
        ),
        out_specs=(P(("orb", "wall")), P(None, ("orb", "wall")), P()),
        check_vma=False,
    )
```

```python
import functools

import jax
import jax.numpy as jnp
from jax import lax
from jax.experimental import pallas as pl
from jax.experimental.pallas import tpu as pltpu
from jax.sharding import PartitionSpec as P

EB = 1
LANES = 128
FEATURES = 64
MOMENTS = 16
CHUNK = 128

smoothing = 0.1
support = 0.3
kernel_norm = 21.0 / (2.0 * 3.141592653589793 * support**3)
grad_coeff = -20.0 / support**2 * kernel_norm
tait_coeff = 25.0 / 7.0
visc_coeff = 0.05
cohesion = 2000.0
adhesion = 2000.0
gravity = 9.81
courant = 0.25

center = 0.3
shift = 0.0001 / support**2
approach_coeff = grad_coeff * visc_coeff * 2.0 / (support * 4.0 * cohesion)
press_coeff = -grad_coeff / (4.0 * cohesion)

SPLITS = ((0, 0), (0, 1), (1, 0), (0, 2), (2, 0), (1, 1), (1, 2), (2, 1))


def rounded(value):
    return value.astype(jnp.bfloat16).astype(jnp.float32)


def split(value):
    first = rounded(value)
    rest = value - first
    second = rounded(rest)
    return (first, second, rest - second)


def dotted(left, right):
    return left[0] * right[0] + left[1] * right[1] + left[2] * right[2]


def pressure_ratio(density):
    square = density * density
    return tait_coeff * (square * square * square * density - 1.0) / square


def loaded(ref, row, count, stride):
    return ref[pl.ds(row, count, stride=stride), :]


def scaled_position(ref, count, stride):
    return [(loaded(ref, d, count, stride) - center) * (1.0 / support) for d in range(3)]


def source_rows(pos, vel, extras):
    one = jnp.ones_like(pos[0])
    zero = one * 0.0
    rows = [one, one, one]
    rows += split(dotted(pos, pos))
    rows += split(approach_coeff * dotted(pos, vel)) if vel is not None else [zero] * 3
    for part in (pos, vel) if vel is not None else (pos,):
        for value in part:
            pieces = split(value)
            rows += [pieces[t] for _, t in SPLITS]
    return rows + [zero] * (FEATURES - len(rows) - len(extras)) + extras


def target_rows(pos, vel):
    one = jnp.ones_like(pos[0])
    zero = one * 0.0
    near = list(split(dotted(pos, pos))) + [one] * 3 + [zero] * 3
    along = list(split(approach_coeff * dotted(pos, vel))) + [zero] * 3 + [one] * 3
    for d in range(3):
        pieces = split(-2.0 * pos[d])
        near += [pieces[p] for p, _ in SPLITS]
        pieces = split(-approach_coeff * vel[d])
        along += [pieces[p] for p, _ in SPLITS]
    for d in range(3):
        pieces = split(-approach_coeff * pos[d])
        along += [pieces[p] for p, _ in SPLITS]
    near += [zero] * (FEATURES - len(near))
    along += [zero] * (FEATURES - len(along))
    return near, along


def moment_rows(pos, mass):
    pieces = [split(column) for column in [mass] + [mass * p for p in pos]]
    rows = [piece[p] for p in range(3) for piece in pieces]
    return rows + [mass * 0.0] * (MOMENTS - len(rows))


def put_sources(rows, moments, count, base, extras, stage, src, mom, wide):
    for k, row in enumerate(rows):
        stage[pl.ds(k, count, stride=FEATURES), :] = row

    def turn(b, carry):
        block = stage[pl.ds(pl.multiple_of(b * FEATURES, FEATURES), FEATURES), :]
        turned = block.T
        src[base + b] = turned.astype(jnp.bfloat16)
        for n in range(extras):
            lane = FEATURES - extras + n
            wide[base + b, n] = jnp.broadcast_to(turned[:, lane : lane + 1], (LANES, LANES))
        return carry

    lax.fori_loop(0, count, turn, 0, unroll=8)
    for k, row in enumerate(moments):
        stage[pl.ds(k, count, stride=MOMENTS), :] = row

    def place(b, carry):
        block = stage[pl.ds(pl.multiple_of(b * MOMENTS, MOMENTS), MOMENTS), :]
        mom[base + b] = block.astype(jnp.bfloat16)
        return carry

    lax.fori_loop(0, count, place, 0, unroll=8)


def fluid_sources(ref, count, base, stage, src, mom, wide):
    pos = scaled_position(ref, count, 8)
    vel = [loaded(ref, 3 + d, count, 8) for d in range(3)]
    density = loaded(ref, 6, count, 8)
    mass = loaded(ref, 7, count, 8)
    extras = [mass, density, press_coeff * pressure_ratio(density) - 0.75]
    rows = source_rows(pos, vel, extras)
    put_sources(rows, moment_rows(pos, mass), count, base, 3, stage, src, mom, wide)


def wall_sources(ref, count, stage, src, mom, wide):
    pos = scaled_position(ref, count, 4)
    mass = loaded(ref, 3, count, 4)
    rows = source_rows(pos, None, [mass])
    moments = moment_rows(pos, (adhesion / cohesion) * mass)
    put_sources(rows, moments, count, 0, 1, stage, src, mom, wide)


def put_targets(ref, count, stage, tgt):
    pos = scaled_position(ref, count, 8)
    vel = [loaded(ref, 3 + d, count, 8) for d in range(3)]
    for half, rows in enumerate(target_rows(pos, vel)):
        for k, row in enumerate(rows):
            stage[pl.ds(k, count, stride=FEATURES), :] = row

        def place(b, carry):
            block = stage[pl.ds(pl.multiple_of(b * FEATURES, FEATURES), FEATURES), :]
            tgt[b, :, half * LANES : (half + 1) * LANES] = block.astype(jnp.bfloat16)
            return carry

        lax.fori_loop(0, count, place, 0, unroll=8)


def in_two(value):
    high = value.astype(jnp.bfloat16)
    return high, (value - high.astype(jnp.float32)).astype(jnp.bfloat16)


def falloff_of(dist_sq):
    guarded = jnp.maximum(dist_sq, 1e-30)
    root = guarded * lax.rsqrt(guarded)
    falloff = jnp.maximum(1.0 - root, 0.0)
    return guarded, falloff, falloff * falloff * falloff


def weights_of(product, press_i, rho_i, wide):
    highs, lows = [], []
    rate = jnp.zeros((8, LANES), jnp.float32)
    for first in range(0, LANES, CHUNK):
        rows = slice(first, first + CHUNK)
        approach = product[rows, LANES:]
        guarded, falloff, cubed = falloff_of(product[rows, :LANES])
        blend = falloff + press_i
        if rho_i is not None:
            spread = (guarded + shift) * (wide[1, rows, :] + rho_i)
            blend += wide[2, rows, :]
            blend += jnp.maximum(approach, 0.0) * pl.reciprocal(spread, approx=True)
        high, low = in_two(cubed * blend)
        highs.append(high)
        lows.append(low)
        part = (cubed * approach) * wide[0, rows, :]
        for n in range(0, CHUNK, 8):
            rate += part[n : n + 8]
    halves = [jnp.concatenate(pieces, axis=0) for pieces in (highs, lows)]
    return jnp.concatenate(halves, axis=1), rate


def pair_kernel(
    blocks, walls, own_ref, ghost_ref, wall_ref, pair_ref, wpair_ref, place_ref,
    rate_ref, accel_ref, peak_ref, stage, src, mom, wide, wsrc, wmom, wwide, tgt, press, sums,
    rates, table,
):
    ghosts = ghost_ref.shape[0] // 8
    per_mask = ghosts // 8
    for c in range(blocks):
        table[c] = c
    for mask in range(1, 8):
        for g in range(per_mask):
            table[blocks + (mask - 1) * per_mask + g] = (
                blocks + jnp.bitwise_xor(place_ref[0], mask) * per_mask + g
            )
    fluid_sources(own_ref, blocks, 0, stage, src, mom, wide)
    fluid_sources(ghost_ref, ghosts, blocks, stage, src, mom, wide)
    wall_sources(wall_ref, walls, stage, wsrc, wmom, wwide)
    put_targets(own_ref, blocks, stage, tgt)
    press[...] = press_coeff * pressure_ratio(loaded(own_ref, 6, blocks, 8))

    def per_target(b, carry):
        target = tgt[b]
        rho_i = own_ref[pl.ds(b * 8 + 6, 1), :]
        press_i = press[pl.ds(b, 1), :]
        wall_press = (2.0 * cohesion / adhesion) * press_i - 0.75
        tiles = []
        for k in range(pair_ref.shape[1]):
            s = table[pair_ref[b, k]]
            tiles.append((src.at[s], mom.at[s], wide.at[s], press_i, rho_i))
        for k in range(wpair_ref.shape[1]):
            s = wpair_ref[b, k]
            tiles.append((wsrc.at[s], wmom.at[s], wwide.at[s], wall_press, None))

        def product_of(tile):
            return jnp.dot(tile[0][...], target, preferred_element_type=jnp.float32)

        total = jnp.zeros((MOMENTS, 2 * LANES), jnp.float32)
        rate = jnp.zeros((8, LANES), jnp.float32)
        ahead = product_of(tiles[0])
        waiting = None
        for n, (_, moments, spread, tile_press, tile_rho) in enumerate(tiles):
            product = ahead
            if n + 1 < len(tiles):
                ahead = product_of(tiles[n + 1])
            weights, part = weights_of(product, tile_press, tile_rho, spread)
            rate += part
            if waiting is not None:
                total += jnp.dot(*waiting, preferred_element_type=jnp.float32)
            waiting = (moments[...], weights)
        total += jnp.dot(*waiting, preferred_element_type=jnp.float32)
        rows = pl.ds(pl.multiple_of(b * MOMENTS, MOMENTS), MOMENTS)
        sums[rows, :] = total[:, :LANES] + total[:, LANES:]
        rates[pl.ds(pl.multiple_of(b * 8, 8), 8), :] = rate
        return carry

    lax.fori_loop(0, blocks, per_target, 0)

    pos = scaled_position(own_ref, blocks, 8)
    rate = loaded(rates, 0, blocks, 8)
    for n in range(1, 8):
        rate += loaded(rates, n, blocks, 8)
    rate_ref[...] = (support * grad_coeff / approach_coeff) * rate

    def summed(column):
        parts = [loaded(sums, p * 4 + column, blocks, MOMENTS) for p in range(3)]
        return parts[0] + parts[1] + parts[2]

    mass_sum = summed(0)
    square = jnp.zeros_like(rate)
    for d in range(3):
        force = (4.0 * cohesion * support) * (pos[d] * mass_sum - summed(1 + d))
        if d == 2:
            force -= gravity
        square += force * force
        stage[pl.ds(d, blocks, stride=8), :] = force
    for b in range(blocks):
        accel_ref[:, b * LANES : (b + 1) * LANES] = stage[b * 8 : b * 8 + 3, :]
    peak_ref[...] = jnp.full(peak_ref.shape, jnp.sqrt(jnp.max(square)), jnp.float32)


def pair_pass(own, ghosts, walls, pair_list, wall_pairs, place):
    blocks = own.shape[0] // 8
    ghost_blocks = ghosts.shape[0] // 8
    wall_blocks = walls.shape[0] // 4
    total = blocks + ghost_blocks
    smem = pl.BlockSpec(memory_space=pltpu.SMEM)
    vmem = pl.BlockSpec(memory_space=pltpu.VMEM)
    return pl.pallas_call(
        functools.partial(pair_kernel, blocks, wall_blocks),
        out_shape=(
            jax.ShapeDtypeStruct((blocks, LANES), jnp.float32),
            jax.ShapeDtypeStruct((3, blocks * LANES), jnp.float32),
            jax.ShapeDtypeStruct((8, LANES), jnp.float32),
        ),
        in_specs=[vmem, vmem, vmem, smem, smem, smem],
        out_specs=(vmem, vmem, vmem),
        scratch_shapes=[
            pltpu.VMEM((ghost_blocks * FEATURES, LANES), jnp.float32),
            pltpu.VMEM((total, LANES, FEATURES), jnp.bfloat16),
            pltpu.VMEM((total, MOMENTS, LANES), jnp.bfloat16),
            pltpu.VMEM((total, 3, LANES, LANES), jnp.float32),
            pltpu.VMEM((wall_blocks, LANES, FEATURES), jnp.bfloat16),
            pltpu.VMEM((wall_blocks, MOMENTS, LANES), jnp.bfloat16),
            pltpu.VMEM((wall_blocks, 1, LANES, LANES), jnp.float32),
            pltpu.VMEM((blocks, FEATURES, 2 * LANES), jnp.bfloat16),
            pltpu.VMEM((blocks, LANES), jnp.float32),
            pltpu.VMEM((blocks * MOMENTS, LANES), jnp.float32),
            pltpu.VMEM((blocks * 8, LANES), jnp.float32),
            pltpu.SMEM((total,), jnp.int32),
        ],
        compiler_params=pltpu.CompilerParams(vmem_limit_bytes=40 * 1024 * 1024),
        name="pair_pass",
    )(own, ghosts, walls, pair_list, wall_pairs, place)


def swapped(shard, axis, bit):
    return lax.ppermute(shard, axis, [(i, i ^ 1 << bit) for i in range(lax.axis_size(axis))])


def padded(block, sides, width):
    for axis, dim in sides:
        count = lax.axis_size(axis)
        forward = [(i, i + 1) for i in range(count - 1)]
        backward = [(target, source) for source, target in forward]
        low = lax.ppermute(
            lax.slice_in_dim(block, block.shape[dim] - width, None, axis=dim), axis, forward
        )
        high = lax.ppermute(lax.slice_in_dim(block, 0, width, axis=dim), axis, backward)
        block = jnp.concatenate([low, block, high], axis=dim)
    return block


def per_device(fluid_state, ghost_list, pair_list, wall_state, wall_count, wall_pairs):
    block_total = fluid_state.shape[1] // LANES
    own_blocks = jnp.transpose(fluid_state.reshape(8, block_total, LANES), (1, 0, 2))
    place = lax.axis_index("orb") % 8
    masks = jnp.bitwise_xor(jnp.arange(8, dtype=jnp.int32), place)
    sent = own_blocks[ghost_list[jnp.maximum(masks - 1, 0)]]
    groups = [list(range(g, g + 8)) for g in range(0, lax.axis_size("orb"), 8)]
    landed = lax.all_to_all(
        sent, "orb", 0, 0, axis_index_groups=groups if len(groups) > 1 else None
    )
    alive = (
        (jnp.arange(LANES, dtype=jnp.int32)[None, :] < wall_count[:, None])
        .astype(jnp.float32)
        .reshape(-1)
    )
    wall_live = jnp.concatenate([wall_state[0:3], wall_state[3:4] * alive[None, :]], axis=0)
    extended = padded(wall_live, (("wall", 1),), EB * LANES)
    wall_cands = jnp.transpose(extended.reshape(4, -1, LANES), (1, 0, 2))
    rate, acceleration, local_peak = pair_pass(
        own_blocks.reshape(-1, LANES),
        landed.reshape(-1, LANES),
        wall_cands.reshape(-1, LANES),
        pair_list,
        wall_pairs,
        place.reshape(1),
    )
    peak = local_peak
    for axis in ("wall", "orb"):
        for bit in range((lax.axis_size(axis) - 1).bit_length()):
            peak = jnp.maximum(peak, swapped(peak, axis, bit))
    peak = peak[0, 0]
    time_step = courant * jnp.sqrt(smoothing / (peak + 1e-06))
    return (rate.reshape(-1), acceleration, time_step)


def solution(mesh):
    return jax.shard_map(
        per_device,
        mesh=mesh,
        in_specs=(
            P(None, ("orb", "wall")),
            P(None, ("orb", "wall")),
            P(("orb", "wall"), None),
            P(None, ("orb", "wall")),
            P(("orb", "wall")),
            P(("orb", "wall"), None),
        ),
        out_specs=(P(("orb", "wall")), P(None, ("orb", "wall")), P()),
        check_vma=False,
    )
```

```python
import functools

import jax
import jax.numpy as jnp
import numpy as np
from jax import lax
from jax.experimental import pallas as pl
from jax.experimental.pallas import tpu as pltpu
from jax.sharding import PartitionSpec as P

EB = 1
LANES = 128
ROWS = 8
PIECES = 6 * ROWS
DEPTH = 80
MOMENTS = 4 * ROWS
UNROLL = 4

smoothing = 0.1
support = 0.3
kernel_norm = 21.0 / (2.0 * 3.141592653589793 * support**3)
grad_coeff = -20.0 / support**2 * kernel_norm
tait_coeff = 25.0 / 7.0
visc_coeff = 0.05
cohesion = 2000.0
adhesion = 2000.0
gravity = 9.81
courant = 0.25

center = 0.3
shift = 0.0001 / support**2
press_coeff = -grad_coeff / (4.0 * cohesion)
density_coeff = (support * 4.0 * cohesion) / (-grad_coeff * visc_coeff * 2.0)

SPLITS = ((0, 0), (0, 1), (1, 0), (0, 2), (2, 0), (1, 1), (1, 2), (2, 1))


def y_row(piece, row):
    return piece * ROWS + row


def z_row(piece, row):
    return (3 + piece) * ROWS + row


def selections():
    source = np.zeros((2 * DEPTH, PIECES), np.float32)
    target = np.zeros((PIECES, 4 * LANES), np.float32)
    one = z_row(0, 6)
    k = 0
    for p in range(3):
        for d in range(3):
            target[one, k] = 1.0
            source[k, z_row(p, d)] = 1.0
            source[DEPTH + k, z_row(p, 3 + d)] = -1.0
            target[z_row(p, d), k + 9] = 1.0
            source[k + 9, one] = 1.0
            target[z_row(p, 3 + d), k + 18] = 1.0
            source[DEPTH + k + 18, one] = -1.0
            k += 1
    k = 27
    for d in range(3):
        for p, t in SPLITS:
            target[y_row(p, d), k] = 1.0
            source[k, y_row(t, d)] = -2.0
            source[DEPTH + k, y_row(t, 3 + d)] = 1.0
            target[y_row(p, 3 + d), k + 24] = 1.0
            source[DEPTH + k + 24, y_row(t, d)] = 1.0
            k += 1
    for p in range(3):
        target[y_row(p, 6), LANES : 2 * LANES] = 1.0
        target[z_row(p, 7), 2 * LANES : 3 * LANES] = 1.0
        target[z_row(p, 7), 3 * LANES :] = 2.0 * cohesion / adhesion
    target[one, 2 * LANES :] = -0.75
    return jnp.asarray(source, jnp.bfloat16), jnp.asarray(target, jnp.bfloat16)


def split(value):
    first = value.astype(jnp.bfloat16).astype(jnp.float32)
    rest = value - first
    second = rest.astype(jnp.bfloat16).astype(jnp.float32)
    return [first, second, rest - second]


def pressure_ratio(density):
    square = density * density
    return tait_coeff * (square * square * square * density - 1.0) / square


def row_index():
    return lax.broadcasted_iota(jnp.int32, (ROWS, LANES), 0)


def state_of(block):
    row = row_index()
    y = jnp.where(row < 3, (block - center) * (1.0 / support), block)
    y = jnp.where(row == 6, block * density_coeff, y)
    density = jnp.where(row == 7, pltpu.roll(block, 1, axis=0), 1.0)
    press = press_coeff * pressure_ratio(density)
    z = y * jnp.where(row < 3, y, pltpu.roll(y, 3, axis=0))
    return y, jnp.where(row < 6, z, jnp.where(row == 6, 1.0, press))


def pieces_of(y, z):
    return jnp.concatenate(split(y) + split(z), axis=0)


def put_source(block, choice, s, src, mom, ys, zs, mass_factor=1.0):
    row = row_index()
    y, z = state_of(block)
    pieces = pieces_of(y, z).astype(jnp.bfloat16)
    chosen = jnp.dot(choice, pieces, preferred_element_type=jnp.float32).astype(jnp.bfloat16)
    src[s] = jnp.concatenate([chosen[:DEPTH], chosen[DEPTH:]], axis=1)
    moment = (mass_factor * block[7:8]) * jnp.where(row == 6, 1.0, y)
    rows = split(moment) + [jnp.zeros_like(moment)]
    moments = jnp.concatenate(rows, axis=0).astype(jnp.bfloat16)
    mom[s] = jnp.concatenate([moments, moments], axis=1)
    ys[s] = y
    zs[s] = z
    return y, z


def put_target(y, z, choice, b, tgt, wide):
    pieces = pieces_of(y, z).T.astype(jnp.bfloat16)
    chosen = jnp.dot(pieces, choice, preferred_element_type=jnp.float32)
    tgt[b] = chosen[:, :DEPTH].astype(jnp.bfloat16)
    for n in range(3):
        wide[b, n] = chosen[:, (n + 1) * LANES : (n + 2) * LANES]


def rows_at(index):
    return pl.ds(pl.multiple_of(index * ROWS, ROWS), ROWS)


def weights_of(product, wide, n_wide, y, z):
    guarded = jnp.maximum(product[:, :LANES], 1e-30)
    approach = product[:, LANES:]
    falloff = jnp.maximum(1.0 - guarded * lax.rsqrt(guarded), 0.0)
    cubed = falloff * falloff * falloff
    blend = falloff + wide[n_wide]
    if z is not None:
        spread = (guarded + shift) * (wide[0] + y[6:7])
        blend += z[7:8]
        blend += jnp.maximum(approach, 0.0) * pl.reciprocal(spread, approx=True)
    weight = cubed * blend
    high = weight.astype(jnp.bfloat16)
    low = (weight - high.astype(jnp.float32)).astype(jnp.bfloat16)
    return jnp.concatenate([high, low], axis=1), (cubed * approach) * y[7:8]


def across(left, right):
    return lax.dot_general(
        left, right, (((1,), (1,)), ((), ())), preferred_element_type=jnp.float32
    )


def run_tiles(target, wide, n_wide, tiles):
    def product_of(tile):
        return jnp.dot(target, tile[0][...], preferred_element_type=jnp.float32)

    total = jnp.zeros((MOMENTS, LANES), jnp.float32)
    rate = jnp.zeros((LANES, LANES), jnp.float32)
    ahead = product_of(tiles[0])
    waiting = None
    for n, (_, moments, y, z) in enumerate(tiles):
        product = ahead
        if n + 1 < len(tiles):
            ahead = product_of(tiles[n + 1])
        weights, part = weights_of(product, wide, n_wide, y, z)
        rate += part
        if waiting is not None:
            total += across(*waiting)
        waiting = (moments[...], weights)
    total += across(*waiting)
    ones = jnp.ones((ROWS, 3 * LANES), jnp.bfloat16)
    rates = across(ones, jnp.concatenate(split(rate), axis=1).astype(jnp.bfloat16))
    return total, rates


def moments_at(b):
    return pl.ds(pl.multiple_of(b * MOMENTS, MOMENTS), MOMENTS)


def own_kernel(
    blocks, walls, own_ref, wall_ref, wpair_ref, choice, target_choice,
    src, mom, ys, zs, tgt, wide, sums, rates, wsrc, wmom, wys, wzs,
):
    def build(b, carry):
        y, z = put_source(own_ref[rows_at(b), :], choice[...], b, src, mom, ys, zs)
        put_target(y, z, target_choice[...], b, tgt, wide)
        return carry

    lax.fori_loop(0, blocks, build, 0, unroll=UNROLL)
    row = row_index()
    for c in range(walls):
        held = wall_ref[4 * c : 4 * c + 4, :]
        both = jnp.concatenate([held, held], axis=0)
        block = jnp.where(
            (row < 3) | (row == 7), both, jnp.where(row == 6, 1.0, 0.0)
        )
        put_source(block, choice[...], c, wsrc, wmom, wys, wzs, adhesion / cohesion)

    def per_target(b, carry):
        tiles = []
        for k in range(wpair_ref.shape[1]):
            s = wpair_ref[b, k]
            tiles.append((wsrc.at[s], wmom.at[s], wys.at[s], None))
        total, rate = run_tiles(tgt[b], wide.at[b], 2, tiles)
        sums[moments_at(b), :] = total
        rates[rows_at(b), :] = rate
        return carry

    lax.fori_loop(0, blocks, per_target, 0, unroll=UNROLL)


def fluid_kernel(
    blocks, own_ref, ghost_ref, pair_ref, place_ref, choice, own_src, own_mom, own_ys, own_zs,
    tgt, wide, own_sums, own_rates, rate_ref, accel_ref, peak_ref,
    src, mom, ys, zs, sums, rates, stage, table,
):
    ghosts = ghost_ref.shape[0] // ROWS
    per_mask = ghosts // 8
    for c in range(blocks):
        table[c] = c
    for mask in range(1, 8):
        for g in range(per_mask):
            table[blocks + (mask - 1) * per_mask + g] = (
                blocks + jnp.bitwise_xor(place_ref[0], mask) * per_mask + g
            )
    src[:blocks] = own_src[...]
    mom[:blocks] = own_mom[...]
    ys[:blocks] = own_ys[...]
    zs[:blocks] = own_zs[...]

    def build(g, carry):
        put_source(ghost_ref[rows_at(g), :], choice[...], blocks + g, src, mom, ys, zs)
        return carry

    lax.fori_loop(0, ghosts, build, 0, unroll=UNROLL)

    def per_target(b, carry):
        tiles = []
        for k in range(pair_ref.shape[1]):
            s = table[pair_ref[b, k]]
            tiles.append((src.at[s], mom.at[s], ys.at[s], zs.at[s]))
        total, rate = run_tiles(tgt[b], wide.at[b], 1, tiles)
        sums[moments_at(b), :] = own_sums[moments_at(b), :] + total
        rates[rows_at(b), :] = own_rates[rows_at(b), :] + rate
        return carry

    lax.fori_loop(0, blocks, per_target, 0)

    rate_ref[...] = (-support * grad_coeff) * rates[pl.ds(0, blocks, stride=ROWS), :]

    def summed(row):
        parts = [sums[pl.ds(y_row(p, row), blocks, stride=MOMENTS), :] for p in range(3)]
        return parts[0] + parts[1] + parts[2]

    mass_sum = summed(6)
    square = jnp.zeros_like(mass_sum)
    for d in range(3):
        pos = (own_ref[pl.ds(d, blocks, stride=ROWS), :] - center) * (1.0 / support)
        force = (4.0 * cohesion * support) * (pos * mass_sum - summed(d))
        if d == 2:
            force -= gravity
        square += force * force
        stage[pl.ds(d, blocks, stride=ROWS), :] = force
    for b in range(blocks):
        accel_ref[:, b * LANES : (b + 1) * LANES] = stage[b * ROWS : b * ROWS + 3, :]
    peak_ref[...] = jnp.full(peak_ref.shape, jnp.sqrt(jnp.max(square)), jnp.float32)


SMEM = pl.BlockSpec(memory_space=pltpu.SMEM)
VMEM = pl.BlockSpec(memory_space=pltpu.VMEM)
PARAMS = pltpu.CompilerParams(vmem_limit_bytes=32 * 1024 * 1024)


def tile_cost(tiles):
    return pl.CostEstimate(
        flops=tiles * LANES * LANES * 1000, bytes_accessed=0, transcendentals=0
    )


def source_shapes(count):
    return [
        ((count, DEPTH, 2 * LANES), jnp.bfloat16),
        ((count, MOMENTS, 2 * LANES), jnp.bfloat16),
        ((count, ROWS, LANES), jnp.float32),
        ((count, ROWS, LANES), jnp.float32),
    ]


def own_pass(own, walls, wall_pairs, choices):
    blocks = own.shape[0] // ROWS
    wall_blocks = walls.shape[0] // 4
    outs = source_shapes(blocks) + [
        ((blocks, LANES, DEPTH), jnp.bfloat16),
        ((blocks, 3, LANES, LANES), jnp.float32),
        ((blocks * MOMENTS, LANES), jnp.float32),
        ((blocks * ROWS, LANES), jnp.float32),
    ]
    return pl.pallas_call(
        functools.partial(own_kernel, blocks, wall_blocks),
        out_shape=[jax.ShapeDtypeStruct(*out) for out in outs],
        in_specs=[VMEM, VMEM, SMEM, VMEM, VMEM],
        out_specs=[VMEM] * len(outs),
        scratch_shapes=[pltpu.VMEM(*shape) for shape in source_shapes(wall_blocks)],
        compiler_params=PARAMS,
        cost_estimate=tile_cost(wall_pairs.size),
        name="own_pass",
    )(own, walls, wall_pairs, *choices)


def fluid_pass(own, ghosts, pair_list, place, choice, own_results):
    blocks = own.shape[0] // ROWS
    total = blocks + ghosts.shape[0] // ROWS
    return pl.pallas_call(
        functools.partial(fluid_kernel, blocks),
        out_shape=(
            jax.ShapeDtypeStruct((blocks, LANES), jnp.float32),
            jax.ShapeDtypeStruct((3, blocks * LANES), jnp.float32),
            jax.ShapeDtypeStruct((ROWS, LANES), jnp.float32),
        ),
        in_specs=[VMEM, VMEM, SMEM, SMEM, VMEM] + [VMEM] * len(own_results),
        out_specs=(VMEM, VMEM, VMEM),
        scratch_shapes=[pltpu.VMEM(*shape) for shape in source_shapes(total)]
        + [
            pltpu.VMEM((blocks * MOMENTS, LANES), jnp.float32),
            pltpu.VMEM((blocks * ROWS, LANES), jnp.float32),
            pltpu.VMEM((blocks * ROWS, LANES), jnp.float32),
            pltpu.SMEM((total,), jnp.int32),
        ],
        compiler_params=PARAMS,
        cost_estimate=tile_cost(pair_list.size),
        name="fluid_pass",
    )(own, ghosts, pair_list, place, choice, *own_results)


def outgoing_kernel(own_ref, list_ref, place_ref, sent_ref):
    for slot in range(8):
        mask = jnp.bitwise_xor(place_ref[0], slot)
        for g in range(list_ref.shape[1]):
            block = list_ref[jnp.maximum(mask - 1, 0), g]
            first = (slot * list_ref.shape[1] + g) * ROWS
            sent_ref[first : first + ROWS, :] = own_ref[rows_at(block), :]


def outgoing_pass(own, ghost_list, place):
    count = 8 * ghost_list.shape[1]
    return pl.pallas_call(
        outgoing_kernel,
        out_shape=jax.ShapeDtypeStruct((count * ROWS, LANES), jnp.float32),
        in_specs=[VMEM, SMEM, SMEM],
        out_specs=VMEM,
        name="outgoing_pass",
    )(own, ghost_list, place)


def swapped(shard, axis, bit):
    return lax.ppermute(shard, axis, [(i, i ^ 1 << bit) for i in range(lax.axis_size(axis))])


def padded(block, sides, width):
    for axis, dim in sides:
        count = lax.axis_size(axis)
        forward = [(i, i + 1) for i in range(count - 1)]
        backward = [(target, source) for source, target in forward]
        low = lax.ppermute(
            lax.slice_in_dim(block, block.shape[dim] - width, None, axis=dim), axis, forward
        )
        high = lax.ppermute(lax.slice_in_dim(block, 0, width, axis=dim), axis, backward)
        block = jnp.concatenate([low, block, high], axis=dim)
    return block


def per_device(fluid_state, ghost_list, pair_list, wall_state, wall_count, wall_pairs):
    block_total = fluid_state.shape[1] // LANES
    own = jnp.transpose(fluid_state.reshape(8, block_total, LANES), (1, 0, 2)).reshape(-1, LANES)
    place = (lax.axis_index("orb") % 8).reshape(1)
    groups = [list(range(g, g + 8)) for g in range(0, lax.axis_size("orb"), 8)]
    landed = lax.all_to_all(
        outgoing_pass(own, ghost_list, place).reshape(8, -1, LANES),
        "orb",
        0,
        0,
        axis_index_groups=groups if len(groups) > 1 else None,
    )
    alive = (
        (jnp.arange(LANES, dtype=jnp.int32)[None, :] < wall_count[:, None])
        .astype(jnp.float32)
        .reshape(-1)
    )
    wall_live = jnp.concatenate([wall_state[0:3], wall_state[3:4] * alive[None, :]], axis=0)
    extended = padded(wall_live, (("wall", 1),), EB * LANES)
    wall_cands = jnp.transpose(extended.reshape(4, -1, LANES), (1, 0, 2))
    choices = selections()
    own_results = own_pass(own, wall_cands.reshape(-1, LANES), wall_pairs, choices)
    rate, acceleration, local_peak = fluid_pass(
        own, landed.reshape(-1, LANES), pair_list, place, choices[0], own_results
    )
    peak = local_peak
    for axis in ("wall", "orb"):
        for bit in range((lax.axis_size(axis) - 1).bit_length()):
            peak = jnp.maximum(peak, swapped(peak, axis, bit))
    peak = peak[0, 0]
    time_step = courant * jnp.sqrt(smoothing / (peak + 1e-06))
    return (rate.reshape(-1), acceleration, time_step)


def solution(mesh):
    return jax.shard_map(
        per_device,
        mesh=mesh,
        in_specs=(
            P(None, ("orb", "wall")),
            P(None, ("orb", "wall")),
            P(("orb", "wall"), None),
            P(None, ("orb", "wall")),
            P(("orb", "wall")),
            P(("orb", "wall"), None),
        ),
        out_specs=(P(("orb", "wall")), P(None, ("orb", "wall")), P()),
        check_vma=False,
    )
```

```python
import functools

import jax
import jax.numpy as jnp
import numpy as np
from jax import lax
from jax.experimental import pallas as pl
from jax.experimental.pallas import tpu as pltpu
from jax.sharding import PartitionSpec as P

EB = 1
LANES = 128
ROWS = 8
PIECES = 6 * ROWS
DEPTH = 80
MOMENTS = 4 * ROWS
UNROLL = 4

smoothing = 0.1
support = 0.3
kernel_norm = 21.0 / (2.0 * 3.141592653589793 * support**3)
grad_coeff = -20.0 / support**2 * kernel_norm
tait_coeff = 25.0 / 7.0
visc_coeff = 0.05
cohesion = 2000.0
adhesion = 2000.0
gravity = 9.81
courant = 0.25

center = 0.3
shift = 0.0001 / support**2
press_coeff = -grad_coeff / (4.0 * cohesion)
density_coeff = (support * 4.0 * cohesion) / (-grad_coeff * visc_coeff * 2.0)

SPLITS = ((0, 0), (0, 1), (1, 0), (0, 2), (2, 0), (1, 1), (1, 2), (2, 1))


def y_row(piece, row):
    return piece * ROWS + row


def z_row(piece, row):
    return (3 + piece) * ROWS + row


def selections():
    source = np.zeros((2 * DEPTH, PIECES), np.float32)
    target = np.zeros((PIECES, 4 * LANES), np.float32)
    one = z_row(0, 6)
    k = 0
    for p in range(3):
        for d in range(3):
            target[one, k] = 1.0
            source[k, z_row(p, d)] = 1.0
            source[DEPTH + k, z_row(p, 3 + d)] = -1.0
            target[z_row(p, d), k + 9] = 1.0
            source[k + 9, one] = 1.0
            target[z_row(p, 3 + d), k + 18] = 1.0
            source[DEPTH + k + 18, one] = -1.0
            k += 1
    k = 27
    for d in range(3):
        for p, t in SPLITS:
            target[y_row(p, d), k] = 1.0
            source[k, y_row(t, d)] = -2.0
            source[DEPTH + k, y_row(t, 3 + d)] = 1.0
            target[y_row(p, 3 + d), k + 24] = 1.0
            source[DEPTH + k + 24, y_row(t, d)] = 1.0
            k += 1
    for p in range(3):
        target[y_row(p, 6), LANES : 2 * LANES] = 1.0
        target[z_row(p, 7), 2 * LANES : 3 * LANES] = 1.0
        target[z_row(p, 7), 3 * LANES :] = 2.0 * cohesion / adhesion
    target[one, 2 * LANES :] = -0.75
    return jnp.asarray(source, jnp.bfloat16), jnp.asarray(target, jnp.bfloat16)


def split(value):
    first = value.astype(jnp.bfloat16).astype(jnp.float32)
    rest = value - first
    second = rest.astype(jnp.bfloat16).astype(jnp.float32)
    return [first, second, rest - second]


def pressure_ratio(density):
    square = density * density
    return tait_coeff * (square * square * square * density - 1.0) / square


def row_index():
    return lax.broadcasted_iota(jnp.int32, (ROWS, LANES), 0)


def state_of(block):
    row = row_index()
    y = jnp.where(row < 3, (block - center) * (1.0 / support), block)
    y = jnp.where(row == 6, block * density_coeff, y)
    density = jnp.where(row == 7, pltpu.roll(block, 1, axis=0), 1.0)
    press = press_coeff * pressure_ratio(density)
    z = y * jnp.where(row < 3, y, pltpu.roll(y, 3, axis=0))
    return y, jnp.where(row < 6, z, jnp.where(row == 6, 1.0, press))


def pieces_of(y, z):
    return jnp.concatenate(split(y) + split(z), axis=0)


def put_source(block, choice, s, src, mom, ys, zs, mass_factor=1.0):
    row = row_index()
    y, z = state_of(block)
    pieces = pieces_of(y, z).astype(jnp.bfloat16)
    chosen = jnp.dot(choice, pieces, preferred_element_type=jnp.float32).astype(jnp.bfloat16)
    src[s] = jnp.concatenate([chosen[:DEPTH], chosen[DEPTH:]], axis=1)
    moment = (mass_factor * block[7:8]) * jnp.where(row == 6, 1.0, y)
    rows = split(moment) + [jnp.zeros_like(moment)]
    moments = jnp.concatenate(rows, axis=0).astype(jnp.bfloat16)
    mom[s] = jnp.concatenate([moments, moments], axis=1)
    ys[s] = y
    zs[s] = z
    return y, z


def put_target(y, z, choice, b, tgt, wide):
    pieces = pieces_of(y, z).T.astype(jnp.bfloat16)
    chosen = jnp.dot(pieces, choice, preferred_element_type=jnp.float32)
    tgt[b] = chosen[:, :DEPTH].astype(jnp.bfloat16)
    for n in range(3):
        wide[b, n] = chosen[:, (n + 1) * LANES : (n + 2) * LANES]


def rows_at(index):
    return pl.ds(pl.multiple_of(index * ROWS, ROWS), ROWS)


def weights_of(product, wide, n_wide, y, z):
    guarded = jnp.maximum(product[:, :LANES], 1e-30)
    approach = product[:, LANES:]
    if z is not None:
        spread = (guarded + shift) * (wide[0] + y[6:7])
        scaled = guarded * spread
        inverse = lax.rsqrt(scaled * spread)
        root = scaled * inverse
        viscous = jnp.maximum(approach, 0.0) * (inverse * root)
    else:
        root = guarded * lax.rsqrt(guarded)
    falloff = jnp.maximum(1.0 - root, 0.0)
    cubed = falloff * falloff * falloff
    blend = falloff + wide[n_wide]
    if z is not None:
        blend += z[7:8]
        blend += viscous
    weight = cubed * blend
    high = weight.astype(jnp.bfloat16)
    low = (weight - high.astype(jnp.float32)).astype(jnp.bfloat16)
    return jnp.concatenate([high, low], axis=1), (cubed * approach) * y[7:8]


def across(left, right):
    return lax.dot_general(
        left, right, (((1,), (1,)), ((), ())), preferred_element_type=jnp.float32
    )


def run_tiles(target, wide, n_wide, tiles):
    def product_of(tile):
        return jnp.dot(target, tile[0][...], preferred_element_type=jnp.float32)

    total = jnp.zeros((MOMENTS, LANES), jnp.float32)
    rate = jnp.zeros((LANES, LANES), jnp.float32)
    ahead = product_of(tiles[0])
    waiting = None
    for n, (_, moments, y, z) in enumerate(tiles):
        product = ahead
        if n + 1 < len(tiles):
            ahead = product_of(tiles[n + 1])
        weights, part = weights_of(product, wide, n_wide, y, z)
        rate += part
        if waiting is not None:
            total += across(*waiting)
        waiting = (moments[...], weights)
    total += across(*waiting)
    ones = jnp.ones((ROWS, 3 * LANES), jnp.bfloat16)
    rates = across(ones, jnp.concatenate(split(rate), axis=1).astype(jnp.bfloat16))
    return total, rates


def moments_at(b):
    return pl.ds(pl.multiple_of(b * MOMENTS, MOMENTS), MOMENTS)


def own_kernel(
    blocks, walls, own_ref, wall_ref, wpair_ref, choice, target_choice,
    src, mom, ys, zs, tgt, wide, sums, rates, wsrc, wmom, wys, wzs,
):
    def build(b, carry):
        y, z = put_source(own_ref[rows_at(b), :], choice[...], b, src, mom, ys, zs)
        put_target(y, z, target_choice[...], b, tgt, wide)
        return carry

    lax.fori_loop(0, blocks, build, 0, unroll=UNROLL)
    row = row_index()
    for c in range(walls):
        held = wall_ref[4 * c : 4 * c + 4, :]
        both = jnp.concatenate([held, held], axis=0)
        block = jnp.where(
            (row < 3) | (row == 7), both, jnp.where(row == 6, 1.0, 0.0)
        )
        put_source(block, choice[...], c, wsrc, wmom, wys, wzs, adhesion / cohesion)

    def per_target(b, carry):
        tiles = []
        for k in range(wpair_ref.shape[1]):
            s = wpair_ref[b, k]
            tiles.append((wsrc.at[s], wmom.at[s], wys.at[s], None))
        total, rate = run_tiles(tgt[b], wide.at[b], 2, tiles)
        sums[moments_at(b), :] = total
        rates[rows_at(b), :] = rate
        return carry

    lax.fori_loop(0, blocks, per_target, 0, unroll=UNROLL)


def fluid_kernel(
    blocks, own_ref, ghost_ref, pair_ref, place_ref, choice, own_src, own_mom, own_ys, own_zs,
    tgt, wide, own_sums, own_rates, rate_ref, accel_ref, peak_ref,
    src, mom, ys, zs, sums, rates, stage, table,
):
    ghosts = ghost_ref.shape[0] // ROWS
    per_mask = ghosts // 8
    for c in range(blocks):
        table[c] = c
    for mask in range(1, 8):
        for g in range(per_mask):
            table[blocks + (mask - 1) * per_mask + g] = (
                blocks + jnp.bitwise_xor(place_ref[0], mask) * per_mask + g
            )
    src[:blocks] = own_src[...]
    mom[:blocks] = own_mom[...]
    ys[:blocks] = own_ys[...]
    zs[:blocks] = own_zs[...]

    def build(g, carry):
        put_source(ghost_ref[rows_at(g), :], choice[...], blocks + g, src, mom, ys, zs)
        return carry

    lax.fori_loop(0, ghosts, build, 0, unroll=UNROLL)

    def per_target(b, carry):
        tiles = []
        for k in range(pair_ref.shape[1]):
            s = table[pair_ref[b, k]]
            tiles.append((src.at[s], mom.at[s], ys.at[s], zs.at[s]))
        total, rate = run_tiles(tgt[b], wide.at[b], 1, tiles)
        sums[moments_at(b), :] = own_sums[moments_at(b), :] + total
        rates[rows_at(b), :] = own_rates[rows_at(b), :] + rate
        return carry

    lax.fori_loop(0, blocks, per_target, 0)

    rate_ref[...] = (-support * grad_coeff) * rates[pl.ds(0, blocks, stride=ROWS), :]

    def summed(row):
        parts = [sums[pl.ds(y_row(p, row), blocks, stride=MOMENTS), :] for p in range(3)]
        return parts[0] + parts[1] + parts[2]

    mass_sum = summed(6)
    square = jnp.zeros_like(mass_sum)
    for d in range(3):
        pos = (own_ref[pl.ds(d, blocks, stride=ROWS), :] - center) * (1.0 / support)
        force = (4.0 * cohesion * support) * (pos * mass_sum - summed(d))
        if d == 2:
            force -= gravity
        square += force * force
        stage[pl.ds(d, blocks, stride=ROWS), :] = force
    for b in range(blocks):
        accel_ref[:, b * LANES : (b + 1) * LANES] = stage[b * ROWS : b * ROWS + 3, :]
    peak_ref[...] = jnp.full(peak_ref.shape, jnp.sqrt(jnp.max(square)), jnp.float32)


SMEM = pl.BlockSpec(memory_space=pltpu.SMEM)
VMEM = pl.BlockSpec(memory_space=pltpu.VMEM)
PARAMS = pltpu.CompilerParams(vmem_limit_bytes=32 * 1024 * 1024)


def tile_cost(tiles):
    return pl.CostEstimate(
        flops=tiles * LANES * LANES * 1000, bytes_accessed=0, transcendentals=0
    )


def source_shapes(count):
    return [
        ((count, DEPTH, 2 * LANES), jnp.bfloat16),
        ((count, MOMENTS, 2 * LANES), jnp.bfloat16),
        ((count, ROWS, LANES), jnp.float32),
        ((count, ROWS, LANES), jnp.float32),
    ]


def own_pass(own, walls, wall_pairs, choices):
    blocks = own.shape[0] // ROWS
    wall_blocks = walls.shape[0] // 4
    outs = source_shapes(blocks) + [
        ((blocks, LANES, DEPTH), jnp.bfloat16),
        ((blocks, 3, LANES, LANES), jnp.float32),
        ((blocks * MOMENTS, LANES), jnp.float32),
        ((blocks * ROWS, LANES), jnp.float32),
    ]
    return pl.pallas_call(
        functools.partial(own_kernel, blocks, wall_blocks),
        out_shape=[jax.ShapeDtypeStruct(*out) for out in outs],
        in_specs=[VMEM, VMEM, SMEM, VMEM, VMEM],
        out_specs=[VMEM] * len(outs),
        scratch_shapes=[pltpu.VMEM(*shape) for shape in source_shapes(wall_blocks)],
        compiler_params=PARAMS,
        cost_estimate=tile_cost(wall_pairs.size),
        name="own_pass",
    )(own, walls, wall_pairs, *choices)


def fluid_pass(own, ghosts, pair_list, place, choice, own_results):
    blocks = own.shape[0] // ROWS
    total = blocks + ghosts.shape[0] // ROWS
    return pl.pallas_call(
        functools.partial(fluid_kernel, blocks),
        out_shape=(
            jax.ShapeDtypeStruct((blocks, LANES), jnp.float32),
            jax.ShapeDtypeStruct((3, blocks * LANES), jnp.float32),
            jax.ShapeDtypeStruct((ROWS, LANES), jnp.float32),
        ),
        in_specs=[VMEM, VMEM, SMEM, SMEM, VMEM] + [VMEM] * len(own_results),
        out_specs=(VMEM, VMEM, VMEM),
        scratch_shapes=[pltpu.VMEM(*shape) for shape in source_shapes(total)]
        + [
            pltpu.VMEM((blocks * MOMENTS, LANES), jnp.float32),
            pltpu.VMEM((blocks * ROWS, LANES), jnp.float32),
            pltpu.VMEM((blocks * ROWS, LANES), jnp.float32),
            pltpu.SMEM((total,), jnp.int32),
        ],
        compiler_params=PARAMS,
        cost_estimate=tile_cost(pair_list.size),
        name="fluid_pass",
    )(own, ghosts, pair_list, place, choice, *own_results)


def outgoing_kernel(own_ref, list_ref, place_ref, sent_ref):
    for slot in range(8):
        mask = jnp.bitwise_xor(place_ref[0], slot)
        for g in range(list_ref.shape[1]):
            block = list_ref[jnp.maximum(mask - 1, 0), g]
            first = (slot * list_ref.shape[1] + g) * ROWS
            sent_ref[first : first + ROWS, :] = own_ref[rows_at(block), :]


def outgoing_pass(own, ghost_list, place):
    count = 8 * ghost_list.shape[1]
    return pl.pallas_call(
        outgoing_kernel,
        out_shape=jax.ShapeDtypeStruct((count * ROWS, LANES), jnp.float32),
        in_specs=[VMEM, SMEM, SMEM],
        out_specs=VMEM,
        name="outgoing_pass",
    )(own, ghost_list, place)


def swapped(shard, axis, bit):
    return lax.ppermute(shard, axis, [(i, i ^ 1 << bit) for i in range(lax.axis_size(axis))])


def padded(block, sides, width):
    for axis, dim in sides:
        count = lax.axis_size(axis)
        forward = [(i, i + 1) for i in range(count - 1)]
        backward = [(target, source) for source, target in forward]
        low = lax.ppermute(
            lax.slice_in_dim(block, block.shape[dim] - width, None, axis=dim), axis, forward
        )
        high = lax.ppermute(lax.slice_in_dim(block, 0, width, axis=dim), axis, backward)
        block = jnp.concatenate([low, block, high], axis=dim)
    return block


def per_device(fluid_state, ghost_list, pair_list, wall_state, wall_count, wall_pairs):
    block_total = fluid_state.shape[1] // LANES
    own = jnp.transpose(fluid_state.reshape(8, block_total, LANES), (1, 0, 2)).reshape(-1, LANES)
    place = (lax.axis_index("orb") % 8).reshape(1)
    groups = [list(range(g, g + 8)) for g in range(0, lax.axis_size("orb"), 8)]
    landed = lax.all_to_all(
        outgoing_pass(own, ghost_list, place).reshape(8, -1, LANES),
        "orb",
        0,
        0,
        axis_index_groups=groups if len(groups) > 1 else None,
    )
    alive = (
        (jnp.arange(LANES, dtype=jnp.int32)[None, :] < wall_count[:, None])
        .astype(jnp.float32)
        .reshape(-1)
    )
    wall_live = jnp.concatenate([wall_state[0:3], wall_state[3:4] * alive[None, :]], axis=0)
    extended = padded(wall_live, (("wall", 1),), EB * LANES)
    wall_cands = jnp.transpose(extended.reshape(4, -1, LANES), (1, 0, 2))
    choices = selections()
    own_results = own_pass(own, wall_cands.reshape(-1, LANES), wall_pairs, choices)
    rate, acceleration, local_peak = fluid_pass(
        own, landed.reshape(-1, LANES), pair_list, place, choices[0], own_results
    )
    peak = local_peak
    for axis in ("wall", "orb"):
        for bit in range((lax.axis_size(axis) - 1).bit_length()):
            peak = jnp.maximum(peak, swapped(peak, axis, bit))
    peak = peak[0, 0]
    time_step = courant * jnp.sqrt(smoothing / (peak + 1e-06))
    return (rate.reshape(-1), acceleration, time_step)


def solution(mesh):
    return jax.shard_map(
        per_device,
        mesh=mesh,
        in_specs=(
            P(None, ("orb", "wall")),
            P(None, ("orb", "wall")),
            P(("orb", "wall"), None),
            P(None, ("orb", "wall")),
            P(("orb", "wall")),
            P(("orb", "wall"), None),
        ),
        out_specs=(P(("orb", "wall")), P(None, ("orb", "wall")), P()),
        check_vma=False,
    )
```

```python
import functools

import jax
import jax.numpy as jnp
import numpy as np
from jax import lax
from jax.experimental import pallas as pl
from jax.experimental.pallas import tpu as pltpu
from jax.sharding import PartitionSpec as P

EB = 1
LANES = 128
ROWS = 8
PIECES = 6 * ROWS
DEPTH = 64
MOMENTS = 4 * ROWS
UNROLL = 4
GROUP = 2

smoothing = 0.1
support = 0.3
kernel_norm = 21.0 / (2.0 * 3.141592653589793 * support**3)
grad_coeff = -20.0 / support**2 * kernel_norm
tait_coeff = 25.0 / 7.0
visc_coeff = 0.05
cohesion = 2000.0
adhesion = 2000.0
gravity = 9.81
courant = 0.25

center = 0.3
shift = 0.0001 / support**2
press_coeff = -grad_coeff / (4.0 * cohesion)
density_coeff = (support * 4.0 * cohesion) / (-grad_coeff * visc_coeff * 2.0)

SPLITS = ((0, 0), (0, 1), (1, 0), (0, 2), (2, 0), (1, 1))


def y_row(piece, row):
    return piece * ROWS + row


def z_row(piece, row):
    return (3 + piece) * ROWS + row


def selections():
    source = np.zeros((2 * DEPTH, LANES), np.float32)
    target = np.zeros((PIECES, LANES), np.float32)
    one = z_row(0, 6)
    k = 0
    for p in range(3):
        for d in range(3):
            target[one, k] = 1.0
            source[k, z_row(p, d)] = 1.0
            source[DEPTH + k, z_row(p, 3 + d)] = -1.0
            target[z_row(p, d), k + 9] = 1.0
            source[k + 9, one] = 1.0
            target[z_row(p, 3 + d), k + 18] = 1.0
            source[DEPTH + k + 18, one] = -1.0
            k += 1
    k = 27
    for d in range(3):
        for p, t in SPLITS:
            target[y_row(p, d), k] = 1.0
            source[k, y_row(t, d)] = -2.0
            source[DEPTH + k, y_row(t, 3 + d)] = 1.0
            target[y_row(p, 3 + d), k + 18] = 1.0
            source[DEPTH + k + 18, y_row(t, d)] = 1.0
            k += 1
    spread = np.zeros((3, LANES, LANES), np.float32)
    for p in range(3):
        target[y_row(p, 6), DEPTH + p] = 1.0
        target[z_row(p, 7), DEPTH + 3 + p] = 1.0
        spread[0, DEPTH + p] = 1.0
        spread[1, DEPTH + 3 + p] = 1.0
        spread[2, DEPTH + 3 + p] = 2.0 * cohesion / adhesion
    target[one, DEPTH + 6] = 1.0
    spread[1:, DEPTH + 6] = -0.75
    parts = [source, target, spread.reshape(-1, LANES)]
    return jnp.asarray(np.concatenate(parts), jnp.bfloat16)


def source_choice(choices):
    return choices[: 2 * DEPTH, :PIECES]


def target_choice(choices):
    return choices[2 * DEPTH : 2 * DEPTH + PIECES, :]


def spread_choice(choices, which):
    first = 2 * DEPTH + PIECES + which * LANES
    return choices[first : first + LANES, :]


def split(value):
    first = value.astype(jnp.bfloat16).astype(jnp.float32)
    rest = value - first
    second = rest.astype(jnp.bfloat16).astype(jnp.float32)
    return [first, second, rest - second]


def pressure_ratio(density):
    square = density * density
    return tait_coeff * (square * square * square * density - 1.0) / square


def row_index():
    return lax.broadcasted_iota(jnp.int32, (ROWS, LANES), 0)


def state_of(block):
    row = row_index()
    y = jnp.where(row < 3, (block - center) * (1.0 / support), block)
    y = jnp.where(row == 6, block * density_coeff, y)
    density = jnp.where(row == 7, pltpu.roll(block, 1, axis=0), 1.0)
    press = press_coeff * pressure_ratio(density)
    z = y * jnp.where(row < 3, y, pltpu.roll(y, 3, axis=0))
    return y, jnp.where(row < 6, z, jnp.where(row == 6, 1.0, press))


def pieces_of(y, z):
    return jnp.concatenate(split(y) + split(z), axis=0)


def put_source(block, choices, s, src, mom, rows, mass_factor=1.0):
    row = row_index()
    y, z = state_of(block)
    pieces = pieces_of(y, z).astype(jnp.bfloat16)
    chosen = jnp.dot(source_choice(choices), pieces, preferred_element_type=jnp.float32)
    chosen = chosen.astype(jnp.bfloat16)
    src[s] = jnp.concatenate([chosen[:DEPTH], chosen[DEPTH:]], axis=1)
    moment = (mass_factor * block[7:8]) * jnp.where(row == 6, 1.0, y)
    moments = jnp.concatenate(split(moment) + [jnp.zeros_like(moment)], axis=0)
    moments = moments.astype(jnp.bfloat16)
    mom[s] = jnp.concatenate([moments, moments], axis=1)
    rows[s, :ROWS] = y
    rows[s, ROWS:] = z
    return y, z


def put_target(y, z, choices, b, tgt):
    pieces = pieces_of(y, z).T.astype(jnp.bfloat16)
    chosen = jnp.dot(pieces, target_choice(choices), preferred_element_type=jnp.float32)
    tgt[b] = chosen.astype(jnp.bfloat16)


def rows_at(index):
    return pl.ds(pl.multiple_of(index * ROWS, ROWS), ROWS)


def weights_of(product, press_i, rho_i, rows):
    guarded = jnp.maximum(product[:, :LANES], 1e-30)
    approach = product[:, LANES:]
    falloff = jnp.maximum(1.0 - guarded * lax.rsqrt(guarded), 0.0)
    cubed = falloff * falloff * falloff
    blend = falloff + press_i
    if rho_i is not None:
        spread = (guarded + shift) * (rho_i + rows[6:7])
        blend += rows[ROWS + 7 : ROWS + 8]
        blend += jnp.maximum(approach, 0.0) * pl.reciprocal(spread, approx=True)
    weight = cubed * blend
    high = weight.astype(jnp.bfloat16)
    low = (weight - high.astype(jnp.float32)).astype(jnp.bfloat16)
    return [high, low], (cubed * approach) * rows[7:8]


def across(left, right):
    return lax.dot_general(
        left, right, (((1,), (1,)), ((), ())), preferred_element_type=jnp.float32
    )


def run_tiles(target, press_i, rho_i, tiles):
    features = target[:, :DEPTH]

    def product_of(group):
        columns = jnp.concatenate([tile[0][...] for tile in group], axis=1)
        return jnp.dot(features, columns, preferred_element_type=jnp.float32)

    groups = [tiles[n : n + GROUP] for n in range(0, len(tiles), GROUP)]
    total = jnp.zeros((MOMENTS, LANES), jnp.float32)
    rate = jnp.zeros((LANES, LANES), jnp.float32)
    ahead = product_of(groups[0])
    waiting = None
    for n, group in enumerate(groups):
        product = ahead
        if n + 1 < len(groups):
            ahead = product_of(groups[n + 1])
        weights = []
        for m, (_, _, rows) in enumerate(group):
            columns = slice(2 * m * LANES, 2 * (m + 1) * LANES)
            pair, part = weights_of(product[:, columns], press_i, rho_i, rows)
            weights += pair
            rate += part
        if waiting is not None:
            total += across(*waiting)
        moments = jnp.concatenate([tile[1][...] for tile in group], axis=1)
        waiting = (moments, jnp.concatenate(weights, axis=1))
    total += across(*waiting)
    ones = jnp.ones((ROWS, 3 * LANES), jnp.bfloat16)
    rates = across(ones, jnp.concatenate(split(rate), axis=1).astype(jnp.bfloat16))
    return total, rates


def moments_at(b):
    return pl.ds(pl.multiple_of(b * MOMENTS, MOMENTS), MOMENTS)


def spread_of(target, choices, which):
    return jnp.dot(target, spread_choice(choices, which), preferred_element_type=jnp.float32)


def own_kernel(
    own_ref, low_ref, wall_ref, high_ref, wpair_ref, choices,
    src, mom, rows, tgt, sums, rates, wsrc, wmom, wrows,
):
    blocks = tgt.shape[0]

    def build(b, carry):
        y, z = put_source(own_ref[rows_at(b), :], choices, b, src, mom, rows)
        put_target(y, z, choices, b, tgt)
        return carry

    lax.fori_loop(0, blocks, build, 0, unroll=UNROLL)
    row = row_index()
    count = 0
    for ref in (low_ref, wall_ref, high_ref):
        for c in range(ref.shape[0] // 4):
            held = ref[4 * c : 4 * c + 4, :]
            both = jnp.concatenate([held, held], axis=0)
            density = jnp.where(row == 6, 1.0, 0.0)
            block = jnp.where((row < 3) | (row == 7), both, density)
            put_source(block, choices, count, wsrc, wmom, wrows, adhesion / cohesion)
            count += 1

    def per_target(b, carry):
        tiles = []
        for k in range(wpair_ref.shape[1]):
            s = wpair_ref[b, k]
            tiles.append((wsrc.at[s], wmom.at[s], wrows.at[s]))
        target = tgt[b]
        total, rate = run_tiles(target, spread_of(target, choices, 2), None, tiles)
        sums[moments_at(b), :] = total
        rates[rows_at(b), :] = rate
        return carry

    lax.fori_loop(0, blocks, per_target, 0, unroll=UNROLL)


def fluid_kernel(
    own_ref, ghost_ref, pair_ref, place_ref, choices, own_src, own_mom, own_rows,
    tgt, own_sums, own_rates, rate_ref, accel_ref, peak_ref,
    src, mom, rows, sums, rates, stage, table,
):
    blocks = tgt.shape[0]
    ghosts = ghost_ref.shape[0] // ROWS
    per_mask = ghosts // 8
    for c in range(blocks):
        table[c] = c
    for mask in range(1, 8):
        for g in range(per_mask):
            table[blocks + (mask - 1) * per_mask + g] = (
                blocks + jnp.bitwise_xor(place_ref[0], mask) * per_mask + g
            )
    src[:blocks] = own_src[...]
    mom[:blocks] = own_mom[...]
    rows[:blocks] = own_rows[...]

    def build(g, carry):
        put_source(ghost_ref[rows_at(g), :], choices, blocks + g, src, mom, rows)
        return carry

    lax.fori_loop(0, ghosts, build, 0, unroll=UNROLL)

    def per_target(b, carry):
        tiles = []
        for k in range(pair_ref.shape[1]):
            s = table[pair_ref[b, k]]
            tiles.append((src.at[s], mom.at[s], rows.at[s]))
        target = tgt[b]
        spreads = [spread_of(target, choices, which) for which in (1, 0)]
        total, rate = run_tiles(target, *spreads, tiles)
        sums[moments_at(b), :] = own_sums[moments_at(b), :] + total
        rates[rows_at(b), :] = own_rates[rows_at(b), :] + rate
        return carry

    lax.fori_loop(0, blocks, per_target, 0)

    rate_ref[...] = (-support * grad_coeff) * rates[pl.ds(0, blocks, stride=ROWS), :]

    def summed(row):
        parts = [sums[pl.ds(y_row(p, row), blocks, stride=MOMENTS), :] for p in range(3)]
        return parts[0] + parts[1] + parts[2]

    mass_sum = summed(6)
    square = jnp.zeros_like(mass_sum)
    for d in range(3):
        pos = (own_ref[pl.ds(d, blocks, stride=ROWS), :] - center) * (1.0 / support)
        force = (4.0 * cohesion * support) * (pos * mass_sum - summed(d))
        if d == 2:
            force -= gravity
        square += force * force
        stage[pl.ds(d, blocks, stride=ROWS), :] = force
    for b in range(blocks):
        accel_ref[:, b * LANES : (b + 1) * LANES] = stage[b * ROWS : b * ROWS + 3, :]
    peak_ref[...] = jnp.full(peak_ref.shape, jnp.sqrt(jnp.max(square)), jnp.float32)


SMEM = pl.BlockSpec(memory_space=pltpu.SMEM)
VMEM = pl.BlockSpec(memory_space=pltpu.VMEM)
PARAMS = pltpu.CompilerParams(vmem_limit_bytes=32 * 1024 * 1024)


def tile_cost(tiles):
    return pl.CostEstimate(
        flops=tiles * LANES * LANES * 1000, bytes_accessed=0, transcendentals=0
    )


def source_shapes(count):
    return [
        ((count, DEPTH, 2 * LANES), jnp.bfloat16),
        ((count, MOMENTS, 2 * LANES), jnp.bfloat16),
        ((count, 2 * ROWS, LANES), jnp.float32),
    ]


def own_pass(own, walls, wall_pairs, choices):
    blocks = own.shape[0] // ROWS
    wall_blocks = sum(part.shape[0] for part in walls) // 4
    outs = source_shapes(blocks) + [
        ((blocks, LANES, LANES), jnp.bfloat16),
        ((blocks * MOMENTS, LANES), jnp.float32),
        ((blocks * ROWS, LANES), jnp.float32),
    ]
    return pl.pallas_call(
        own_kernel,
        out_shape=[jax.ShapeDtypeStruct(*out) for out in outs],
        in_specs=[VMEM, VMEM, VMEM, VMEM, SMEM, VMEM],
        out_specs=[VMEM] * len(outs),
        scratch_shapes=[pltpu.VMEM(*shape) for shape in source_shapes(wall_blocks)],
        compiler_params=PARAMS,
        cost_estimate=tile_cost(wall_pairs.size),
        name="own_pass",
    )(own, *walls, wall_pairs, choices)


def fluid_pass(own, ghosts, pair_list, place, choices, own_results):
    blocks = own.shape[0] // ROWS
    total = blocks + ghosts.shape[0] // ROWS
    return pl.pallas_call(
        fluid_kernel,
        out_shape=(
            jax.ShapeDtypeStruct((blocks, LANES), jnp.float32),
            jax.ShapeDtypeStruct((3, blocks * LANES), jnp.float32),
            jax.ShapeDtypeStruct((ROWS, LANES), jnp.float32),
        ),
        in_specs=[VMEM, VMEM, SMEM, SMEM, VMEM] + [VMEM] * len(own_results),
        out_specs=(VMEM, VMEM, VMEM),
        scratch_shapes=[pltpu.VMEM(*shape) for shape in source_shapes(total)]
        + [
            pltpu.VMEM((blocks * MOMENTS, LANES), jnp.float32),
            pltpu.VMEM((blocks * ROWS, LANES), jnp.float32),
            pltpu.VMEM((blocks * ROWS, LANES), jnp.float32),
            pltpu.SMEM((total,), jnp.int32),
        ],
        compiler_params=PARAMS,
        cost_estimate=tile_cost(pair_list.size),
        name="fluid_pass",
    )(own, ghosts, pair_list, place, choices, *own_results)


def outgoing_kernel(own_ref, list_ref, place_ref, wall_ref, count_ref, sent_ref, live_ref):
    for slot in range(8):
        mask = jnp.bitwise_xor(place_ref[0], slot)
        for g in range(list_ref.shape[1]):
            block = list_ref[jnp.maximum(mask - 1, 0), g]
            first = (slot * list_ref.shape[1] + g) * ROWS
            sent_ref[first : first + ROWS, :] = own_ref[rows_at(block), :]
    lane = lax.broadcasted_iota(jnp.int32, (4, LANES), 1)
    row = lax.broadcasted_iota(jnp.int32, (4, LANES), 0)
    for c in range(wall_ref.shape[1] // LANES):
        block = wall_ref[:, c * LANES : (c + 1) * LANES]
        kept = (row < 3) | (lane < count_ref[c])
        live_ref[4 * c : 4 * c + 4, :] = jnp.where(kept, block, 0.0)


def outgoing_pass(own, ghost_list, place, wall_state, wall_count):
    count = 8 * ghost_list.shape[1]
    walls = wall_state.shape[1] // LANES
    return pl.pallas_call(
        outgoing_kernel,
        out_shape=(
            jax.ShapeDtypeStruct((count * ROWS, LANES), jnp.float32),
            jax.ShapeDtypeStruct((walls * 4, LANES), jnp.float32),
        ),
        in_specs=[VMEM, SMEM, SMEM, VMEM, SMEM],
        out_specs=(VMEM, VMEM),
        name="outgoing_pass",
    )(own, ghost_list, place, wall_state, wall_count)


def swapped(shard, axis, bit):
    return lax.ppermute(shard, axis, [(i, i ^ 1 << bit) for i in range(lax.axis_size(axis))])


def edges(walls, axis, width):
    count = lax.axis_size(axis)
    forward = [(i, i + 1) for i in range(count - 1)]
    backward = [(target, source) for source, target in forward]
    return (
        lax.ppermute(walls[walls.shape[0] - width :], axis, forward),
        lax.ppermute(walls[:width], axis, backward),
    )


def per_device(fluid_state, ghost_list, pair_list, wall_state, wall_count, wall_pairs):
    block_total = fluid_state.shape[1] // LANES
    own = jnp.transpose(fluid_state.reshape(8, block_total, LANES), (1, 0, 2)).reshape(-1, LANES)
    place = (lax.axis_index("orb") % 8).reshape(1)
    sent, walls = outgoing_pass(own, ghost_list, place, wall_state, wall_count)
    low, high = edges(walls, "wall", 4 * EB)
    groups = [list(range(g, g + 8)) for g in range(0, lax.axis_size("orb"), 8)]
    landed = lax.all_to_all(
        sent.reshape(8, -1, LANES),
        "orb",
        0,
        0,
        axis_index_groups=groups if len(groups) > 1 else None,
    )
    choices = selections()
    own_results = own_pass(own, (low, walls, high), wall_pairs, choices)
    rate, acceleration, local_peak = fluid_pass(
        own, landed.reshape(-1, LANES), pair_list, place, choices, own_results
    )
    peak = local_peak
    for axis in ("wall", "orb"):
        for bit in range((lax.axis_size(axis) - 1).bit_length()):
            peak = jnp.maximum(peak, swapped(peak, axis, bit))
    peak = peak[0, 0]
    time_step = courant * jnp.sqrt(smoothing / (peak + 1e-06))
    return (rate.reshape(-1), acceleration, time_step)


def solution(mesh):
    return jax.shard_map(
        per_device,
        mesh=mesh,
        in_specs=(
            P(None, ("orb", "wall")),
            P(None, ("orb", "wall")),
            P(("orb", "wall"), None),
            P(None, ("orb", "wall")),
            P(("orb", "wall")),
            P(("orb", "wall"), None),
        ),
        out_specs=(P(("orb", "wall")), P(None, ("orb", "wall")), P()),
        check_vma=False,
    )
```

```python
import functools

import jax
import jax.numpy as jnp
from jax import lax
from jax.experimental import pallas as pl
from jax.experimental.pallas import tpu as pltpu
from jax.sharding import PartitionSpec as P

EB = 1
LANES = 128
ROWS = 8
DEPTH = 12 * ROWS
MOMENTS = 4 * ROWS
UNROLL = 4

smoothing = 0.1
support = 0.3
kernel_norm = 21.0 / (2.0 * 3.141592653589793 * support**3)
grad_coeff = -20.0 / support**2 * kernel_norm
tait_coeff = 25.0 / 7.0
visc_coeff = 0.05
cohesion = 2000.0
adhesion = 2000.0
gravity = 9.81
courant = 0.25

center = 0.3
shift = 0.0001 / support**2
press_coeff = -grad_coeff / (4.0 * cohesion)
density_coeff = (support * 4.0 * cohesion) / (-grad_coeff * visc_coeff * 2.0)

SPLITS = ((0, 0), (0, 1), (1, 0), (0, 2), (2, 0), (1, 1))


def split(value):
    first = value.astype(jnp.bfloat16).astype(jnp.float32)
    rest = value - first
    second = rest.astype(jnp.bfloat16).astype(jnp.float32)
    return [first, second, rest - second]


def pressure_ratio(density):
    square = density * density
    return tait_coeff * (square * square * square * density - 1.0) / square


def row_index():
    return lax.broadcasted_iota(jnp.int32, (ROWS, LANES), 0)


def state_of(block):
    row = row_index()
    y = jnp.where(row < 3, (block - center) * (1.0 / support), block)
    y = jnp.where(row == 6, block * density_coeff, y)
    products = y * jnp.where(row < 3, y, pltpu.roll(y, 3, axis=0))
    sums = products + pltpu.roll(products, ROWS - 1, axis=0) + pltpu.roll(products, ROWS - 2, axis=0)

    def everywhere(value, index):
        return jnp.broadcast_to(value[index : index + 1], (ROWS, LANES))

    press = press_coeff * pressure_ratio(everywhere(block, 6))
    return (
        y, everywhere(sums, 0), everywhere(sums, 3), everywhere(y, 6), everywhere(y, 7), press,
    )


def chosen(default, *cases):
    row = row_index()
    value = jnp.full((ROWS, LANES), default, jnp.float32)
    for index, case in cases:
        value = jnp.where(row == index, case, value)
    return value


def target_groups(state):
    y, n, e, r, _, press = state
    row = row_index()
    first = jnp.where(row < 6, y, jnp.where(row == 6, n + shift, e))
    scaled = r * jnp.where(row < 3, y, jnp.where(row == 3, 1.0, n + shift))
    second = jnp.where(row < 5, scaled, chosen(0.0, (5, press), (6, 1.0)))
    return first, second


def source_groups(state, wall):
    y, n, e, r, m, press = state
    row = row_index()
    minus = jnp.where(row < 3, -2.0 * y, 0.0)
    near = chosen(minus, (6, 1.0)), chosen(0.0, (6, n - shift))
    turned = jnp.where(row < 3, pltpu.roll(y, 5, axis=0), pltpu.roll(y, 3, axis=0))
    along = m * jnp.where(row < 6, turned, chosen(0.0, (7, -1.0))), chosen(0.0, (6, -m * e))
    if wall:
        press_part = chosen(0.0, (5, 2.0 * cohesion / adhesion), (6, -0.75))
        return near, along, (None, press_part)
    spread = m * r * near[0], m * chosen(minus, (3, n), (4, 1.0), (6, r * n))
    return near, along, spread, (None, chosen(0.0, (5, 1.0), (6, press - 0.75)))


def put_source(block, s, src, mom, mass_factor=1.0, wall=False):
    state = state_of(block)
    for n, (first, second) in enumerate(source_groups(state, wall)):
        firsts = split(first) if first is not None else [jnp.zeros((ROWS, LANES))] * 3
        pieces = [
            jnp.concatenate(pair, axis=0).astype(jnp.bfloat16)
            for pair in zip(firsts, split(second))
        ]
        lanes = slice(n * LANES, (n + 1) * LANES)
        for k, (_, piece) in enumerate(SPLITS):
            src[s, 2 * ROWS * k : 2 * ROWS * (k + 1), lanes] = pieces[piece]
    moment = (mass_factor * state[4]) * jnp.where(row_index() == 6, 1.0, state[0])
    moments = jnp.concatenate(split(moment) + [jnp.zeros_like(moment)], axis=0)
    moments = moments.astype(jnp.bfloat16)
    mom[s] = jnp.concatenate([moments, moments], axis=1)
    return state


def put_target(state, b, tgt):
    pieces = [jnp.concatenate(pair, axis=0) for pair in zip(*map(split, target_groups(state)))]
    rows = jnp.concatenate([pieces[piece] for piece, _ in SPLITS], axis=0)
    tgt[b] = rows.T.astype(jnp.bfloat16)


def rows_at(index):
    return pl.ds(pl.multiple_of(index * ROWS, ROWS), ROWS)


def weights_of(product, wall):
    values = [product[:, n * LANES : (n + 1) * LANES] for n in range(3 if wall else 4)]
    guarded = jnp.maximum(values[0], 1e-30)
    approach, press = values[1], values[-1]
    falloff = jnp.maximum(1.0 - guarded * lax.rsqrt(guarded), 0.0)
    cubed = falloff * falloff * falloff
    blend = falloff + press
    if not wall:
        blend += jnp.maximum(approach, 0.0) * pl.reciprocal(values[2], approx=True)
    weight = cubed * blend
    high = weight.astype(jnp.bfloat16)
    low = (weight - high.astype(jnp.float32)).astype(jnp.bfloat16)
    return jnp.concatenate([high, low], axis=1), cubed * approach


def across(left, right):
    return lax.dot_general(
        left, right, (((1,), (1,)), ((), ())), preferred_element_type=jnp.float32
    )


def run_tiles(target, tiles, wall):
    def product_of(tile):
        return jnp.dot(target, tile[0][...], preferred_element_type=jnp.float32)

    total = jnp.zeros((MOMENTS, LANES), jnp.float32)
    rate = jnp.zeros((LANES, LANES), jnp.float32)
    ahead = product_of(tiles[0])
    waiting = None
    for n, (_, moments) in enumerate(tiles):
        product = ahead
        if n + 1 < len(tiles):
            ahead = product_of(tiles[n + 1])
        weights, part = weights_of(product, wall)
        rate += part
        if waiting is not None:
            total += across(*waiting)
        waiting = (moments[...], weights)
    total += across(*waiting)
    ones = jnp.ones((ROWS, 3 * LANES), jnp.bfloat16)
    rates = across(ones, jnp.concatenate(split(rate), axis=1).astype(jnp.bfloat16))
    return total, rates


def moments_at(b):
    return pl.ds(pl.multiple_of(b * MOMENTS, MOMENTS), MOMENTS)


def own_kernel(
    own_ref, wall_ref, edge0_ref, edge1_ref, wpair_ref, odd_ref,
    src, mom, tgt, sums, rates, wsrc, wmom, table,
):
    blocks = tgt.shape[0]

    def build(b, carry):
        state = put_source(own_ref[rows_at(b), :], b, src, mom)
        put_target(state, b, tgt)
        return carry

    lax.fori_loop(0, blocks, build, 0, unroll=UNROLL)
    row = row_index()
    count = 0
    for ref in (wall_ref, edge0_ref, edge1_ref):
        for c in range(ref.shape[0] // 4):
            held = ref[4 * c : 4 * c + 4, :]
            both = jnp.concatenate([held, held], axis=0)
            density = jnp.where(row == 6, 1.0, 0.0)
            block = jnp.where((row < 3) | (row == 7), both, density)
            put_source(block, count, wsrc, wmom, adhesion / cohesion, True)
            count += 1
    inner, edge = wall_ref.shape[0] // 4, edge0_ref.shape[0] // 4
    odd = odd_ref[0]
    for c in range(inner):
        table[edge + c] = c
    for c in range(edge):
        table[c] = inner + (1 - odd) * edge + c
        table[edge + inner + c] = inner + odd * edge + c

    def per_target(b, carry):
        tiles = []
        for k in range(wpair_ref.shape[1]):
            s = table[wpair_ref[b, k]]
            tiles.append((wsrc.at[s], wmom.at[s]))
        total, rate = run_tiles(tgt[b], tiles, True)
        sums[moments_at(b), :] = total
        rates[rows_at(b), :] = rate
        return carry

    lax.fori_loop(0, blocks, per_target, 0, unroll=UNROLL)


def fluid_kernel(
    own_ref, ghost_ref, pair_ref, place_ref, own_src, own_mom,
    tgt, own_sums, own_rates, rate_ref, accel_ref, peak_ref,
    src, mom, sums, rates, stage, table, copied,
):
    blocks = tgt.shape[0]
    ghosts = ghost_ref.shape[0] // ROWS
    per_mask = ghosts // 8
    copies = [
        pltpu.make_async_copy(own_src, src.at[pl.ds(0, blocks)], copied.at[0]),
        pltpu.make_async_copy(own_mom, mom.at[pl.ds(0, blocks)], copied.at[1]),
    ]
    for copy in copies:
        copy.start()
    for c in range(blocks):
        table[c] = c
    for mask in range(1, 8):
        for g in range(per_mask):
            table[blocks + (mask - 1) * per_mask + g] = (
                blocks + jnp.bitwise_xor(place_ref[0], mask) * per_mask + g
            )

    def build(g, carry):
        put_source(ghost_ref[rows_at(g), :], blocks + g, src, mom)
        return carry

    lax.fori_loop(0, ghosts, build, 0, unroll=UNROLL)
    for copy in copies:
        copy.wait()

    def per_target(b, carry):
        tiles = []
        for k in range(pair_ref.shape[1]):
            s = table[pair_ref[b, k]]
            tiles.append((src.at[s], mom.at[s]))
        total, rate = run_tiles(tgt[b], tiles, False)
        sums[moments_at(b), :] = own_sums[moments_at(b), :] + total
        rates[rows_at(b), :] = own_rates[rows_at(b), :] + rate
        return carry

    lax.fori_loop(0, blocks, per_target, 0)

    rate_ref[...] = (-support * grad_coeff) * rates[pl.ds(0, blocks, stride=ROWS), :]

    def summed(row):
        parts = [sums[pl.ds(p * ROWS + row, blocks, stride=MOMENTS), :] for p in range(3)]
        return parts[0] + parts[1] + parts[2]

    mass_sum = summed(6)
    square = jnp.zeros_like(mass_sum)
    for d in range(3):
        pos = (own_ref[pl.ds(d, blocks, stride=ROWS), :] - center) * (1.0 / support)
        force = (4.0 * cohesion * support) * (pos * mass_sum - summed(d))
        if d == 2:
            force -= gravity
        square += force * force
        stage[pl.ds(d, blocks, stride=ROWS), :] = force
    for b in range(blocks):
        accel_ref[:, b * LANES : (b + 1) * LANES] = stage[b * ROWS : b * ROWS + 3, :]
    peak_ref[...] = jnp.full(peak_ref.shape, jnp.sqrt(jnp.max(square)), jnp.float32)


SMEM = pl.BlockSpec(memory_space=pltpu.SMEM)
VMEM = pl.BlockSpec(memory_space=pltpu.VMEM)
PARAMS = pltpu.CompilerParams(vmem_limit_bytes=32 * 1024 * 1024)


def tile_cost(tiles):
    return pl.CostEstimate(
        flops=tiles * LANES * LANES * 1000, bytes_accessed=0, transcendentals=0
    )


def source_shapes(count, values):
    return [
        ((count, DEPTH, values * LANES), jnp.bfloat16),
        ((count, MOMENTS, 2 * LANES), jnp.bfloat16),
    ]


def own_pass(own, walls, edges, wall_pairs, odd):
    blocks = own.shape[0] // ROWS
    wall_blocks = (walls.shape[0] + 2 * edges[0].shape[0]) // 4
    outs = source_shapes(blocks, 4) + [
        ((blocks, LANES, DEPTH), jnp.bfloat16),
        ((blocks * MOMENTS, LANES), jnp.float32),
        ((blocks * ROWS, LANES), jnp.float32),
    ]
    return pl.pallas_call(
        own_kernel,
        out_shape=[jax.ShapeDtypeStruct(*out) for out in outs],
        in_specs=[VMEM, VMEM, VMEM, VMEM, SMEM, SMEM],
        out_specs=[VMEM] * len(outs),
        scratch_shapes=[pltpu.VMEM(*shape) for shape in source_shapes(wall_blocks, 3)]
        + [pltpu.SMEM((wall_blocks,), jnp.int32)],
        compiler_params=PARAMS,
        cost_estimate=tile_cost(wall_pairs.size),
        name="own_pass",
    )(own, walls, *edges, wall_pairs, odd)


def fluid_pass(own, ghosts, pair_list, place, own_results):
    blocks = own.shape[0] // ROWS
    total = blocks + ghosts.shape[0] // ROWS
    return pl.pallas_call(
        fluid_kernel,
        out_shape=(
            jax.ShapeDtypeStruct((blocks, LANES), jnp.float32),
            jax.ShapeDtypeStruct((3, blocks * LANES), jnp.float32),
            jax.ShapeDtypeStruct((ROWS, LANES), jnp.float32),
        ),
        in_specs=[VMEM, VMEM, SMEM, SMEM] + [VMEM] * len(own_results),
        out_specs=(VMEM, VMEM, VMEM),
        scratch_shapes=[pltpu.VMEM(*shape) for shape in source_shapes(total, 4)]
        + [
            pltpu.VMEM((blocks * MOMENTS, LANES), jnp.float32),
            pltpu.VMEM((blocks * ROWS, LANES), jnp.float32),
            pltpu.VMEM((blocks * ROWS, LANES), jnp.float32),
            pltpu.SMEM((total,), jnp.int32),
            pltpu.SemaphoreType.DMA((2,)),
        ],
        compiler_params=PARAMS,
        cost_estimate=tile_cost(pair_list.size),
        name="fluid_pass",
    )(own, ghosts, pair_list, place, *own_results)


def outgoing_kernel(own_ref, list_ref, place_ref, wall_ref, count_ref, sent_ref, live_ref):
    for slot in range(8):
        mask = jnp.bitwise_xor(place_ref[0], slot)
        for g in range(list_ref.shape[1]):
            block = list_ref[jnp.maximum(mask - 1, 0), g]
            first = (slot * list_ref.shape[1] + g) * ROWS
            sent_ref[first : first + ROWS, :] = own_ref[rows_at(block), :]
    lane = lax.broadcasted_iota(jnp.int32, (4, LANES), 1)
    row = lax.broadcasted_iota(jnp.int32, (4, LANES), 0)
    for c in range(wall_ref.shape[1] // LANES):
        block = wall_ref[:, c * LANES : (c + 1) * LANES]
        kept = (row < 3) | (lane < count_ref[c])
        live_ref[4 * c : 4 * c + 4, :] = jnp.where(kept, block, 0.0)


def outgoing_pass(own, ghost_list, place, wall_state, wall_count):
    count = 8 * ghost_list.shape[1]
    walls = wall_state.shape[1] // LANES
    return pl.pallas_call(
        outgoing_kernel,
        out_shape=(
            jax.ShapeDtypeStruct((count * ROWS, LANES), jnp.float32),
            jax.ShapeDtypeStruct((walls * 4, LANES), jnp.float32),
        ),
        in_specs=[VMEM, SMEM, SMEM, VMEM, SMEM],
        out_specs=(VMEM, VMEM),
        name="outgoing_pass",
    )(own, ghost_list, place, wall_state, wall_count)


def swapped(shard, axis, bit):
    return lax.ppermute(shard, axis, [(i, i ^ 1 << bit) for i in range(lax.axis_size(axis))])


def edges(walls, axis, width):
    count = lax.axis_size(axis)
    odd = lax.axis_index(axis) % 2
    first, last = walls[:width], walls[walls.shape[0] - width :]
    landed = []
    for start in range(2):
        pairs = [(i, i + 1) for i in range(start, count - 1, 2)]
        pairs += [(j, i) for i, j in pairs]
        sent = jnp.where(odd == start, last, first)
        landed.append(lax.ppermute(sent, axis, pairs))
    return landed, odd.reshape(1)


def per_device(fluid_state, ghost_list, pair_list, wall_state, wall_count, wall_pairs):
    block_total = fluid_state.shape[1] // LANES
    own = jnp.transpose(fluid_state.reshape(8, block_total, LANES), (1, 0, 2)).reshape(-1, LANES)
    place = (lax.axis_index("orb") % 8).reshape(1)
    sent, walls = outgoing_pass(own, ghost_list, place, wall_state, wall_count)
    facing, odd = edges(walls, "wall", 4 * EB)
    groups = [list(range(g, g + 8)) for g in range(0, lax.axis_size("orb"), 8)]
    landed = lax.all_to_all(
        sent.reshape(8, -1, LANES),
        "orb",
        0,
        0,
        axis_index_groups=groups if len(groups) > 1 else None,
    )
    own_results = own_pass(own, walls, facing, wall_pairs, odd)
    rate, acceleration, local_peak = fluid_pass(
        own, landed.reshape(-1, LANES), pair_list, place, own_results
    )
    peak = local_peak
    for axis in ("wall", "orb"):
        for bit in range((lax.axis_size(axis) - 1).bit_length()):
            peak = jnp.maximum(peak, swapped(peak, axis, bit))
    peak = peak[0, 0]
    time_step = courant * jnp.sqrt(smoothing / (peak + 1e-06))
    return (rate.reshape(-1), acceleration, time_step)


def solution(mesh):
    return jax.shard_map(
        per_device,
        mesh=mesh,
        in_specs=(
            P(None, ("orb", "wall")),
            P(None, ("orb", "wall")),
            P(("orb", "wall"), None),
            P(None, ("orb", "wall")),
            P(("orb", "wall")),
            P(("orb", "wall"), None),
        ),
        out_specs=(P(("orb", "wall")), P(None, ("orb", "wall")), P()),
        check_vma=False,
    )
```

```python
import functools

import jax
import jax.numpy as jnp
from jax import lax
from jax.experimental import pallas as pl
from jax.experimental.pallas import tpu as pltpu
from jax.sharding import PartitionSpec as P

EB = 1
LANES = 128
ROWS = 8
DEPTH = 12 * ROWS
MOMENTS = 4 * ROWS
UNROLL = 4
WALL_TARGETS = 6
FLUID_TARGETS = 3

smoothing = 0.1
support = 0.3
kernel_norm = 21.0 / (2.0 * 3.141592653589793 * support**3)
grad_coeff = -20.0 / support**2 * kernel_norm
tait_coeff = 25.0 / 7.0
visc_coeff = 0.05
cohesion = 2000.0
adhesion = 2000.0
gravity = 9.81
courant = 0.25

center = 0.3
shift = 0.0001 / support**2
press_coeff = -grad_coeff / (4.0 * cohesion)
density_coeff = (support * 4.0 * cohesion) / (-grad_coeff * visc_coeff * 2.0)

SPLITS = ((0, 0), (0, 1), (1, 0), (0, 2), (2, 0), (1, 1))


def split(value):
    first = value.astype(jnp.bfloat16).astype(jnp.float32)
    rest = value - first
    second = rest.astype(jnp.bfloat16).astype(jnp.float32)
    return [first, second, rest - second]


def pressure_ratio(density):
    square = density * density
    return tait_coeff * (square * square * square * density - 1.0) / square


def row_index():
    return lax.broadcasted_iota(jnp.int32, (ROWS, LANES), 0)


def state_of(block):
    row = row_index()
    y = jnp.where(row < 3, (block - center) * (1.0 / support), block)
    y = jnp.where(row == 6, block * density_coeff, y)
    products = y * jnp.where(row < 3, y, pltpu.roll(y, 3, axis=0))
    sums = products + pltpu.roll(products, ROWS - 1, axis=0) + pltpu.roll(products, ROWS - 2, axis=0)

    def everywhere(value, index):
        return jnp.broadcast_to(value[index : index + 1], (ROWS, LANES))

    press = press_coeff * pressure_ratio(everywhere(block, 6))
    return (
        y, everywhere(sums, 0), everywhere(sums, 3), everywhere(y, 6), everywhere(y, 7), press,
    )


def chosen(default, *cases):
    row = row_index()
    value = jnp.full((ROWS, LANES), default, jnp.float32)
    for index, case in cases:
        value = jnp.where(row == index, case, value)
    return value


def target_groups(state):
    y, n, e, r, _, press = state
    row = row_index()
    first = jnp.where(row < 6, y, jnp.where(row == 6, n + shift, e))
    scaled = r * jnp.where(row < 3, y, jnp.where(row == 3, 1.0, n + shift))
    second = jnp.where(row < 5, scaled, chosen(0.0, (5, press), (6, 1.0)))
    return first, second


def source_groups(state, wall):
    y, n, e, r, m, press = state
    row = row_index()
    minus = jnp.where(row < 3, -2.0 * y, 0.0)
    near = chosen(minus, (6, 1.0)), chosen(0.0, (6, n - shift))
    turned = jnp.where(row < 3, pltpu.roll(y, 5, axis=0), pltpu.roll(y, 3, axis=0))
    along = m * jnp.where(row < 6, turned, chosen(0.0, (7, -1.0))), chosen(0.0, (6, -m * e))
    if wall:
        press_part = chosen(0.0, (5, 2.0 * cohesion / adhesion), (6, -0.75))
        return near, along, (None, press_part)
    spread = m * r * near[0], m * chosen(minus, (3, n), (4, 1.0), (6, r * n))
    return near, along, spread, (None, chosen(0.0, (5, 1.0), (6, press - 0.75)))


def put_source(block, s, src, mom, mass_factor=1.0, wall=False):
    state = state_of(block)
    for n, (first, second) in enumerate(source_groups(state, wall)):
        firsts = split(first) if first is not None else [jnp.zeros((ROWS, LANES))] * 3
        pieces = [
            jnp.concatenate(pair, axis=0).astype(jnp.bfloat16)
            for pair in zip(firsts, split(second))
        ]
        lanes = slice(n * LANES, (n + 1) * LANES)
        for k, (_, piece) in enumerate(SPLITS):
            src[s, 2 * ROWS * k : 2 * ROWS * (k + 1), lanes] = pieces[piece]
    moment = (mass_factor * state[4]) * jnp.where(row_index() == 6, 1.0, state[0])
    moments = jnp.concatenate(split(moment) + [jnp.zeros_like(moment)], axis=0)
    moments = moments.astype(jnp.bfloat16)
    mom[s] = jnp.concatenate([moments, moments], axis=1)
    return state


def put_target(state, b, tgt):
    pieces = [jnp.concatenate(pair, axis=0) for pair in zip(*map(split, target_groups(state)))]
    rows = jnp.concatenate([pieces[piece] for piece, _ in SPLITS], axis=0)
    tgt[b] = rows.T.astype(jnp.bfloat16)


def rows_at(index):
    return pl.ds(pl.multiple_of(index * ROWS, ROWS), ROWS)


def weights_of(product, wall):
    values = [product[:, n * LANES : (n + 1) * LANES] for n in range(3 if wall else 4)]
    guarded = jnp.maximum(values[0], 1e-30)
    approach, press = values[1], values[-1]
    falloff = jnp.maximum(1.0 - guarded * lax.rsqrt(guarded), 0.0)
    cubed = falloff * falloff * falloff
    blend = falloff + press
    if not wall:
        blend += jnp.maximum(approach, 0.0) * pl.reciprocal(values[2], approx=True)
    weight = cubed * blend
    high = weight.astype(jnp.bfloat16)
    low = (weight - high.astype(jnp.float32)).astype(jnp.bfloat16)
    return jnp.concatenate([high, low], axis=1), cubed * approach


def across(left, right):
    return lax.dot_general(
        left, right, (((1,), (1,)), ((), ())), preferred_element_type=jnp.float32
    )


def run_targets(targets, wall, finish):
    steps = [(n, tile) for n, (_, tiles) in enumerate(targets) for tile in tiles]
    totals = [jnp.zeros((MOMENTS, LANES), jnp.float32)] * len(targets)
    rates = [jnp.zeros((LANES, LANES), jnp.float32)] * len(targets)

    def product_of(step):
        n, tile = step
        return jnp.dot(targets[n][0], tile[0][...], preferred_element_type=jnp.float32)

    def add_up(n, moments, weights, last):
        totals[n] += across(moments, weights)
        if last:
            ones = jnp.ones((ROWS, 3 * LANES), jnp.bfloat16)
            pieces = jnp.concatenate(split(rates[n]), axis=1).astype(jnp.bfloat16)
            finish(n, totals[n], across(ones, pieces))

    ahead = product_of(steps[0])
    waiting = None
    for k, (n, (_, moments)) in enumerate(steps):
        product = ahead
        if k + 1 < len(steps):
            ahead = product_of(steps[k + 1])
        weights, part = weights_of(product, wall)
        rates[n] += part
        if waiting is not None:
            add_up(*waiting, waiting[0] != n)
        waiting = (n, moments[...], weights)
    add_up(*waiting, True)


def moments_at(b):
    return pl.ds(pl.multiple_of(b * MOMENTS, MOMENTS), MOMENTS)


def own_kernel(
    own_ref, wall_ref, edge0_ref, edge1_ref, wpair_ref, odd_ref,
    src, mom, tgt, sums, rates, wsrc, wmom, table,
):
    blocks = tgt.shape[0]

    def build(b, carry):
        state = put_source(own_ref[rows_at(b), :], b, src, mom)
        put_target(state, b, tgt)
        return carry

    lax.fori_loop(0, blocks, build, 0, unroll=UNROLL)
    row = row_index()
    count = 0
    for ref in (wall_ref, edge0_ref, edge1_ref):
        for c in range(ref.shape[0] // 4):
            held = ref[4 * c : 4 * c + 4, :]
            both = jnp.concatenate([held, held], axis=0)
            density = jnp.where(row == 6, 1.0, 0.0)
            block = jnp.where((row < 3) | (row == 7), both, density)
            put_source(block, count, wsrc, wmom, adhesion / cohesion, True)
            count += 1
    inner, edge = wall_ref.shape[0] // 4, edge0_ref.shape[0] // 4
    odd = odd_ref[0]
    for c in range(inner):
        table[edge + c] = c
    for c in range(edge):
        table[c] = inner + (1 - odd) * edge + c
        table[edge + inner + c] = inner + odd * edge + c

    def targets_from(i, carry):
        first = i * WALL_TARGETS
        targets = []
        for n in range(WALL_TARGETS):
            slots = [table[wpair_ref[first + n, k]] for k in range(wpair_ref.shape[1])]
            targets.append((tgt[first + n], [(wsrc.at[s], wmom.at[s]) for s in slots]))

        def finish(n, total, rate):
            sums[moments_at(first + n), :] = total
            rates[rows_at(first + n), :] = rate

        run_targets(targets, True, finish)
        return carry

    lax.fori_loop(0, blocks // WALL_TARGETS, targets_from, 0)


def fluid_kernel(
    own_ref, ghost_ref, pair_ref, place_ref, own_src, own_mom,
    tgt, own_sums, own_rates, rate_ref, accel_ref, peak_ref,
    src, mom, sums, rates, stage, table, copied,
):
    blocks = tgt.shape[0]
    ghosts = ghost_ref.shape[0] // ROWS
    per_mask = ghosts // 8
    copies = [
        pltpu.make_async_copy(own_src, src.at[pl.ds(0, blocks)], copied.at[0]),
        pltpu.make_async_copy(own_mom, mom.at[pl.ds(0, blocks)], copied.at[1]),
    ]
    for copy in copies:
        copy.start()
    for c in range(blocks):
        table[c] = c
    for mask in range(1, 8):
        for g in range(per_mask):
            table[blocks + (mask - 1) * per_mask + g] = (
                blocks + jnp.bitwise_xor(place_ref[0], mask) * per_mask + g
            )

    def build(g, carry):
        put_source(ghost_ref[rows_at(g), :], blocks + g, src, mom)
        return carry

    lax.fori_loop(0, ghosts, build, 0, unroll=UNROLL)
    for copy in copies:
        copy.wait()

    def targets_from(i, carry):
        first = i * FLUID_TARGETS
        targets = []
        for n in range(FLUID_TARGETS):
            slots = [table[pair_ref[first + n, k]] for k in range(pair_ref.shape[1])]
            targets.append((tgt[first + n], [(src.at[s], mom.at[s]) for s in slots]))

        def finish(n, total, rate):
            b = first + n
            sums[moments_at(b), :] = own_sums[moments_at(b), :] + total
            rates[rows_at(b), :] = own_rates[rows_at(b), :] + rate

        run_targets(targets, False, finish)
        return carry

    lax.fori_loop(0, blocks // FLUID_TARGETS, targets_from, 0)

    rate_ref[...] = (-support * grad_coeff) * rates[pl.ds(0, blocks, stride=ROWS), :]

    def summed(row):
        parts = [sums[pl.ds(p * ROWS + row, blocks, stride=MOMENTS), :] for p in range(3)]
        return parts[0] + parts[1] + parts[2]

    mass_sum = summed(6)
    square = jnp.zeros_like(mass_sum)
    for d in range(3):
        pos = (own_ref[pl.ds(d, blocks, stride=ROWS), :] - center) * (1.0 / support)
        force = (4.0 * cohesion * support) * (pos * mass_sum - summed(d))
        if d == 2:
            force -= gravity
        square += force * force
        stage[pl.ds(d, blocks, stride=ROWS), :] = force
    for b in range(blocks):
        accel_ref[:, b * LANES : (b + 1) * LANES] = stage[b * ROWS : b * ROWS + 3, :]
    peak_ref[...] = jnp.full(peak_ref.shape, jnp.sqrt(jnp.max(square)), jnp.float32)


SMEM = pl.BlockSpec(memory_space=pltpu.SMEM)
VMEM = pl.BlockSpec(memory_space=pltpu.VMEM)
PARAMS = pltpu.CompilerParams(vmem_limit_bytes=18 * 1024 * 1024)


def tile_cost(tiles):
    return pl.CostEstimate(
        flops=tiles * LANES * LANES * 1000, bytes_accessed=0, transcendentals=0
    )


def source_shapes(count, values):
    return [
        ((count, DEPTH, values * LANES), jnp.bfloat16),
        ((count, MOMENTS, 2 * LANES), jnp.bfloat16),
    ]


def own_pass(own, walls, edges, wall_pairs, odd):
    blocks = own.shape[0] // ROWS
    wall_blocks = (walls.shape[0] + 2 * edges[0].shape[0]) // 4
    outs = source_shapes(blocks, 4) + [
        ((blocks, LANES, DEPTH), jnp.bfloat16),
        ((blocks * MOMENTS, LANES), jnp.float32),
        ((blocks * ROWS, LANES), jnp.float32),
    ]
    return pl.pallas_call(
        own_kernel,
        out_shape=[jax.ShapeDtypeStruct(*out) for out in outs],
        in_specs=[VMEM, VMEM, VMEM, VMEM, SMEM, SMEM],
        out_specs=[VMEM] * len(outs),
        scratch_shapes=[pltpu.VMEM(*shape) for shape in source_shapes(wall_blocks, 3)]
        + [pltpu.SMEM((wall_blocks,), jnp.int32)],
        compiler_params=PARAMS,
        cost_estimate=tile_cost(wall_pairs.size),
        name="own_pass",
    )(own, walls, *edges, wall_pairs, odd)


def fluid_pass(own, ghosts, pair_list, place, own_results):
    blocks = own.shape[0] // ROWS
    total = blocks + ghosts.shape[0] // ROWS
    return pl.pallas_call(
        fluid_kernel,
        out_shape=(
            jax.ShapeDtypeStruct((blocks, LANES), jnp.float32),
            jax.ShapeDtypeStruct((3, blocks * LANES), jnp.float32),
            jax.ShapeDtypeStruct((ROWS, LANES), jnp.float32),
        ),
        in_specs=[VMEM, VMEM, SMEM, SMEM] + [VMEM] * len(own_results),
        out_specs=(VMEM, VMEM, VMEM),
        scratch_shapes=[pltpu.VMEM(*shape) for shape in source_shapes(total, 4)]
        + [
            pltpu.VMEM((blocks * MOMENTS, LANES), jnp.float32),
            pltpu.VMEM((blocks * ROWS, LANES), jnp.float32),
            pltpu.VMEM((blocks * ROWS, LANES), jnp.float32),
            pltpu.SMEM((total,), jnp.int32),
            pltpu.SemaphoreType.DMA((2,)),
        ],
        compiler_params=PARAMS,
        cost_estimate=tile_cost(pair_list.size),
        name="fluid_pass",
    )(own, ghosts, pair_list, place, *own_results)


def outgoing_kernel(own_ref, list_ref, place_ref, wall_ref, count_ref, sent_ref, live_ref):
    for slot in range(8):
        mask = jnp.bitwise_xor(place_ref[0], slot)
        for g in range(list_ref.shape[1]):
            block = list_ref[jnp.maximum(mask - 1, 0), g]
            first = (slot * list_ref.shape[1] + g) * ROWS
            sent_ref[first : first + ROWS, :] = own_ref[rows_at(block), :]
    lane = lax.broadcasted_iota(jnp.int32, (4, LANES), 1)
    row = lax.broadcasted_iota(jnp.int32, (4, LANES), 0)
    for c in range(wall_ref.shape[1] // LANES):
        block = wall_ref[:, c * LANES : (c + 1) * LANES]
        kept = (row < 3) | (lane < count_ref[c])
        live_ref[4 * c : 4 * c + 4, :] = jnp.where(kept, block, 0.0)


def outgoing_pass(own, ghost_list, place, wall_state, wall_count):
    count = 8 * ghost_list.shape[1]
    walls = wall_state.shape[1] // LANES
    return pl.pallas_call(
        outgoing_kernel,
        out_shape=(
            jax.ShapeDtypeStruct((count * ROWS, LANES), jnp.float32),
            jax.ShapeDtypeStruct((walls * 4, LANES), jnp.float32),
        ),
        in_specs=[VMEM, SMEM, SMEM, VMEM, SMEM],
        out_specs=(VMEM, VMEM),
        compiler_params=PARAMS,
        name="outgoing_pass",
    )(own, ghost_list, place, wall_state, wall_count)


def swapped(shard, axis, bit):
    return lax.ppermute(shard, axis, [(i, i ^ 1 << bit) for i in range(lax.axis_size(axis))])


def edges(walls, axis, width):
    count = lax.axis_size(axis)
    odd = lax.axis_index(axis) % 2
    first, last = walls[:width], walls[walls.shape[0] - width :]
    landed = []
    for start in range(2):
        pairs = [(i, i + 1) for i in range(start, count - 1, 2)]
        pairs += [(j, i) for i, j in pairs]
        sent = jnp.where(odd == start, last, first)
        landed.append(lax.ppermute(sent, axis, pairs))
    return landed, odd.reshape(1)


def per_device(fluid_state, ghost_list, pair_list, wall_state, wall_count, wall_pairs):
    block_total = fluid_state.shape[1] // LANES
    own = jnp.transpose(fluid_state.reshape(8, block_total, LANES), (1, 0, 2)).reshape(-1, LANES)
    place = (lax.axis_index("orb") % 8).reshape(1)
    sent, walls = outgoing_pass(own, ghost_list, place, wall_state, wall_count)
    facing, odd = edges(walls, "wall", 4 * EB)
    groups = [list(range(g, g + 8)) for g in range(0, lax.axis_size("orb"), 8)]
    landed = lax.all_to_all(
        sent.reshape(8, -1, LANES),
        "orb",
        0,
        0,
        axis_index_groups=groups if len(groups) > 1 else None,
    )
    own_results = own_pass(own, walls, facing, wall_pairs, odd)
    rate, acceleration, local_peak = fluid_pass(
        own, landed.reshape(-1, LANES), pair_list, place, own_results
    )
    peak = local_peak
    for axis in ("wall", "orb"):
        for bit in range((lax.axis_size(axis) - 1).bit_length()):
            peak = jnp.maximum(peak, swapped(peak, axis, bit))
    peak = peak[0, 0]
    time_step = courant * jnp.sqrt(smoothing / (peak + 1e-06))
    return (rate.reshape(-1), acceleration, time_step)


def solution(mesh):
    return jax.shard_map(
        per_device,
        mesh=mesh,
        in_specs=(
            P(None, ("orb", "wall")),
            P(None, ("orb", "wall")),
            P(("orb", "wall"), None),
            P(None, ("orb", "wall")),
            P(("orb", "wall")),
            P(("orb", "wall"), None),
        ),
        out_specs=(P(("orb", "wall")), P(None, ("orb", "wall")), P()),
        check_vma=False,
    )
```

```python
import functools

import jax
import jax.numpy as jnp
from jax import lax
from jax.experimental import pallas as pl
from jax.experimental.pallas import tpu as pltpu
from jax.sharding import PartitionSpec as P

EB = 1
LANES = 128
ROWS = 8
DEPTH = 12 * ROWS
MOMENTS = 4 * ROWS
SUMS = MOMENTS + ROWS
UNROLL = 4
WALL_TARGETS = 12
FLUID_TARGETS = 6

smoothing = 0.1
support = 0.3
kernel_norm = 21.0 / (2.0 * 3.141592653589793 * support**3)
grad_coeff = -20.0 / support**2 * kernel_norm
tait_coeff = 25.0 / 7.0
visc_coeff = 0.05
cohesion = 2000.0
adhesion = 2000.0
gravity = 9.81
courant = 0.25

center = 0.3
shift = 0.0001 / support**2
press_coeff = -grad_coeff / (4.0 * cohesion)
density_coeff = (support * 4.0 * cohesion) / (-grad_coeff * visc_coeff * 2.0)

SPLITS = ((0, 0), (0, 1), (1, 0), (0, 2), (2, 0), (1, 1))


def split(value):
    first = value.astype(jnp.bfloat16).astype(jnp.float32)
    rest = value - first
    second = rest.astype(jnp.bfloat16).astype(jnp.float32)
    return [first, second, rest - second]


def pressure_ratio(density):
    square = density * density
    return tait_coeff * (square * square * square * density - 1.0) / square


def row_index():
    return lax.broadcasted_iota(jnp.int32, (ROWS, LANES), 0)


def state_of(block):
    row = row_index()
    y = jnp.where(row < 3, (block - center) * (1.0 / support), block)
    y = jnp.where(row == 6, block * density_coeff, y)
    products = y * jnp.where(row < 3, y, pltpu.roll(y, 3, axis=0))
    sums = products + pltpu.roll(products, ROWS - 1, axis=0) + pltpu.roll(products, ROWS - 2, axis=0)

    def everywhere(value, index):
        return jnp.broadcast_to(value[index : index + 1], (ROWS, LANES))

    press = press_coeff * pressure_ratio(everywhere(block, 6))
    return (
        y, everywhere(sums, 0), everywhere(sums, 3), everywhere(y, 6), everywhere(y, 7), press,
    )


def chosen(default, *cases):
    row = row_index()
    value = jnp.full((ROWS, LANES), default, jnp.float32)
    for index, case in cases:
        value = jnp.where(row == index, case, value)
    return value


def target_groups(state):
    y, n, e, r, _, press = state
    row = row_index()
    first = jnp.where(row < 6, y, jnp.where(row == 6, n + shift, e))
    scaled = r * jnp.where(row < 3, y, jnp.where(row == 3, 1.0, n + shift))
    second = jnp.where(row < 5, scaled, chosen(0.0, (5, press), (6, 1.0)))
    return first, second


def source_groups(state, wall):
    y, n, e, r, m, press = state
    row = row_index()
    minus = jnp.where(row < 3, -2.0 * y, 0.0)
    near = chosen(minus, (6, 1.0)), chosen(0.0, (6, n - shift))
    turned = jnp.where(row < 3, pltpu.roll(y, 5, axis=0), pltpu.roll(y, 3, axis=0))
    along = m * jnp.where(row < 6, turned, chosen(0.0, (7, -1.0))), chosen(0.0, (6, -m * e))
    if wall:
        press_part = chosen(0.0, (5, 2.0 * cohesion / adhesion), (6, -0.75))
        return near, along, (None, press_part)
    spread = m * r * near[0], m * chosen(minus, (3, n), (4, 1.0), (6, r * n))
    return near, along, spread, (None, chosen(0.0, (5, 1.0), (6, press - 0.75)))


def put_source(block, s, src, mass_factor=1.0, wall=False):
    state = state_of(block)
    for n, (first, second) in enumerate(source_groups(state, wall)):
        firsts = split(first) if first is not None else [jnp.zeros((ROWS, LANES))] * 3
        pieces = [
            jnp.concatenate(pair, axis=0).astype(jnp.bfloat16)
            for pair in zip(firsts, split(second))
        ]
        lanes = slice(n * LANES, (n + 1) * LANES)
        for k, (_, piece) in enumerate(SPLITS):
            src[s, 2 * ROWS * k : 2 * ROWS * (k + 1), lanes] = pieces[piece]
    moment = (mass_factor * state[4]) * jnp.where(row_index() == 6, 1.0, state[0])
    moments = jnp.concatenate(split(moment) + [jnp.zeros_like(moment)], axis=0)
    moments = moments.astype(jnp.bfloat16)
    for n in range(MOMENTS // (2 * ROWS)):
        part = moments[2 * ROWS * n : 2 * ROWS * (n + 1)]
        lanes = slice(2 * n * LANES, 2 * (n + 1) * LANES)
        src[s, DEPTH:, lanes] = jnp.concatenate([part, part], axis=1)
    return state


def put_target(state, b, tgt):
    pieces = [jnp.concatenate(pair, axis=0) for pair in zip(*map(split, target_groups(state)))]
    rows = jnp.concatenate([pieces[piece] for piece, _ in SPLITS], axis=0)
    tgt[b] = rows.T.astype(jnp.bfloat16)


def rows_at(index):
    return pl.ds(pl.multiple_of(index * ROWS, ROWS), ROWS)


def weights_of(product, wall):
    values = [product[:, n * LANES : (n + 1) * LANES] for n in range(3 if wall else 4)]
    guarded = jnp.maximum(values[0], 1e-30)
    approach, press = values[1], values[-1]
    falloff = jnp.maximum(1.0 - guarded * lax.rsqrt(guarded), 0.0)
    cubed = falloff * falloff * falloff
    blend = falloff + press
    if not wall:
        blend += jnp.maximum(approach, 0.0) * pl.reciprocal(values[2], approx=True)
    weight = cubed * blend
    high = weight.astype(jnp.bfloat16)
    low = (weight - high.astype(jnp.float32)).astype(jnp.bfloat16)
    return jnp.concatenate([high, low], axis=1), cubed * approach


def across(left, right):
    return lax.dot_general(
        left, right, (((1,), (1,)), ((), ())), preferred_element_type=jnp.float32
    )


def run_targets(targets, wall, finish):
    steps = [(n, tile) for n, (_, tiles) in enumerate(targets) for tile in tiles]
    totals = [jnp.zeros((MOMENTS, LANES), jnp.float32)] * len(targets)
    rates = [jnp.zeros((LANES, LANES), jnp.float32)] * len(targets)

    def product_of(step):
        n, tile = step
        columns = tile[:DEPTH, : (3 if wall else 4) * LANES]
        return jnp.dot(targets[n][0], columns, preferred_element_type=jnp.float32)

    def add_up(n, moments, weights, last):
        totals[n] += across(moments, weights)
        if last:
            ones = jnp.ones((ROWS, 3 * LANES), jnp.bfloat16)
            pieces = jnp.concatenate(split(rates[n]), axis=1).astype(jnp.bfloat16)
            finish(n, jnp.concatenate([totals[n], across(ones, pieces)], axis=0))

    ahead = product_of(steps[0])
    waiting = None
    for k, (n, tile) in enumerate(steps):
        product = ahead
        if k + 1 < len(steps):
            ahead = product_of(steps[k + 1])
        weights, part = weights_of(product, wall)
        rates[n] += part
        if waiting is not None:
            add_up(*waiting, waiting[0] != n)
        halves = [tile[DEPTH:, lanes] for lanes in (slice(0, 2 * LANES), slice(2 * LANES, None))]
        waiting = (n, jnp.concatenate(halves, axis=0), weights)
    add_up(*waiting, True)


def sums_at(b):
    return pl.ds(pl.multiple_of(b * SUMS, ROWS), SUMS)


def own_kernel(
    own_ref, wall_ref, edge0_ref, edge1_ref, wpair_ref, odd_ref,
    tgt, sums, wsrc, table,
):
    blocks = tgt.shape[0]

    def build(b, carry):
        put_target(state_of(own_ref[rows_at(b), :]), b, tgt)
        return carry

    lax.fori_loop(0, blocks, build, 0, unroll=UNROLL)
    row = row_index()
    count = 0
    for ref in (wall_ref, edge0_ref, edge1_ref):
        for c in range(ref.shape[0] // 4):
            held = ref[4 * c : 4 * c + 4, :]
            both = jnp.concatenate([held, held], axis=0)
            density = jnp.where(row == 6, 1.0, 0.0)
            block = jnp.where((row < 3) | (row == 7), both, density)
            put_source(block, count, wsrc, adhesion / cohesion, True)
            count += 1
    inner, edge = wall_ref.shape[0] // 4, edge0_ref.shape[0] // 4
    odd = odd_ref[0]
    for c in range(inner):
        table[edge + c] = c
    for c in range(edge):
        table[c] = inner + (1 - odd) * edge + c
        table[edge + inner + c] = inner + odd * edge + c

    def targets_from(i, carry):
        first = i * WALL_TARGETS
        targets = []
        for n in range(WALL_TARGETS):
            slots = [table[wpair_ref[first + n, k]] for k in range(wpair_ref.shape[1])]
            targets.append((tgt[first + n], [wsrc.at[s] for s in slots]))

        def finish(n, total):
            sums[sums_at(first + n), :] = total

        run_targets(targets, True, finish)
        return carry

    lax.fori_loop(0, blocks // WALL_TARGETS, targets_from, 0)


def fluid_kernel(
    own_ref, ghost_ref, pair_ref, place_ref, tgt, own_sums,
    rate_ref, accel_ref, peak_ref, src, sums, stage, table,
):
    blocks = tgt.shape[0]
    ghosts = ghost_ref.shape[0] // ROWS
    per_mask = ghosts // 8
    for c in range(blocks):
        table[c] = c
    for mask in range(1, 8):
        for g in range(per_mask):
            table[blocks + (mask - 1) * per_mask + g] = (
                blocks + jnp.bitwise_xor(place_ref[0], mask) * per_mask + g
            )

    def build_own(b, carry):
        put_source(own_ref[rows_at(b), :], b, src)
        return carry

    def build(g, carry):
        put_source(ghost_ref[rows_at(g), :], blocks + g, src)
        return carry

    lax.fori_loop(0, blocks, build_own, 0, unroll=UNROLL)

    lax.fori_loop(0, ghosts, build, 0, unroll=UNROLL)

    def targets_from(i, carry):
        first = i * FLUID_TARGETS
        targets = []
        for n in range(FLUID_TARGETS):
            slots = [table[pair_ref[first + n, k]] for k in range(pair_ref.shape[1])]
            targets.append((tgt[first + n], [src.at[s] for s in slots]))

        def finish(n, total):
            rows = sums_at(first + n)
            sums[rows, :] = own_sums[rows, :] + total

        run_targets(targets, False, finish)
        return carry

    lax.fori_loop(0, blocks // FLUID_TARGETS, targets_from, 0)

    rate_ref[...] = (-support * grad_coeff) * sums[pl.ds(MOMENTS, blocks, stride=SUMS), :]

    def summed(row):
        parts = [sums[pl.ds(p * ROWS + row, blocks, stride=SUMS), :] for p in range(3)]
        return parts[0] + parts[1] + parts[2]

    mass_sum = summed(6)
    square = jnp.zeros_like(mass_sum)
    for d in range(3):
        pos = (own_ref[pl.ds(d, blocks, stride=ROWS), :] - center) * (1.0 / support)
        force = (4.0 * cohesion * support) * (pos * mass_sum - summed(d))
        if d == 2:
            force -= gravity
        square += force * force
        stage[pl.ds(d, blocks, stride=ROWS), :] = force
    for b in range(blocks):
        accel_ref[:, b * LANES : (b + 1) * LANES] = stage[b * ROWS : b * ROWS + 3, :]
    peak_ref[...] = jnp.full(peak_ref.shape, jnp.sqrt(jnp.max(square)), jnp.float32)


SMEM = pl.BlockSpec(memory_space=pltpu.SMEM)
VMEM = pl.BlockSpec(memory_space=pltpu.VMEM)
PARAMS = pltpu.CompilerParams(vmem_limit_bytes=18 * 1024 * 1024)


def tile_cost(tiles):
    return pl.CostEstimate(
        flops=tiles * LANES * LANES * 1000, bytes_accessed=0, transcendentals=0
    )


def source_shape(count):
    return (count, DEPTH + 2 * ROWS, 4 * LANES), jnp.bfloat16


def own_pass(own, walls, edges, wall_pairs, odd):
    blocks = own.shape[0] // ROWS
    wall_blocks = (walls.shape[0] + 2 * edges[0].shape[0]) // 4
    outs = [
        ((blocks, LANES, DEPTH), jnp.bfloat16),
        ((blocks * SUMS, LANES), jnp.float32),
    ]
    return pl.pallas_call(
        own_kernel,
        out_shape=[jax.ShapeDtypeStruct(*out) for out in outs],
        in_specs=[VMEM, VMEM, VMEM, VMEM, SMEM, SMEM],
        out_specs=[VMEM] * len(outs),
        scratch_shapes=[
            pltpu.VMEM(*source_shape(wall_blocks)),
            pltpu.SMEM((wall_blocks,), jnp.int32),
        ],
        compiler_params=PARAMS,
        cost_estimate=tile_cost(wall_pairs.size),
        name="own_pass",
    )(own, walls, *edges, wall_pairs, odd)


def fluid_pass(own, ghosts, pair_list, place, own_results):
    blocks = own.shape[0] // ROWS
    total = blocks + ghosts.shape[0] // ROWS
    return pl.pallas_call(
        fluid_kernel,
        out_shape=(
            jax.ShapeDtypeStruct((blocks, LANES), jnp.float32),
            jax.ShapeDtypeStruct((3, blocks * LANES), jnp.float32),
            jax.ShapeDtypeStruct((ROWS, LANES), jnp.float32),
        ),
        in_specs=[VMEM, VMEM, SMEM, SMEM] + [VMEM] * len(own_results),
        out_specs=(VMEM, VMEM, VMEM),
        scratch_shapes=[
            pltpu.VMEM(*source_shape(total)),
            pltpu.VMEM((blocks * SUMS, LANES), jnp.float32),
            pltpu.VMEM((blocks * ROWS, LANES), jnp.float32),
            pltpu.SMEM((total,), jnp.int32),
        ],
        compiler_params=PARAMS,
        cost_estimate=tile_cost(pair_list.size),
        name="fluid_pass",
    )(own, ghosts, pair_list, place, *own_results)


def outgoing_kernel(own_ref, list_ref, place_ref, wall_ref, count_ref, sent_ref, live_ref):
    for slot in range(8):
        mask = jnp.bitwise_xor(place_ref[0], slot)
        for g in range(list_ref.shape[1]):
            block = list_ref[jnp.maximum(mask - 1, 0), g]
            first = (slot * list_ref.shape[1] + g) * ROWS
            sent_ref[first : first + ROWS, :] = own_ref[rows_at(block), :]
    lane = lax.broadcasted_iota(jnp.int32, (4, LANES), 1)
    row = lax.broadcasted_iota(jnp.int32, (4, LANES), 0)
    for c in range(wall_ref.shape[1] // LANES):
        block = wall_ref[:, c * LANES : (c + 1) * LANES]
        kept = (row < 3) | (lane < count_ref[c])
        live_ref[4 * c : 4 * c + 4, :] = jnp.where(kept, block, 0.0)


def outgoing_pass(own, ghost_list, place, wall_state, wall_count):
    count = 8 * ghost_list.shape[1]
    walls = wall_state.shape[1] // LANES
    return pl.pallas_call(
        outgoing_kernel,
        out_shape=(
            jax.ShapeDtypeStruct((count * ROWS, LANES), jnp.float32),
            jax.ShapeDtypeStruct((walls * 4, LANES), jnp.float32),
        ),
        in_specs=[VMEM, SMEM, SMEM, VMEM, SMEM],
        out_specs=(VMEM, VMEM),
        name="outgoing_pass",
    )(own, ghost_list, place, wall_state, wall_count)


def swapped(shard, axis, bit):
    return lax.ppermute(shard, axis, [(i, i ^ 1 << bit) for i in range(lax.axis_size(axis))])


def edges(walls, axis, width):
    count = lax.axis_size(axis)
    odd = lax.axis_index(axis) % 2
    first, last = walls[:width], walls[walls.shape[0] - width :]
    landed = []
    for start in range(2):
        pairs = [(i, i + 1) for i in range(start, count - 1, 2)]
        pairs += [(j, i) for i, j in pairs]
        sent = jnp.where(odd == start, last, first)
        landed.append(lax.ppermute(sent, axis, pairs))
    return landed, odd.reshape(1)


def per_device(fluid_state, ghost_list, pair_list, wall_state, wall_count, wall_pairs):
    block_total = fluid_state.shape[1] // LANES
    own = jnp.transpose(fluid_state.reshape(8, block_total, LANES), (1, 0, 2)).reshape(-1, LANES)
    place = (lax.axis_index("orb") % 8).reshape(1)
    sent, walls = outgoing_pass(own, ghost_list, place, wall_state, wall_count)
    facing, odd = edges(walls, "wall", 4 * EB)
    groups = [list(range(g, g + 8)) for g in range(0, lax.axis_size("orb"), 8)]
    landed = lax.all_to_all(
        sent.reshape(8, -1, LANES),
        "orb",
        0,
        0,
        axis_index_groups=groups if len(groups) > 1 else None,
    )
    own_results = own_pass(own, walls, facing, wall_pairs, odd)
    rate, acceleration, local_peak = fluid_pass(
        own, landed.reshape(-1, LANES), pair_list, place, own_results
    )
    peak = local_peak
    for axis in ("wall", "orb"):
        for bit in range((lax.axis_size(axis) - 1).bit_length()):
            peak = jnp.maximum(peak, swapped(peak, axis, bit))
    peak = peak[0, 0]
    time_step = courant * jnp.sqrt(smoothing / (peak + 1e-06))
    return (rate.reshape(-1), acceleration, time_step)


def solution(mesh):
    return jax.shard_map(
        per_device,
        mesh=mesh,
        in_specs=(
            P(None, ("orb", "wall")),
            P(None, ("orb", "wall")),
            P(("orb", "wall"), None),
            P(None, ("orb", "wall")),
            P(("orb", "wall")),
            P(("orb", "wall"), None),
        ),
        out_specs=(P(("orb", "wall")), P(None, ("orb", "wall")), P()),
        check_vma=False,
    )
```

```python
import functools

import jax
import jax.numpy as jnp
from jax import lax
from jax.experimental import pallas as pl
from jax.experimental.pallas import tpu as pltpu
from jax.sharding import PartitionSpec as P

EB = 1
LANES = 128
ROWS = 8
DEPTH = 12 * ROWS
MOMENTS = 4 * ROWS
SUMS = MOMENTS + ROWS
UNROLL = 4
WALL_TARGETS = 12
FLUID_TARGETS = 6

smoothing = 0.1
support = 0.3
kernel_norm = 21.0 / (2.0 * 3.141592653589793 * support**3)
grad_coeff = -20.0 / support**2 * kernel_norm
tait_coeff = 25.0 / 7.0
visc_coeff = 0.05
cohesion = 2000.0
adhesion = 2000.0
gravity = 9.81
courant = 0.25

center = 0.3
shift = 0.0001 / support**2
press_coeff = -grad_coeff / (4.0 * cohesion)
density_coeff = (support * 4.0 * cohesion) / (-grad_coeff * visc_coeff * 2.0)

SPLITS = ((0, 0), (0, 1), (1, 0), (0, 2), (2, 0), (1, 1))


def split(value):
    first = value.astype(jnp.bfloat16).astype(jnp.float32)
    rest = value - first
    second = rest.astype(jnp.bfloat16).astype(jnp.float32)
    return [first, second, rest - second]


def pressure_ratio(density):
    square = density * density
    return tait_coeff * (square * square * square * density - 1.0) / square


def row_index():
    return lax.broadcasted_iota(jnp.int32, (ROWS, LANES), 0)


def state_of(block):
    row = row_index()
    y = jnp.where(row < 3, (block - center) * (1.0 / support), block)
    y = jnp.where(row == 6, block * density_coeff, y)
    products = y * jnp.where(row < 3, y, pltpu.roll(y, 3, axis=0))
    sums = products + pltpu.roll(products, ROWS - 1, axis=0) + pltpu.roll(products, ROWS - 2, axis=0)

    def everywhere(value, index):
        return jnp.broadcast_to(value[index : index + 1], (ROWS, LANES))

    press = press_coeff * pressure_ratio(everywhere(block, 6))
    return (
        y, everywhere(sums, 0), everywhere(sums, 3), everywhere(y, 6), everywhere(y, 7), press,
    )


def chosen(default, *cases):
    row = row_index()
    value = jnp.full((ROWS, LANES), default, jnp.float32)
    for index, case in cases:
        value = jnp.where(row == index, case, value)
    return value


def target_groups(state):
    y, n, e, r, _, press = state
    row = row_index()
    first = jnp.where(row < 6, y, jnp.where(row == 6, n + shift, e))
    scaled = r * jnp.where(row < 3, y, jnp.where(row == 3, 1.0, n + shift))
    second = jnp.where(row < 5, scaled, chosen(0.0, (5, press), (6, 1.0)))
    return first, second


def source_groups(state, wall):
    y, n, e, r, m, press = state
    row = row_index()
    minus = jnp.where(row < 3, -2.0 * y, 0.0)
    near = chosen(minus, (6, 1.0)), chosen(0.0, (6, n - shift))
    turned = jnp.where(row < 3, pltpu.roll(y, 5, axis=0), pltpu.roll(y, 3, axis=0))
    along = m * jnp.where(row < 6, turned, chosen(0.0, (7, -1.0))), chosen(0.0, (6, -m * e))
    if wall:
        press_part = chosen(0.0, (5, 2.0 * cohesion / adhesion), (6, -0.75))
        return near, along, (None, press_part)
    spread = m * r * near[0], m * chosen(minus, (3, n), (4, 1.0), (6, r * n))
    return near, along, spread, (None, chosen(0.0, (5, 1.0), (6, press - 0.75)))


def put_source(block, s, src, mass_factor=1.0, wall=False):
    state = state_of(block)
    for n, (first, second) in enumerate(source_groups(state, wall)):
        firsts = split(first) if first is not None else [jnp.zeros((ROWS, LANES))] * 3
        pieces = [
            jnp.concatenate(pair, axis=0).astype(jnp.bfloat16)
            for pair in zip(firsts, split(second))
        ]
        lanes = slice(n * LANES, (n + 1) * LANES)
        for k, (_, piece) in enumerate(SPLITS):
            src[s, 2 * ROWS * k : 2 * ROWS * (k + 1), lanes] = pieces[piece]
    moment = (mass_factor * state[4]) * jnp.where(row_index() == 6, 1.0, state[0])
    moments = jnp.concatenate(split(moment) + [jnp.zeros_like(moment)], axis=0)
    moments = moments.astype(jnp.bfloat16)
    for n in range(MOMENTS // (2 * ROWS)):
        part = moments[2 * ROWS * n : 2 * ROWS * (n + 1)]
        lanes = slice(2 * n * LANES, 2 * (n + 1) * LANES)
        src[s, DEPTH:, lanes] = jnp.concatenate([part, part], axis=1)
    return state


def put_target(state, b, tgt):
    pieces = [jnp.concatenate(pair, axis=0) for pair in zip(*map(split, target_groups(state)))]
    rows = jnp.concatenate([pieces[piece] for piece, _ in SPLITS], axis=0)
    tgt[b] = rows.T.astype(jnp.bfloat16)


def rows_at(index):
    return pl.ds(pl.multiple_of(index * ROWS, ROWS), ROWS)


def weights_of(product, wall):
    values = [product[:, n * LANES : (n + 1) * LANES] for n in range(3 if wall else 4)]
    guarded = jnp.maximum(values[0], 1e-30)
    approach, press = values[1], values[-1]
    falloff = jnp.maximum(1.0 - guarded * lax.rsqrt(guarded), 0.0)
    cubed = falloff * falloff * falloff
    blend = falloff + press
    if not wall:
        blend += jnp.maximum(approach, 0.0) * pl.reciprocal(values[2], approx=True)
    weight = cubed * blend
    high = weight.astype(jnp.bfloat16)
    low = (weight - high.astype(jnp.float32)).astype(jnp.bfloat16)
    return jnp.concatenate([high, low], axis=1), cubed * approach


def across(left, right):
    return lax.dot_general(
        left, right, (((1,), (1,)), ((), ())), preferred_element_type=jnp.float32
    )


def run_targets(targets, wall, finish):
    steps = [(n, tile) for n, (_, tiles) in enumerate(targets) for tile in tiles]
    totals = [jnp.zeros((MOMENTS, LANES), jnp.float32)] * len(targets)
    rates = [jnp.zeros((LANES, LANES), jnp.float32)] * len(targets)

    def product_of(step):
        n, tile = step
        columns = tile[:DEPTH, : (3 if wall else 4) * LANES]
        return jnp.dot(targets[n][0], columns, preferred_element_type=jnp.float32)

    def add_up(n, moments, weights, last):
        totals[n] += across(moments, weights)
        if last:
            ones = jnp.ones((ROWS, 3 * LANES), jnp.bfloat16)
            pieces = jnp.concatenate(split(rates[n]), axis=1).astype(jnp.bfloat16)
            finish(n, jnp.concatenate([totals[n], across(ones, pieces)], axis=0))

    ahead = product_of(steps[0])
    waiting = None
    for k, (n, tile) in enumerate(steps):
        product = ahead
        if k + 1 < len(steps):
            ahead = product_of(steps[k + 1])
        weights, part = weights_of(product, wall)
        rates[n] += part
        if waiting is not None:
            add_up(*waiting, waiting[0] != n)
        halves = [tile[DEPTH:, lanes] for lanes in (slice(0, 2 * LANES), slice(2 * LANES, None))]
        waiting = (n, jnp.concatenate(halves, axis=0), weights)
    add_up(*waiting, True)


def sums_at(b):
    return pl.ds(pl.multiple_of(b * SUMS, ROWS), SUMS)


def own_kernel(
    own_ref, wall_ref, edge0_ref, edge1_ref, wpair_ref, odd_ref,
    tgt, sums, wsrc, table,
):
    blocks = tgt.shape[0]

    def build(b, carry):
        put_target(state_of(own_ref[rows_at(b), :]), b, tgt)
        return carry

    lax.fori_loop(0, blocks, build, 0, unroll=UNROLL)
    row = row_index()
    count = 0
    for ref in (wall_ref, edge0_ref, edge1_ref):
        for c in range(ref.shape[0] // 4):
            held = ref[4 * c : 4 * c + 4, :]
            both = jnp.concatenate([held, held], axis=0)
            density = jnp.where(row == 6, 1.0, 0.0)
            block = jnp.where((row < 3) | (row == 7), both, density)
            put_source(block, count, wsrc, adhesion / cohesion, True)
            count += 1
    inner, edge = wall_ref.shape[0] // 4, edge0_ref.shape[0] // 4
    odd = odd_ref[0]
    for c in range(inner):
        table[edge + c] = c
    for c in range(edge):
        table[c] = inner + (1 - odd) * edge + c
        table[edge + inner + c] = inner + odd * edge + c

    def targets_from(i, carry):
        first = i * WALL_TARGETS
        targets = []
        for n in range(WALL_TARGETS):
            slots = [table[wpair_ref[first + n, k]] for k in range(wpair_ref.shape[1])]
            targets.append((tgt[first + n], [wsrc.at[s] for s in slots]))

        def finish(n, total):
            sums[sums_at(first + n), :] = total

        run_targets(targets, True, finish)
        return carry

    lax.fori_loop(0, blocks // WALL_TARGETS, targets_from, 0)


def fluid_kernel(own_ref, pair_ref, tgt, own_sums, *refs):
    *ghost_refs, rate_ref, accel_ref, peak_ref, src, sums, stage = refs
    blocks = tgt.shape[0]

    def build_own(b, carry):
        put_source(own_ref[rows_at(b), :], b, src)
        return carry

    lax.fori_loop(0, blocks, build_own, 0, unroll=UNROLL)
    per_mask = ghost_refs[0].shape[0] // ROWS
    for n, ghost_ref in enumerate(ghost_refs):
        for g in range(per_mask):
            put_source(ghost_ref[g * ROWS : (g + 1) * ROWS, :], blocks + n * per_mask + g, src)

    def targets_from(i, carry):
        first = i * FLUID_TARGETS
        targets = []
        for n in range(FLUID_TARGETS):
            slots = [pair_ref[first + n, k] for k in range(pair_ref.shape[1])]
            targets.append((tgt[first + n], [src.at[s] for s in slots]))

        def finish(n, total):
            rows = sums_at(first + n)
            sums[rows, :] = own_sums[rows, :] + total

        run_targets(targets, False, finish)
        return carry

    lax.fori_loop(0, blocks // FLUID_TARGETS, targets_from, 0)

    rate_ref[...] = (-support * grad_coeff) * sums[pl.ds(MOMENTS, blocks, stride=SUMS), :]

    def summed(row):
        parts = [sums[pl.ds(p * ROWS + row, blocks, stride=SUMS), :] for p in range(3)]
        return parts[0] + parts[1] + parts[2]

    mass_sum = summed(6)
    square = jnp.zeros_like(mass_sum)
    for d in range(3):
        pos = (own_ref[pl.ds(d, blocks, stride=ROWS), :] - center) * (1.0 / support)
        force = (4.0 * cohesion * support) * (pos * mass_sum - summed(d))
        if d == 2:
            force -= gravity
        square += force * force
        stage[pl.ds(d, blocks, stride=ROWS), :] = force
    for b in range(blocks):
        accel_ref[:, b * LANES : (b + 1) * LANES] = stage[b * ROWS : b * ROWS + 3, :]
    peak_ref[...] = jnp.full(peak_ref.shape, jnp.sqrt(jnp.max(square)), jnp.float32)


SMEM = pl.BlockSpec(memory_space=pltpu.SMEM)
VMEM = pl.BlockSpec(memory_space=pltpu.VMEM)
PARAMS = pltpu.CompilerParams(vmem_limit_bytes=18 * 1024 * 1024)


def tile_cost(tiles):
    return pl.CostEstimate(
        flops=tiles * LANES * LANES * 1000, bytes_accessed=0, transcendentals=0
    )


def source_shape(count):
    return (count, DEPTH + 2 * ROWS, 4 * LANES), jnp.bfloat16


def own_pass(own, walls, edges, wall_pairs, odd):
    blocks = own.shape[0] // ROWS
    wall_blocks = (walls.shape[0] + 2 * edges[0].shape[0]) // 4
    outs = [
        ((blocks, LANES, DEPTH), jnp.bfloat16),
        ((blocks * SUMS, LANES), jnp.float32),
    ]
    return pl.pallas_call(
        own_kernel,
        out_shape=[jax.ShapeDtypeStruct(*out) for out in outs],
        in_specs=[VMEM, VMEM, VMEM, VMEM, SMEM, SMEM],
        out_specs=[VMEM] * len(outs),
        scratch_shapes=[
            pltpu.VMEM(*source_shape(wall_blocks)),
            pltpu.SMEM((wall_blocks,), jnp.int32),
        ],
        compiler_params=PARAMS,
        cost_estimate=tile_cost(wall_pairs.size),
        name="own_pass",
    )(own, walls, *edges, wall_pairs, odd)


def fluid_pass(own, ghosts, pair_list, own_results):
    blocks = own.shape[0] // ROWS
    total = blocks + sum(part.shape[0] for part in ghosts) // ROWS
    return pl.pallas_call(
        fluid_kernel,
        out_shape=(
            jax.ShapeDtypeStruct((blocks, LANES), jnp.float32),
            jax.ShapeDtypeStruct((3, blocks * LANES), jnp.float32),
            jax.ShapeDtypeStruct((ROWS, LANES), jnp.float32),
        ),
        in_specs=[VMEM, SMEM, VMEM, VMEM] + [VMEM] * len(ghosts),
        out_specs=(VMEM, VMEM, VMEM),
        scratch_shapes=[
            pltpu.VMEM(*source_shape(total)),
            pltpu.VMEM((blocks * SUMS, LANES), jnp.float32),
            pltpu.VMEM((blocks * ROWS, LANES), jnp.float32),
        ],
        compiler_params=PARAMS,
        cost_estimate=tile_cost(pair_list.size),
        name="fluid_pass",
    )(own, pair_list, *own_results, *ghosts)


def outgoing_kernel(own_ref, list_ref, wall_ref, count_ref, odd_ref, *outs):
    sent_refs, (live_ref, edge0_ref, edge1_ref) = outs[:-3], outs[-3:]
    for n, sent_ref in enumerate(sent_refs):
        for g in range(list_ref.shape[1]):
            sent_ref[rows_at(g), :] = own_ref[rows_at(list_ref[n, g]), :]
    lane = lax.broadcasted_iota(jnp.int32, (4, LANES), 1)
    row = lax.broadcasted_iota(jnp.int32, (4, LANES), 0)
    for c in range(wall_ref.shape[1] // LANES):
        block = wall_ref[:, c * LANES : (c + 1) * LANES]
        kept = (row < 3) | (lane < count_ref[c])
        live_ref[4 * c : 4 * c + 4, :] = jnp.where(kept, block, 0.0)
    first = live_ref[: edge0_ref.shape[0], :]
    last = live_ref[live_ref.shape[0] - edge0_ref.shape[0] :, :]
    edge0_ref[...] = jnp.where(odd_ref[0] == 0, last, first)
    edge1_ref[...] = jnp.where(odd_ref[0] == 0, first, last)


def outgoing_pass(own, ghost_list, wall_state, wall_count, odd):
    masks, count = ghost_list.shape
    walls = wall_state.shape[1] // LANES
    rows = [count * ROWS] * masks + [walls * 4, EB * 4, EB * 4]
    return pl.pallas_call(
        outgoing_kernel,
        out_shape=[jax.ShapeDtypeStruct((row, LANES), jnp.float32) for row in rows],
        in_specs=[VMEM, SMEM, VMEM, SMEM, SMEM],
        out_specs=[VMEM] * len(rows),
        name="outgoing_pass",
    )(own, ghost_list, wall_state, wall_count, odd)


def swapped(shard, axis, mask):
    return lax.ppermute(shard, axis, [(i, i ^ mask) for i in range(lax.axis_size(axis))])


def largest(peak, axis):
    bits = (lax.axis_size(axis) - 1).bit_length()
    for low in range(0, bits, 3):
        masks = range(1, 1 << min(3, bits - low))
        for other in [swapped(peak, axis, mask << low) for mask in masks]:
            peak = jnp.maximum(peak, other)
    return peak


def facing(edges, axis):
    count = lax.axis_size(axis)
    landed = []
    for start, sent in enumerate(edges):
        pairs = [(i, i + 1) for i in range(start, count - 1, 2)]
        landed.append(lax.ppermute(sent, axis, pairs + [(j, i) for i, j in pairs]))
    return landed


def per_device(fluid_state, ghost_list, pair_list, wall_state, wall_count, wall_pairs):
    block_total = fluid_state.shape[1] // LANES
    own = jnp.transpose(fluid_state.reshape(8, block_total, LANES), (1, 0, 2)).reshape(-1, LANES)
    odd = (lax.axis_index("wall") % 2).reshape(1)
    *sent, walls, edge0, edge1 = outgoing_pass(own, ghost_list, wall_state, wall_count, odd)
    edges = facing((edge0, edge1), "wall")
    ghosts = [swapped(blocks, "orb", n + 1) for n, blocks in enumerate(sent)]
    own_results = own_pass(own, walls, edges, wall_pairs, odd)
    rate, acceleration, local_peak = fluid_pass(own, ghosts, pair_list, own_results)
    peak = largest(largest(local_peak, "wall"), "orb")[0, 0]
    time_step = courant * jnp.sqrt(smoothing / (peak + 1e-06))
    return (rate.reshape(-1), acceleration, time_step)


def solution(mesh):
    return jax.shard_map(
        per_device,
        mesh=mesh,
        in_specs=(
            P(None, ("orb", "wall")),
            P(None, ("orb", "wall")),
            P(("orb", "wall"), None),
            P(None, ("orb", "wall")),
            P(("orb", "wall")),
            P(("orb", "wall"), None),
        ),
        out_specs=(P(("orb", "wall")), P(None, ("orb", "wall")), P()),
        check_vma=False,
    )
```

```python
import math

import jax
import jax.numpy as jnp
from jax import lax
from jax.experimental import pallas as pl
from jax.experimental.pallas import tpu as pltpu
from jax.sharding import PartitionSpec as P

EB = 1
LANES = 128
ROWS = 8
DEPTH = 12 * ROWS
MOMENTS = 4 * ROWS
SUMS = MOMENTS + ROWS
UNROLL = 4
VALUES = 3
GROUP = 2
WALL_TARGETS = 24
FLUID_TARGETS = 8

smoothing = 0.1
support = 0.3
kernel_norm = 21.0 / (2.0 * 3.141592653589793 * support**3)
grad_coeff = -20.0 / support**2 * kernel_norm
tait_coeff = 25.0 / 7.0
visc_coeff = 0.05
cohesion = 2000.0
adhesion = 2000.0
gravity = 9.81
courant = 0.25

center = 0.3
shift = 0.0001 / support**2
press_coeff = -grad_coeff / (4.0 * cohesion)
density_coeff = (support * 4.0 * cohesion) / (-grad_coeff * visc_coeff * 2.0)

SPLITS = ((0, 0), (0, 1), (1, 0), (0, 2), (2, 0), (1, 1))


def split(value):
    first = value.astype(jnp.bfloat16).astype(jnp.float32)
    rest = value - first
    second = rest.astype(jnp.bfloat16).astype(jnp.float32)
    return [first, second, rest - second]


def pressure_ratio(density):
    square = density * density
    return tait_coeff * (square * square * square * density - 1.0) / square


def row_index():
    return lax.broadcasted_iota(jnp.int32, (ROWS, LANES), 0)


def state_of(block):
    row = row_index()
    y = jnp.where(row < 3, (block - center) * (1.0 / support), block)
    y = jnp.where(row == 6, block * density_coeff, y)
    products = y * jnp.where(row < 3, y, pltpu.roll(y, 3, axis=0))
    sums = products + pltpu.roll(products, ROWS - 1, axis=0) + pltpu.roll(products, ROWS - 2, axis=0)

    def everywhere(value, index):
        return jnp.broadcast_to(value[index : index + 1], (ROWS, LANES))

    press = press_coeff * pressure_ratio(everywhere(block, 6))
    return (
        y, everywhere(sums, 0), everywhere(sums, 3), everywhere(y, 6), everywhere(y, 7), press,
    )


def chosen(default, *cases):
    row = row_index()
    value = jnp.full((ROWS, LANES), default, jnp.float32)
    for index, case in cases:
        value = jnp.where(row == index, case, value)
    return value


def target_groups(state):
    y, n, e, r, _, press = state
    row = row_index()
    first = jnp.where(row < 6, y, jnp.where(row == 6, n + shift, e))
    scaled = r * jnp.where(row < 3, y, jnp.where(row == 3, 1.0, n + shift))
    second = jnp.where(row < 5, scaled, chosen(0.0, (5, press), (6, 1.0)))
    return first, second


def source_groups(state, wall):
    y, n, e, r, m, press = state
    row = row_index()
    minus = jnp.where(row < 3, -2.0 * y, 0.0)
    near = chosen(minus, (6, 1.0)), chosen(0.0, (6, n - shift))
    turned = jnp.where(row < 3, pltpu.roll(y, 5, axis=0), pltpu.roll(y, 3, axis=0))
    along = m * jnp.where(row < 6, turned, chosen(0.0, (7, -1.0))), chosen(0.0, (6, -m * e))
    if wall:
        press_part = chosen(0.0, (5, 2.0 * cohesion / adhesion), (6, -0.75))
        return near, along, (None, press_part)
    return near, along, (m * r * near[0], m * chosen(minus, (3, n), (4, 1.0), (6, r * n)))


def put_source(block, s, src, press=None, mass_factor=1.0):
    state = state_of(block)
    for n, (first, second) in enumerate(source_groups(state, press is None)):
        firsts = split(first) if first is not None else [jnp.zeros((ROWS, LANES))] * 3
        pieces = [
            jnp.concatenate(pair, axis=0).astype(jnp.bfloat16)
            for pair in zip(firsts, split(second))
        ]
        lanes = slice(n * LANES, (n + 1) * LANES)
        for k, (_, piece) in enumerate(SPLITS):
            src[s, 2 * ROWS * k : 2 * ROWS * (k + 1), lanes] = pieces[piece]
    moment = (mass_factor * state[4]) * jnp.where(row_index() == 6, 1.0, state[0])
    moments = split(moment) + [jnp.zeros_like(moment)]
    for n in range(2):
        half = jnp.concatenate(moments[2 * n : 2 * n + 2], axis=0)
        src[s, DEPTH:, n * LANES : (n + 1) * LANES] = half.astype(jnp.bfloat16)
    if press is not None:
        press[s] = state[5]


def put_target(state, b, tgt):
    pieces = [jnp.concatenate(pair, axis=0) for pair in zip(*map(split, target_groups(state)))]
    rows = jnp.concatenate([pieces[piece] for piece, _ in SPLITS], axis=0).astype(jnp.bfloat16)
    row = lax.broadcasted_iota(jnp.int32, (LANES, LANES), 0)
    lane = lax.broadcasted_iota(jnp.int32, (LANES, LANES), 1)
    unit = jnp.where(row == lane, 1.0, 0.0).astype(jnp.bfloat16)
    tgt[b] = across(unit, rows).astype(jnp.bfloat16)


def press_choice():
    row = lax.broadcasted_iota(jnp.int32, (DEPTH, LANES), 0)
    value = jnp.where(row == ROWS + 6, -0.75, 0.0)
    for k, (_, piece) in enumerate(SPLITS):
        if piece == 0:
            value = jnp.where(row == 2 * ROWS * k + ROWS + 5, 1.0, value)
    return value.astype(jnp.bfloat16)


def rows_at(index):
    return pl.ds(pl.multiple_of(index * ROWS, ROWS), ROWS)


def weights_of(product, press_i, press_j):
    near, approach, last = [product[:, n * LANES : (n + 1) * LANES] for n in range(VALUES)]
    guarded = jnp.maximum(near, 1e-30)
    falloff = jnp.maximum(1.0 - guarded * lax.rsqrt(guarded), 0.0)
    cubed = falloff * falloff * falloff
    if press_j is None:
        blend = falloff + last
    else:
        blend = falloff + press_i
        blend += jnp.concatenate([press_j[...]] * (LANES // ROWS), axis=0)
        blend += jnp.maximum(approach, 0.0) * pl.reciprocal(last, approx=True)
    weight = cubed * blend
    high = weight.astype(jnp.bfloat16)
    low = (weight - high.astype(jnp.float32)).astype(jnp.bfloat16)
    return [high, low], cubed * approach


def across(left, right):
    return lax.dot_general(
        left, right, (((1,), (1,)), ((), ())), preferred_element_type=jnp.float32
    )


def run_targets(targets, finish):
    steps = [
        (n, tiles[k : k + GROUP])
        for n, (_, _, tiles) in enumerate(targets)
        for k in range(0, len(tiles), GROUP)
    ]
    totals = [jnp.zeros((MOMENTS, LANES), jnp.float32)] * len(targets)
    rates = [jnp.zeros((LANES, LANES), jnp.float32)] * len(targets)

    def product_of(step):
        n, group = step
        columns = jnp.concatenate([source[:DEPTH, :] for source, _ in group], axis=1)
        return jnp.dot(targets[n][0], columns, preferred_element_type=jnp.float32)

    def add_up(n, moments, weights, last):
        totals[n] += across(moments, weights)
        if last:
            ones = jnp.ones((ROWS, 3 * LANES), jnp.bfloat16)
            pieces = jnp.concatenate(split(rates[n]), axis=1).astype(jnp.bfloat16)
            finish(n, jnp.concatenate([totals[n], across(ones, pieces)], axis=0))

    ahead = product_of(steps[0])
    waiting = None
    for k, (n, group) in enumerate(steps):
        product = ahead
        if k + 1 < len(steps):
            ahead = product_of(steps[k + 1])
        moments, weights = [], []
        for m, (source, press_j) in enumerate(group):
            columns = slice(m * VALUES * LANES, (m + 1) * VALUES * LANES)
            pair, part = weights_of(product[:, columns], targets[n][1], press_j)
            rates[n] += part
            weights += pair
            halves = [source[DEPTH:, :LANES], source[DEPTH:, LANES : 2 * LANES]]
            moments += [jnp.concatenate(halves, axis=0)] * 2
        if waiting is not None:
            add_up(*waiting, waiting[0] != n)
        waiting = (n, jnp.concatenate(moments, axis=1), jnp.concatenate(weights, axis=1))
    add_up(*waiting, True)


def sums_at(b):
    return pl.ds(pl.multiple_of(b * SUMS, ROWS), SUMS)


def own_kernel(
    own_ref, wall_ref, edge0_ref, edge1_ref, wpair_ref, odd_ref,
    tgt, sums, wsrc, table,
):
    blocks = tgt.shape[0]

    def build(b, carry):
        put_target(state_of(own_ref[rows_at(b), :]), b, tgt)
        return carry

    lax.fori_loop(0, blocks, build, 0, unroll=UNROLL)
    row = row_index()
    count = 0
    for ref in (wall_ref, edge0_ref, edge1_ref):
        for c in range(ref.shape[0] // 4):
            held = ref[4 * c : 4 * c + 4, :]
            both = jnp.concatenate([held, held], axis=0)
            density = jnp.where(row == 6, 1.0, 0.0)
            block = jnp.where((row < 3) | (row == 7), both, density)
            put_source(block, count, wsrc, None, adhesion / cohesion)
            count += 1
    inner, edge = wall_ref.shape[0] // 4, edge0_ref.shape[0] // 4
    odd = odd_ref[0]
    for c in range(inner):
        table[edge + c] = c
    for c in range(edge):
        table[c] = inner + (1 - odd) * edge + c
        table[edge + inner + c] = inner + odd * edge + c

    together = math.gcd(blocks, WALL_TARGETS)

    def targets_from(i, carry):
        first = i * together
        targets = []
        for n in range(together):
            slots = [table[wpair_ref[first + n, k]] for k in range(wpair_ref.shape[1])]
            targets.append((tgt[first + n], None, [(wsrc.at[s], None) for s in slots]))

        def finish(n, total):
            sums[sums_at(first + n), :] = total

        run_targets(targets, finish)
        return carry

    lax.fori_loop(0, blocks // together, targets_from, 0)


def fluid_kernel(
    own_ref, ghost_ref, pair_ref, place_ref, tgt, own_sums,
    rate_ref, accel_ref, peak_ref, src, press, sums, stage, table,
):
    blocks = tgt.shape[0]
    ghosts = ghost_ref.shape[0] // ROWS
    per_mask = ghosts // 8
    for c in range(blocks):
        table[c] = c
    for mask in range(1, 8):
        for g in range(per_mask):
            table[blocks + (mask - 1) * per_mask + g] = (
                blocks + jnp.bitwise_xor(place_ref[0], mask) * per_mask + g
            )

    def build_own(b, carry):
        put_source(own_ref[rows_at(b), :], b, src, press)
        return carry

    def build(g, carry):
        put_source(ghost_ref[rows_at(g), :], blocks + g, src, press)
        return carry

    lax.fori_loop(0, blocks, build_own, 0, unroll=UNROLL)

    lax.fori_loop(0, ghosts, build, 0, unroll=UNROLL)

    choice = press_choice()
    together = math.gcd(blocks, FLUID_TARGETS)

    def targets_from(i, carry):
        first = i * together
        targets = []
        for n in range(together):
            slots = [table[pair_ref[first + n, k]] for k in range(pair_ref.shape[1])]
            target = tgt[first + n]
            press_i = jnp.dot(target, choice, preferred_element_type=jnp.float32)
            targets.append((target, press_i, [(src.at[s], press.at[s]) for s in slots]))

        def finish(n, total):
            rows = sums_at(first + n)
            sums[rows, :] = own_sums[rows, :] + total

        run_targets(targets, finish)
        return carry

    lax.fori_loop(0, blocks // together, targets_from, 0)

    rate_ref[...] = (-support * grad_coeff) * sums[pl.ds(MOMENTS, blocks, stride=SUMS), :]

    def summed(row):
        parts = [sums[pl.ds(p * ROWS + row, blocks, stride=SUMS), :] for p in range(3)]
        return parts[0] + parts[1] + parts[2]

    mass_sum = summed(6)
    square = jnp.zeros_like(mass_sum)
    for d in range(3):
        pos = (own_ref[pl.ds(d, blocks, stride=ROWS), :] - center) * (1.0 / support)
        force = (4.0 * cohesion * support) * (pos * mass_sum - summed(d))
        if d == 2:
            force -= gravity
        square += force * force
        stage[pl.ds(d, blocks, stride=ROWS), :] = force
    for b in range(blocks):
        accel_ref[:, b * LANES : (b + 1) * LANES] = stage[b * ROWS : b * ROWS + 3, :]
    peak_ref[...] = jnp.full(peak_ref.shape, jnp.sqrt(jnp.max(square)), jnp.float32)


SMEM = pl.BlockSpec(memory_space=pltpu.SMEM)
VMEM = pl.BlockSpec(memory_space=pltpu.VMEM)
PARAMS = pltpu.CompilerParams(vmem_limit_bytes=18 * 1024 * 1024)


def tile_cost(tiles):
    return pl.CostEstimate(
        flops=tiles * LANES * LANES * 1000, bytes_accessed=0, transcendentals=0
    )


def source_shape(count):
    return (count, DEPTH + 2 * ROWS, VALUES * LANES), jnp.bfloat16


def own_pass(own, walls, edges, wall_pairs, odd):
    blocks = own.shape[0] // ROWS
    wall_blocks = (walls.shape[0] + 2 * edges[0].shape[0]) // 4
    outs = [
        ((blocks, LANES, DEPTH), jnp.bfloat16),
        ((blocks * SUMS, LANES), jnp.float32),
    ]
    return pl.pallas_call(
        own_kernel,
        out_shape=[jax.ShapeDtypeStruct(*out) for out in outs],
        in_specs=[VMEM, VMEM, VMEM, VMEM, SMEM, SMEM],
        out_specs=[VMEM] * len(outs),
        scratch_shapes=[
            pltpu.VMEM(*source_shape(wall_blocks)),
            pltpu.SMEM((wall_blocks,), jnp.int32),
        ],
        compiler_params=PARAMS,
        cost_estimate=tile_cost(wall_pairs.size),
        name="own_pass",
    )(own, walls, *edges, wall_pairs, odd)


def fluid_pass(own, ghosts, pair_list, place, own_results):
    blocks = own.shape[0] // ROWS
    total = blocks + ghosts.shape[0] // ROWS
    return pl.pallas_call(
        fluid_kernel,
        out_shape=(
            jax.ShapeDtypeStruct((blocks, LANES), jnp.float32),
            jax.ShapeDtypeStruct((3, blocks * LANES), jnp.float32),
            jax.ShapeDtypeStruct((ROWS, LANES), jnp.float32),
        ),
        in_specs=[VMEM, VMEM, SMEM, SMEM] + [VMEM] * len(own_results),
        out_specs=(VMEM, VMEM, VMEM),
        scratch_shapes=[
            pltpu.VMEM(*source_shape(total)),
            pltpu.VMEM((total, ROWS, LANES), jnp.float32),
            pltpu.VMEM((blocks * SUMS, LANES), jnp.float32),
            pltpu.VMEM((blocks * ROWS, LANES), jnp.float32),
            pltpu.SMEM((total,), jnp.int32),
        ],
        compiler_params=PARAMS,
        cost_estimate=tile_cost(pair_list.size),
        name="fluid_pass",
    )(own, ghosts, pair_list, place, *own_results)


def outgoing_kernel(own_ref, list_ref, place_ref, wall_ref, count_ref, sent_ref, live_ref):
    for slot in range(8):
        mask = jnp.bitwise_xor(place_ref[0], slot)
        for g in range(list_ref.shape[1]):
            block = list_ref[jnp.maximum(mask - 1, 0), g]
            first = (slot * list_ref.shape[1] + g) * ROWS
            sent_ref[first : first + ROWS, :] = own_ref[rows_at(block), :]
    lane = lax.broadcasted_iota(jnp.int32, (4, LANES), 1)
    row = lax.broadcasted_iota(jnp.int32, (4, LANES), 0)
    for c in range(wall_ref.shape[1] // LANES):
        block = wall_ref[:, c * LANES : (c + 1) * LANES]
        kept = (row < 3) | (lane < count_ref[c])
        live_ref[4 * c : 4 * c + 4, :] = jnp.where(kept, block, 0.0)


def outgoing_pass(own, ghost_list, place, wall_state, wall_count):
    count = 8 * ghost_list.shape[1]
    walls = wall_state.shape[1] // LANES
    return pl.pallas_call(
        outgoing_kernel,
        out_shape=(
            jax.ShapeDtypeStruct((count * ROWS, LANES), jnp.float32),
            jax.ShapeDtypeStruct((walls * 4, LANES), jnp.float32),
        ),
        in_specs=[VMEM, SMEM, SMEM, VMEM, SMEM],
        out_specs=(VMEM, VMEM),
        name="outgoing_pass",
    )(own, ghost_list, place, wall_state, wall_count)


def swapped(shard, axis, bit):
    return lax.ppermute(shard, axis, [(i, i ^ 1 << bit) for i in range(lax.axis_size(axis))])


def edges(walls, axis, width):
    count = lax.axis_size(axis)
    odd = lax.axis_index(axis) % 2
    first, last = walls[:width], walls[walls.shape[0] - width :]
    landed = []
    for start in range(2):
        pairs = [(i, i + 1) for i in range(start, count - 1, 2)]
        pairs += [(j, i) for i, j in pairs]
        sent = jnp.where(odd == start, last, first)
        landed.append(lax.ppermute(sent, axis, pairs))
    return landed, odd.reshape(1)


def per_device(fluid_state, ghost_list, pair_list, wall_state, wall_count, wall_pairs):
    block_total = fluid_state.shape[1] // LANES
    own = jnp.transpose(fluid_state.reshape(8, block_total, LANES), (1, 0, 2)).reshape(-1, LANES)
    place = (lax.axis_index("orb") % 8).reshape(1)
    sent, walls = outgoing_pass(own, ghost_list, place, wall_state, wall_count)
    facing, odd = edges(walls, "wall", 4 * EB)
    groups = [list(range(g, g + 8)) for g in range(0, lax.axis_size("orb"), 8)]
    landed = lax.all_to_all(
        sent.reshape(8, -1, LANES),
        "orb",
        0,
        0,
        axis_index_groups=groups if len(groups) > 1 else None,
    )
    own_results = own_pass(own, walls, facing, wall_pairs, odd)
    rate, acceleration, local_peak = fluid_pass(
        own, landed.reshape(-1, LANES), pair_list, place, own_results
    )
    peak = local_peak
    for axis in ("wall", "orb"):
        for bit in range((lax.axis_size(axis) - 1).bit_length()):
            peak = jnp.maximum(peak, swapped(peak, axis, bit))
    peak = peak[0, 0]
    time_step = courant * jnp.sqrt(smoothing / (peak + 1e-06))
    return (rate.reshape(-1), acceleration, time_step)


def solution(mesh):
    return jax.shard_map(
        per_device,
        mesh=mesh,
        in_specs=(
            P(None, ("orb", "wall")),
            P(None, ("orb", "wall")),
            P(("orb", "wall"), None),
            P(None, ("orb", "wall")),
            P(("orb", "wall")),
            P(("orb", "wall"), None),
        ),
        out_specs=(P(("orb", "wall")), P(None, ("orb", "wall")), P()),
        check_vma=False,
    )
```

```python
import math

import jax
import jax.numpy as jnp
from jax import lax
from jax.experimental import pallas as pl
from jax.experimental.pallas import tpu as pltpu
from jax.sharding import PartitionSpec as P

EB = 1
LANES = 128
ROWS = 8
DEPTH = 12 * ROWS
MOMENTS = 4 * ROWS
SUMS = MOMENTS + ROWS
UNROLL = 12
VALUES = 3
GROUP = 2
WALL_TARGETS = 24
FLUID_TARGETS = 12

smoothing = 0.1
support = 0.3
kernel_norm = 21.0 / (2.0 * 3.141592653589793 * support**3)
grad_coeff = -20.0 / support**2 * kernel_norm
tait_coeff = 25.0 / 7.0
visc_coeff = 0.05
cohesion = 2000.0
adhesion = 2000.0
gravity = 9.81
courant = 0.25

center = 0.3
shift = 0.0001 / support**2
press_coeff = -grad_coeff / (4.0 * cohesion)
density_coeff = (support * 4.0 * cohesion) / (-grad_coeff * visc_coeff * 2.0)

SPLITS = ((0, 0), (0, 1), (1, 0), (0, 2), (2, 0), (1, 1))


def split(value):
    first = value.astype(jnp.bfloat16).astype(jnp.float32)
    rest = value - first
    second = rest.astype(jnp.bfloat16).astype(jnp.float32)
    return [first, second, rest - second]


def pressure_ratio(density):
    square = density * density
    return tait_coeff * (square * square * square * density - 1.0) / square


def row_index():
    return lax.broadcasted_iota(jnp.int32, (ROWS, LANES), 0)


def state_of(block):
    row = row_index()
    y = jnp.where(row < 3, (block - center) * (1.0 / support), block)
    y = jnp.where(row == 6, block * density_coeff, y)
    products = y * jnp.where(row < 3, y, pltpu.roll(y, 3, axis=0))
    sums = products + pltpu.roll(products, ROWS - 1, axis=0) + pltpu.roll(products, ROWS - 2, axis=0)

    def everywhere(value, index):
        return jnp.broadcast_to(value[index : index + 1], (ROWS, LANES))

    press = press_coeff * pressure_ratio(everywhere(block, 6))
    return (
        y, everywhere(sums, 0), everywhere(sums, 3), everywhere(y, 6), everywhere(y, 7), press,
    )


def chosen(default, *cases):
    row = row_index()
    value = jnp.full((ROWS, LANES), default, jnp.float32)
    for index, case in cases:
        value = jnp.where(row == index, case, value)
    return value


def target_groups(state):
    y, n, e, r, _, press = state
    row = row_index()
    first = jnp.where(row < 6, y, jnp.where(row == 6, n + shift, e))
    scaled = r * jnp.where(row < 3, y, jnp.where(row == 3, 1.0, n + shift))
    second = jnp.where(row < 5, scaled, chosen(0.0, (5, press), (6, 1.0)))
    return first, second


def source_groups(state, wall):
    y, n, e, r, m, press = state
    row = row_index()
    minus = jnp.where(row < 3, -2.0 * y, 0.0)
    near = chosen(minus, (6, 1.0)), chosen(0.0, (6, n - shift))
    turned = jnp.where(row < 3, pltpu.roll(y, 5, axis=0), pltpu.roll(y, 3, axis=0))
    along = m * jnp.where(row < 6, turned, chosen(0.0, (7, -1.0))), chosen(0.0, (6, -m * e))
    if wall:
        press_part = chosen(0.0, (5, 2.0 * cohesion / adhesion), (6, -0.75))
        return near, along, (None, press_part)
    return near, along, (m * r * near[0], m * chosen(minus, (3, n), (4, 1.0), (6, r * n)))


def put_source(block, s, src, press=None, mass_factor=1.0):
    state = state_of(block)
    for n, (first, second) in enumerate(source_groups(state, press is None)):
        firsts = split(first) if first is not None else [jnp.zeros((ROWS, LANES))] * 3
        pieces = [
            jnp.concatenate(pair, axis=0).astype(jnp.bfloat16)
            for pair in zip(firsts, split(second))
        ]
        lanes = slice(n * LANES, (n + 1) * LANES)
        for k, (_, piece) in enumerate(SPLITS):
            src[s, 2 * ROWS * k : 2 * ROWS * (k + 1), lanes] = pieces[piece]
    moment = (mass_factor * state[4]) * jnp.where(row_index() == 6, 1.0, state[0])
    moments = split(moment) + [jnp.zeros_like(moment)]
    for n in range(2):
        half = jnp.concatenate(moments[2 * n : 2 * n + 2], axis=0)
        src[s, DEPTH:, n * LANES : (n + 1) * LANES] = half.astype(jnp.bfloat16)
    if press is not None:
        press[s] = state[5]


def put_target(state, b, tgt):
    pieces = [jnp.concatenate(pair, axis=0) for pair in zip(*map(split, target_groups(state)))]
    rows = jnp.concatenate([pieces[piece] for piece, _ in SPLITS], axis=0).astype(jnp.bfloat16)
    row = lax.broadcasted_iota(jnp.int32, (LANES, LANES), 0)
    lane = lax.broadcasted_iota(jnp.int32, (LANES, LANES), 1)
    unit = jnp.where(row == lane, 1.0, 0.0).astype(jnp.bfloat16)
    tgt[b] = across(unit, rows).astype(jnp.bfloat16)


def press_choice():
    row = lax.broadcasted_iota(jnp.int32, (DEPTH, LANES), 0)
    value = jnp.where(row == ROWS + 6, -0.75, 0.0)
    for k, (_, piece) in enumerate(SPLITS):
        if piece == 0:
            value = jnp.where(row == 2 * ROWS * k + ROWS + 5, 1.0, value)
    return value.astype(jnp.bfloat16)


def rows_at(index):
    return pl.ds(pl.multiple_of(index * ROWS, ROWS), ROWS)


def weights_of(product, press_i, press_j):
    near, approach, last = [product[:, n * LANES : (n + 1) * LANES] for n in range(VALUES)]
    guarded = jnp.maximum(near, 1e-30)
    falloff = jnp.maximum(1.0 - guarded * lax.rsqrt(guarded), 0.0)
    cubed = falloff * falloff * falloff
    if press_j is None:
        blend = falloff + last
    else:
        blend = falloff + press_i
        blend += jnp.concatenate([press_j[...]] * (LANES // ROWS), axis=0)
        blend += jnp.maximum(approach, 0.0) * pl.reciprocal(last, approx=True)
    weight = cubed * blend
    high = weight.astype(jnp.bfloat16)
    low = (weight - high.astype(jnp.float32)).astype(jnp.bfloat16)
    return [high, low], cubed * approach


def across(left, right):
    return lax.dot_general(
        left, right, (((1,), (1,)), ((), ())), preferred_element_type=jnp.float32
    )


def run_targets(targets, finish):
    steps = [
        (n, tiles[k : k + GROUP])
        for n, (_, _, tiles) in enumerate(targets)
        for k in range(0, len(tiles), GROUP)
    ]
    totals = [jnp.zeros((MOMENTS, LANES), jnp.float32)] * len(targets)
    rates = [jnp.zeros((LANES, LANES), jnp.float32)] * len(targets)

    def product_of(step):
        n, group = step
        columns = jnp.concatenate([source[:DEPTH, :] for source, _ in group], axis=1)
        return jnp.dot(targets[n][0], columns, preferred_element_type=jnp.float32)

    def add_up(n, moments, weights, last):
        totals[n] += across(moments, weights)
        if last:
            ones = jnp.ones((ROWS, 3 * LANES), jnp.bfloat16)
            pieces = jnp.concatenate(split(rates[n]), axis=1).astype(jnp.bfloat16)
            finish(n, jnp.concatenate([totals[n], across(ones, pieces)], axis=0))

    ahead = product_of(steps[0])
    waiting = None
    for k, (n, group) in enumerate(steps):
        product = ahead
        if k + 1 < len(steps):
            ahead = product_of(steps[k + 1])
        moments, weights = [], []
        for m, (source, press_j) in enumerate(group):
            columns = slice(m * VALUES * LANES, (m + 1) * VALUES * LANES)
            pair, part = weights_of(product[:, columns], targets[n][1], press_j)
            rates[n] += part
            weights += pair
            halves = [source[DEPTH:, :LANES], source[DEPTH:, LANES : 2 * LANES]]
            moments += [jnp.concatenate(halves, axis=0)] * 2
        if waiting is not None:
            add_up(*waiting, waiting[0] != n)
        waiting = (n, jnp.concatenate(moments, axis=1), jnp.concatenate(weights, axis=1))
    add_up(*waiting, True)


def sums_at(b):
    return pl.ds(pl.multiple_of(b * SUMS, ROWS), SUMS)


def own_kernel(
    own_ref, wall_ref, edge0_ref, edge1_ref, wpair_ref, odd_ref,
    tgt, sums, wsrc, table,
):
    blocks = tgt.shape[0]

    def build(b, carry):
        put_target(state_of(own_ref[rows_at(b), :]), b, tgt)
        return carry

    lax.fori_loop(0, blocks, build, 0, unroll=UNROLL)
    row = row_index()
    count = 0
    for ref in (wall_ref, edge0_ref, edge1_ref):
        for c in range(ref.shape[0] // 4):
            held = ref[4 * c : 4 * c + 4, :]
            both = jnp.concatenate([held, held], axis=0)
            density = jnp.where(row == 6, 1.0, 0.0)
            block = jnp.where((row < 3) | (row == 7), both, density)
            put_source(block, count, wsrc, None, adhesion / cohesion)
            count += 1
    inner, edge = wall_ref.shape[0] // 4, edge0_ref.shape[0] // 4
    odd = odd_ref[0]
    for c in range(inner):
        table[edge + c] = c
    for c in range(edge):
        table[c] = inner + (1 - odd) * edge + c
        table[edge + inner + c] = inner + odd * edge + c

    together = math.gcd(blocks, WALL_TARGETS)

    def targets_from(i, carry):
        first = i * together
        targets = []
        for n in range(together):
            slots = [table[wpair_ref[first + n, k]] for k in range(wpair_ref.shape[1])]
            targets.append((tgt[first + n], None, [(wsrc.at[s], None) for s in slots]))

        def finish(n, total):
            sums[sums_at(first + n), :] = total

        run_targets(targets, finish)
        return carry

    lax.fori_loop(0, blocks // together, targets_from, 0)


def fluid_kernel(
    own_ref, ghost_ref, pair_ref, place_ref, tgt, own_sums,
    rate_ref, accel_ref, peak_ref, src, press, sums, stage, table,
):
    blocks = tgt.shape[0]
    ghosts = ghost_ref.shape[0] // ROWS
    per_mask = ghosts // 8
    for c in range(blocks):
        table[c] = c
    for mask in range(1, 8):
        for g in range(per_mask):
            table[blocks + (mask - 1) * per_mask + g] = (
                blocks + jnp.bitwise_xor(place_ref[0], mask) * per_mask + g
            )

    def build_own(b, carry):
        put_source(own_ref[rows_at(b), :], b, src, press)
        return carry

    def build(g, carry):
        put_source(ghost_ref[rows_at(g), :], blocks + g, src, press)
        return carry

    lax.fori_loop(0, blocks, build_own, 0, unroll=UNROLL)

    lax.fori_loop(0, ghosts, build, 0, unroll=UNROLL)

    choice = press_choice()
    together = math.gcd(blocks, FLUID_TARGETS)

    def targets_from(i, carry):
        first = i * together
        targets = []
        for n in range(together):
            slots = [table[pair_ref[first + n, k]] for k in range(pair_ref.shape[1])]
            target = tgt[first + n]
            press_i = jnp.dot(target, choice, preferred_element_type=jnp.float32)
            targets.append((target, press_i, [(src.at[s], press.at[s]) for s in slots]))

        def finish(n, total):
            rows = sums_at(first + n)
            sums[rows, :] = own_sums[rows, :] + total

        run_targets(targets, finish)
        return carry

    lax.fori_loop(0, blocks // together, targets_from, 0)

    rate_ref[...] = (-support * grad_coeff) * sums[pl.ds(MOMENTS, blocks, stride=SUMS), :]

    def summed(row):
        parts = [sums[pl.ds(p * ROWS + row, blocks, stride=SUMS), :] for p in range(3)]
        return parts[0] + parts[1] + parts[2]

    mass_sum = summed(6)
    square = jnp.zeros_like(mass_sum)
    for d in range(3):
        pos = (own_ref[pl.ds(d, blocks, stride=ROWS), :] - center) * (1.0 / support)
        force = (4.0 * cohesion * support) * (pos * mass_sum - summed(d))
        if d == 2:
            force -= gravity
        square += force * force
        stage[pl.ds(d, blocks, stride=ROWS), :] = force
    for b in range(blocks):
        accel_ref[:, b * LANES : (b + 1) * LANES] = stage[b * ROWS : b * ROWS + 3, :]
    peak_ref[...] = jnp.full(peak_ref.shape, jnp.sqrt(jnp.max(square)), jnp.float32)


SMEM = pl.BlockSpec(memory_space=pltpu.SMEM)
VMEM = pl.BlockSpec(memory_space=pltpu.VMEM)
PARAMS = pltpu.CompilerParams(vmem_limit_bytes=18 * 1024 * 1024)


def tile_cost(tiles):
    return pl.CostEstimate(
        flops=tiles * LANES * LANES * 1000, bytes_accessed=0, transcendentals=0
    )


def source_shape(count):
    return (count, DEPTH + 2 * ROWS, VALUES * LANES), jnp.bfloat16


def own_pass(own, walls, edges, wall_pairs, odd):
    blocks = own.shape[0] // ROWS
    wall_blocks = (walls.shape[0] + 2 * edges[0].shape[0]) // 4
    outs = [
        ((blocks, LANES, DEPTH), jnp.bfloat16),
        ((blocks * SUMS, LANES), jnp.float32),
    ]
    return pl.pallas_call(
        own_kernel,
        out_shape=[jax.ShapeDtypeStruct(*out) for out in outs],
        in_specs=[VMEM, VMEM, VMEM, VMEM, SMEM, SMEM],
        out_specs=[VMEM] * len(outs),
        scratch_shapes=[
            pltpu.VMEM(*source_shape(wall_blocks)),
            pltpu.SMEM((wall_blocks,), jnp.int32),
        ],
        compiler_params=PARAMS,
        cost_estimate=tile_cost(wall_pairs.size),
        name="own_pass",
    )(own, walls, *edges, wall_pairs, odd)


def fluid_pass(own, ghosts, pair_list, place, own_results):
    blocks = own.shape[0] // ROWS
    total = blocks + ghosts.shape[0] // ROWS
    return pl.pallas_call(
        fluid_kernel,
        out_shape=(
            jax.ShapeDtypeStruct((blocks, LANES), jnp.float32),
            jax.ShapeDtypeStruct((3, blocks * LANES), jnp.float32),
            jax.ShapeDtypeStruct((ROWS, LANES), jnp.float32),
        ),
        in_specs=[VMEM, VMEM, SMEM, SMEM] + [VMEM] * len(own_results),
        out_specs=(VMEM, VMEM, VMEM),
        scratch_shapes=[
            pltpu.VMEM(*source_shape(total)),
            pltpu.VMEM((total, ROWS, LANES), jnp.float32),
            pltpu.VMEM((blocks * SUMS, LANES), jnp.float32),
            pltpu.VMEM((blocks * ROWS, LANES), jnp.float32),
            pltpu.SMEM((total,), jnp.int32),
        ],
        compiler_params=PARAMS,
        cost_estimate=tile_cost(pair_list.size),
        name="fluid_pass",
    )(own, ghosts, pair_list, place, *own_results)


def outgoing_kernel(
    own_ref, list_ref, place_ref, wall_ref, count_ref, odd_ref, sent_ref, live_ref, edge0_ref, edge1_ref,
):
    for slot in range(8):
        mask = jnp.bitwise_xor(place_ref[0], slot)
        for g in range(list_ref.shape[1]):
            block = list_ref[jnp.maximum(mask - 1, 0), g]
            first = (slot * list_ref.shape[1] + g) * ROWS
            sent_ref[first : first + ROWS, :] = own_ref[rows_at(block), :]
    lane = lax.broadcasted_iota(jnp.int32, (4, LANES), 1)
    row = lax.broadcasted_iota(jnp.int32, (4, LANES), 0)
    for c in range(wall_ref.shape[1] // LANES):
        block = wall_ref[:, c * LANES : (c + 1) * LANES]
        kept = (row < 3) | (lane < count_ref[c])
        live_ref[4 * c : 4 * c + 4, :] = jnp.where(kept, block, 0.0)
    first = live_ref[: edge0_ref.shape[0], :]
    last = live_ref[live_ref.shape[0] - edge0_ref.shape[0] :, :]
    edge0_ref[...] = jnp.where(odd_ref[0] == 0, last, first)
    edge1_ref[...] = jnp.where(odd_ref[0] == 0, first, last)


def outgoing_pass(own, ghost_list, place, wall_state, wall_count, odd):
    walls = wall_state.shape[1] // LANES
    rows = [8 * ghost_list.shape[1] * ROWS, walls * 4, EB * 4, EB * 4]
    return pl.pallas_call(
        outgoing_kernel,
        out_shape=[jax.ShapeDtypeStruct((row, LANES), jnp.float32) for row in rows],
        in_specs=[VMEM, SMEM, SMEM, VMEM, SMEM, SMEM],
        out_specs=[VMEM] * len(rows),
        name="outgoing_pass",
    )(own, ghost_list, place, wall_state, wall_count, odd)


def swapped(shard, axis, bit):
    return lax.ppermute(shard, axis, [(i, i ^ 1 << bit) for i in range(lax.axis_size(axis))])


def facing(edges, axis):
    count = lax.axis_size(axis)
    landed = []
    for start, sent in enumerate(edges):
        pairs = [(i, i + 1) for i in range(start, count - 1, 2)]
        landed.append(lax.ppermute(sent, axis, pairs + [(j, i) for i, j in pairs]))
    return landed


def per_device(fluid_state, ghost_list, pair_list, wall_state, wall_count, wall_pairs):
    block_total = fluid_state.shape[1] // LANES
    own = jnp.transpose(fluid_state.reshape(8, block_total, LANES), (1, 0, 2)).reshape(-1, LANES)
    place = (lax.axis_index("orb") % 8).reshape(1)
    odd = (lax.axis_index("wall") % 2).reshape(1)
    sent, walls, *edges = outgoing_pass(own, ghost_list, place, wall_state, wall_count, odd)
    edges = facing(edges, "wall")
    groups = [list(range(g, g + 8)) for g in range(0, lax.axis_size("orb"), 8)]
    landed = lax.all_to_all(
        sent.reshape(8, -1, LANES),
        "orb",
        0,
        0,
        axis_index_groups=groups if len(groups) > 1 else None,
    )
    own_results = own_pass(own, walls, edges, wall_pairs, odd)
    rate, acceleration, local_peak = fluid_pass(
        own, landed.reshape(-1, LANES), pair_list, place, own_results
    )
    peak = local_peak
    for axis in ("wall", "orb"):
        for bit in range((lax.axis_size(axis) - 1).bit_length()):
            peak = jnp.maximum(peak, swapped(peak, axis, bit))
    peak = peak[0, 0]
    time_step = courant * jnp.sqrt(smoothing / (peak + 1e-06))
    return (rate.reshape(-1), acceleration, time_step)


def solution(mesh):
    return jax.shard_map(
        per_device,
        mesh=mesh,
        in_specs=(
            P(None, ("orb", "wall")),
            P(None, ("orb", "wall")),
            P(("orb", "wall"), None),
            P(None, ("orb", "wall")),
            P(("orb", "wall")),
            P(("orb", "wall"), None),
        ),
        out_specs=(P(("orb", "wall")), P(None, ("orb", "wall")), P()),
        check_vma=False,
    )
```

```python
import math

import jax
import jax.numpy as jnp
from jax import lax
from jax.experimental import pallas as pl
from jax.experimental.pallas import tpu as pltpu
from jax.sharding import PartitionSpec as P

EB = 1
LANES = 128
ROWS = 8
DEPTH = 12 * ROWS
MOMENTS = 4 * ROWS
SUMS = MOMENTS + ROWS
UNROLL = 12
VALUES = 3
GROUP = 2
WALL_TARGETS = 24
FLUID_TARGETS = 12

smoothing = 0.1
support = 0.3
kernel_norm = 21.0 / (2.0 * 3.141592653589793 * support**3)
grad_coeff = -20.0 / support**2 * kernel_norm
tait_coeff = 25.0 / 7.0
visc_coeff = 0.05
cohesion = 2000.0
adhesion = 2000.0
gravity = 9.81
courant = 0.25

center = 0.3
shift = 0.0001 / support**2
press_coeff = -grad_coeff / (4.0 * cohesion)
density_coeff = (support * 4.0 * cohesion) / (-grad_coeff * visc_coeff * 2.0)

SPLITS = ((0, 0), (0, 1), (1, 0), (0, 2), (2, 0), (1, 1))


def split(value):
    first = value.astype(jnp.bfloat16).astype(jnp.float32)
    rest = value - first
    second = rest.astype(jnp.bfloat16).astype(jnp.float32)
    return [first, second, rest - second]


def pressure_ratio(density):
    square = density * density
    return tait_coeff * (square * square * square * density - 1.0) / square


def row_index():
    return lax.broadcasted_iota(jnp.int32, (ROWS, LANES), 0)


def state_of(block):
    row = row_index()
    y = jnp.where(row < 3, (block - center) * (1.0 / support), block)
    y = jnp.where(row == 6, block * density_coeff, y)
    products = y * jnp.where(row < 3, y, pltpu.roll(y, 3, axis=0))
    sums = products + pltpu.roll(products, ROWS - 1, axis=0) + pltpu.roll(products, ROWS - 2, axis=0)

    def everywhere(value, index):
        return jnp.broadcast_to(value[index : index + 1], (ROWS, LANES))

    press = press_coeff * pressure_ratio(everywhere(block, 6))
    return (
        y, everywhere(sums, 0), everywhere(sums, 3), everywhere(y, 6), everywhere(y, 7), press,
    )


def chosen(default, *cases):
    row = row_index()
    value = jnp.full((ROWS, LANES), default, jnp.float32)
    for index, case in cases:
        value = jnp.where(row == index, case, value)
    return value


def target_groups(state):
    y, n, e, r, _, press = state
    row = row_index()
    first = jnp.where(row < 6, y, jnp.where(row == 6, n + shift, e))
    scaled = r * jnp.where(row < 3, y, jnp.where(row == 3, 1.0, n + shift))
    second = jnp.where(row < 5, scaled, chosen(0.0, (5, press), (6, 1.0)))
    return first, second


def source_groups(state, wall):
    y, n, e, r, m, press = state
    row = row_index()
    minus = jnp.where(row < 3, -2.0 * y, 0.0)
    near = chosen(minus, (6, 1.0)), chosen(0.0, (6, n - shift))
    turned = jnp.where(row < 3, pltpu.roll(y, 5, axis=0), pltpu.roll(y, 3, axis=0))
    along = m * jnp.where(row < 6, turned, chosen(0.0, (7, -1.0))), chosen(0.0, (6, -m * e))
    if wall:
        press_part = chosen(0.0, (5, 2.0 * cohesion / adhesion), (6, -0.75))
        return near, along, (None, press_part)
    return near, along, (m * r * near[0], m * chosen(minus, (3, n), (4, 1.0), (6, r * n)))


def put_source(block, s, src, press=None, mass_factor=1.0):
    state = state_of(block)
    for n, (first, second) in enumerate(source_groups(state, press is None)):
        firsts = split(first) if first is not None else [jnp.zeros((ROWS, LANES))] * 3
        pieces = [
            jnp.concatenate(pair, axis=0).astype(jnp.bfloat16)
            for pair in zip(firsts, split(second))
        ]
        lanes = slice(n * LANES, (n + 1) * LANES)
        for k, (_, piece) in enumerate(SPLITS):
            src[s, 2 * ROWS * k : 2 * ROWS * (k + 1), lanes] = pieces[piece]
    moment = (mass_factor * state[4]) * jnp.where(row_index() == 6, 1.0, state[0])
    moments = split(moment) + [jnp.zeros_like(moment)]
    for n in range(2):
        half = jnp.concatenate(moments[2 * n : 2 * n + 2], axis=0)
        src[s, DEPTH:, n * LANES : (n + 1) * LANES] = half.astype(jnp.bfloat16)
    if press is not None:
        press[s] = state[5]


def put_target(state, b, tgt):
    pieces = [jnp.concatenate(pair, axis=0) for pair in zip(*map(split, target_groups(state)))]
    rows = jnp.concatenate([pieces[piece] for piece, _ in SPLITS], axis=0).astype(jnp.bfloat16)
    row = lax.broadcasted_iota(jnp.int32, (LANES, LANES), 0)
    lane = lax.broadcasted_iota(jnp.int32, (LANES, LANES), 1)
    unit = jnp.where(row == lane, 1.0, 0.0).astype(jnp.bfloat16)
    tgt[b] = across(unit, rows).astype(jnp.bfloat16)


def press_choice():
    row = lax.broadcasted_iota(jnp.int32, (DEPTH, LANES), 0)
    value = jnp.where(row == ROWS + 6, -0.75, 0.0)
    for k, (_, piece) in enumerate(SPLITS):
        if piece == 0:
            value = jnp.where(row == 2 * ROWS * k + ROWS + 5, 1.0, value)
    return value.astype(jnp.bfloat16)


def rows_at(index):
    return pl.ds(pl.multiple_of(index * ROWS, ROWS), ROWS)


def weights_of(product, press_i, press_j):
    near, approach, last = [product[:, n * LANES : (n + 1) * LANES] for n in range(VALUES)]
    guarded = jnp.maximum(near, 1e-30)
    falloff = jnp.maximum(1.0 - guarded * lax.rsqrt(guarded), 0.0)
    cubed = falloff * falloff * falloff
    if press_j is None:
        blend = falloff + last
    else:
        blend = falloff + press_i
        blend += jnp.concatenate([press_j[...]] * (LANES // ROWS), axis=0)
        blend += jnp.maximum(approach, 0.0) * pl.reciprocal(last, approx=True)
    weight = cubed * blend
    high = weight.astype(jnp.bfloat16)
    low = (weight - high.astype(jnp.float32)).astype(jnp.bfloat16)
    return [high, low], cubed * approach


def across(left, right):
    return lax.dot_general(
        left, right, (((1,), (1,)), ((), ())), preferred_element_type=jnp.float32
    )


def run_targets(targets, finish):
    steps = [
        (n, tiles[k : k + GROUP])
        for n, (_, _, tiles) in enumerate(targets)
        for k in range(0, len(tiles), GROUP)
    ]
    totals = [jnp.zeros((MOMENTS, LANES), jnp.float32)] * len(targets)
    rates = [jnp.zeros((LANES, LANES), jnp.float32)] * len(targets)

    def product_of(step):
        n, group = step
        columns = jnp.concatenate([source[:DEPTH, :] for source, _ in group], axis=1)
        return jnp.dot(targets[n][0], columns, preferred_element_type=jnp.float32)

    def add_up(n, moments, weights, last):
        totals[n] += across(moments, weights)
        if last:
            ones = jnp.ones((ROWS, 3 * LANES), jnp.bfloat16)
            pieces = jnp.concatenate(split(rates[n]), axis=1).astype(jnp.bfloat16)
            finish(n, jnp.concatenate([totals[n], across(ones, pieces)], axis=0))

    ahead = product_of(steps[0])
    waiting = None
    for k, (n, group) in enumerate(steps):
        product = ahead
        if k + 1 < len(steps):
            ahead = product_of(steps[k + 1])
        moments, weights = [], []
        for m, (source, press_j) in enumerate(group):
            columns = slice(m * VALUES * LANES, (m + 1) * VALUES * LANES)
            pair, part = weights_of(product[:, columns], targets[n][1], press_j)
            rates[n] += part
            weights += pair
            halves = [source[DEPTH:, :LANES], source[DEPTH:, LANES : 2 * LANES]]
            moments += [jnp.concatenate(halves, axis=0)] * 2
        if waiting is not None:
            add_up(*waiting, waiting[0] != n)
        waiting = (n, jnp.concatenate(moments, axis=1), jnp.concatenate(weights, axis=1))
    add_up(*waiting, True)


def sums_at(b):
    return pl.ds(pl.multiple_of(b * SUMS, ROWS), SUMS)


def own_kernel(
    own_ref, wall_ref, edge0_ref, edge1_ref, wpair_ref, odd_ref,
    tgt, sums, wsrc, table,
):
    blocks = tgt.shape[0]

    def build(b, carry):
        put_target(state_of(own_ref[rows_at(b), :]), b, tgt)
        return carry

    lax.fori_loop(0, blocks, build, 0, unroll=UNROLL)
    row = row_index()
    count = 0
    for ref in (wall_ref, edge0_ref, edge1_ref):
        for c in range(ref.shape[0] // 4):
            held = ref[4 * c : 4 * c + 4, :]
            both = jnp.concatenate([held, held], axis=0)
            density = jnp.where(row == 6, 1.0, 0.0)
            block = jnp.where((row < 3) | (row == 7), both, density)
            put_source(block, count, wsrc, None, adhesion / cohesion)
            count += 1
    inner, edge = wall_ref.shape[0] // 4, edge0_ref.shape[0] // 4
    odd = odd_ref[0]
    for c in range(inner):
        table[edge + c] = c
    for c in range(edge):
        table[c] = inner + (1 - odd) * edge + c
        table[edge + inner + c] = inner + odd * edge + c

    together = math.gcd(blocks, WALL_TARGETS)

    def targets_from(i, carry):
        first = i * together
        targets = []
        for n in range(together):
            slots = [table[wpair_ref[first + n, k]] for k in range(wpair_ref.shape[1])]
            targets.append((tgt[first + n], None, [(wsrc.at[s], None) for s in slots]))

        def finish(n, total):
            sums[sums_at(first + n), :] = total

        run_targets(targets, finish)
        return carry

    lax.fori_loop(0, blocks // together, targets_from, 0)


def fluid_kernel(
    own_ref, ghost_ref, pair_ref, place_ref, tgt, own_sums,
    rate_ref, accel_ref, peak_ref, src, press, sums, stage, table,
):
    blocks = tgt.shape[0]
    ghosts = ghost_ref.shape[0] // ROWS
    per_mask = ghosts // 8
    for c in range(blocks):
        table[c] = c
    for mask in range(1, 8):
        for g in range(per_mask):
            table[blocks + (mask - 1) * per_mask + g] = (
                blocks + jnp.bitwise_xor(place_ref[0], mask) * per_mask + g
            )

    def build_own(b, carry):
        put_source(own_ref[rows_at(b), :], b, src, press)
        return carry

    def build(g, carry):
        put_source(ghost_ref[rows_at(g), :], blocks + g, src, press)
        return carry

    lax.fori_loop(0, blocks, build_own, 0, unroll=UNROLL)

    lax.fori_loop(0, ghosts, build, 0, unroll=UNROLL)

    choice = press_choice()
    together = math.gcd(blocks, FLUID_TARGETS)

    def targets_from(i, carry):
        first = i * together
        targets = []
        for n in range(together):
            slots = [table[pair_ref[first + n, k]] for k in range(pair_ref.shape[1])]
            target = tgt[first + n]
            press_i = jnp.dot(target, choice, preferred_element_type=jnp.float32)
            targets.append((target, press_i, [(src.at[s], press.at[s]) for s in slots]))

        def finish(n, total):
            rows = sums_at(first + n)
            sums[rows, :] = own_sums[rows, :] + total

        run_targets(targets, finish)
        return carry

    lax.fori_loop(0, blocks // together, targets_from, 0)

    rate_ref[...] = (-support * grad_coeff) * sums[pl.ds(MOMENTS, blocks, stride=SUMS), :]

    def summed(row):
        parts = [sums[pl.ds(p * ROWS + row, blocks, stride=SUMS), :] for p in range(3)]
        return parts[0] + parts[1] + parts[2]

    mass_sum = summed(6)
    square = jnp.zeros_like(mass_sum)
    for d in range(3):
        pos = (own_ref[pl.ds(d, blocks, stride=ROWS), :] - center) * (1.0 / support)
        force = (4.0 * cohesion * support) * (pos * mass_sum - summed(d))
        if d == 2:
            force -= gravity
        square += force * force
        stage[pl.ds(d, blocks, stride=ROWS), :] = force
    for b in range(blocks):
        accel_ref[:, b * LANES : (b + 1) * LANES] = stage[b * ROWS : b * ROWS + 3, :]
    peak_ref[...] = jnp.full(peak_ref.shape, jnp.sqrt(jnp.max(square)), jnp.float32)


SMEM = pl.BlockSpec(memory_space=pltpu.SMEM)
VMEM = pl.BlockSpec(memory_space=pltpu.VMEM)
PARAMS = pltpu.CompilerParams(vmem_limit_bytes=18 * 1024 * 1024)


def tile_cost(tiles):
    return pl.CostEstimate(
        flops=tiles * LANES * LANES * 1000, bytes_accessed=0, transcendentals=0
    )


def source_shape(count):
    return (count, DEPTH + 2 * ROWS, VALUES * LANES), jnp.bfloat16


def own_pass(own, walls, edges, wall_pairs, odd):
    blocks = own.shape[0] // ROWS
    wall_blocks = (walls.shape[0] + 2 * edges[0].shape[0]) // 4
    outs = [
        ((blocks, LANES, DEPTH), jnp.bfloat16),
        ((blocks * SUMS, LANES), jnp.float32),
    ]
    return pl.pallas_call(
        own_kernel,
        out_shape=[jax.ShapeDtypeStruct(*out) for out in outs],
        in_specs=[VMEM, VMEM, VMEM, VMEM, SMEM, SMEM],
        out_specs=[VMEM] * len(outs),
        scratch_shapes=[
            pltpu.VMEM(*source_shape(wall_blocks)),
            pltpu.SMEM((wall_blocks,), jnp.int32),
        ],
        compiler_params=PARAMS,
        cost_estimate=tile_cost(wall_pairs.size),
        name="own_pass",
    )(own, walls, *edges, wall_pairs, odd)


def fluid_pass(own, ghosts, pair_list, place, own_results):
    blocks = own.shape[0] // ROWS
    total = blocks + ghosts.shape[0] // ROWS
    return pl.pallas_call(
        fluid_kernel,
        out_shape=(
            jax.ShapeDtypeStruct((blocks, LANES), jnp.float32),
            jax.ShapeDtypeStruct((3, blocks * LANES), jnp.float32),
            jax.ShapeDtypeStruct((ROWS, LANES), jnp.float32),
        ),
        in_specs=[VMEM, VMEM, SMEM, SMEM] + [VMEM] * len(own_results),
        out_specs=(VMEM, VMEM, VMEM),
        scratch_shapes=[
            pltpu.VMEM(*source_shape(total)),
            pltpu.VMEM((total, ROWS, LANES), jnp.float32),
            pltpu.VMEM((blocks * SUMS, LANES), jnp.float32),
            pltpu.VMEM((blocks * ROWS, LANES), jnp.float32),
            pltpu.SMEM((total,), jnp.int32),
        ],
        compiler_params=PARAMS,
        cost_estimate=tile_cost(pair_list.size),
        name="fluid_pass",
    )(own, ghosts, pair_list, place, *own_results)


def outgoing_kernel(
    own_ref, list_ref, place_ref, wall_ref, count_ref, odd_ref, sent_ref, live_ref, edge0_ref, edge1_ref,
):
    for slot in range(8):
        mask = jnp.bitwise_xor(place_ref[0], slot)
        for g in range(list_ref.shape[1]):
            block = list_ref[jnp.maximum(mask - 1, 0), g]
            first = (slot * list_ref.shape[1] + g) * ROWS
            sent_ref[first : first + ROWS, :] = own_ref[rows_at(block), :]
    lane = lax.broadcasted_iota(jnp.int32, (4, LANES), 1)
    row = lax.broadcasted_iota(jnp.int32, (4, LANES), 0)
    for c in range(wall_ref.shape[1] // LANES):
        block = wall_ref[:, c * LANES : (c + 1) * LANES]
        kept = (row < 3) | (lane < count_ref[c])
        live_ref[4 * c : 4 * c + 4, :] = jnp.where(kept, block, 0.0)
    first = live_ref[: edge0_ref.shape[0], :]
    last = live_ref[live_ref.shape[0] - edge0_ref.shape[0] :, :]
    edge0_ref[...] = jnp.where(odd_ref[0] == 0, last, first)
    edge1_ref[...] = jnp.where(odd_ref[0] == 0, first, last)


def outgoing_pass(own, ghost_list, place, wall_state, wall_count, odd):
    walls = wall_state.shape[1] // LANES
    rows = [8 * ghost_list.shape[1] * ROWS, walls * 4, EB * 4, EB * 4]
    return pl.pallas_call(
        outgoing_kernel,
        out_shape=[jax.ShapeDtypeStruct((row, LANES), jnp.float32) for row in rows],
        in_specs=[VMEM, SMEM, SMEM, VMEM, SMEM, SMEM],
        out_specs=[VMEM] * len(rows),
        name="outgoing_pass",
    )(own, ghost_list, place, wall_state, wall_count, odd)


def largest(peak, outer, inner):
    count, width = lax.axis_size(outer), lax.axis_size(inner)
    leaders = [(o, i) for o in range(count) for i in range(width) if i % 2 == 1]

    def exchanged(value, outer_mask, inner_mask, places):
        steps = [(o * width + i, (o ^ outer_mask) * width + (i ^ inner_mask)) for o, i in places]
        return jnp.maximum(value, lax.ppermute(value, (outer, inner), steps))

    if width > 1:
        peak = exchanged(peak, 0, 1, [(o, i) for o in range(count) for i in range(width)])
    for bit in range(1, (width - 1).bit_length()):
        peak = exchanged(peak, 0, 1 << bit, leaders)
    for bit in range((count - 1).bit_length()):
        peak = exchanged(peak, 1 << bit, 0, leaders if width > 1 else [(o, 0) for o in range(count)])
    if width > 1:
        peak = exchanged(peak, 0, 1, leaders)
    return peak


def facing(edges, axis):
    count = lax.axis_size(axis)
    landed = []
    for start, sent in enumerate(edges):
        pairs = [(i, i + 1) for i in range(start, count - 1, 2)]
        landed.append(lax.ppermute(sent, axis, pairs + [(j, i) for i, j in pairs]))
    return landed


def per_device(fluid_state, ghost_list, pair_list, wall_state, wall_count, wall_pairs):
    block_total = fluid_state.shape[1] // LANES
    own = jnp.transpose(fluid_state.reshape(8, block_total, LANES), (1, 0, 2)).reshape(-1, LANES)
    place = (lax.axis_index("orb") % 8).reshape(1)
    odd = (lax.axis_index("wall") % 2).reshape(1)
    sent, walls, *edges = outgoing_pass(own, ghost_list, place, wall_state, wall_count, odd)
    edges = facing(edges, "wall")
    groups = [list(range(g, g + 8)) for g in range(0, lax.axis_size("orb"), 8)]
    landed = lax.all_to_all(
        sent.reshape(8, -1, LANES),
        "orb",
        0,
        0,
        axis_index_groups=groups if len(groups) > 1 else None,
    )
    own_results = own_pass(own, walls, edges, wall_pairs, odd)
    rate, acceleration, local_peak = fluid_pass(
        own, landed.reshape(-1, LANES), pair_list, place, own_results
    )
    peak = largest(local_peak, "orb", "wall")[0, 0]
    time_step = courant * jnp.sqrt(smoothing / (peak + 1e-06))
    return (rate.reshape(-1), acceleration, time_step)


def solution(mesh):
    return jax.shard_map(
        per_device,
        mesh=mesh,
        in_specs=(
            P(None, ("orb", "wall")),
            P(None, ("orb", "wall")),
            P(("orb", "wall"), None),
            P(None, ("orb", "wall")),
            P(("orb", "wall")),
            P(("orb", "wall"), None),
        ),
        out_specs=(P(("orb", "wall")), P(None, ("orb", "wall")), P()),
        check_vma=False,
    )
```

```python
import math

import jax
import jax.numpy as jnp
from jax import lax
from jax.experimental import pallas as pl
from jax.experimental.pallas import tpu as pltpu
from jax.sharding import PartitionSpec as P

EB = 1
LANES = 128
ROWS = 8
DEPTH = 12 * ROWS
MOMENTS = 4 * ROWS
SUMS = MOMENTS + ROWS
UNROLL = 12
VALUES = 3
GROUP = 2
WALL_TARGETS = 24
FLUID_TARGETS = 12

smoothing = 0.1
support = 0.3
kernel_norm = 21.0 / (2.0 * 3.141592653589793 * support**3)
grad_coeff = -20.0 / support**2 * kernel_norm
tait_coeff = 25.0 / 7.0
visc_coeff = 0.05
cohesion = 2000.0
adhesion = 2000.0
gravity = 9.81
courant = 0.25

center = 0.3
shift = 0.0001 / support**2
press_coeff = -grad_coeff / (4.0 * cohesion)
density_coeff = (support * 4.0 * cohesion) / (-grad_coeff * visc_coeff * 2.0)

SPLITS = ((0, 0), (0, 1), (1, 0), (0, 2), (2, 0), (1, 1))


def split(value):
    first = value.astype(jnp.bfloat16).astype(jnp.float32)
    rest = value - first
    second = rest.astype(jnp.bfloat16).astype(jnp.float32)
    return [first, second, rest - second]


def pressure_ratio(density):
    square = density * density
    return tait_coeff * (square * square * square * density - 1.0) / square


def row_index():
    return lax.broadcasted_iota(jnp.int32, (ROWS, LANES), 0)


def state_of(block):
    row = row_index()
    y = jnp.where(row < 3, (block - center) * (1.0 / support), block)
    y = jnp.where(row == 6, block * density_coeff, y)
    products = y * jnp.where(row < 3, y, pltpu.roll(y, 3, axis=0))
    sums = products + pltpu.roll(products, ROWS - 1, axis=0) + pltpu.roll(products, ROWS - 2, axis=0)

    def everywhere(value, index):
        return jnp.broadcast_to(value[index : index + 1], (ROWS, LANES))

    press = press_coeff * pressure_ratio(everywhere(block, 6))
    return (
        y, everywhere(sums, 0), everywhere(sums, 3), everywhere(y, 6), everywhere(y, 7), press,
    )


def chosen(default, *cases):
    row = row_index()
    value = jnp.full((ROWS, LANES), default, jnp.float32)
    for index, case in cases:
        value = jnp.where(row == index, case, value)
    return value


def target_groups(state):
    y, n, e, r, _, press = state
    row = row_index()
    first = jnp.where(row < 6, y, jnp.where(row == 6, n + shift, e))
    scaled = r * jnp.where(row < 3, y, jnp.where(row == 3, 1.0, n + shift))
    second = jnp.where(row < 5, scaled, chosen(0.0, (5, press), (6, 1.0)))
    return first, second


def source_groups(state, wall):
    y, n, e, r, m, press = state
    row = row_index()
    minus = jnp.where(row < 3, -2.0 * y, 0.0)
    near = chosen(minus, (6, 1.0)), chosen(0.0, (6, n - shift))
    turned = jnp.where(row < 3, pltpu.roll(y, 5, axis=0), pltpu.roll(y, 3, axis=0))
    along = m * jnp.where(row < 6, turned, chosen(0.0, (7, -1.0))), chosen(0.0, (6, -m * e))
    if wall:
        press_part = chosen(0.0, (5, 2.0 * cohesion / adhesion), (6, -0.75))
        return near, along, (None, press_part)
    return near, along, (m * r * near[0], m * chosen(minus, (3, n), (4, 1.0), (6, r * n)))


def put_source(block, s, src, press=None, mass_factor=1.0):
    state = state_of(block)
    for n, (first, second) in enumerate(source_groups(state, press is None)):
        firsts = split(first) if first is not None else [jnp.zeros((ROWS, LANES))] * 3
        pieces = [
            jnp.concatenate(pair, axis=0).astype(jnp.bfloat16)
            for pair in zip(firsts, split(second))
        ]
        lanes = slice(n * LANES, (n + 1) * LANES)
        for k, (_, piece) in enumerate(SPLITS):
            src[s, 2 * ROWS * k : 2 * ROWS * (k + 1), lanes] = pieces[piece]
    moment = (mass_factor * state[4]) * jnp.where(row_index() == 6, 1.0, state[0])
    moments = split(moment) + [jnp.zeros_like(moment)]
    for n in range(2):
        half = jnp.concatenate(moments[2 * n : 2 * n + 2], axis=0)
        src[s, DEPTH:, n * LANES : (n + 1) * LANES] = half.astype(jnp.bfloat16)
    if press is not None:
        press[s] = state[5]


def put_target(state, b, tgt):
    pieces = [jnp.concatenate(pair, axis=0) for pair in zip(*map(split, target_groups(state)))]
    rows = jnp.concatenate([pieces[piece] for piece, _ in SPLITS], axis=0).astype(jnp.bfloat16)
    row = lax.broadcasted_iota(jnp.int32, (LANES, LANES), 0)
    lane = lax.broadcasted_iota(jnp.int32, (LANES, LANES), 1)
    unit = jnp.where(row == lane, 1.0, 0.0).astype(jnp.bfloat16)
    tgt[b] = across(unit, rows).astype(jnp.bfloat16)


def press_choice():
    row = lax.broadcasted_iota(jnp.int32, (DEPTH, LANES), 0)
    value = jnp.where(row == ROWS + 6, -0.75, 0.0)
    for k, (_, piece) in enumerate(SPLITS):
        if piece == 0:
            value = jnp.where(row == 2 * ROWS * k + ROWS + 5, 1.0, value)
    return value.astype(jnp.bfloat16)


def rows_at(index):
    return pl.ds(pl.multiple_of(index * ROWS, ROWS), ROWS)


def weights_of(product, press_i, press_j):
    near, approach, last = [product[:, n * LANES : (n + 1) * LANES] for n in range(VALUES)]
    guarded = jnp.maximum(near, 1e-30)
    falloff = jnp.maximum(1.0 - guarded * lax.rsqrt(guarded), 0.0)
    cubed = falloff * falloff * falloff
    if press_j is None:
        blend = falloff + last
    else:
        blend = falloff + press_i
        blend += jnp.concatenate([press_j[...]] * (LANES // ROWS), axis=0)
        blend += jnp.maximum(approach, 0.0) * pl.reciprocal(last, approx=True)
    weight = cubed * blend
    high = weight.astype(jnp.bfloat16)
    low = (weight - high.astype(jnp.float32)).astype(jnp.bfloat16)
    return [high, low], cubed * approach


def across(left, right):
    return lax.dot_general(
        left, right, (((1,), (1,)), ((), ())), preferred_element_type=jnp.float32
    )


def run_targets(targets, finish):
    steps = [
        (n, tiles[k : k + GROUP])
        for n, (_, _, tiles) in enumerate(targets)
        for k in range(0, len(tiles), GROUP)
    ]
    totals = [jnp.zeros((MOMENTS, LANES), jnp.float32)] * len(targets)
    rates = [jnp.zeros((LANES, LANES), jnp.float32)] * len(targets)

    def product_of(step):
        n, group = step
        columns = jnp.concatenate([source[:DEPTH, :] for source, _ in group], axis=1)
        return jnp.dot(targets[n][0], columns, preferred_element_type=jnp.float32)

    def add_up(n, moments, weights, last):
        totals[n] += across(moments, weights)
        if last:
            ones = jnp.ones((ROWS, 3 * LANES), jnp.bfloat16)
            pieces = jnp.concatenate(split(rates[n]), axis=1).astype(jnp.bfloat16)
            finish(n, jnp.concatenate([totals[n], across(ones, pieces)], axis=0))

    ahead = product_of(steps[0])
    waiting = None
    for k, (n, group) in enumerate(steps):
        product = ahead
        if k + 1 < len(steps):
            ahead = product_of(steps[k + 1])
        moments, weights = [], []
        for m, (source, press_j) in enumerate(group):
            columns = slice(m * VALUES * LANES, (m + 1) * VALUES * LANES)
            pair, part = weights_of(product[:, columns], targets[n][1], press_j)
            rates[n] += part
            weights += pair
            halves = [source[DEPTH:, :LANES], source[DEPTH:, LANES : 2 * LANES]]
            moments += [jnp.concatenate(halves, axis=0)] * 2
        if waiting is not None:
            add_up(*waiting, waiting[0] != n)
        waiting = (n, jnp.concatenate(moments, axis=1), jnp.concatenate(weights, axis=1))
    add_up(*waiting, True)


def sums_at(b):
    return pl.ds(pl.multiple_of(b * SUMS, ROWS), SUMS)


def own_kernel(
    own_ref, wall_ref, edge0_ref, edge1_ref, wpair_ref, odd_ref,
    tgt, sums, wsrc, table,
):
    blocks = tgt.shape[0]

    def build(b, carry):
        put_target(state_of(own_ref[rows_at(b), :]), b, tgt)
        return carry

    lax.fori_loop(0, blocks, build, 0, unroll=UNROLL)
    row = row_index()
    count = 0
    for ref in (wall_ref, edge0_ref, edge1_ref):
        for c in range(ref.shape[0] // 4):
            held = ref[4 * c : 4 * c + 4, :]
            both = jnp.concatenate([held, held], axis=0)
            density = jnp.where(row == 6, 1.0, 0.0)
            block = jnp.where((row < 3) | (row == 7), both, density)
            put_source(block, count, wsrc, None, adhesion / cohesion)
            count += 1
    inner, edge = wall_ref.shape[0] // 4, edge0_ref.shape[0] // 4
    odd = odd_ref[0]
    for c in range(inner):
        table[edge + c] = c
    for c in range(edge):
        table[c] = inner + (1 - odd) * edge + c
        table[edge + inner + c] = inner + odd * edge + c

    together = math.gcd(blocks, WALL_TARGETS)

    def targets_from(i, carry):
        first = i * together
        targets = []
        for n in range(together):
            slots = [table[wpair_ref[first + n, k]] for k in range(wpair_ref.shape[1])]
            targets.append((tgt[first + n], None, [(wsrc.at[s], None) for s in slots]))

        def finish(n, total):
            sums[sums_at(first + n), :] = total

        run_targets(targets, finish)
        return carry

    lax.fori_loop(0, blocks // together, targets_from, 0)


def fluid_kernel(
    own_ref, ghost_ref, pair_ref, place_ref, tgt, own_sums,
    rate_ref, accel_ref, peak_ref, src, press, sums, stage, table,
):
    blocks = tgt.shape[0]
    ghosts = ghost_ref.shape[0] // ROWS
    per_mask = ghosts // 8
    for c in range(blocks):
        table[c] = c
    for mask in range(1, 8):
        for g in range(per_mask):
            table[blocks + (mask - 1) * per_mask + g] = (
                blocks + jnp.bitwise_xor(place_ref[0], mask) * per_mask + g
            )

    def build_own(b, carry):
        put_source(own_ref[rows_at(b), :], b, src, press)
        return carry

    def build(g, carry):
        put_source(ghost_ref[rows_at(g), :], blocks + g, src, press)
        return carry

    lax.fori_loop(0, blocks, build_own, 0, unroll=UNROLL)

    lax.fori_loop(0, ghosts, build, 0, unroll=UNROLL)

    choice = press_choice()
    together = math.gcd(blocks, FLUID_TARGETS)

    def targets_from(i, carry):
        first = i * together
        targets = []
        for n in range(together):
            slots = [table[pair_ref[first + n, k]] for k in range(pair_ref.shape[1])]
            target = tgt[first + n]
            press_i = jnp.dot(target, choice, preferred_element_type=jnp.float32)
            targets.append((target, press_i, [(src.at[s], press.at[s]) for s in slots]))

        def finish(n, total):
            rows = sums_at(first + n)
            sums[rows, :] = own_sums[rows, :] + total

        run_targets(targets, finish)
        return carry

    lax.fori_loop(0, blocks // together, targets_from, 0)

    rate_ref[...] = (-support * grad_coeff) * sums[pl.ds(MOMENTS, blocks, stride=SUMS), :]

    def summed(row):
        parts = [sums[pl.ds(p * ROWS + row, blocks, stride=SUMS), :] for p in range(3)]
        return parts[0] + parts[1] + parts[2]

    mass_sum = summed(6)
    square = jnp.zeros_like(mass_sum)
    for d in range(3):
        pos = (own_ref[pl.ds(d, blocks, stride=ROWS), :] - center) * (1.0 / support)
        force = (4.0 * cohesion * support) * (pos * mass_sum - summed(d))
        if d == 2:
            force -= gravity
        square += force * force
        stage[pl.ds(d, blocks, stride=ROWS), :] = force
    for b in range(blocks):
        accel_ref[:, b * LANES : (b + 1) * LANES] = stage[b * ROWS : b * ROWS + 3, :]
    peak_ref[...] = jnp.full(peak_ref.shape, jnp.sqrt(jnp.max(square)), jnp.float32)


SMEM = pl.BlockSpec(memory_space=pltpu.SMEM)
VMEM = pl.BlockSpec(memory_space=pltpu.VMEM)
PARAMS = pltpu.CompilerParams(vmem_limit_bytes=18 * 1024 * 1024)


def tile_cost(tiles):
    return pl.CostEstimate(
        flops=tiles * LANES * LANES * 1000, bytes_accessed=0, transcendentals=0
    )


def source_shape(count):
    return (count, DEPTH + 2 * ROWS, VALUES * LANES), jnp.bfloat16


def own_pass(own, walls, edges, wall_pairs, odd):
    blocks = own.shape[0] // ROWS
    wall_blocks = (walls.shape[0] + 2 * edges[0].shape[0]) // 4
    outs = [
        ((blocks, LANES, DEPTH), jnp.bfloat16),
        ((blocks * SUMS, LANES), jnp.float32),
    ]
    return pl.pallas_call(
        own_kernel,
        out_shape=[jax.ShapeDtypeStruct(*out) for out in outs],
        in_specs=[VMEM, VMEM, VMEM, VMEM, SMEM, SMEM],
        out_specs=[VMEM] * len(outs),
        scratch_shapes=[
            pltpu.VMEM(*source_shape(wall_blocks)),
            pltpu.SMEM((wall_blocks,), jnp.int32),
        ],
        compiler_params=PARAMS,
        cost_estimate=tile_cost(wall_pairs.size),
        name="own_pass",
    )(own, walls, *edges, wall_pairs, odd)


def fluid_pass(own, ghosts, pair_list, place, own_results):
    blocks = own.shape[0] // ROWS
    total = blocks + ghosts.shape[0] // ROWS
    return pl.pallas_call(
        fluid_kernel,
        out_shape=(
            jax.ShapeDtypeStruct((blocks, LANES), jnp.float32),
            jax.ShapeDtypeStruct((3, blocks * LANES), jnp.float32),
            jax.ShapeDtypeStruct((ROWS, LANES), jnp.float32),
        ),
        in_specs=[VMEM, VMEM, SMEM, SMEM] + [VMEM] * len(own_results),
        out_specs=(VMEM, VMEM, VMEM),
        scratch_shapes=[
            pltpu.VMEM(*source_shape(total)),
            pltpu.VMEM((total, ROWS, LANES), jnp.float32),
            pltpu.VMEM((blocks * SUMS, LANES), jnp.float32),
            pltpu.VMEM((blocks * ROWS, LANES), jnp.float32),
            pltpu.SMEM((total,), jnp.int32),
        ],
        compiler_params=PARAMS,
        cost_estimate=tile_cost(pair_list.size),
        name="fluid_pass",
    )(own, ghosts, pair_list, place, *own_results)


def outgoing_kernel(
    own_ref, list_ref, place_ref, wall_ref, count_ref, odd_ref, sent_ref, live_ref, edge0_ref, edge1_ref,
):
    for slot in range(8):
        mask = jnp.bitwise_xor(place_ref[0], slot)
        for g in range(list_ref.shape[1]):
            block = list_ref[jnp.maximum(mask - 1, 0), g]
            first = (slot * list_ref.shape[1] + g) * ROWS
            sent_ref[first : first + ROWS, :] = own_ref[rows_at(block), :]
    lane = lax.broadcasted_iota(jnp.int32, (4, LANES), 1)
    row = lax.broadcasted_iota(jnp.int32, (4, LANES), 0)
    for c in range(wall_ref.shape[1] // LANES):
        block = wall_ref[:, c * LANES : (c + 1) * LANES]
        kept = (row < 3) | (lane < count_ref[c])
        live_ref[4 * c : 4 * c + 4, :] = jnp.where(kept, block, 0.0)
    first = live_ref[: edge0_ref.shape[0], :]
    last = live_ref[live_ref.shape[0] - edge0_ref.shape[0] :, :]
    edge0_ref[...] = jnp.where(odd_ref[0] == 0, last, first)
    inside = jnp.where(odd_ref[1] == 0, 1.0, 0.0)
    edge1_ref[...] = jnp.where(odd_ref[0] == 0, first, last) * inside


def outgoing_pass(own, ghost_list, place, wall_state, wall_count, odd):
    walls = wall_state.shape[1] // LANES
    rows = [8 * ghost_list.shape[1] * ROWS, walls * 4, EB * 4, EB * 4]
    return pl.pallas_call(
        outgoing_kernel,
        out_shape=[jax.ShapeDtypeStruct((row, LANES), jnp.float32) for row in rows],
        in_specs=[VMEM, SMEM, SMEM, VMEM, SMEM, SMEM],
        out_specs=[VMEM] * len(rows),
        name="outgoing_pass",
    )(own, ghost_list, place, wall_state, wall_count, odd)


def largest(peak, outer, inner):
    count, width = lax.axis_size(outer), lax.axis_size(inner)
    leaders = [(o, i) for o in range(count) for i in range(width) if i % 2 == 1]

    def exchanged(value, outer_mask, inner_mask, places):
        steps = [(n, n) for n in range(count * width)]
        for o, i in places:
            steps[o * width + i] = (o * width + i, (o ^ outer_mask) * width + (i ^ inner_mask))
        return jnp.maximum(value, lax.ppermute(value, (outer, inner), steps))

    if width > 1:
        peak = exchanged(peak, 0, 1, [(o, i) for o in range(count) for i in range(width)])
    for bit in range(1, (width - 1).bit_length()):
        peak = exchanged(peak, 0, 1 << bit, leaders)
    for bit in range((count - 1).bit_length()):
        peak = exchanged(peak, 1 << bit, 0, leaders if width > 1 else [(o, 0) for o in range(count)])
    if width > 1:
        peak = exchanged(peak, 0, 1, [(o, i) for o in range(count) for i in range(width)])
    return peak


def facing(edges, axis):
    count = lax.axis_size(axis)
    landed = []
    for start, sent in enumerate(edges):
        pairs = [(i, (i + 1) % count) for i in range(start, count - count % 2, 2)]
        landed.append(lax.ppermute(sent, axis, pairs + [(j, i) for i, j in pairs]))
    return landed


def per_device(fluid_state, ghost_list, pair_list, wall_state, wall_count, wall_pairs):
    block_total = fluid_state.shape[1] // LANES
    own = jnp.transpose(fluid_state.reshape(8, block_total, LANES), (1, 0, 2)).reshape(-1, LANES)
    place = (lax.axis_index("orb") % 8).reshape(1)
    along, row_length = lax.axis_index("wall"), lax.axis_size("wall")
    at_end = (along == 0) | (along == row_length - row_length % 2 - 1)
    odd = jnp.stack([along % 2, at_end.astype(along.dtype)])
    sent, walls, *edges = outgoing_pass(own, ghost_list, place, wall_state, wall_count, odd)
    edges = facing(edges, "wall")
    groups = [list(range(g, g + 8)) for g in range(0, lax.axis_size("orb"), 8)]
    landed = lax.all_to_all(
        sent.reshape(8, -1, LANES),
        "orb",
        0,
        0,
        axis_index_groups=groups if len(groups) > 1 else None,
    )
    own_results = own_pass(own, walls, edges, wall_pairs, odd)
    rate, acceleration, local_peak = fluid_pass(
        own, landed.reshape(-1, LANES), pair_list, place, own_results
    )
    peak = largest(local_peak, "orb", "wall")[0, 0]
    time_step = courant * jnp.sqrt(smoothing / (peak + 1e-06))
    return (rate.reshape(-1), acceleration, time_step)


def solution(mesh):
    return jax.shard_map(
        per_device,
        mesh=mesh,
        in_specs=(
            P(None, ("orb", "wall")),
            P(None, ("orb", "wall")),
            P(("orb", "wall"), None),
            P(None, ("orb", "wall")),
            P(("orb", "wall")),
            P(("orb", "wall"), None),
        ),
        out_specs=(P(("orb", "wall")), P(None, ("orb", "wall")), P()),
        check_vma=False,
    )
```

```python
import functools
import math

import jax
import jax.numpy as jnp
from jax import lax
from jax.experimental import pallas as pl
from jax.experimental.pallas import tpu as pltpu
from jax.sharding import PartitionSpec as P

EB = 1
LANES = 128
ROWS = 8
DEPTH = 12 * ROWS
MOMENTS = 4 * ROWS
SUMS = MOMENTS + ROWS
UNROLL = 12
VALUES = 3
GROUP = 2
WALL_TARGETS = 24
FLUID_TARGETS = 12

smoothing = 0.1
support = 0.3
kernel_norm = 21.0 / (2.0 * 3.141592653589793 * support**3)
grad_coeff = -20.0 / support**2 * kernel_norm
tait_coeff = 25.0 / 7.0
visc_coeff = 0.05
cohesion = 2000.0
adhesion = 2000.0
gravity = 9.81
courant = 0.25

center = 0.3
shift = 0.0001 / support**2
press_coeff = -grad_coeff / (4.0 * cohesion)
density_coeff = (support * 4.0 * cohesion) / (-grad_coeff * visc_coeff * 2.0)

SPLITS = ((0, 0), (0, 1), (1, 0), (0, 2), (2, 0), (1, 1))


def split(value):
    first = value.astype(jnp.bfloat16).astype(jnp.float32)
    rest = value - first
    second = rest.astype(jnp.bfloat16).astype(jnp.float32)
    return [first, second, rest - second]


def pressure_ratio(density):
    square = density * density
    return tait_coeff * (square * square * square * density - 1.0) / square


def row_index():
    return lax.broadcasted_iota(jnp.int32, (ROWS, LANES), 0)


def state_of(block):
    row = row_index()
    y = jnp.where(row < 3, (block - center) * (1.0 / support), block)
    y = jnp.where(row == 6, block * density_coeff, y)
    products = y * jnp.where(row < 3, y, pltpu.roll(y, 3, axis=0))
    sums = products + pltpu.roll(products, ROWS - 1, axis=0) + pltpu.roll(products, ROWS - 2, axis=0)

    def everywhere(value, index):
        return jnp.broadcast_to(value[index : index + 1], (ROWS, LANES))

    press = press_coeff * pressure_ratio(everywhere(block, 6))
    return (
        y, everywhere(sums, 0), everywhere(sums, 3), everywhere(y, 6), everywhere(y, 7), press,
    )


def chosen(default, *cases):
    row = row_index()
    value = jnp.full((ROWS, LANES), default, jnp.float32)
    for index, case in cases:
        value = jnp.where(row == index, case, value)
    return value


def target_groups(state):
    y, n, e, r, _, press = state
    row = row_index()
    first = jnp.where(row < 6, y, jnp.where(row == 6, n + shift, e))
    scaled = r * jnp.where(row < 3, y, jnp.where(row == 3, 1.0, n + shift))
    second = jnp.where(row < 5, scaled, chosen(0.0, (5, press), (6, 1.0)))
    return first, second


def source_groups(state, wall):
    y, n, e, r, m, press = state
    row = row_index()
    minus = jnp.where(row < 3, -2.0 * y, 0.0)
    near = chosen(minus, (6, 1.0)), chosen(0.0, (6, n - shift))
    turned = jnp.where(row < 3, pltpu.roll(y, 5, axis=0), pltpu.roll(y, 3, axis=0))
    along = m * jnp.where(row < 6, turned, chosen(0.0, (7, -1.0))), chosen(0.0, (6, -m * e))
    if wall:
        press_part = chosen(0.0, (5, 2.0 * cohesion / adhesion), (6, -0.75))
        return near, along, (None, press_part)
    return near, along, (m * r * near[0], m * chosen(minus, (3, n), (4, 1.0), (6, r * n)))


def put_source(block, s, src, press=None, mass_factor=1.0):
    state = state_of(block)
    for n, (first, second) in enumerate(source_groups(state, press is None)):
        firsts = split(first) if first is not None else [jnp.zeros((ROWS, LANES))] * 3
        pieces = [
            jnp.concatenate(pair, axis=0).astype(jnp.bfloat16)
            for pair in zip(firsts, split(second))
        ]
        lanes = slice(n * LANES, (n + 1) * LANES)
        for k, (_, piece) in enumerate(SPLITS):
            src[s, 2 * ROWS * k : 2 * ROWS * (k + 1), lanes] = pieces[piece]
    moment = (mass_factor * state[4]) * jnp.where(row_index() == 6, 1.0, state[0])
    moments = split(moment) + [jnp.zeros_like(moment)]
    for n in range(2):
        half = jnp.concatenate(moments[2 * n : 2 * n + 2], axis=0)
        src[s, DEPTH:, n * LANES : (n + 1) * LANES] = half.astype(jnp.bfloat16)
    if press is not None:
        press[s] = state[5]


def put_target(state, b, tgt):
    pieces = [jnp.concatenate(pair, axis=0) for pair in zip(*map(split, target_groups(state)))]
    rows = jnp.concatenate([pieces[piece] for piece, _ in SPLITS], axis=0).astype(jnp.bfloat16)
    row = lax.broadcasted_iota(jnp.int32, (LANES, LANES), 0)
    lane = lax.broadcasted_iota(jnp.int32, (LANES, LANES), 1)
    unit = jnp.where(row == lane, 1.0, 0.0).astype(jnp.bfloat16)
    tgt[b] = across(unit, rows).astype(jnp.bfloat16)


def press_choice():
    row = lax.broadcasted_iota(jnp.int32, (DEPTH, LANES), 0)
    value = jnp.where(row == ROWS + 6, -0.75, 0.0)
    for k, (_, piece) in enumerate(SPLITS):
        if piece == 0:
            value = jnp.where(row == 2 * ROWS * k + ROWS + 5, 1.0, value)
    return value.astype(jnp.bfloat16)


def rows_at(index):
    return pl.ds(pl.multiple_of(index * ROWS, ROWS), ROWS)


def weights_of(product, press_i, press_j):
    near, approach, last = [product[:, n * LANES : (n + 1) * LANES] for n in range(VALUES)]
    guarded = jnp.maximum(near, 1e-30)
    falloff = jnp.maximum(1.0 - guarded * lax.rsqrt(guarded), 0.0)
    cubed = falloff * falloff * falloff
    if press_j is None:
        blend = falloff + last
    else:
        blend = falloff + press_i
        blend += jnp.concatenate([press_j[...]] * (LANES // ROWS), axis=0)
        blend += jnp.maximum(approach, 0.0) * pl.reciprocal(last, approx=True)
    weight = cubed * blend
    high = weight.astype(jnp.bfloat16)
    low = (weight - high.astype(jnp.float32)).astype(jnp.bfloat16)
    return [high, low], cubed * approach


def across(left, right):
    return lax.dot_general(
        left, right, (((1,), (1,)), ((), ())), preferred_element_type=jnp.float32
    )


def run_targets(targets, finish):
    steps = [
        (n, tiles[k : k + GROUP])
        for n, (_, _, tiles) in enumerate(targets)
        for k in range(0, len(tiles), GROUP)
    ]
    totals = [jnp.zeros((MOMENTS, LANES), jnp.float32)] * len(targets)
    rates = [jnp.zeros((LANES, LANES), jnp.float32)] * len(targets)

    def product_of(step):
        n, group = step
        columns = jnp.concatenate([source[:DEPTH, :] for source, _ in group], axis=1)
        return jnp.dot(targets[n][0], columns, preferred_element_type=jnp.float32)

    def add_up(n, moments, weights, last):
        totals[n] += across(moments, weights)
        if last:
            ones = jnp.ones((ROWS, 3 * LANES), jnp.bfloat16)
            pieces = jnp.concatenate(split(rates[n]), axis=1).astype(jnp.bfloat16)
            finish(n, jnp.concatenate([totals[n], across(ones, pieces)], axis=0))

    ahead = product_of(steps[0])
    waiting = None
    for k, (n, group) in enumerate(steps):
        product = ahead
        if k + 1 < len(steps):
            ahead = product_of(steps[k + 1])
        moments, weights = [], []
        for m, (source, press_j) in enumerate(group):
            columns = slice(m * VALUES * LANES, (m + 1) * VALUES * LANES)
            pair, part = weights_of(product[:, columns], targets[n][1], press_j)
            rates[n] += part
            weights += pair
            halves = [source[DEPTH:, :LANES], source[DEPTH:, LANES : 2 * LANES]]
            moments += [jnp.concatenate(halves, axis=0)] * 2
        if waiting is not None:
            add_up(*waiting, waiting[0] != n)
        waiting = (n, jnp.concatenate(moments, axis=1), jnp.concatenate(weights, axis=1))
    add_up(*waiting, True)


def sums_at(b):
    return pl.ds(pl.multiple_of(b * SUMS, ROWS), SUMS)


def own_kernel(
    own_ref, wall_ref, edge0_ref, edge1_ref, wpair_ref, along_ref,
    tgt, sums, wsrc, table,
):
    blocks = tgt.shape[0]

    def build(b, carry):
        put_target(state_of(own_ref[rows_at(b), :]), b, tgt)
        return carry

    lax.fori_loop(0, blocks, build, 0, unroll=UNROLL)
    row = row_index()
    count = 0
    for ref in (wall_ref, edge0_ref, edge1_ref):
        for c in range(ref.shape[0] // 4):
            held = ref[4 * c : 4 * c + 4, :]
            both = jnp.concatenate([held, held], axis=0)
            density = jnp.where(row == 6, 1.0, 0.0)
            block = jnp.where((row < 3) | (row == 7), both, density)
            put_source(block, count, wsrc, None, adhesion / cohesion)
            count += 1
    inner, edge = wall_ref.shape[0] // 4, edge0_ref.shape[0] // 4
    odd = along_ref[0] % 2
    for c in range(inner):
        table[edge + c] = c
    for c in range(edge):
        table[c] = inner + (1 - odd) * edge + c
        table[edge + inner + c] = inner + odd * edge + c

    together = math.gcd(blocks, WALL_TARGETS)

    def targets_from(i, carry):
        first = i * together
        targets = []
        for n in range(together):
            slots = [table[wpair_ref[first + n, k]] for k in range(wpair_ref.shape[1])]
            targets.append((tgt[first + n], None, [(wsrc.at[s], None) for s in slots]))

        def finish(n, total):
            sums[sums_at(first + n), :] = total

        run_targets(targets, finish)
        return carry

    lax.fori_loop(0, blocks // together, targets_from, 0)


def fluid_kernel(
    own_ref, ghost_ref, pair_ref, place_ref, tgt, own_sums,
    rate_ref, accel_ref, peak_ref, src, press, sums, stage, table,
):
    blocks = tgt.shape[0]
    ghosts = ghost_ref.shape[0] // ROWS
    per_mask = ghosts // 8
    for c in range(blocks):
        table[c] = c
    for mask in range(1, 8):
        for g in range(per_mask):
            table[blocks + (mask - 1) * per_mask + g] = (
                blocks + jnp.bitwise_xor(place_ref[0], mask) * per_mask + g
            )

    def build_own(b, carry):
        put_source(own_ref[rows_at(b), :], b, src, press)
        return carry

    def build(g, carry):
        put_source(ghost_ref[rows_at(g), :], blocks + g, src, press)
        return carry

    lax.fori_loop(0, blocks, build_own, 0, unroll=UNROLL)

    lax.fori_loop(0, ghosts, build, 0, unroll=UNROLL)

    choice = press_choice()
    together = math.gcd(blocks, FLUID_TARGETS)

    def targets_from(i, carry):
        first = i * together
        targets = []
        for n in range(together):
            slots = [table[pair_ref[first + n, k]] for k in range(pair_ref.shape[1])]
            target = tgt[first + n]
            press_i = jnp.dot(target, choice, preferred_element_type=jnp.float32)
            targets.append((target, press_i, [(src.at[s], press.at[s]) for s in slots]))

        def finish(n, total):
            rows = sums_at(first + n)
            sums[rows, :] = own_sums[rows, :] + total

        run_targets(targets, finish)
        return carry

    lax.fori_loop(0, blocks // together, targets_from, 0)

    rate_ref[...] = (-support * grad_coeff) * sums[pl.ds(MOMENTS, blocks, stride=SUMS), :]

    def summed(row):
        parts = [sums[pl.ds(p * ROWS + row, blocks, stride=SUMS), :] for p in range(3)]
        return parts[0] + parts[1] + parts[2]

    mass_sum = summed(6)
    square = jnp.zeros_like(mass_sum)
    for d in range(3):
        pos = (own_ref[pl.ds(d, blocks, stride=ROWS), :] - center) * (1.0 / support)
        force = (4.0 * cohesion * support) * (pos * mass_sum - summed(d))
        if d == 2:
            force -= gravity
        square += force * force
        stage[pl.ds(d, blocks, stride=ROWS), :] = force
    for b in range(blocks):
        accel_ref[:, b * LANES : (b + 1) * LANES] = stage[b * ROWS : b * ROWS + 3, :]
    peak_ref[...] = jnp.full(peak_ref.shape, jnp.sqrt(jnp.max(square)), jnp.float32)


SMEM = pl.BlockSpec(memory_space=pltpu.SMEM)
VMEM = pl.BlockSpec(memory_space=pltpu.VMEM)
PARAMS = pltpu.CompilerParams(vmem_limit_bytes=18 * 1024 * 1024)


def tile_cost(tiles):
    return pl.CostEstimate(
        flops=tiles * LANES * LANES * 1000, bytes_accessed=0, transcendentals=0
    )


def source_shape(count):
    return (count, DEPTH + 2 * ROWS, VALUES * LANES), jnp.bfloat16


def own_pass(own, walls, edges, wall_pairs, along):
    blocks = own.shape[0] // ROWS
    wall_blocks = (walls.shape[0] + 2 * edges[0].shape[0]) // 4
    outs = [
        ((blocks, LANES, DEPTH), jnp.bfloat16),
        ((blocks * SUMS, LANES), jnp.float32),
    ]
    return pl.pallas_call(
        own_kernel,
        out_shape=[jax.ShapeDtypeStruct(*out) for out in outs],
        in_specs=[VMEM, VMEM, VMEM, VMEM, SMEM, SMEM],
        out_specs=[VMEM] * len(outs),
        scratch_shapes=[
            pltpu.VMEM(*source_shape(wall_blocks)),
            pltpu.SMEM((wall_blocks,), jnp.int32),
        ],
        compiler_params=PARAMS,
        cost_estimate=tile_cost(wall_pairs.size),
        name="own_pass",
    )(own, walls, *edges, wall_pairs, along)


def fluid_pass(own, ghosts, pair_list, place, own_results):
    blocks = own.shape[0] // ROWS
    total = blocks + ghosts.shape[0] // ROWS
    return pl.pallas_call(
        fluid_kernel,
        out_shape=(
            jax.ShapeDtypeStruct((blocks, LANES), jnp.float32),
            jax.ShapeDtypeStruct((3, blocks * LANES), jnp.float32),
            jax.ShapeDtypeStruct((ROWS, LANES), jnp.float32),
        ),
        in_specs=[VMEM, VMEM, SMEM, SMEM] + [VMEM] * len(own_results),
        out_specs=(VMEM, VMEM, VMEM),
        scratch_shapes=[
            pltpu.VMEM(*source_shape(total)),
            pltpu.VMEM((total, ROWS, LANES), jnp.float32),
            pltpu.VMEM((blocks * SUMS, LANES), jnp.float32),
            pltpu.VMEM((blocks * ROWS, LANES), jnp.float32),
            pltpu.SMEM((total,), jnp.int32),
        ],
        compiler_params=PARAMS,
        cost_estimate=tile_cost(pair_list.size),
        name="fluid_pass",
    )(own, ghosts, pair_list, place, *own_results)


def outgoing_kernel(
    row_length, own_ref, list_ref, place_ref, wall_ref, count_ref, along_ref,
    sent_ref, live_ref, edge0_ref, edge1_ref,
):
    for slot in range(8):
        mask = jnp.bitwise_xor(place_ref[0], slot)
        for g in range(list_ref.shape[1]):
            block = list_ref[jnp.maximum(mask - 1, 0), g]
            first = (slot * list_ref.shape[1] + g) * ROWS
            sent_ref[first : first + ROWS, :] = own_ref[rows_at(block), :]
    lane = lax.broadcasted_iota(jnp.int32, (4, LANES), 1)
    row = lax.broadcasted_iota(jnp.int32, (4, LANES), 0)
    for c in range(wall_ref.shape[1] // LANES):
        block = wall_ref[:, c * LANES : (c + 1) * LANES]
        kept = (row < 3) | (lane < count_ref[c])
        live_ref[4 * c : 4 * c + 4, :] = jnp.where(kept, block, 0.0)
    first = live_ref[: edge0_ref.shape[0], :]
    last = live_ref[live_ref.shape[0] - edge0_ref.shape[0] :, :]
    along = along_ref[0]
    edge0_ref[...] = jnp.where(along % 2 == 0, last, first)
    end = row_length - row_length % 2 - 1
    inside = jnp.where((along == 0) | (along == end), 0.0, 1.0)
    edge1_ref[...] = jnp.where(along % 2 == 0, first, last) * inside


def outgoing_pass(own, ghost_list, place, wall_state, wall_count, along):
    walls = wall_state.shape[1] // LANES
    rows = [8 * ghost_list.shape[1] * ROWS, walls * 4, EB * 4, EB * 4]
    return pl.pallas_call(
        functools.partial(outgoing_kernel, lax.axis_size("wall")),
        out_shape=[jax.ShapeDtypeStruct((row, LANES), jnp.float32) for row in rows],
        in_specs=[VMEM, SMEM, SMEM, VMEM, SMEM, SMEM],
        out_specs=[VMEM] * len(rows),
        name="outgoing_pass",
    )(own, ghost_list, place, wall_state, wall_count, along)


def swapped(shard, axis, bit):
    return lax.ppermute(shard, axis, [(i, i ^ 1 << bit) for i in range(lax.axis_size(axis))])


def facing(edges, axis):
    count = lax.axis_size(axis)
    landed = []
    for start, sent in enumerate(edges):
        pairs = [(i, (i + 1) % count) for i in range(start, count - count % 2, 2)]
        landed.append(lax.ppermute(sent, axis, pairs + [(j, i) for i, j in pairs]))
    return landed


def per_device(fluid_state, ghost_list, pair_list, wall_state, wall_count, wall_pairs):
    block_total = fluid_state.shape[1] // LANES
    own = jnp.transpose(fluid_state.reshape(8, block_total, LANES), (1, 0, 2)).reshape(-1, LANES)
    place = (lax.axis_index("orb") % 8).reshape(1)
    along = lax.axis_index("wall").reshape(1)
    sent, walls, *edges = outgoing_pass(own, ghost_list, place, wall_state, wall_count, along)
    edges = facing(edges, "wall")
    groups = [list(range(g, g + 8)) for g in range(0, lax.axis_size("orb"), 8)]
    landed = lax.all_to_all(
        sent.reshape(8, -1, LANES),
        "orb",
        0,
        0,
        axis_index_groups=groups if len(groups) > 1 else None,
    )
    own_results = own_pass(own, walls, edges, wall_pairs, along)
    rate, acceleration, local_peak = fluid_pass(
        own, landed.reshape(-1, LANES), pair_list, place, own_results
    )
    peak = local_peak
    for axis in ("wall", "orb"):
        for bit in range((lax.axis_size(axis) - 1).bit_length()):
            peak = jnp.maximum(peak, swapped(peak, axis, bit))
    peak = peak[0, 0]
    time_step = courant * jnp.sqrt(smoothing / (peak + 1e-06))
    return (rate.reshape(-1), acceleration, time_step)


def solution(mesh):
    return jax.shard_map(
        per_device,
        mesh=mesh,
        in_specs=(
            P(None, ("orb", "wall")),
            P(None, ("orb", "wall")),
            P(("orb", "wall"), None),
            P(None, ("orb", "wall")),
            P(("orb", "wall")),
            P(("orb", "wall"), None),
        ),
        out_specs=(P(("orb", "wall")), P(None, ("orb", "wall")), P()),
        check_vma=False,
    )
```

```python
import functools
import math

import jax
import jax.numpy as jnp
from jax import lax
from jax.experimental import pallas as pl
from jax.experimental.pallas import tpu as pltpu
from jax.sharding import PartitionSpec as P

EB = 1
LANES = 128
ROWS = 8
DEPTH = 12 * ROWS
MOMENTS = 4 * ROWS
SUMS = MOMENTS + ROWS
UNROLL = 24
VALUES = 3
GROUP = 2
WALL_TARGETS = 24
FLUID_TARGETS = 12

smoothing = 0.1
support = 0.3
kernel_norm = 21.0 / (2.0 * 3.141592653589793 * support**3)
grad_coeff = -20.0 / support**2 * kernel_norm
tait_coeff = 25.0 / 7.0
visc_coeff = 0.05
cohesion = 2000.0
adhesion = 2000.0
gravity = 9.81
courant = 0.25

center = 0.3
shift = 0.0001 / support**2
press_coeff = -grad_coeff / (4.0 * cohesion)
density_coeff = (support * 4.0 * cohesion) / (-grad_coeff * visc_coeff * 2.0)

SPLITS = ((0, 0), (0, 1), (1, 0), (0, 2), (2, 0), (1, 1))


def split(value):
    first = value.astype(jnp.bfloat16).astype(jnp.float32)
    rest = value - first
    second = rest.astype(jnp.bfloat16).astype(jnp.float32)
    return [first, second, rest - second]


def pressure_ratio(density):
    square = density * density
    return tait_coeff * (square * square * square * density - 1.0) / square


def row_index():
    return lax.broadcasted_iota(jnp.int32, (ROWS, LANES), 0)


def state_of(block):
    row = row_index()
    y = jnp.where(row < 3, (block - center) * (1.0 / support), block)
    y = jnp.where(row == 6, block * density_coeff, y)
    products = y * jnp.where(row < 3, y, pltpu.roll(y, 3, axis=0))
    sums = products + pltpu.roll(products, ROWS - 1, axis=0) + pltpu.roll(products, ROWS - 2, axis=0)

    def everywhere(value, index):
        return jnp.broadcast_to(value[index : index + 1], (ROWS, LANES))

    press = press_coeff * pressure_ratio(everywhere(block, 6))
    return (
        y, everywhere(sums, 0), everywhere(sums, 3), everywhere(y, 6), everywhere(y, 7), press,
    )


def chosen(default, *cases):
    row = row_index()
    value = jnp.full((ROWS, LANES), default, jnp.float32)
    for index, case in cases:
        value = jnp.where(row == index, case, value)
    return value


def target_groups(state):
    y, n, e, r, _, press = state
    row = row_index()
    first = jnp.where(row < 6, y, jnp.where(row == 6, n + shift, e))
    scaled = r * jnp.where(row < 3, y, jnp.where(row == 3, 1.0, n + shift))
    second = jnp.where(row < 5, scaled, chosen(0.0, (5, press), (6, 1.0)))
    return first, second


def source_groups(state, wall):
    y, n, e, r, m, press = state
    row = row_index()
    minus = jnp.where(row < 3, -2.0 * y, 0.0)
    near = chosen(minus, (6, 1.0)), chosen(0.0, (6, n - shift))
    turned = jnp.where(row < 3, pltpu.roll(y, 5, axis=0), pltpu.roll(y, 3, axis=0))
    along = m * jnp.where(row < 6, turned, chosen(0.0, (7, -1.0))), chosen(0.0, (6, -m * e))
    if wall:
        press_part = chosen(0.0, (5, 2.0 * cohesion / adhesion), (6, -0.75))
        return near, along, (None, press_part)
    return near, along, (m * r * near[0], m * chosen(minus, (3, n), (4, 1.0), (6, r * n)))


def put_source(block, s, src, press=None, mass_factor=1.0):
    state = state_of(block)
    for n, (first, second) in enumerate(source_groups(state, press is None)):
        firsts = split(first) if first is not None else [jnp.zeros((ROWS, LANES))] * 3
        pieces = [
            jnp.concatenate(pair, axis=0).astype(jnp.bfloat16)
            for pair in zip(firsts, split(second))
        ]
        lanes = slice(n * LANES, (n + 1) * LANES)
        for k, (_, piece) in enumerate(SPLITS):
            src[s, 2 * ROWS * k : 2 * ROWS * (k + 1), lanes] = pieces[piece]
    moment = (mass_factor * state[4]) * jnp.where(row_index() == 6, 1.0, state[0])
    moments = split(moment) + [jnp.zeros_like(moment)]
    for n in range(2):
        half = jnp.concatenate(moments[2 * n : 2 * n + 2], axis=0)
        src[s, DEPTH:, n * LANES : (n + 1) * LANES] = half.astype(jnp.bfloat16)
    if press is not None:
        press[s] = state[5]


def put_target(state, b, tgt):
    pieces = [jnp.concatenate(pair, axis=0) for pair in zip(*map(split, target_groups(state)))]
    rows = jnp.concatenate([pieces[piece] for piece, _ in SPLITS], axis=0).astype(jnp.bfloat16)
    row = lax.broadcasted_iota(jnp.int32, (LANES, LANES), 0)
    lane = lax.broadcasted_iota(jnp.int32, (LANES, LANES), 1)
    unit = jnp.where(row == lane, 1.0, 0.0).astype(jnp.bfloat16)
    tgt[b] = across(unit, rows).astype(jnp.bfloat16)


def press_choice():
    row = lax.broadcasted_iota(jnp.int32, (DEPTH, LANES), 0)
    value = jnp.where(row == ROWS + 6, -0.75, 0.0)
    for k, (_, piece) in enumerate(SPLITS):
        if piece == 0:
            value = jnp.where(row == 2 * ROWS * k + ROWS + 5, 1.0, value)
    return value.astype(jnp.bfloat16)


def rows_at(index):
    return pl.ds(pl.multiple_of(index * ROWS, ROWS), ROWS)


def weights_of(product, press_i, press_j):
    near, approach, last = [product[:, n * LANES : (n + 1) * LANES] for n in range(VALUES)]
    guarded = jnp.maximum(near, 1e-30)
    falloff = jnp.maximum(1.0 - guarded * lax.rsqrt(guarded), 0.0)
    cubed = falloff * falloff * falloff
    if press_j is None:
        blend = falloff + last
    else:
        blend = falloff + press_i
        blend += jnp.concatenate([press_j[...]] * (LANES // ROWS), axis=0)
        blend += jnp.maximum(approach, 0.0) * pl.reciprocal(last, approx=True)
    weight = cubed * blend
    high = weight.astype(jnp.bfloat16)
    low = (weight - high.astype(jnp.float32)).astype(jnp.bfloat16)
    return [high, low], cubed * approach


def across(left, right):
    return lax.dot_general(
        left, right, (((1,), (1,)), ((), ())), preferred_element_type=jnp.float32
    )


def run_targets(targets, finish):
    steps = [
        (n, tiles[k : k + GROUP])
        for n, (_, _, tiles) in enumerate(targets)
        for k in range(0, len(tiles), GROUP)
    ]
    totals = [jnp.zeros((MOMENTS, LANES), jnp.float32)] * len(targets)
    rates = [jnp.zeros((LANES, LANES), jnp.float32)] * len(targets)

    def product_of(step):
        n, group = step
        columns = jnp.concatenate([source[:DEPTH, :] for source, _ in group], axis=1)
        return jnp.dot(targets[n][0], columns, preferred_element_type=jnp.float32)

    def add_up(n, moments, weights, last):
        totals[n] += across(moments, weights)
        if last:
            ones = jnp.ones((ROWS, 3 * LANES), jnp.bfloat16)
            pieces = jnp.concatenate(split(rates[n]), axis=1).astype(jnp.bfloat16)
            finish(n, jnp.concatenate([totals[n], across(ones, pieces)], axis=0))

    ahead = product_of(steps[0])
    waiting = None
    for k, (n, group) in enumerate(steps):
        product = ahead
        if k + 1 < len(steps):
            ahead = product_of(steps[k + 1])
        moments, weights = [], []
        for m, (source, press_j) in enumerate(group):
            columns = slice(m * VALUES * LANES, (m + 1) * VALUES * LANES)
            pair, part = weights_of(product[:, columns], targets[n][1], press_j)
            rates[n] += part
            weights += pair
            halves = [source[DEPTH:, :LANES], source[DEPTH:, LANES : 2 * LANES]]
            moments += [jnp.concatenate(halves, axis=0)] * 2
        if waiting is not None:
            add_up(*waiting, waiting[0] != n)
        waiting = (n, jnp.concatenate(moments, axis=1), jnp.concatenate(weights, axis=1))
    add_up(*waiting, True)


def sums_at(b):
    return pl.ds(pl.multiple_of(b * SUMS, ROWS), SUMS)


def own_kernel(
    own_ref, wall_ref, edge0_ref, edge1_ref, wpair_ref, along_ref,
    tgt, sums, wsrc, table,
):
    blocks = tgt.shape[0]

    def build(b, carry):
        put_target(state_of(own_ref[rows_at(b), :]), b, tgt)
        return carry

    lax.fori_loop(0, blocks, build, 0, unroll=UNROLL)
    row = row_index()
    count = 0
    for ref in (wall_ref, edge0_ref, edge1_ref):
        for c in range(ref.shape[0] // 4):
            held = ref[4 * c : 4 * c + 4, :]
            both = jnp.concatenate([held, held], axis=0)
            density = jnp.where(row == 6, 1.0, 0.0)
            block = jnp.where((row < 3) | (row == 7), both, density)
            put_source(block, count, wsrc, None, adhesion / cohesion)
            count += 1
    inner, edge = wall_ref.shape[0] // 4, edge0_ref.shape[0] // 4
    odd = along_ref[0] % 2
    for c in range(inner):
        table[edge + c] = c
    for c in range(edge):
        table[c] = inner + (1 - odd) * edge + c
        table[edge + inner + c] = inner + odd * edge + c

    together = math.gcd(blocks, WALL_TARGETS)

    def targets_from(i, carry):
        first = i * together
        targets = []
        for n in range(together):
            slots = [table[wpair_ref[first + n, k]] for k in range(wpair_ref.shape[1])]
            targets.append((tgt[first + n], None, [(wsrc.at[s], None) for s in slots]))

        def finish(n, total):
            sums[sums_at(first + n), :] = total

        run_targets(targets, finish)
        return carry

    lax.fori_loop(0, blocks // together, targets_from, 0)


def fluid_kernel(
    own_ref, ghost_ref, pair_ref, place_ref, tgt, own_sums,
    rate_ref, accel_ref, peak_ref, src, press, sums, stage, table,
):
    blocks = tgt.shape[0]
    ghosts = ghost_ref.shape[0] // ROWS
    per_mask = ghosts // 8
    for c in range(blocks):
        table[c] = c
    for mask in range(1, 8):
        for g in range(per_mask):
            table[blocks + (mask - 1) * per_mask + g] = (
                blocks + jnp.bitwise_xor(place_ref[0], mask) * per_mask + g
            )

    def build_own(b, carry):
        put_source(own_ref[rows_at(b), :], b, src, press)
        return carry

    def build(g, carry):
        put_source(ghost_ref[rows_at(g), :], blocks + g, src, press)
        return carry

    lax.fori_loop(0, blocks, build_own, 0, unroll=UNROLL)

    lax.fori_loop(0, ghosts, build, 0, unroll=UNROLL)

    choice = press_choice()
    together = math.gcd(blocks, FLUID_TARGETS)

    def targets_from(i, carry):
        first = i * together
        targets = []
        for n in range(together):
            slots = [table[pair_ref[first + n, k]] for k in range(pair_ref.shape[1])]
            target = tgt[first + n]
            press_i = jnp.dot(target, choice, preferred_element_type=jnp.float32)
            targets.append((target, press_i, [(src.at[s], press.at[s]) for s in slots]))

        def finish(n, total):
            rows = sums_at(first + n)
            sums[rows, :] = own_sums[rows, :] + total

        run_targets(targets, finish)
        return carry

    lax.fori_loop(0, blocks // together, targets_from, 0)

    rate_ref[...] = (-support * grad_coeff) * sums[pl.ds(MOMENTS, blocks, stride=SUMS), :]

    def summed(row):
        parts = [sums[pl.ds(p * ROWS + row, blocks, stride=SUMS), :] for p in range(3)]
        return parts[0] + parts[1] + parts[2]

    mass_sum = summed(6)
    square = jnp.zeros_like(mass_sum)
    for d in range(3):
        pos = (own_ref[pl.ds(d, blocks, stride=ROWS), :] - center) * (1.0 / support)
        force = (4.0 * cohesion * support) * (pos * mass_sum - summed(d))
        if d == 2:
            force -= gravity
        square += force * force
        stage[pl.ds(d, blocks, stride=ROWS), :] = force
    for b in range(blocks):
        accel_ref[:, b * LANES : (b + 1) * LANES] = stage[b * ROWS : b * ROWS + 3, :]
    peak_ref[...] = jnp.full(peak_ref.shape, jnp.sqrt(jnp.max(square)), jnp.float32)


SMEM = pl.BlockSpec(memory_space=pltpu.SMEM)
VMEM = pl.BlockSpec(memory_space=pltpu.VMEM)
PARAMS = pltpu.CompilerParams(vmem_limit_bytes=18 * 1024 * 1024)


def tile_cost(tiles):
    return pl.CostEstimate(
        flops=tiles * LANES * LANES * 1000, bytes_accessed=0, transcendentals=0
    )


def source_shape(count):
    return (count, DEPTH + 2 * ROWS, VALUES * LANES), jnp.bfloat16


def own_pass(own, walls, edges, wall_pairs, along):
    blocks = own.shape[0] // ROWS
    wall_blocks = (walls.shape[0] + 2 * edges[0].shape[0]) // 4
    outs = [
        ((blocks, LANES, DEPTH), jnp.bfloat16),
        ((blocks * SUMS, LANES), jnp.float32),
    ]
    return pl.pallas_call(
        own_kernel,
        out_shape=[jax.ShapeDtypeStruct(*out) for out in outs],
        in_specs=[VMEM, VMEM, VMEM, VMEM, SMEM, SMEM],
        out_specs=[VMEM] * len(outs),
        scratch_shapes=[
            pltpu.VMEM(*source_shape(wall_blocks)),
            pltpu.SMEM((wall_blocks,), jnp.int32),
        ],
        compiler_params=PARAMS,
        cost_estimate=tile_cost(wall_pairs.size),
        name="own_pass",
    )(own, walls, *edges, wall_pairs, along)


def fluid_pass(own, ghosts, pair_list, place, own_results):
    blocks = own.shape[0] // ROWS
    total = blocks + ghosts.shape[0] // ROWS
    return pl.pallas_call(
        fluid_kernel,
        out_shape=(
            jax.ShapeDtypeStruct((blocks, LANES), jnp.float32),
            jax.ShapeDtypeStruct((3, blocks * LANES), jnp.float32),
            jax.ShapeDtypeStruct((ROWS, LANES), jnp.float32),
        ),
        in_specs=[VMEM, VMEM, SMEM, SMEM] + [VMEM] * len(own_results),
        out_specs=(VMEM, VMEM, VMEM),
        scratch_shapes=[
            pltpu.VMEM(*source_shape(total)),
            pltpu.VMEM((total, ROWS, LANES), jnp.float32),
            pltpu.VMEM((blocks * SUMS, LANES), jnp.float32),
            pltpu.VMEM((blocks * ROWS, LANES), jnp.float32),
            pltpu.SMEM((total,), jnp.int32),
        ],
        compiler_params=PARAMS,
        cost_estimate=tile_cost(pair_list.size),
        name="fluid_pass",
    )(own, ghosts, pair_list, place, *own_results)


def outgoing_kernel(
    row_length, own_ref, list_ref, place_ref, wall_ref, count_ref, along_ref,
    sent_ref, live_ref, edge0_ref, edge1_ref,
):
    for slot in range(8):
        mask = jnp.bitwise_xor(place_ref[0], slot)
        for g in range(list_ref.shape[1]):
            block = list_ref[jnp.maximum(mask - 1, 0), g]
            first = (slot * list_ref.shape[1] + g) * ROWS
            sent_ref[first : first + ROWS, :] = own_ref[rows_at(block), :]
    lane = lax.broadcasted_iota(jnp.int32, (4, LANES), 1)
    row = lax.broadcasted_iota(jnp.int32, (4, LANES), 0)
    for c in range(wall_ref.shape[1] // LANES):
        block = wall_ref[:, c * LANES : (c + 1) * LANES]
        kept = (row < 3) | (lane < count_ref[c])
        live_ref[4 * c : 4 * c + 4, :] = jnp.where(kept, block, 0.0)
    first = live_ref[: edge0_ref.shape[0], :]
    last = live_ref[live_ref.shape[0] - edge0_ref.shape[0] :, :]
    along = along_ref[0]
    edge0_ref[...] = jnp.where(along % 2 == 0, last, first)
    end = row_length - row_length % 2 - 1
    inside = jnp.where((along == 0) | (along == end), 0.0, 1.0)
    edge1_ref[...] = jnp.where(along % 2 == 0, first, last) * inside


def outgoing_pass(own, ghost_list, place, wall_state, wall_count, along):
    walls = wall_state.shape[1] // LANES
    rows = [8 * ghost_list.shape[1] * ROWS, walls * 4, EB * 4, EB * 4]
    return pl.pallas_call(
        functools.partial(outgoing_kernel, lax.axis_size("wall")),
        out_shape=[jax.ShapeDtypeStruct((row, LANES), jnp.float32) for row in rows],
        in_specs=[VMEM, SMEM, SMEM, VMEM, SMEM, SMEM],
        out_specs=[VMEM] * len(rows),
        name="outgoing_pass",
    )(own, ghost_list, place, wall_state, wall_count, along)


def swapped(shard, axis, mask):
    count = math.prod(lax.axis_size(name) for name in axis)
    return lax.ppermute(shard, axis, [(i, i ^ mask) for i in range(count)])


def largest(peak, outer, inner):
    count, width = lax.axis_size(outer), lax.axis_size(inner)
    other = 1 if width > 1 else 0
    masks = [other] if other else []
    masks += [1 << bit | other for bit in range(1, (width - 1).bit_length())]
    masks += [width << bit | other for bit in range((count - 1).bit_length())]
    for mask in masks:
        peak = jnp.maximum(peak, swapped(peak, (outer, inner), mask))
    return peak


def facing(edges, axis):
    count = lax.axis_size(axis)
    landed = []
    for start, sent in enumerate(edges):
        pairs = [(i, (i + 1) % count) for i in range(start, count - count % 2, 2)]
        landed.append(lax.ppermute(sent, axis, pairs + [(j, i) for i, j in pairs]))
    return landed


def per_device(fluid_state, ghost_list, pair_list, wall_state, wall_count, wall_pairs):
    block_total = fluid_state.shape[1] // LANES
    own = jnp.transpose(fluid_state.reshape(8, block_total, LANES), (1, 0, 2)).reshape(-1, LANES)
    place = (lax.axis_index("orb") % 8).reshape(1)
    along = lax.axis_index("wall").reshape(1)
    sent, walls, *edges = outgoing_pass(own, ghost_list, place, wall_state, wall_count, along)
    edges = facing(edges, "wall")
    groups = [list(range(g, g + 8)) for g in range(0, lax.axis_size("orb"), 8)]
    landed = lax.all_to_all(
        sent.reshape(8, -1, LANES),
        "orb",
        0,
        0,
        axis_index_groups=groups if len(groups) > 1 else None,
    )
    own_results = own_pass(own, walls, edges, wall_pairs, along)
    rate, acceleration, local_peak = fluid_pass(
        own, landed.reshape(-1, LANES), pair_list, place, own_results
    )
    peak = largest(local_peak, "orb", "wall")[0, 0]
    time_step = courant * jnp.sqrt(smoothing / (peak + 1e-06))
    return (rate.reshape(-1), acceleration, time_step)


def solution(mesh):
    return jax.shard_map(
        per_device,
        mesh=mesh,
        in_specs=(
            P(None, ("orb", "wall")),
            P(None, ("orb", "wall")),
            P(("orb", "wall"), None),
            P(None, ("orb", "wall")),
            P(("orb", "wall")),
            P(("orb", "wall"), None),
        ),
        out_specs=(P(("orb", "wall")), P(None, ("orb", "wall")), P()),
        check_vma=False,
    )
```

```python
import functools
import math

import jax
import jax.numpy as jnp
from jax import lax
from jax.experimental import pallas as pl
from jax.experimental.pallas import tpu as pltpu
from jax.sharding import PartitionSpec as P

EB = 1
LANES = 128
ROWS = 8
DEPTH = 12 * ROWS
MOMENTS = 4 * ROWS
SUMS = MOMENTS + ROWS
UNROLL = 24
VALUES = 3
GROUP = 2
WALL_TARGETS = 24
FLUID_TARGETS = 12

smoothing = 0.1
support = 0.3
kernel_norm = 21.0 / (2.0 * 3.141592653589793 * support**3)
grad_coeff = -20.0 / support**2 * kernel_norm
tait_coeff = 25.0 / 7.0
visc_coeff = 0.05
cohesion = 2000.0
adhesion = 2000.0
gravity = 9.81
courant = 0.25

center = 0.3
shift = 0.0001 / support**2
press_coeff = -grad_coeff / (4.0 * cohesion)
density_coeff = (support * 4.0 * cohesion) / (-grad_coeff * visc_coeff * 2.0)

SPLITS = ((0, 0), (0, 1), (1, 0), (0, 2), (2, 0), (1, 1))


def split(value):
    first = value.astype(jnp.bfloat16).astype(jnp.float32)
    rest = value - first
    second = rest.astype(jnp.bfloat16).astype(jnp.float32)
    return [first, second, rest - second]


def pressure_ratio(density):
    square = density * density
    return tait_coeff * (square * square * square * density - 1.0) / square


def row_index():
    return lax.broadcasted_iota(jnp.int32, (ROWS, LANES), 0)


def state_of(block):
    row = row_index()
    y = jnp.where(row < 3, (block - center) * (1.0 / support), block)
    y = jnp.where(row == 6, block * density_coeff, y)
    products = y * jnp.where(row < 3, y, pltpu.roll(y, 3, axis=0))
    sums = products + pltpu.roll(products, ROWS - 1, axis=0) + pltpu.roll(products, ROWS - 2, axis=0)

    def everywhere(value, index):
        return jnp.broadcast_to(value[index : index + 1], (ROWS, LANES))

    press = press_coeff * pressure_ratio(everywhere(block, 6))
    return (
        y, everywhere(sums, 0), everywhere(sums, 3), everywhere(y, 6), everywhere(y, 7), press,
    )


def chosen(default, *cases):
    row = row_index()
    value = jnp.full((ROWS, LANES), default, jnp.float32)
    for index, case in cases:
        value = jnp.where(row == index, case, value)
    return value


def target_groups(state):
    y, n, e, r, _, press = state
    row = row_index()
    first = jnp.where(row < 6, y, jnp.where(row == 6, n + shift, e))
    scaled = r * jnp.where(row < 3, y, jnp.where(row == 3, 1.0, n + shift))
    second = jnp.where(row < 5, scaled, chosen(0.0, (5, press), (6, 1.0)))
    return first, second


def source_groups(state, wall):
    y, n, e, r, m, press = state
    row = row_index()
    minus = jnp.where(row < 3, -2.0 * y, 0.0)
    near = chosen(minus, (6, 1.0)), chosen(0.0, (6, n - shift))
    turned = jnp.where(row < 3, pltpu.roll(y, 5, axis=0), pltpu.roll(y, 3, axis=0))
    along = m * jnp.where(row < 6, turned, chosen(0.0, (7, -1.0))), chosen(0.0, (6, -m * e))
    if wall:
        press_part = chosen(0.0, (5, 2.0 * cohesion / adhesion), (6, -0.75))
        return near, along, (None, press_part)
    return near, along, (m * r * near[0], m * chosen(minus, (3, n), (4, 1.0), (6, r * n)))


def put_source(block, s, src, press=None, mass_factor=1.0):
    state = state_of(block)
    for n, (first, second) in enumerate(source_groups(state, press is None)):
        firsts = split(first) if first is not None else [jnp.zeros((ROWS, LANES))] * 3
        pieces = [
            jnp.concatenate(pair, axis=0).astype(jnp.bfloat16)
            for pair in zip(firsts, split(second))
        ]
        lanes = slice(n * LANES, (n + 1) * LANES)
        for k, (_, piece) in enumerate(SPLITS):
            src[s, 2 * ROWS * k : 2 * ROWS * (k + 1), lanes] = pieces[piece]
    moment = (mass_factor * state[4]) * jnp.where(row_index() == 6, 1.0, state[0])
    moments = split(moment) + [jnp.zeros_like(moment)]
    for n in range(2):
        half = jnp.concatenate(moments[2 * n : 2 * n + 2], axis=0)
        src[s, DEPTH:, n * LANES : (n + 1) * LANES] = half.astype(jnp.bfloat16)
    if press is not None:
        press[s] = state[5]


def put_target(state, b, tgt):
    pieces = [jnp.concatenate(pair, axis=0) for pair in zip(*map(split, target_groups(state)))]
    rows = jnp.concatenate([pieces[piece] for piece, _ in SPLITS], axis=0).astype(jnp.bfloat16)
    row = lax.broadcasted_iota(jnp.int32, (LANES, LANES), 0)
    lane = lax.broadcasted_iota(jnp.int32, (LANES, LANES), 1)
    unit = jnp.where(row == lane, 1.0, 0.0).astype(jnp.bfloat16)
    tgt[b] = across(unit, rows).astype(jnp.bfloat16)


def press_choice():
    row = lax.broadcasted_iota(jnp.int32, (DEPTH, LANES), 0)
    value = jnp.where(row == ROWS + 6, -0.75, 0.0)
    for k, (_, piece) in enumerate(SPLITS):
        if piece == 0:
            value = jnp.where(row == 2 * ROWS * k + ROWS + 5, 1.0, value)
    return value.astype(jnp.bfloat16)


def rows_at(index):
    return pl.ds(pl.multiple_of(index * ROWS, ROWS), ROWS)


def weights_of(product, press_i, press_j):
    near, approach, last = [product[:, n * LANES : (n + 1) * LANES] for n in range(VALUES)]
    guarded = jnp.maximum(near, 1e-30)
    falloff = jnp.maximum(1.0 - guarded * lax.rsqrt(guarded), 0.0)
    cubed = falloff * falloff * falloff
    if press_j is None:
        blend = falloff + last
    else:
        blend = falloff + press_i
        blend += jnp.concatenate([press_j[...]] * (LANES // ROWS), axis=0)
        blend += jnp.maximum(approach, 0.0) * pl.reciprocal(last, approx=True)
    weight = cubed * blend
    high = weight.astype(jnp.bfloat16)
    low = (weight - high.astype(jnp.float32)).astype(jnp.bfloat16)
    return [high, low], cubed * approach


def across(left, right):
    return lax.dot_general(
        left, right, (((1,), (1,)), ((), ())), preferred_element_type=jnp.float32
    )


def run_targets(targets, finish):
    steps = [
        (n, tiles[k : k + GROUP])
        for n, (_, _, tiles) in enumerate(targets)
        for k in range(0, len(tiles), GROUP)
    ]
    totals = [jnp.zeros((MOMENTS, LANES), jnp.float32)] * len(targets)
    rates = [jnp.zeros((LANES, LANES), jnp.float32)] * len(targets)

    def product_of(step):
        n, group = step
        columns = jnp.concatenate([source[:DEPTH, :] for source, _ in group], axis=1)
        return jnp.dot(targets[n][0], columns, preferred_element_type=jnp.float32)

    def add_up(n, moments, weights, last):
        totals[n] += across(moments, weights)
        if last:
            ones = jnp.ones((ROWS, 3 * LANES), jnp.bfloat16)
            pieces = jnp.concatenate(split(rates[n]), axis=1).astype(jnp.bfloat16)
            finish(n, jnp.concatenate([totals[n], across(ones, pieces)], axis=0))

    ahead = product_of(steps[0])
    waiting = None
    for k, (n, group) in enumerate(steps):
        product = ahead
        if k + 1 < len(steps):
            ahead = product_of(steps[k + 1])
        moments, weights = [], []
        for m, (source, press_j) in enumerate(group):
            columns = slice(m * VALUES * LANES, (m + 1) * VALUES * LANES)
            pair, part = weights_of(product[:, columns], targets[n][1], press_j)
            rates[n] += part
            weights += pair
            halves = [source[DEPTH:, :LANES], source[DEPTH:, LANES : 2 * LANES]]
            moments += [jnp.concatenate(halves, axis=0)] * 2
        if waiting is not None:
            add_up(*waiting, waiting[0] != n)
        waiting = (n, jnp.concatenate(moments, axis=1), jnp.concatenate(weights, axis=1))
    add_up(*waiting, True)


def sums_at(b):
    return pl.ds(pl.multiple_of(b * SUMS, ROWS), SUMS)


def target_kernel(own_ref, tgt):
    def build(b, carry):
        put_target(state_of(own_ref[rows_at(b), :]), b, tgt)
        return carry

    lax.fori_loop(0, tgt.shape[0], build, 0, unroll=UNROLL)


def wall_kernel(tgt, wall_ref, edge0_ref, edge1_ref, wpair_ref, along_ref, sums, wsrc, table):
    blocks = tgt.shape[0]
    row = row_index()
    count = 0
    for ref in (wall_ref, edge0_ref, edge1_ref):
        for c in range(ref.shape[0] // 4):
            held = ref[4 * c : 4 * c + 4, :]
            both = jnp.concatenate([held, held], axis=0)
            density = jnp.where(row == 6, 1.0, 0.0)
            block = jnp.where((row < 3) | (row == 7), both, density)
            put_source(block, count, wsrc, None, adhesion / cohesion)
            count += 1
    inner, edge = wall_ref.shape[0] // 4, edge0_ref.shape[0] // 4
    odd = along_ref[0] % 2
    for c in range(inner):
        table[edge + c] = c
    for c in range(edge):
        table[c] = inner + (1 - odd) * edge + c
        table[edge + inner + c] = inner + odd * edge + c

    together = math.gcd(blocks, WALL_TARGETS)

    def targets_from(i, carry):
        first = i * together
        targets = []
        for n in range(together):
            slots = [table[wpair_ref[first + n, k]] for k in range(wpair_ref.shape[1])]
            targets.append((tgt[first + n], None, [(wsrc.at[s], None) for s in slots]))

        def finish(n, total):
            sums[sums_at(first + n), :] = total

        run_targets(targets, finish)
        return carry

    lax.fori_loop(0, blocks // together, targets_from, 0)


def fluid_kernel(
    own_ref, ghost_ref, pair_ref, place_ref, tgt, own_sums,
    rate_ref, accel_ref, peak_ref, src, press, sums, stage, table,
):
    blocks = tgt.shape[0]
    ghosts = ghost_ref.shape[0] // ROWS
    per_mask = ghosts // 8
    for c in range(blocks):
        table[c] = c
    for mask in range(1, 8):
        for g in range(per_mask):
            table[blocks + (mask - 1) * per_mask + g] = (
                blocks + jnp.bitwise_xor(place_ref[0], mask) * per_mask + g
            )

    def build_own(b, carry):
        put_source(own_ref[rows_at(b), :], b, src, press)
        return carry

    def build(g, carry):
        put_source(ghost_ref[rows_at(g), :], blocks + g, src, press)
        return carry

    lax.fori_loop(0, blocks, build_own, 0, unroll=UNROLL)

    lax.fori_loop(0, ghosts, build, 0, unroll=UNROLL)

    choice = press_choice()
    together = math.gcd(blocks, FLUID_TARGETS)

    def targets_from(i, carry):
        first = i * together
        targets = []
        for n in range(together):
            slots = [table[pair_ref[first + n, k]] for k in range(pair_ref.shape[1])]
            target = tgt[first + n]
            press_i = jnp.dot(target, choice, preferred_element_type=jnp.float32)
            targets.append((target, press_i, [(src.at[s], press.at[s]) for s in slots]))

        def finish(n, total):
            rows = sums_at(first + n)
            sums[rows, :] = own_sums[rows, :] + total

        run_targets(targets, finish)
        return carry

    lax.fori_loop(0, blocks // together, targets_from, 0)

    rate_ref[...] = (-support * grad_coeff) * sums[pl.ds(MOMENTS, blocks, stride=SUMS), :]

    def summed(row):
        parts = [sums[pl.ds(p * ROWS + row, blocks, stride=SUMS), :] for p in range(3)]
        return parts[0] + parts[1] + parts[2]

    mass_sum = summed(6)
    square = jnp.zeros_like(mass_sum)
    for d in range(3):
        pos = (own_ref[pl.ds(d, blocks, stride=ROWS), :] - center) * (1.0 / support)
        force = (4.0 * cohesion * support) * (pos * mass_sum - summed(d))
        if d == 2:
            force -= gravity
        square += force * force
        stage[pl.ds(d, blocks, stride=ROWS), :] = force
    for b in range(blocks):
        accel_ref[:, b * LANES : (b + 1) * LANES] = stage[b * ROWS : b * ROWS + 3, :]
    peak_ref[...] = jnp.full(peak_ref.shape, jnp.sqrt(jnp.max(square)), jnp.float32)


SMEM = pl.BlockSpec(memory_space=pltpu.SMEM)
VMEM = pl.BlockSpec(memory_space=pltpu.VMEM)
ANY = pl.BlockSpec(memory_space=pl.ANY)
PARAMS = pltpu.CompilerParams(vmem_limit_bytes=18 * 1024 * 1024)


def tile_cost(tiles):
    return pl.CostEstimate(
        flops=tiles * LANES * LANES * 1000, bytes_accessed=0, transcendentals=0
    )


def source_shape(count):
    return (count, DEPTH + 2 * ROWS, VALUES * LANES), jnp.bfloat16


def target_pass(own):
    blocks = own.shape[0] // ROWS
    return pl.pallas_call(
        target_kernel,
        out_shape=jax.ShapeDtypeStruct((blocks, LANES, DEPTH), jnp.bfloat16),
        in_specs=[VMEM],
        out_specs=VMEM,
        compiler_params=PARAMS,
        cost_estimate=tile_cost(blocks),
        name="target_pass",
    )(own)


def wall_pass(tgt, walls, edges, wall_pairs, along):
    blocks = tgt.shape[0]
    wall_blocks = (walls.shape[0] + 2 * edges[0].shape[0]) // 4
    return pl.pallas_call(
        wall_kernel,
        out_shape=jax.ShapeDtypeStruct((blocks * SUMS, LANES), jnp.float32),
        in_specs=[VMEM, VMEM, VMEM, VMEM, SMEM, SMEM],
        out_specs=VMEM,
        scratch_shapes=[
            pltpu.VMEM(*source_shape(wall_blocks)),
            pltpu.SMEM((wall_blocks,), jnp.int32),
        ],
        compiler_params=PARAMS,
        cost_estimate=tile_cost(wall_pairs.size),
        name="wall_pass",
    )(tgt, walls, *edges, wall_pairs, along)


def fluid_pass(own, ghosts, pair_list, place, own_results):
    blocks = own.shape[0] // ROWS
    total = blocks + ghosts.shape[0] // ROWS
    return pl.pallas_call(
        fluid_kernel,
        out_shape=(
            jax.ShapeDtypeStruct((blocks, LANES), jnp.float32),
            jax.ShapeDtypeStruct((3, blocks * LANES), jnp.float32),
            jax.ShapeDtypeStruct((ROWS, LANES), jnp.float32),
        ),
        in_specs=[VMEM, VMEM, SMEM, SMEM] + [VMEM] * len(own_results),
        out_specs=(VMEM, VMEM, VMEM),
        scratch_shapes=[
            pltpu.VMEM(*source_shape(total)),
            pltpu.VMEM((total, ROWS, LANES), jnp.float32),
            pltpu.VMEM((blocks * SUMS, LANES), jnp.float32),
            pltpu.VMEM((blocks * ROWS, LANES), jnp.float32),
            pltpu.SMEM((total,), jnp.int32),
        ],
        compiler_params=PARAMS,
        cost_estimate=tile_cost(pair_list.size),
        name="fluid_pass",
    )(own, ghosts, pair_list, place, *own_results)


def outgoing_kernel(
    row_length, own_ref, list_ref, place_ref, wall_ref, count_ref, along_ref,
    sent_ref, live_ref, edge0_ref, edge1_ref, copied,
):
    copies = []
    for slot in range(8):
        mask = jnp.bitwise_xor(place_ref[0], slot)
        for g in range(list_ref.shape[1]):
            block = list_ref[jnp.maximum(mask - 1, 0), g]
            n = slot * list_ref.shape[1] + g
            target = sent_ref.at[n * ROWS : (n + 1) * ROWS, :]
            copies.append(pltpu.make_async_copy(own_ref.at[rows_at(block), :], target, copied.at[n]))
            copies[-1].start()
    lane = lax.broadcasted_iota(jnp.int32, (4, LANES), 1)
    row = lax.broadcasted_iota(jnp.int32, (4, LANES), 0)
    for c in range(wall_ref.shape[1] // LANES):
        block = wall_ref[:, c * LANES : (c + 1) * LANES]
        kept = (row < 3) | (lane < count_ref[c])
        live_ref[4 * c : 4 * c + 4, :] = jnp.where(kept, block, 0.0)
    first = live_ref[: edge0_ref.shape[0], :]
    last = live_ref[live_ref.shape[0] - edge0_ref.shape[0] :, :]
    along = along_ref[0]
    edge0_ref[...] = jnp.where(along % 2 == 0, last, first)
    end = row_length - row_length % 2 - 1
    inside = jnp.where((along == 0) | (along == end), 0.0, 1.0)
    edge1_ref[...] = jnp.where(along % 2 == 0, first, last) * inside
    for copy in copies:
        copy.wait()


def outgoing_pass(own, ghost_list, place, wall_state, wall_count, along):
    walls = wall_state.shape[1] // LANES
    rows = [8 * ghost_list.shape[1] * ROWS, walls * 4, EB * 4, EB * 4]
    return pl.pallas_call(
        functools.partial(outgoing_kernel, lax.axis_size("wall")),
        out_shape=[jax.ShapeDtypeStruct((row, LANES), jnp.float32) for row in rows],
        in_specs=[ANY, SMEM, SMEM, VMEM, SMEM, SMEM],
        out_specs=[ANY] + [VMEM] * (len(rows) - 1),
        scratch_shapes=[pltpu.SemaphoreType.DMA((8 * ghost_list.shape[1],))],
        name="outgoing_pass",
    )(own, ghost_list, place, wall_state, wall_count, along)


def swapped(shard, axis, mask):
    count = math.prod(lax.axis_size(name) for name in axis)
    return lax.ppermute(shard, axis, [(i, i ^ mask) for i in range(count)])


def largest(peak, outer, inner):
    count, width = lax.axis_size(outer), lax.axis_size(inner)
    other = 1 if width > 1 else 0
    masks = [other] if other else []
    masks += [1 << bit | other for bit in range(1, (width - 1).bit_length())]
    masks += [width << bit | other for bit in range((count - 1).bit_length())]
    for mask in masks:
        peak = jnp.maximum(peak, swapped(peak, (outer, inner), mask))
    return peak


def facing(edges, axis):
    count = lax.axis_size(axis)
    landed = []
    for start, sent in enumerate(edges):
        pairs = [(i, (i + 1) % count) for i in range(start, count - count % 2, 2)]
        landed.append(lax.ppermute(sent, axis, pairs + [(j, i) for i, j in pairs]))
    return landed


def per_device(fluid_state, ghost_list, pair_list, wall_state, wall_count, wall_pairs):
    block_total = fluid_state.shape[1] // LANES
    own = jnp.transpose(fluid_state.reshape(8, block_total, LANES), (1, 0, 2)).reshape(-1, LANES)
    place = (lax.axis_index("orb") % 8).reshape(1)
    along = lax.axis_index("wall").reshape(1)
    sent, walls, *edges = outgoing_pass(own, ghost_list, place, wall_state, wall_count, along)
    edges = facing(edges, "wall")
    groups = [list(range(g, g + 8)) for g in range(0, lax.axis_size("orb"), 8)]
    landed = lax.all_to_all(
        sent.reshape(8, -1, LANES),
        "orb",
        0,
        0,
        axis_index_groups=groups if len(groups) > 1 else None,
    )
    tgt = target_pass(own)
    own_results = (tgt, wall_pass(tgt, walls, edges, wall_pairs, along))
    rate, acceleration, local_peak = fluid_pass(
        own, landed.reshape(-1, LANES), pair_list, place, own_results
    )
    peak = jnp.max(largest(local_peak, "orb", "wall"))
    time_step = courant * jnp.sqrt(smoothing / (peak + 1e-06))
    return (rate.reshape(-1), acceleration, time_step)


def solution(mesh):
    return jax.shard_map(
        per_device,
        mesh=mesh,
        in_specs=(
            P(None, ("orb", "wall")),
            P(None, ("orb", "wall")),
            P(("orb", "wall"), None),
            P(None, ("orb", "wall")),
            P(("orb", "wall")),
            P(("orb", "wall"), None),
        ),
        out_specs=(P(("orb", "wall")), P(None, ("orb", "wall")), P()),
        check_vma=False,
    )
```

```python
import functools
import math

import jax
import jax.numpy as jnp
from jax import lax
from jax.experimental import pallas as pl
from jax.experimental.pallas import tpu as pltpu
from jax.sharding import PartitionSpec as P

EB = 1
LANES = 128
ROWS = 8
DEPTH = 12 * ROWS
MOMENTS = 4 * ROWS
SUMS = MOMENTS + ROWS
UNROLL = 24
VALUES = 3
GROUP = 2
WALL_TARGETS = 24
FLUID_TARGETS = 12

smoothing = 0.1
support = 0.3
kernel_norm = 21.0 / (2.0 * 3.141592653589793 * support**3)
grad_coeff = -20.0 / support**2 * kernel_norm
tait_coeff = 25.0 / 7.0
visc_coeff = 0.05
cohesion = 2000.0
adhesion = 2000.0
gravity = 9.81
courant = 0.25

center = 0.3
shift = 0.0001 / support**2
press_coeff = -grad_coeff / (4.0 * cohesion)
density_coeff = (support * 4.0 * cohesion) / (-grad_coeff * visc_coeff * 2.0)

SPLITS = ((0, 0), (0, 1), (1, 0), (0, 2), (2, 0), (1, 1))


def split(value):
    first = value.astype(jnp.bfloat16).astype(jnp.float32)
    rest = value - first
    second = rest.astype(jnp.bfloat16).astype(jnp.float32)
    return [first, second, rest - second]


def pressure_ratio(density):
    square = density * density
    return tait_coeff * (square * square * square * density - 1.0) / square


def row_index():
    return lax.broadcasted_iota(jnp.int32, (ROWS, LANES), 0)


def state_of(block):
    row = row_index()
    y = jnp.where(row < 3, (block - center) * (1.0 / support), block)
    y = jnp.where(row == 6, block * density_coeff, y)
    products = y * jnp.where(row < 3, y, pltpu.roll(y, 3, axis=0))
    sums = products + pltpu.roll(products, ROWS - 1, axis=0) + pltpu.roll(products, ROWS - 2, axis=0)

    def everywhere(value, index):
        return jnp.broadcast_to(value[index : index + 1], (ROWS, LANES))

    press = press_coeff * pressure_ratio(everywhere(block, 6))
    return (
        y, everywhere(sums, 0), everywhere(sums, 3), everywhere(y, 6), everywhere(y, 7), press,
    )


def chosen(default, *cases):
    row = row_index()
    value = jnp.full((ROWS, LANES), default, jnp.float32)
    for index, case in cases:
        value = jnp.where(row == index, case, value)
    return value


def target_groups(state):
    y, n, e, r, _, press = state
    row = row_index()
    first = jnp.where(row < 6, y, jnp.where(row == 6, n + shift, e))
    scaled = r * jnp.where(row < 3, y, jnp.where(row == 3, 1.0, n + shift))
    second = jnp.where(row < 5, scaled, chosen(0.0, (5, press), (6, 1.0)))
    return first, second


def source_groups(state, wall):
    y, n, e, r, m, press = state
    row = row_index()
    minus = jnp.where(row < 3, -2.0 * y, 0.0)
    near = chosen(minus, (6, 1.0)), chosen(0.0, (6, n - shift))
    turned = jnp.where(row < 3, pltpu.roll(y, 5, axis=0), pltpu.roll(y, 3, axis=0))
    along = m * jnp.where(row < 6, turned, chosen(0.0, (7, -1.0))), chosen(0.0, (6, -m * e))
    if wall:
        return near, along
    return near, along, (m * r * near[0], m * chosen(minus, (3, n), (4, 1.0), (6, r * n)))


def put_source(block, s, src, press=None, mass_factor=1.0):
    state = state_of(block)
    for n, (first, second) in enumerate(source_groups(state, press is None)):
        pieces = [
            jnp.concatenate(pair, axis=0).astype(jnp.bfloat16)
            for pair in zip(split(first), split(second))
        ]
        lanes = slice(n * LANES, (n + 1) * LANES)
        for k, (_, piece) in enumerate(SPLITS):
            src[s, 2 * ROWS * k : 2 * ROWS * (k + 1), lanes] = pieces[piece]
    moment = (mass_factor * state[4]) * jnp.where(row_index() == 6, 1.0, state[0])
    moments = split(moment) + [jnp.zeros_like(moment)]
    for n in range(2):
        half = jnp.concatenate(moments[2 * n : 2 * n + 2], axis=0)
        src[s, DEPTH:, n * LANES : (n + 1) * LANES] = half.astype(jnp.bfloat16)
    if press is not None:
        press[s] = state[5]


def put_target(state, b, choice, tgt, wide):
    pieces = [jnp.concatenate(pair, axis=0) for pair in zip(*map(split, target_groups(state)))]
    rows = jnp.concatenate([pieces[piece] for piece, _ in SPLITS], axis=0).astype(jnp.bfloat16)
    row = lax.broadcasted_iota(jnp.int32, (LANES, LANES), 0)
    lane = lax.broadcasted_iota(jnp.int32, (LANES, LANES), 1)
    unit = jnp.where(row == lane, 1.0, 0.0).astype(jnp.bfloat16)
    features = across(unit, rows).astype(jnp.bfloat16)
    tgt[b] = features
    wide[b] = jnp.dot(features, choice, preferred_element_type=jnp.float32)


def press_choice():
    row = lax.broadcasted_iota(jnp.int32, (DEPTH, LANES), 0)
    value = jnp.where(row == ROWS + 6, -0.75, 0.0)
    for k, (_, piece) in enumerate(SPLITS):
        if piece == 0:
            value = jnp.where(row == 2 * ROWS * k + ROWS + 5, 1.0, value)
    return value.astype(jnp.bfloat16)


def rows_at(index):
    return pl.ds(pl.multiple_of(index * ROWS, ROWS), ROWS)


def weights_of(product, press_i, press_j):
    values = [product[:, first : first + LANES] for first in range(0, product.shape[1], LANES)]
    guarded = jnp.maximum(values[0], 1e-30)
    falloff = jnp.maximum(1.0 - guarded * lax.rsqrt(guarded), 0.0)
    cubed = falloff * falloff * falloff
    blend = falloff + press_i
    if press_j is not None:
        blend += jnp.concatenate([press_j[...]] * (LANES // ROWS), axis=0)
        blend += jnp.maximum(values[1], 0.0) * pl.reciprocal(values[2], approx=True)
    weight = cubed * blend
    high = weight.astype(jnp.bfloat16)
    low = (weight - high.astype(jnp.float32)).astype(jnp.bfloat16)
    return [high, low], cubed * values[1]


def across(left, right):
    return lax.dot_general(
        left, right, (((1,), (1,)), ((), ())), preferred_element_type=jnp.float32
    )


def run_targets(targets, values, finish):
    steps = [
        (n, tiles[k : k + GROUP])
        for n, (_, _, tiles) in enumerate(targets)
        for k in range(0, len(tiles), GROUP)
    ]
    totals = [jnp.zeros((MOMENTS, LANES), jnp.float32)] * len(targets)
    rates = [jnp.zeros((LANES, LANES), jnp.float32)] * len(targets)

    def product_of(step):
        n, group = step
        parts = [source[:DEPTH, : values * LANES] for source, _ in group]
        columns = jnp.concatenate(parts, axis=1)
        return jnp.dot(targets[n][0], columns, preferred_element_type=jnp.float32)

    def add_up(n, moments, weights, last):
        totals[n] += across(moments, weights)
        if last:
            ones = jnp.ones((ROWS, 3 * LANES), jnp.bfloat16)
            pieces = jnp.concatenate(split(rates[n]), axis=1).astype(jnp.bfloat16)
            finish(n, jnp.concatenate([totals[n], across(ones, pieces)], axis=0))

    ahead = product_of(steps[0])
    waiting = None
    for k, (n, group) in enumerate(steps):
        product = ahead
        if k + 1 < len(steps):
            ahead = product_of(steps[k + 1])
        moments, weights = [], []
        for m, (source, press_j) in enumerate(group):
            columns = slice(m * values * LANES, (m + 1) * values * LANES)
            pair, part = weights_of(product[:, columns], targets[n][1], press_j)
            rates[n] += part
            weights += pair
            halves = [source[DEPTH:, :LANES], source[DEPTH:, LANES : 2 * LANES]]
            moments += [jnp.concatenate(halves, axis=0)] * 2
        if waiting is not None:
            add_up(*waiting, waiting[0] != n)
        waiting = (n, jnp.concatenate(moments, axis=1), jnp.concatenate(weights, axis=1))
    add_up(*waiting, True)


def sums_at(b):
    return pl.ds(pl.multiple_of(b * SUMS, ROWS), SUMS)


def own_kernel(
    own_ref, wall_ref, edge0_ref, edge1_ref, wpair_ref, along_ref,
    tgt, sums, wide, wsrc, table,
):
    blocks = tgt.shape[0]

    choice = press_choice()

    def build(b, carry):
        put_target(state_of(own_ref[rows_at(b), :]), b, choice, tgt, wide)
        return carry

    lax.fori_loop(0, blocks, build, 0, unroll=UNROLL)
    row = row_index()
    count = 0
    for ref in (wall_ref, edge0_ref, edge1_ref):
        for c in range(ref.shape[0] // 4):
            held = ref[4 * c : 4 * c + 4, :]
            both = jnp.concatenate([held, held], axis=0)
            density = jnp.where(row == 6, 1.0, 0.0)
            block = jnp.where((row < 3) | (row == 7), both, density)
            put_source(block, count, wsrc, None, adhesion / cohesion)
            count += 1
    inner, edge = wall_ref.shape[0] // 4, edge0_ref.shape[0] // 4
    odd = along_ref[0] % 2
    for c in range(inner):
        table[edge + c] = c
    for c in range(edge):
        table[c] = inner + (1 - odd) * edge + c
        table[edge + inner + c] = inner + odd * edge + c

    together = math.gcd(blocks, WALL_TARGETS)
    factor = 2.0 * cohesion / adhesion

    def targets_from(i, carry):
        first = i * together
        targets = []
        for n in range(together):
            slots = [table[wpair_ref[first + n, k]] for k in range(wpair_ref.shape[1])]
            press_i = factor * wide[first + n] + 0.75 * (factor - 1.0)
            targets.append((tgt[first + n], press_i, [(wsrc.at[s], None) for s in slots]))

        def finish(n, total):
            sums[sums_at(first + n), :] = total

        run_targets(targets, VALUES - 1, finish)
        return carry

    lax.fori_loop(0, blocks // together, targets_from, 0)


def fluid_kernel(
    own_ref, ghost_ref, pair_ref, place_ref, tgt, own_sums,
    rate_ref, accel_ref, peak_ref, src, press, sums, stage, table,
):
    blocks = tgt.shape[0]
    ghosts = ghost_ref.shape[0] // ROWS
    per_mask = ghosts // 8
    for c in range(blocks):
        table[c] = c
    for mask in range(1, 8):
        for g in range(per_mask):
            table[blocks + (mask - 1) * per_mask + g] = (
                blocks + jnp.bitwise_xor(place_ref[0], mask) * per_mask + g
            )

    def build_own(b, carry):
        put_source(own_ref[rows_at(b), :], b, src, press)
        return carry

    def build(g, carry):
        put_source(ghost_ref[rows_at(g), :], blocks + g, src, press)
        return carry

    lax.fori_loop(0, blocks, build_own, 0, unroll=UNROLL)

    lax.fori_loop(0, ghosts, build, 0, unroll=UNROLL)

    choice = press_choice()
    together = math.gcd(blocks, FLUID_TARGETS)

    def targets_from(i, carry):
        first = i * together
        targets = []
        for n in range(together):
            slots = [table[pair_ref[first + n, k]] for k in range(pair_ref.shape[1])]
            target = tgt[first + n]
            press_i = jnp.dot(target, choice, preferred_element_type=jnp.float32)
            targets.append((target, press_i, [(src.at[s], press.at[s]) for s in slots]))

        def finish(n, total):
            rows = sums_at(first + n)
            sums[rows, :] = own_sums[rows, :] + total

        run_targets(targets, VALUES, finish)
        return carry

    lax.fori_loop(0, blocks // together, targets_from, 0)

    rate_ref[...] = (-support * grad_coeff) * sums[pl.ds(MOMENTS, blocks, stride=SUMS), :]

    def summed(row):
        parts = [sums[pl.ds(p * ROWS + row, blocks, stride=SUMS), :] for p in range(3)]
        return parts[0] + parts[1] + parts[2]

    mass_sum = summed(6)
    square = jnp.zeros_like(mass_sum)
    for d in range(3):
        pos = (own_ref[pl.ds(d, blocks, stride=ROWS), :] - center) * (1.0 / support)
        force = (4.0 * cohesion * support) * (pos * mass_sum - summed(d))
        if d == 2:
            force -= gravity
        square += force * force
        stage[pl.ds(d, blocks, stride=ROWS), :] = force
    for b in range(blocks):
        accel_ref[:, b * LANES : (b + 1) * LANES] = stage[b * ROWS : b * ROWS + 3, :]
    peak_ref[...] = jnp.full(peak_ref.shape, jnp.sqrt(jnp.max(square)), jnp.float32)


SMEM = pl.BlockSpec(memory_space=pltpu.SMEM)
VMEM = pl.BlockSpec(memory_space=pltpu.VMEM)
PARAMS = pltpu.CompilerParams(vmem_limit_bytes=18 * 1024 * 1024)


def tile_cost(tiles):
    return pl.CostEstimate(
        flops=tiles * LANES * LANES * 1000, bytes_accessed=0, transcendentals=0
    )


def source_shape(count):
    return (count, DEPTH + 2 * ROWS, VALUES * LANES), jnp.bfloat16


def own_pass(own, walls, edges, wall_pairs, along):
    blocks = own.shape[0] // ROWS
    wall_blocks = (walls.shape[0] + 2 * edges[0].shape[0]) // 4
    outs = [
        ((blocks, LANES, DEPTH), jnp.bfloat16),
        ((blocks * SUMS, LANES), jnp.float32),
    ]
    return pl.pallas_call(
        own_kernel,
        out_shape=[jax.ShapeDtypeStruct(*out) for out in outs],
        in_specs=[VMEM, VMEM, VMEM, VMEM, SMEM, SMEM],
        out_specs=[VMEM] * len(outs),
        scratch_shapes=[
            pltpu.VMEM((blocks, LANES, LANES), jnp.float32),
            pltpu.VMEM(*source_shape(wall_blocks)),
            pltpu.SMEM((wall_blocks,), jnp.int32),
        ],
        compiler_params=PARAMS,
        cost_estimate=tile_cost(wall_pairs.size),
        name="own_pass",
    )(own, walls, *edges, wall_pairs, along)


def fluid_pass(own, ghosts, pair_list, place, own_results):
    blocks = own.shape[0] // ROWS
    total = blocks + ghosts.shape[0] // ROWS
    return pl.pallas_call(
        fluid_kernel,
        out_shape=(
            jax.ShapeDtypeStruct((blocks, LANES), jnp.float32),
            jax.ShapeDtypeStruct((3, blocks * LANES), jnp.float32),
            jax.ShapeDtypeStruct((ROWS, LANES), jnp.float32),
        ),
        in_specs=[VMEM, VMEM, SMEM, SMEM] + [VMEM] * len(own_results),
        out_specs=(VMEM, VMEM, VMEM),
        scratch_shapes=[
            pltpu.VMEM(*source_shape(total)),
            pltpu.VMEM((total, ROWS, LANES), jnp.float32),
            pltpu.VMEM((blocks * SUMS, LANES), jnp.float32),
            pltpu.VMEM((blocks * ROWS, LANES), jnp.float32),
            pltpu.SMEM((total,), jnp.int32),
        ],
        compiler_params=PARAMS,
        cost_estimate=tile_cost(pair_list.size),
        name="fluid_pass",
    )(own, ghosts, pair_list, place, *own_results)


def outgoing_kernel(
    row_length, own_ref, list_ref, place_ref, wall_ref, count_ref, along_ref,
    sent_ref, live_ref, edge0_ref, edge1_ref,
):
    for slot in range(8):
        mask = jnp.bitwise_xor(place_ref[0], slot)
        for g in range(list_ref.shape[1]):
            block = list_ref[jnp.maximum(mask - 1, 0), g]
            first = (slot * list_ref.shape[1] + g) * ROWS
            sent_ref[first : first + ROWS, :] = own_ref[rows_at(block), :]
    lane = lax.broadcasted_iota(jnp.int32, (4, LANES), 1)
    row = lax.broadcasted_iota(jnp.int32, (4, LANES), 0)
    for c in range(wall_ref.shape[1] // LANES):
        block = wall_ref[:, c * LANES : (c + 1) * LANES]
        kept = (row < 3) | (lane < count_ref[c])
        live_ref[4 * c : 4 * c + 4, :] = jnp.where(kept, block, 0.0)
    first = live_ref[: edge0_ref.shape[0], :]
    last = live_ref[live_ref.shape[0] - edge0_ref.shape[0] :, :]
    along = along_ref[0]
    edge0_ref[...] = jnp.where(along % 2 == 0, last, first)
    end = row_length - row_length % 2 - 1
    inside = jnp.where((along == 0) | (along == end), 0.0, 1.0)
    edge1_ref[...] = jnp.where(along % 2 == 0, first, last) * inside


def outgoing_pass(own, ghost_list, place, wall_state, wall_count, along):
    walls = wall_state.shape[1] // LANES
    rows = [8 * ghost_list.shape[1] * ROWS, walls * 4, EB * 4, EB * 4]
    return pl.pallas_call(
        functools.partial(outgoing_kernel, lax.axis_size("wall")),
        out_shape=[jax.ShapeDtypeStruct((row, LANES), jnp.float32) for row in rows],
        in_specs=[VMEM, SMEM, SMEM, VMEM, SMEM, SMEM],
        out_specs=[VMEM] * len(rows),
        name="outgoing_pass",
    )(own, ghost_list, place, wall_state, wall_count, along)


def swapped(shard, axis, mask):
    count = math.prod(lax.axis_size(name) for name in axis)
    return lax.ppermute(shard, axis, [(i, i ^ mask) for i in range(count)])


def largest(peak, outer, inner):
    count, width = lax.axis_size(outer), lax.axis_size(inner)
    other = 1 if width > 1 else 0
    masks = [other] if other else []
    masks += [1 << bit | other for bit in range(1, (width - 1).bit_length())]
    masks += [width << bit | other for bit in range((count - 1).bit_length())]
    for mask in masks:
        peak = jnp.maximum(peak, swapped(peak, (outer, inner), mask))
    return peak


def facing(edges, axis):
    count = lax.axis_size(axis)
    landed = []
    for start, sent in enumerate(edges):
        pairs = [(i, (i + 1) % count) for i in range(start, count - count % 2, 2)]
        landed.append(lax.ppermute(sent, axis, pairs + [(j, i) for i, j in pairs]))
    return landed


def per_device(fluid_state, ghost_list, pair_list, wall_state, wall_count, wall_pairs):
    block_total = fluid_state.shape[1] // LANES
    own = jnp.transpose(fluid_state.reshape(8, block_total, LANES), (1, 0, 2)).reshape(-1, LANES)
    place = (lax.axis_index("orb") % 8).reshape(1)
    along = lax.axis_index("wall").reshape(1)
    sent, walls, *edges = outgoing_pass(own, ghost_list, place, wall_state, wall_count, along)
    edges = facing(edges, "wall")
    groups = [list(range(g, g + 8)) for g in range(0, lax.axis_size("orb"), 8)]
    landed = lax.all_to_all(
        sent.reshape(8, -1, LANES),
        "orb",
        0,
        0,
        axis_index_groups=groups if len(groups) > 1 else None,
    )
    own_results = own_pass(own, walls, edges, wall_pairs, along)
    rate, acceleration, local_peak = fluid_pass(
        own, landed.reshape(-1, LANES), pair_list, place, own_results
    )
    peak = largest(local_peak, "orb", "wall")[0, 0]
    time_step = courant * jnp.sqrt(smoothing / (peak + 1e-06))
    return (rate.reshape(-1), acceleration, time_step)


def solution(mesh):
    return jax.shard_map(
        per_device,
        mesh=mesh,
        in_specs=(
            P(None, ("orb", "wall")),
            P(None, ("orb", "wall")),
            P(("orb", "wall"), None),
            P(None, ("orb", "wall")),
            P(("orb", "wall")),
            P(("orb", "wall"), None),
        ),
        out_specs=(P(("orb", "wall")), P(None, ("orb", "wall")), P()),
        check_vma=False,
    )
```

```python
import functools
import math

import jax
import jax.numpy as jnp
from jax import lax
from jax.experimental import pallas as pl
from jax.experimental.pallas import tpu as pltpu
from jax.sharding import PartitionSpec as P

EB = 1
LANES = 128
ROWS = 8
DEPTH = 12 * ROWS
MOMENTS = 4 * ROWS
SUMS = MOMENTS + ROWS
UNROLL = 24
GROUP = 2
WALL_TARGETS = 24
FLUID_TARGETS = 12

smoothing = 0.1
support = 0.3
kernel_norm = 21.0 / (2.0 * 3.141592653589793 * support**3)
grad_coeff = -20.0 / support**2 * kernel_norm
tait_coeff = 25.0 / 7.0
visc_coeff = 0.05
cohesion = 2000.0
adhesion = 2000.0
gravity = 9.81
courant = 0.25

center = 0.3
shift = 0.0001 / support**2
press_coeff = -grad_coeff / (4.0 * cohesion)
density_coeff = (support * 4.0 * cohesion) / (-grad_coeff * visc_coeff * 2.0)

SPLITS = ((0, 0), (0, 1), (1, 0), (0, 2), (2, 0), (1, 1))


def split(value):
    first = value.astype(jnp.bfloat16).astype(jnp.float32)
    rest = value - first
    second = rest.astype(jnp.bfloat16).astype(jnp.float32)
    return [first, second, rest - second]


def pressure_ratio(density):
    square = density * density
    return tait_coeff * (square * square * square * density - 1.0) / square


def row_index():
    return lax.broadcasted_iota(jnp.int32, (ROWS, LANES), 0)


def state_of(block):
    row = row_index()
    y = jnp.where(row < 3, (block - center) * (1.0 / support), block)
    y = jnp.where(row == 6, block * density_coeff, y)
    products = y * jnp.where(row < 3, y, pltpu.roll(y, 3, axis=0))
    sums = products + pltpu.roll(products, ROWS - 1, axis=0) + pltpu.roll(products, ROWS - 2, axis=0)

    def everywhere(value, index):
        return jnp.broadcast_to(value[index : index + 1], (ROWS, LANES))

    press = press_coeff * pressure_ratio(everywhere(block, 6))
    return (
        y, everywhere(sums, 0), everywhere(sums, 3), everywhere(y, 6), everywhere(y, 7), press,
    )


def chosen(default, *cases):
    row = row_index()
    value = jnp.full((ROWS, LANES), default, jnp.float32)
    for index, case in cases:
        value = jnp.where(row == index, case, value)
    return value


def target_groups(state):
    y, n, e, r, _, press = state
    row = row_index()
    first = jnp.where(row < 6, y, jnp.where(row == 6, n + shift, e))
    scaled = r * jnp.where(row < 3, y, jnp.where(row == 3, 1.0, n + shift))
    second = jnp.where(row < 5, scaled, chosen(0.0, (5, press), (6, 1.0)))
    return first, second


def source_groups(state, wall):
    y, n, e, r, m, press = state
    row = row_index()
    minus = jnp.where(row < 3, -2.0 * y, 0.0)
    near = chosen(minus, (6, 1.0)), chosen(0.0, (6, n - shift))
    turned = jnp.where(row < 3, pltpu.roll(y, 5, axis=0), pltpu.roll(y, 3, axis=0))
    along = m * jnp.where(row < 6, turned, chosen(0.0, (7, -1.0))), chosen(0.0, (6, -m * e))
    if wall:
        press_part = chosen(0.0, (5, 2.0 * cohesion / adhesion), (6, -0.75))
        return near, along, (None, press_part)
    spread = m * r * near[0], m * chosen(minus, (3, n), (4, 1.0), (6, r * n))
    return near, along, spread, (None, chosen(0.0, (5, 1.0), (6, press - 0.75)))


def put_source(block, s, src, wall=False, mass_factor=1.0):
    state = state_of(block)
    for n, (first, second) in enumerate(source_groups(state, wall)):
        firsts = split(first) if first is not None else [jnp.zeros((ROWS, LANES))] * 3
        pieces = [
            jnp.concatenate(pair, axis=0).astype(jnp.bfloat16)
            for pair in zip(firsts, split(second))
        ]
        lanes = slice(n * LANES, (n + 1) * LANES)
        for k, (_, piece) in enumerate(SPLITS):
            src[s, 2 * ROWS * k : 2 * ROWS * (k + 1), lanes] = pieces[piece]
    moment = (mass_factor * state[4]) * jnp.where(row_index() == 6, 1.0, state[0])
    moments = split(moment) + [jnp.zeros_like(moment)]
    for n in range(2):
        half = jnp.concatenate(moments[2 * n : 2 * n + 2], axis=0)
        src[s, DEPTH:, n * LANES : (n + 1) * LANES] = half.astype(jnp.bfloat16)


def put_target(state, b, tgt):
    pieces = [jnp.concatenate(pair, axis=0) for pair in zip(*map(split, target_groups(state)))]
    rows = jnp.concatenate([pieces[piece] for piece, _ in SPLITS], axis=0).astype(jnp.bfloat16)
    row = lax.broadcasted_iota(jnp.int32, (LANES, LANES), 0)
    lane = lax.broadcasted_iota(jnp.int32, (LANES, LANES), 1)
    unit = jnp.where(row == lane, 1.0, 0.0).astype(jnp.bfloat16)
    tgt[b] = across(unit, rows).astype(jnp.bfloat16)


def rows_at(index):
    return pl.ds(pl.multiple_of(index * ROWS, ROWS), ROWS)


def weights_of(product):
    near, approach, *spread, press = [
        product[:, first : first + LANES] for first in range(0, product.shape[1], LANES)
    ]
    guarded = jnp.maximum(near, 1e-30)
    falloff = jnp.maximum(1.0 - guarded * lax.rsqrt(guarded), 0.0)
    cubed = falloff * falloff * falloff
    blend = falloff + press
    if spread:
        blend += jnp.maximum(approach, 0.0) * pl.reciprocal(spread[0], approx=True)
    weight = cubed * blend
    high = weight.astype(jnp.bfloat16)
    low = (weight - high.astype(jnp.float32)).astype(jnp.bfloat16)
    return [high, low], cubed * approach


def across(left, right):
    return lax.dot_general(
        left, right, (((1,), (1,)), ((), ())), preferred_element_type=jnp.float32
    )


def run_targets(targets, finish):
    steps = [
        (n, tiles[k : k + GROUP])
        for n, (_, tiles) in enumerate(targets)
        for k in range(0, len(tiles), GROUP)
    ]
    totals = [jnp.zeros((MOMENTS, LANES), jnp.float32)] * len(targets)
    rates = [jnp.zeros((LANES, LANES), jnp.float32)] * len(targets)

    def product_of(step):
        n, group = step
        columns = jnp.concatenate([source[:DEPTH, :] for source in group], axis=1)
        return jnp.dot(targets[n][0], columns, preferred_element_type=jnp.float32)

    def add_up(n, moments, weights, last):
        totals[n] += across(moments, weights)
        if last:
            ones = jnp.ones((ROWS, 3 * LANES), jnp.bfloat16)
            pieces = jnp.concatenate(split(rates[n]), axis=1).astype(jnp.bfloat16)
            finish(n, jnp.concatenate([totals[n], across(ones, pieces)], axis=0))

    ahead = product_of(steps[0])
    waiting = None
    for k, (n, group) in enumerate(steps):
        product = ahead
        if k + 1 < len(steps):
            ahead = product_of(steps[k + 1])
        moments, weights = [], []
        width = product.shape[1] // len(group)
        for m, source in enumerate(group):
            pair, part = weights_of(product[:, m * width : (m + 1) * width])
            rates[n] += part
            weights += pair
            halves = [source[DEPTH:, :LANES], source[DEPTH:, LANES : 2 * LANES]]
            moments += [jnp.concatenate(halves, axis=0)] * 2
        if waiting is not None:
            add_up(*waiting, waiting[0] != n)
        waiting = (n, jnp.concatenate(moments, axis=1), jnp.concatenate(weights, axis=1))
    add_up(*waiting, True)


def sums_at(b):
    return pl.ds(pl.multiple_of(b * SUMS, ROWS), SUMS)


def own_kernel(
    own_ref, wall_ref, edge0_ref, edge1_ref, wpair_ref, along_ref,
    tgt, sums, wsrc, table,
):
    blocks = tgt.shape[0]

    def build(b, carry):
        put_target(state_of(own_ref[rows_at(b), :]), b, tgt)
        return carry

    lax.fori_loop(0, blocks, build, 0, unroll=UNROLL)
    row = row_index()
    count = 0
    for ref in (wall_ref, edge0_ref, edge1_ref):
        for c in range(ref.shape[0] // 4):
            held = ref[4 * c : 4 * c + 4, :]
            both = jnp.concatenate([held, held], axis=0)
            density = jnp.where(row == 6, 1.0, 0.0)
            block = jnp.where((row < 3) | (row == 7), both, density)
            put_source(block, count, wsrc, True, adhesion / cohesion)
            count += 1
    inner, edge = wall_ref.shape[0] // 4, edge0_ref.shape[0] // 4
    odd = along_ref[0] % 2
    for c in range(inner):
        table[edge + c] = c
    for c in range(edge):
        table[c] = inner + (1 - odd) * edge + c
        table[edge + inner + c] = inner + odd * edge + c

    together = math.gcd(blocks, WALL_TARGETS)

    def targets_from(i, carry):
        first = i * together
        targets = []
        for n in range(together):
            slots = [table[wpair_ref[first + n, k]] for k in range(wpair_ref.shape[1])]
            targets.append((tgt[first + n], [wsrc.at[s] for s in slots]))

        def finish(n, total):
            sums[sums_at(first + n), :] = total

        run_targets(targets, finish)
        return carry

    lax.fori_loop(0, blocks // together, targets_from, 0)


def fluid_kernel(
    own_ref, ghost_ref, pair_ref, place_ref, tgt, own_sums,
    rate_ref, accel_ref, peak_ref, src, sums, stage, table,
):
    blocks = tgt.shape[0]
    ghosts = ghost_ref.shape[0] // ROWS
    per_mask = ghosts // 8
    for c in range(blocks):
        table[c] = c
    for mask in range(1, 8):
        for g in range(per_mask):
            table[blocks + (mask - 1) * per_mask + g] = (
                blocks + jnp.bitwise_xor(place_ref[0], mask) * per_mask + g
            )

    def build_own(b, carry):
        put_source(own_ref[rows_at(b), :], b, src)
        return carry

    def build(g, carry):
        put_source(ghost_ref[rows_at(g), :], blocks + g, src)
        return carry

    lax.fori_loop(0, blocks, build_own, 0, unroll=UNROLL)

    lax.fori_loop(0, ghosts, build, 0, unroll=UNROLL)

    together = math.gcd(blocks, FLUID_TARGETS)

    def targets_from(i, carry):
        first = i * together
        targets = []
        for n in range(together):
            slots = [table[pair_ref[first + n, k]] for k in range(pair_ref.shape[1])]
            targets.append((tgt[first + n], [src.at[s] for s in slots]))

        def finish(n, total):
            rows = sums_at(first + n)
            sums[rows, :] = own_sums[rows, :] + total

        run_targets(targets, finish)
        return carry

    lax.fori_loop(0, blocks // together, targets_from, 0)

    rate_ref[...] = (-support * grad_coeff) * sums[pl.ds(MOMENTS, blocks, stride=SUMS), :]

    def summed(row):
        parts = [sums[pl.ds(p * ROWS + row, blocks, stride=SUMS), :] for p in range(3)]
        return parts[0] + parts[1] + parts[2]

    mass_sum = summed(6)
    square = jnp.zeros_like(mass_sum)
    for d in range(3):
        pos = (own_ref[pl.ds(d, blocks, stride=ROWS), :] - center) * (1.0 / support)
        force = (4.0 * cohesion * support) * (pos * mass_sum - summed(d))
        if d == 2:
            force -= gravity
        square += force * force
        stage[pl.ds(d, blocks, stride=ROWS), :] = force
    for b in range(blocks):
        accel_ref[:, b * LANES : (b + 1) * LANES] = stage[b * ROWS : b * ROWS + 3, :]
    peak_ref[...] = jnp.full(peak_ref.shape, jnp.sqrt(jnp.max(square)), jnp.float32)


SMEM = pl.BlockSpec(memory_space=pltpu.SMEM)
VMEM = pl.BlockSpec(memory_space=pltpu.VMEM)
PARAMS = pltpu.CompilerParams(vmem_limit_bytes=18 * 1024 * 1024)


def tile_cost(tiles):
    return pl.CostEstimate(
        flops=tiles * LANES * LANES * 1000, bytes_accessed=0, transcendentals=0
    )


def source_shape(count, values):
    return (count, DEPTH + 2 * ROWS, values * LANES), jnp.bfloat16


def own_pass(own, walls, edges, wall_pairs, along):
    blocks = own.shape[0] // ROWS
    wall_blocks = (walls.shape[0] + 2 * edges[0].shape[0]) // 4
    outs = [
        ((blocks, LANES, DEPTH), jnp.bfloat16),
        ((blocks * SUMS, LANES), jnp.float32),
    ]
    return pl.pallas_call(
        own_kernel,
        out_shape=[jax.ShapeDtypeStruct(*out) for out in outs],
        in_specs=[VMEM, VMEM, VMEM, VMEM, SMEM, SMEM],
        out_specs=[VMEM] * len(outs),
        scratch_shapes=[
            pltpu.VMEM(*source_shape(wall_blocks, 3)),
            pltpu.SMEM((wall_blocks,), jnp.int32),
        ],
        compiler_params=PARAMS,
        cost_estimate=tile_cost(wall_pairs.size),
        name="own_pass",
    )(own, walls, *edges, wall_pairs, along)


def fluid_pass(own, ghosts, pair_list, place, own_results):
    blocks = own.shape[0] // ROWS
    total = blocks + ghosts.shape[0] // ROWS
    return pl.pallas_call(
        fluid_kernel,
        out_shape=(
            jax.ShapeDtypeStruct((blocks, LANES), jnp.float32),
            jax.ShapeDtypeStruct((3, blocks * LANES), jnp.float32),
            jax.ShapeDtypeStruct((ROWS, LANES), jnp.float32),
        ),
        in_specs=[VMEM, VMEM, SMEM, SMEM] + [VMEM] * len(own_results),
        out_specs=(VMEM, VMEM, VMEM),
        scratch_shapes=[
            pltpu.VMEM(*source_shape(total, 4)),
            pltpu.VMEM((blocks * SUMS, LANES), jnp.float32),
            pltpu.VMEM((blocks * ROWS, LANES), jnp.float32),
            pltpu.SMEM((total,), jnp.int32),
        ],
        compiler_params=PARAMS,
        cost_estimate=tile_cost(pair_list.size),
        name="fluid_pass",
    )(own, ghosts, pair_list, place, *own_results)


def outgoing_kernel(
    row_length, own_ref, list_ref, place_ref, wall_ref, count_ref, along_ref,
    sent_ref, live_ref, edge0_ref, edge1_ref,
):
    for slot in range(8):
        mask = jnp.bitwise_xor(place_ref[0], slot)
        for g in range(list_ref.shape[1]):
            block = list_ref[jnp.maximum(mask - 1, 0), g]
            first = (slot * list_ref.shape[1] + g) * ROWS
            sent_ref[first : first + ROWS, :] = own_ref[rows_at(block), :]
    lane = lax.broadcasted_iota(jnp.int32, (4, LANES), 1)
    row = lax.broadcasted_iota(jnp.int32, (4, LANES), 0)
    for c in range(wall_ref.shape[1] // LANES):
        block = wall_ref[:, c * LANES : (c + 1) * LANES]
        kept = (row < 3) | (lane < count_ref[c])
        live_ref[4 * c : 4 * c + 4, :] = jnp.where(kept, block, 0.0)
    first = live_ref[: edge0_ref.shape[0], :]
    last = live_ref[live_ref.shape[0] - edge0_ref.shape[0] :, :]
    along = along_ref[0]
    edge0_ref[...] = jnp.where(along % 2 == 0, last, first)
    end = row_length - row_length % 2 - 1
    inside = jnp.where((along == 0) | (along == end), 0.0, 1.0)
    edge1_ref[...] = jnp.where(along % 2 == 0, first, last) * inside


def outgoing_pass(own, ghost_list, place, wall_state, wall_count, along):
    walls = wall_state.shape[1] // LANES
    rows = [8 * ghost_list.shape[1] * ROWS, walls * 4, EB * 4, EB * 4]
    return pl.pallas_call(
        functools.partial(outgoing_kernel, lax.axis_size("wall")),
        out_shape=[jax.ShapeDtypeStruct((row, LANES), jnp.float32) for row in rows],
        in_specs=[VMEM, SMEM, SMEM, VMEM, SMEM, SMEM],
        out_specs=[VMEM] * len(rows),
        name="outgoing_pass",
    )(own, ghost_list, place, wall_state, wall_count, along)


def swapped(shard, axis, mask):
    count = math.prod(lax.axis_size(name) for name in axis)
    return lax.ppermute(shard, axis, [(i, i ^ mask) for i in range(count)])


def largest(peak, outer, inner):
    count, width = lax.axis_size(outer), lax.axis_size(inner)
    other = 1 if width > 1 else 0
    masks = [other] if other else []
    masks += [1 << bit | other for bit in range(1, (width - 1).bit_length())]
    masks += [width << bit | other for bit in range((count - 1).bit_length())]
    for mask in masks:
        peak = jnp.maximum(peak, swapped(peak, (outer, inner), mask))
    return peak


def facing(edges, axis):
    count = lax.axis_size(axis)
    landed = []
    for start, sent in enumerate(edges):
        pairs = [(i, (i + 1) % count) for i in range(start, count - count % 2, 2)]
        landed.append(lax.ppermute(sent, axis, pairs + [(j, i) for i, j in pairs]))
    return landed


def per_device(fluid_state, ghost_list, pair_list, wall_state, wall_count, wall_pairs):
    block_total = fluid_state.shape[1] // LANES
    own = jnp.transpose(fluid_state.reshape(8, block_total, LANES), (1, 0, 2)).reshape(-1, LANES)
    place = (lax.axis_index("orb") % 8).reshape(1)
    along = lax.axis_index("wall").reshape(1)
    sent, walls, *edges = outgoing_pass(own, ghost_list, place, wall_state, wall_count, along)
    edges = facing(edges, "wall")
    groups = [list(range(g, g + 8)) for g in range(0, lax.axis_size("orb"), 8)]
    landed = lax.all_to_all(
        sent.reshape(8, -1, LANES),
        "orb",
        0,
        0,
        axis_index_groups=groups if len(groups) > 1 else None,
    )
    own_results = own_pass(own, walls, edges, wall_pairs, along)
    rate, acceleration, local_peak = fluid_pass(
        own, landed.reshape(-1, LANES), pair_list, place, own_results
    )
    peak = largest(local_peak, "orb", "wall")[0, 0]
    time_step = courant * jnp.sqrt(smoothing / (peak + 1e-06))
    return (rate.reshape(-1), acceleration, time_step)


def solution(mesh):
    return jax.shard_map(
        per_device,
        mesh=mesh,
        in_specs=(
            P(None, ("orb", "wall")),
            P(None, ("orb", "wall")),
            P(("orb", "wall"), None),
            P(None, ("orb", "wall")),
            P(("orb", "wall")),
            P(("orb", "wall"), None),
        ),
        out_specs=(P(("orb", "wall")), P(None, ("orb", "wall")), P()),
        check_vma=False,
    )
```

```python
import functools
import math

import jax
import jax.numpy as jnp
from jax import lax
from jax.experimental import pallas as pl
from jax.experimental.pallas import tpu as pltpu
from jax.sharding import PartitionSpec as P

EB = 1
LANES = 128
ROWS = 8
DEPTH = 12 * ROWS
MOMENTS = 4 * ROWS
SUMS = MOMENTS + ROWS
UNROLL = 24
VALUES = 3
GROUP = 7
WALL_TARGETS = 24
FLUID_TARGETS = 12

smoothing = 0.1
support = 0.3
kernel_norm = 21.0 / (2.0 * 3.141592653589793 * support**3)
grad_coeff = -20.0 / support**2 * kernel_norm
tait_coeff = 25.0 / 7.0
visc_coeff = 0.05
cohesion = 2000.0
adhesion = 2000.0
gravity = 9.81
courant = 0.25

center = 0.3
shift = 0.0001 / support**2
press_coeff = -grad_coeff / (4.0 * cohesion)
density_coeff = (support * 4.0 * cohesion) / (-grad_coeff * visc_coeff * 2.0)

SPLITS = ((0, 0), (0, 1), (1, 0), (0, 2), (2, 0), (1, 1))


def split(value):
    first = value.astype(jnp.bfloat16).astype(jnp.float32)
    rest = value - first
    second = rest.astype(jnp.bfloat16).astype(jnp.float32)
    return [first, second, rest - second]


def pressure_ratio(density):
    square = density * density
    return tait_coeff * (square * square * square * density - 1.0) / square


def row_index():
    return lax.broadcasted_iota(jnp.int32, (ROWS, LANES), 0)


def state_of(block):
    row = row_index()
    y = jnp.where(row < 3, (block - center) * (1.0 / support), block)
    y = jnp.where(row == 6, block * density_coeff, y)
    products = y * jnp.where(row < 3, y, pltpu.roll(y, 3, axis=0))
    sums = products + pltpu.roll(products, ROWS - 1, axis=0) + pltpu.roll(products, ROWS - 2, axis=0)

    def everywhere(value, index):
        return jnp.broadcast_to(value[index : index + 1], (ROWS, LANES))

    press = press_coeff * pressure_ratio(everywhere(block, 6))
    return (
        y, everywhere(sums, 0), everywhere(sums, 3), everywhere(y, 6), everywhere(y, 7), press,
    )


def chosen(default, *cases):
    row = row_index()
    value = jnp.full((ROWS, LANES), default, jnp.float32)
    for index, case in cases:
        value = jnp.where(row == index, case, value)
    return value


def target_groups(state):
    y, n, e, r, _, press = state
    row = row_index()
    first = jnp.where(row < 6, y, jnp.where(row == 6, n + shift, e))
    scaled = r * jnp.where(row < 3, y, jnp.where(row == 3, 1.0, n + shift))
    second = jnp.where(row < 5, scaled, chosen(0.0, (5, press), (6, 1.0)))
    return first, second


def source_groups(state, wall):
    y, n, e, r, m, press = state
    row = row_index()
    minus = jnp.where(row < 3, -2.0 * y, 0.0)
    near = chosen(minus, (6, 1.0)), chosen(0.0, (6, n - shift))
    turned = jnp.where(row < 3, pltpu.roll(y, 5, axis=0), pltpu.roll(y, 3, axis=0))
    along = m * jnp.where(row < 6, turned, chosen(0.0, (7, -1.0))), chosen(0.0, (6, -m * e))
    if wall:
        press_part = chosen(0.0, (5, 2.0 * cohesion / adhesion), (6, -0.75))
        return near, along, (None, press_part)
    return near, along, (m * r * near[0], m * chosen(minus, (3, n), (4, 1.0), (6, r * n)))


def put_source(block, s, src, press=None, mass_factor=1.0):
    state = state_of(block)
    for n, (first, second) in enumerate(source_groups(state, press is None)):
        firsts = split(first) if first is not None else [jnp.zeros((ROWS, LANES))] * 3
        pieces = [
            jnp.concatenate(pair, axis=0).astype(jnp.bfloat16)
            for pair in zip(firsts, split(second))
        ]
        lanes = slice(n * LANES, (n + 1) * LANES)
        for k, (_, piece) in enumerate(SPLITS):
            src[s, 2 * ROWS * k : 2 * ROWS * (k + 1), lanes] = pieces[piece]
    moment = (mass_factor * state[4]) * jnp.where(row_index() == 6, 1.0, state[0])
    moments = split(moment) + [jnp.zeros_like(moment)]
    for n in range(2):
        half = jnp.concatenate(moments[2 * n : 2 * n + 2], axis=0)
        src[s, DEPTH:, n * LANES : (n + 1) * LANES] = half.astype(jnp.bfloat16)
    if press is not None:
        press[s] = state[5]


def put_target(state, b, tgt):
    pieces = [jnp.concatenate(pair, axis=0) for pair in zip(*map(split, target_groups(state)))]
    rows = jnp.concatenate([pieces[piece] for piece, _ in SPLITS], axis=0).astype(jnp.bfloat16)
    row = lax.broadcasted_iota(jnp.int32, (LANES, LANES), 0)
    lane = lax.broadcasted_iota(jnp.int32, (LANES, LANES), 1)
    unit = jnp.where(row == lane, 1.0, 0.0).astype(jnp.bfloat16)
    tgt[b] = across(unit, rows).astype(jnp.bfloat16)


def press_choice():
    row = lax.broadcasted_iota(jnp.int32, (DEPTH, LANES), 0)
    value = jnp.where(row == ROWS + 6, -0.75, 0.0)
    for k, (_, piece) in enumerate(SPLITS):
        if piece == 0:
            value = jnp.where(row == 2 * ROWS * k + ROWS + 5, 1.0, value)
    return value.astype(jnp.bfloat16)


def rows_at(index):
    return pl.ds(pl.multiple_of(index * ROWS, ROWS), ROWS)


def weights_of(product, press_i, press_j):
    near, approach, last = [product[:, n * LANES : (n + 1) * LANES] for n in range(VALUES)]
    guarded = jnp.maximum(near, 1e-30)
    falloff = jnp.maximum(1.0 - guarded * lax.rsqrt(guarded), 0.0)
    cubed = falloff * falloff * falloff
    if press_j is None:
        blend = falloff + last
    else:
        blend = falloff + press_i
        blend += jnp.concatenate([press_j[...]] * (LANES // ROWS), axis=0)
        blend += jnp.maximum(approach, 0.0) * pl.reciprocal(last, approx=True)
    weight = cubed * blend
    high = weight.astype(jnp.bfloat16)
    low = (weight - high.astype(jnp.float32)).astype(jnp.bfloat16)
    return [high, low], cubed * approach


def across(left, right):
    return lax.dot_general(
        left, right, (((1,), (1,)), ((), ())), preferred_element_type=jnp.float32
    )


def run_targets(targets, finish):
    steps = [
        (n, tiles[k : k + GROUP])
        for n, (_, _, tiles) in enumerate(targets)
        for k in range(0, len(tiles), GROUP)
    ]
    totals = [jnp.zeros((MOMENTS, LANES), jnp.float32)] * len(targets)
    rates = [jnp.zeros((LANES, LANES), jnp.float32)] * len(targets)

    def product_of(step):
        n, group = step
        columns = jnp.concatenate([source[:DEPTH, :] for source, _ in group], axis=1)
        return jnp.dot(targets[n][0], columns, preferred_element_type=jnp.float32)

    def add_up(n, moments, weights, last):
        totals[n] += across(moments, weights)
        if last:
            ones = jnp.ones((ROWS, 3 * LANES), jnp.bfloat16)
            pieces = jnp.concatenate(split(rates[n]), axis=1).astype(jnp.bfloat16)
            finish(n, jnp.concatenate([totals[n], across(ones, pieces)], axis=0))

    ahead = product_of(steps[0])
    waiting = None
    for k, (n, group) in enumerate(steps):
        product = ahead
        if k + 1 < len(steps):
            ahead = product_of(steps[k + 1])
        moments, weights = [], []
        for m, (source, press_j) in enumerate(group):
            columns = slice(m * VALUES * LANES, (m + 1) * VALUES * LANES)
            pair, part = weights_of(product[:, columns], targets[n][1], press_j)
            rates[n] += part
            weights += pair
            halves = [source[DEPTH:, :LANES], source[DEPTH:, LANES : 2 * LANES]]
            moments += [jnp.concatenate(halves, axis=0)] * 2
        if waiting is not None:
            add_up(*waiting, waiting[0] != n)
        waiting = (n, jnp.concatenate(moments, axis=1), jnp.concatenate(weights, axis=1))
    add_up(*waiting, True)


def sums_at(b):
    return pl.ds(pl.multiple_of(b * SUMS, ROWS), SUMS)


def own_kernel(
    own_ref, wall_ref, edge0_ref, edge1_ref, wpair_ref, along_ref,
    tgt, sums, wsrc, table,
):
    blocks = tgt.shape[0]

    def build(b, carry):
        put_target(state_of(own_ref[rows_at(b), :]), b, tgt)
        return carry

    lax.fori_loop(0, blocks, build, 0, unroll=UNROLL)
    row = row_index()
    count = 0
    for ref in (wall_ref, edge0_ref, edge1_ref):
        for c in range(ref.shape[0] // 4):
            held = ref[4 * c : 4 * c + 4, :]
            both = jnp.concatenate([held, held], axis=0)
            density = jnp.where(row == 6, 1.0, 0.0)
            block = jnp.where((row < 3) | (row == 7), both, density)
            put_source(block, count, wsrc, None, adhesion / cohesion)
            count += 1
    inner, edge = wall_ref.shape[0] // 4, edge0_ref.shape[0] // 4
    odd = along_ref[0] % 2
    for c in range(inner):
        table[edge + c] = c
    for c in range(edge):
        table[c] = inner + (1 - odd) * edge + c
        table[edge + inner + c] = inner + odd * edge + c

    together = math.gcd(blocks, WALL_TARGETS)

    def targets_from(i, carry):
        first = i * together
        targets = []
        for n in range(together):
            slots = [table[wpair_ref[first + n, k]] for k in range(wpair_ref.shape[1])]
            targets.append((tgt[first + n], None, [(wsrc.at[s], None) for s in slots]))

        def finish(n, total):
            sums[sums_at(first + n), :] = total

        run_targets(targets, finish)
        return carry

    lax.fori_loop(0, blocks // together, targets_from, 0)


def fluid_kernel(
    own_ref, ghost_ref, pair_ref, place_ref, tgt, own_sums,
    rate_ref, accel_ref, peak_ref, src, press, sums, stage, table,
):
    blocks = tgt.shape[0]
    ghosts = ghost_ref.shape[0] // ROWS
    per_mask = ghosts // 8
    for c in range(blocks):
        table[c] = c
    for mask in range(1, 8):
        for g in range(per_mask):
            table[blocks + (mask - 1) * per_mask + g] = (
                blocks + jnp.bitwise_xor(place_ref[0], mask) * per_mask + g
            )

    def build_own(b, carry):
        put_source(own_ref[rows_at(b), :], b, src, press)
        return carry

    def build(g, carry):
        put_source(ghost_ref[rows_at(g), :], blocks + g, src, press)
        return carry

    lax.fori_loop(0, blocks, build_own, 0, unroll=UNROLL)

    lax.fori_loop(0, ghosts, build, 0, unroll=UNROLL)

    choice = press_choice()
    together = math.gcd(blocks, FLUID_TARGETS)

    def targets_from(i, carry):
        first = i * together
        targets = []
        for n in range(together):
            slots = [table[pair_ref[first + n, k]] for k in range(pair_ref.shape[1])]
            target = tgt[first + n]
            press_i = jnp.dot(target, choice, preferred_element_type=jnp.float32)
            targets.append((target, press_i, [(src.at[s], press.at[s]) for s in slots]))

        def finish(n, total):
            rows = sums_at(first + n)
            sums[rows, :] = own_sums[rows, :] + total

        run_targets(targets, finish)
        return carry

    lax.fori_loop(0, blocks // together, targets_from, 0)

    rate_ref[...] = (-support * grad_coeff) * sums[pl.ds(MOMENTS, blocks, stride=SUMS), :]

    def summed(row):
        parts = [sums[pl.ds(p * ROWS + row, blocks, stride=SUMS), :] for p in range(3)]
        return parts[0] + parts[1] + parts[2]

    mass_sum = summed(6)
    square = jnp.zeros_like(mass_sum)
    for d in range(3):
        pos = (own_ref[pl.ds(d, blocks, stride=ROWS), :] - center) * (1.0 / support)
        force = (4.0 * cohesion * support) * (pos * mass_sum - summed(d))
        if d == 2:
            force -= gravity
        square += force * force
        stage[pl.ds(d, blocks, stride=ROWS), :] = force
    for b in range(blocks):
        accel_ref[:, b * LANES : (b + 1) * LANES] = stage[b * ROWS : b * ROWS + 3, :]
    peak_ref[...] = jnp.full(peak_ref.shape, jnp.sqrt(jnp.max(square)), jnp.float32)


SMEM = pl.BlockSpec(memory_space=pltpu.SMEM)
VMEM = pl.BlockSpec(memory_space=pltpu.VMEM)
PARAMS = pltpu.CompilerParams(vmem_limit_bytes=18 * 1024 * 1024)


def tile_cost(tiles):
    return pl.CostEstimate(
        flops=tiles * LANES * LANES * 1000, bytes_accessed=0, transcendentals=0
    )


def source_shape(count):
    return (count, DEPTH + 2 * ROWS, VALUES * LANES), jnp.bfloat16


def own_pass(own, walls, edges, wall_pairs, along):
    blocks = own.shape[0] // ROWS
    wall_blocks = (walls.shape[0] + 2 * edges[0].shape[0]) // 4
    outs = [
        ((blocks, LANES, DEPTH), jnp.bfloat16),
        ((blocks * SUMS, LANES), jnp.float32),
    ]
    return pl.pallas_call(
        own_kernel,
        out_shape=[jax.ShapeDtypeStruct(*out) for out in outs],
        in_specs=[VMEM, VMEM, VMEM, VMEM, SMEM, SMEM],
        out_specs=[VMEM] * len(outs),
        scratch_shapes=[
            pltpu.VMEM(*source_shape(wall_blocks)),
            pltpu.SMEM((wall_blocks,), jnp.int32),
        ],
        compiler_params=PARAMS,
        cost_estimate=tile_cost(wall_pairs.size),
        name="own_pass",
    )(own, walls, *edges, wall_pairs, along)


def fluid_pass(own, ghosts, pair_list, place, own_results):
    blocks = own.shape[0] // ROWS
    total = blocks + ghosts.shape[0] // ROWS
    return pl.pallas_call(
        fluid_kernel,
        out_shape=(
            jax.ShapeDtypeStruct((blocks, LANES), jnp.float32),
            jax.ShapeDtypeStruct((3, blocks * LANES), jnp.float32),
            jax.ShapeDtypeStruct((ROWS, LANES), jnp.float32),
        ),
        in_specs=[VMEM, VMEM, SMEM, SMEM] + [VMEM] * len(own_results),
        out_specs=(VMEM, VMEM, VMEM),
        scratch_shapes=[
            pltpu.VMEM(*source_shape(total)),
            pltpu.VMEM((total, ROWS, LANES), jnp.float32),
            pltpu.VMEM((blocks * SUMS, LANES), jnp.float32),
            pltpu.VMEM((blocks * ROWS, LANES), jnp.float32),
            pltpu.SMEM((total,), jnp.int32),
        ],
        compiler_params=PARAMS,
        cost_estimate=tile_cost(pair_list.size),
        name="fluid_pass",
    )(own, ghosts, pair_list, place, *own_results)


def outgoing_kernel(
    row_length, own_ref, list_ref, place_ref, wall_ref, count_ref, along_ref,
    sent_ref, live_ref, edge0_ref, edge1_ref,
):
    for slot in range(8):
        mask = jnp.bitwise_xor(place_ref[0], slot)
        for g in range(list_ref.shape[1]):
            block = list_ref[jnp.maximum(mask - 1, 0), g]
            first = (slot * list_ref.shape[1] + g) * ROWS
            sent_ref[first : first + ROWS, :] = own_ref[rows_at(block), :]
    lane = lax.broadcasted_iota(jnp.int32, (4, LANES), 1)
    row = lax.broadcasted_iota(jnp.int32, (4, LANES), 0)
    for c in range(wall_ref.shape[1] // LANES):
        block = wall_ref[:, c * LANES : (c + 1) * LANES]
        kept = (row < 3) | (lane < count_ref[c])
        live_ref[4 * c : 4 * c + 4, :] = jnp.where(kept, block, 0.0)
    first = live_ref[: edge0_ref.shape[0], :]
    last = live_ref[live_ref.shape[0] - edge0_ref.shape[0] :, :]
    along = along_ref[0]
    edge0_ref[...] = jnp.where(along % 2 == 0, last, first)
    end = row_length - row_length % 2 - 1
    inside = jnp.where((along == 0) | (along == end), 0.0, 1.0)
    edge1_ref[...] = jnp.where(along % 2 == 0, first, last) * inside


def outgoing_pass(own, ghost_list, place, wall_state, wall_count, along):
    walls = wall_state.shape[1] // LANES
    rows = [8 * ghost_list.shape[1] * ROWS, walls * 4, EB * 4, EB * 4]
    return pl.pallas_call(
        functools.partial(outgoing_kernel, lax.axis_size("wall")),
        out_shape=[jax.ShapeDtypeStruct((row, LANES), jnp.float32) for row in rows],
        in_specs=[VMEM, SMEM, SMEM, VMEM, SMEM, SMEM],
        out_specs=[VMEM] * len(rows),
        name="outgoing_pass",
    )(own, ghost_list, place, wall_state, wall_count, along)


def swapped(shard, axis, mask):
    count = math.prod(lax.axis_size(name) for name in axis)
    return lax.ppermute(shard, axis, [(i, i ^ mask) for i in range(count)])


def largest(peak, outer, inner):
    count, width = lax.axis_size(outer), lax.axis_size(inner)
    other = 1 if width > 1 else 0
    masks = [other] if other else []
    masks += [1 << bit | other for bit in range(1, (width - 1).bit_length())]
    masks += [width << bit | other for bit in range((count - 1).bit_length())]
    for mask in masks:
        peak = jnp.maximum(peak, swapped(peak, (outer, inner), mask))
    return peak


def facing(edges, axis):
    count = lax.axis_size(axis)
    landed = []
    for start, sent in enumerate(edges):
        pairs = [(i, (i + 1) % count) for i in range(start, count - count % 2, 2)]
        landed.append(lax.ppermute(sent, axis, pairs + [(j, i) for i, j in pairs]))
    return landed


def per_device(fluid_state, ghost_list, pair_list, wall_state, wall_count, wall_pairs):
    block_total = fluid_state.shape[1] // LANES
    own = jnp.transpose(fluid_state.reshape(8, block_total, LANES), (1, 0, 2)).reshape(-1, LANES)
    place = (lax.axis_index("orb") % 8).reshape(1)
    along = lax.axis_index("wall").reshape(1)
    sent, walls, *edges = outgoing_pass(own, ghost_list, place, wall_state, wall_count, along)
    edges = facing(edges, "wall")
    groups = [list(range(g, g + 8)) for g in range(0, lax.axis_size("orb"), 8)]
    landed = lax.all_to_all(
        sent.reshape(8, -1, LANES),
        "orb",
        0,
        0,
        axis_index_groups=groups if len(groups) > 1 else None,
    )
    own_results = own_pass(own, walls, edges, wall_pairs, along)
    rate, acceleration, local_peak = fluid_pass(
        own, landed.reshape(-1, LANES), pair_list, place, own_results
    )
    peak = largest(local_peak, "orb", "wall")[0, 0]
    time_step = courant * jnp.sqrt(smoothing / (peak + 1e-06))
    return (rate.reshape(-1), acceleration, time_step)


def solution(mesh):
    return jax.shard_map(
        per_device,
        mesh=mesh,
        in_specs=(
            P(None, ("orb", "wall")),
            P(None, ("orb", "wall")),
            P(("orb", "wall"), None),
            P(None, ("orb", "wall")),
            P(("orb", "wall")),
            P(("orb", "wall"), None),
        ),
        out_specs=(P(("orb", "wall")), P(None, ("orb", "wall")), P()),
        check_vma=False,
    )
```

```python
import functools
import math

import jax
import jax.numpy as jnp
from jax import lax
from jax.experimental import pallas as pl
from jax.experimental.pallas import tpu as pltpu
from jax.sharding import PartitionSpec as P

EB = 1
LANES = 128
ROWS = 8
DEPTH = 12 * ROWS
MOMENTS = 4 * ROWS
SUMS = MOMENTS + ROWS
UNROLL = 24
VALUES = 3
GROUP = 1
WALL_TARGETS = 24
FLUID_TARGETS = 12

smoothing = 0.1
support = 0.3
kernel_norm = 21.0 / (2.0 * 3.141592653589793 * support**3)
grad_coeff = -20.0 / support**2 * kernel_norm
tait_coeff = 25.0 / 7.0
visc_coeff = 0.05
cohesion = 2000.0
adhesion = 2000.0
gravity = 9.81
courant = 0.25

center = 0.3
shift = 0.0001 / support**2
press_coeff = -grad_coeff / (4.0 * cohesion)
density_coeff = (support * 4.0 * cohesion) / (-grad_coeff * visc_coeff * 2.0)

SPLITS = ((0, 0), (0, 1), (1, 0), (0, 2), (2, 0), (1, 1))


def split(value):
    first = value.astype(jnp.bfloat16).astype(jnp.float32)
    rest = value - first
    second = rest.astype(jnp.bfloat16).astype(jnp.float32)
    return [first, second, rest - second]


def pressure_ratio(density):
    square = density * density
    return tait_coeff * (square * square * square * density - 1.0) / square


def row_index():
    return lax.broadcasted_iota(jnp.int32, (ROWS, LANES), 0)


def state_of(block):
    row = row_index()
    y = jnp.where(row < 3, (block - center) * (1.0 / support), block)
    y = jnp.where(row == 6, block * density_coeff, y)
    products = y * jnp.where(row < 3, y, pltpu.roll(y, 3, axis=0))
    sums = products + pltpu.roll(products, ROWS - 1, axis=0) + pltpu.roll(products, ROWS - 2, axis=0)

    def everywhere(value, index):
        return jnp.broadcast_to(value[index : index + 1], (ROWS, LANES))

    press = press_coeff * pressure_ratio(everywhere(block, 6))
    return (
        y, everywhere(sums, 0), everywhere(sums, 3), everywhere(y, 6), everywhere(y, 7), press,
    )


def chosen(default, *cases):
    row = row_index()
    value = jnp.full((ROWS, LANES), default, jnp.float32)
    for index, case in cases:
        value = jnp.where(row == index, case, value)
    return value


def target_groups(state):
    y, n, e, r, _, press = state
    row = row_index()
    first = jnp.where(row < 6, y, jnp.where(row == 6, n + shift, e))
    scaled = r * jnp.where(row < 3, y, jnp.where(row == 3, 1.0, n + shift))
    second = jnp.where(row < 5, scaled, chosen(0.0, (5, press), (6, 1.0)))
    return first, second


def source_groups(state, wall):
    y, n, e, r, m, press = state
    row = row_index()
    minus = jnp.where(row < 3, -2.0 * y, 0.0)
    near = chosen(minus, (6, 1.0)), chosen(0.0, (6, n - shift))
    turned = jnp.where(row < 3, pltpu.roll(y, 5, axis=0), pltpu.roll(y, 3, axis=0))
    along = m * jnp.where(row < 6, turned, chosen(0.0, (7, -1.0))), chosen(0.0, (6, -m * e))
    if wall:
        press_part = chosen(0.0, (5, 2.0 * cohesion / adhesion), (6, -0.75))
        return near, along, (None, press_part)
    return near, along, (m * r * near[0], m * chosen(minus, (3, n), (4, 1.0), (6, r * n)))


def put_source(block, s, src, press=None, mass_factor=1.0):
    state = state_of(block)
    for n, (first, second) in enumerate(source_groups(state, press is None)):
        firsts = split(first) if first is not None else [jnp.zeros((ROWS, LANES))] * 3
        pieces = [
            jnp.concatenate(pair, axis=0).astype(jnp.bfloat16)
            for pair in zip(firsts, split(second))
        ]
        lanes = slice(n * LANES, (n + 1) * LANES)
        for k, (_, piece) in enumerate(SPLITS):
            src[s, 2 * ROWS * k : 2 * ROWS * (k + 1), lanes] = pieces[piece]
    moment = (mass_factor * state[4]) * jnp.where(row_index() == 6, 1.0, state[0])
    moments = split(moment) + [jnp.zeros_like(moment)]
    for n in range(2):
        half = jnp.concatenate(moments[2 * n : 2 * n + 2], axis=0)
        src[s, DEPTH:, n * LANES : (n + 1) * LANES] = half.astype(jnp.bfloat16)
    if press is not None:
        press[s] = state[5]


def put_target(state, b, tgt):
    pieces = [jnp.concatenate(pair, axis=0) for pair in zip(*map(split, target_groups(state)))]
    rows = jnp.concatenate([pieces[piece] for piece, _ in SPLITS], axis=0).astype(jnp.bfloat16)
    row = lax.broadcasted_iota(jnp.int32, (LANES, LANES), 0)
    lane = lax.broadcasted_iota(jnp.int32, (LANES, LANES), 1)
    unit = jnp.where(row == lane, 1.0, 0.0).astype(jnp.bfloat16)
    tgt[b] = across(unit, rows).astype(jnp.bfloat16)


def press_choice():
    row = lax.broadcasted_iota(jnp.int32, (DEPTH, LANES), 0)
    value = jnp.where(row == ROWS + 6, -0.75, 0.0)
    for k, (_, piece) in enumerate(SPLITS):
        if piece == 0:
            value = jnp.where(row == 2 * ROWS * k + ROWS + 5, 1.0, value)
    return value.astype(jnp.bfloat16)


def rows_at(index):
    return pl.ds(pl.multiple_of(index * ROWS, ROWS), ROWS)


def weights_of(product, press_i, press_j):
    near, approach, last = [product[:, n * LANES : (n + 1) * LANES] for n in range(VALUES)]
    guarded = jnp.maximum(near, 1e-30)
    falloff = jnp.maximum(1.0 - guarded * lax.rsqrt(guarded), 0.0)
    cubed = falloff * falloff * falloff
    if press_j is None:
        blend = falloff + last
    else:
        blend = falloff + press_i
        blend += jnp.concatenate([press_j[...]] * (LANES // ROWS), axis=0)
        blend += jnp.maximum(approach, 0.0) * pl.reciprocal(last, approx=True)
    weight = cubed * blend
    high = weight.astype(jnp.bfloat16)
    low = (weight - high.astype(jnp.float32)).astype(jnp.bfloat16)
    return [high, low], cubed * approach


def across(left, right):
    return lax.dot_general(
        left, right, (((1,), (1,)), ((), ())), preferred_element_type=jnp.float32
    )


def run_targets(targets, finish):
    steps = [
        (n, tiles[k : k + GROUP])
        for n, (_, _, tiles) in enumerate(targets)
        for k in range(0, len(tiles), GROUP)
    ]
    totals = [jnp.zeros((MOMENTS, LANES), jnp.float32)] * len(targets)
    rates = [jnp.zeros((LANES, LANES), jnp.float32)] * len(targets)

    def product_of(step):
        n, group = step
        columns = jnp.concatenate([source[:DEPTH, :] for source, _ in group], axis=1)
        return jnp.dot(targets[n][0], columns, preferred_element_type=jnp.float32)

    def add_up(n, moments, weights, last):
        totals[n] += across(moments, weights)
        if last:
            ones = jnp.ones((ROWS, 3 * LANES), jnp.bfloat16)
            pieces = jnp.concatenate(split(rates[n]), axis=1).astype(jnp.bfloat16)
            finish(n, jnp.concatenate([totals[n], across(ones, pieces)], axis=0))

    ahead = product_of(steps[0])
    waiting = None
    for k, (n, group) in enumerate(steps):
        product = ahead
        if k + 1 < len(steps):
            ahead = product_of(steps[k + 1])
        moments, weights = [], []
        for m, (source, press_j) in enumerate(group):
            columns = slice(m * VALUES * LANES, (m + 1) * VALUES * LANES)
            pair, part = weights_of(product[:, columns], targets[n][1], press_j)
            rates[n] += part
            weights += pair
            halves = [source[DEPTH:, :LANES], source[DEPTH:, LANES : 2 * LANES]]
            moments += [jnp.concatenate(halves, axis=0)] * 2
        if waiting is not None:
            add_up(*waiting, waiting[0] != n)
        waiting = (n, jnp.concatenate(moments, axis=1), jnp.concatenate(weights, axis=1))
    add_up(*waiting, True)


def sums_at(b):
    return pl.ds(pl.multiple_of(b * SUMS, ROWS), SUMS)


def own_kernel(
    own_ref, wall_ref, edge0_ref, edge1_ref, wpair_ref, along_ref,
    tgt, sums, wsrc, table,
):
    blocks = tgt.shape[0]

    def build(b, carry):
        put_target(state_of(own_ref[rows_at(b), :]), b, tgt)
        return carry

    lax.fori_loop(0, blocks, build, 0, unroll=UNROLL)
    row = row_index()
    count = 0
    for ref in (wall_ref, edge0_ref, edge1_ref):
        for c in range(ref.shape[0] // 4):
            held = ref[4 * c : 4 * c + 4, :]
            both = jnp.concatenate([held, held], axis=0)
            density = jnp.where(row == 6, 1.0, 0.0)
            block = jnp.where((row < 3) | (row == 7), both, density)
            put_source(block, count, wsrc, None, adhesion / cohesion)
            count += 1
    inner, edge = wall_ref.shape[0] // 4, edge0_ref.shape[0] // 4
    odd = along_ref[0] % 2
    for c in range(inner):
        table[edge + c] = c
    for c in range(edge):
        table[c] = inner + (1 - odd) * edge + c
        table[edge + inner + c] = inner + odd * edge + c

    together = math.gcd(blocks, WALL_TARGETS)

    def targets_from(i, carry):
        first = i * together
        targets = []
        for n in range(together):
            slots = [table[wpair_ref[first + n, k]] for k in range(wpair_ref.shape[1])]
            targets.append((tgt[first + n], None, [(wsrc.at[s], None) for s in slots]))

        def finish(n, total):
            sums[sums_at(first + n), :] = total

        run_targets(targets, finish)
        return carry

    lax.fori_loop(0, blocks // together, targets_from, 0)


def fluid_kernel(
    own_ref, ghost_ref, pair_ref, place_ref, tgt, own_sums,
    rate_ref, accel_ref, peak_ref, src, press, sums, stage, table,
):
    blocks = tgt.shape[0]
    ghosts = ghost_ref.shape[0] // ROWS
    per_mask = ghosts // 8
    for c in range(blocks):
        table[c] = c
    for mask in range(1, 8):
        for g in range(per_mask):
            table[blocks + (mask - 1) * per_mask + g] = (
                blocks + jnp.bitwise_xor(place_ref[0], mask) * per_mask + g
            )

    def build_own(b, carry):
        put_source(own_ref[rows_at(b), :], b, src, press)
        return carry

    def build(g, carry):
        put_source(ghost_ref[rows_at(g), :], blocks + g, src, press)
        return carry

    lax.fori_loop(0, blocks, build_own, 0, unroll=UNROLL)

    lax.fori_loop(0, ghosts, build, 0, unroll=UNROLL)

    choice = press_choice()
    together = math.gcd(blocks, FLUID_TARGETS)

    def targets_from(i, carry):
        first = i * together
        targets = []
        for n in range(together):
            slots = [table[pair_ref[first + n, k]] for k in range(pair_ref.shape[1])]
            target = tgt[first + n]
            press_i = jnp.dot(target, choice, preferred_element_type=jnp.float32)
            targets.append((target, press_i, [(src.at[s], press.at[s]) for s in slots]))

        def finish(n, total):
            rows = sums_at(first + n)
            sums[rows, :] = own_sums[rows, :] + total

        run_targets(targets, finish)
        return carry

    lax.fori_loop(0, blocks // together, targets_from, 0)

    rate_ref[...] = (-support * grad_coeff) * sums[pl.ds(MOMENTS, blocks, stride=SUMS), :]

    def summed(row):
        parts = [sums[pl.ds(p * ROWS + row, blocks, stride=SUMS), :] for p in range(3)]
        return parts[0] + parts[1] + parts[2]

    mass_sum = summed(6)
    square = jnp.zeros_like(mass_sum)
    for d in range(3):
        pos = (own_ref[pl.ds(d, blocks, stride=ROWS), :] - center) * (1.0 / support)
        force = (4.0 * cohesion * support) * (pos * mass_sum - summed(d))
        if d == 2:
            force -= gravity
        square += force * force
        stage[pl.ds(d, blocks, stride=ROWS), :] = force
    for b in range(blocks):
        accel_ref[:, b * LANES : (b + 1) * LANES] = stage[b * ROWS : b * ROWS + 3, :]
    peak_ref[...] = jnp.full(peak_ref.shape, jnp.sqrt(jnp.max(square)), jnp.float32)


SMEM = pl.BlockSpec(memory_space=pltpu.SMEM)
VMEM = pl.BlockSpec(memory_space=pltpu.VMEM)
PARAMS = pltpu.CompilerParams(vmem_limit_bytes=18 * 1024 * 1024)


def tile_cost(tiles):
    return pl.CostEstimate(
        flops=tiles * LANES * LANES * 1000, bytes_accessed=0, transcendentals=0
    )


def source_shape(count):
    return (count, DEPTH + 2 * ROWS, VALUES * LANES), jnp.bfloat16


def own_pass(own, walls, edges, wall_pairs, along):
    blocks = own.shape[0] // ROWS
    wall_blocks = (walls.shape[0] + 2 * edges[0].shape[0]) // 4
    outs = [
        ((blocks, LANES, DEPTH), jnp.bfloat16),
        ((blocks * SUMS, LANES), jnp.float32),
    ]
    return pl.pallas_call(
        own_kernel,
        out_shape=[jax.ShapeDtypeStruct(*out) for out in outs],
        in_specs=[VMEM, VMEM, VMEM, VMEM, SMEM, SMEM],
        out_specs=[VMEM] * len(outs),
        scratch_shapes=[
            pltpu.VMEM(*source_shape(wall_blocks)),
            pltpu.SMEM((wall_blocks,), jnp.int32),
        ],
        compiler_params=PARAMS,
        cost_estimate=tile_cost(wall_pairs.size),
        name="own_pass",
    )(own, walls, *edges, wall_pairs, along)


def fluid_pass(own, ghosts, pair_list, place, own_results):
    blocks = own.shape[0] // ROWS
    total = blocks + ghosts.shape[0] // ROWS
    return pl.pallas_call(
        fluid_kernel,
        out_shape=(
            jax.ShapeDtypeStruct((blocks, LANES), jnp.float32),
            jax.ShapeDtypeStruct((3, blocks * LANES), jnp.float32),
            jax.ShapeDtypeStruct((ROWS, LANES), jnp.float32),
        ),
        in_specs=[VMEM, VMEM, SMEM, SMEM] + [VMEM] * len(own_results),
        out_specs=(VMEM, VMEM, VMEM),
        scratch_shapes=[
            pltpu.VMEM(*source_shape(total)),
            pltpu.VMEM((total, ROWS, LANES), jnp.float32),
            pltpu.VMEM((blocks * SUMS, LANES), jnp.float32),
            pltpu.VMEM((blocks * ROWS, LANES), jnp.float32),
            pltpu.SMEM((total,), jnp.int32),
        ],
        compiler_params=PARAMS,
        cost_estimate=tile_cost(pair_list.size),
        name="fluid_pass",
    )(own, ghosts, pair_list, place, *own_results)


def outgoing_kernel(
    row_length, own_ref, list_ref, place_ref, wall_ref, count_ref, along_ref,
    sent_ref, live_ref, edge0_ref, edge1_ref,
):
    for slot in range(8):
        mask = jnp.bitwise_xor(place_ref[0], slot)
        for g in range(list_ref.shape[1]):
            block = list_ref[jnp.maximum(mask - 1, 0), g]
            first = (slot * list_ref.shape[1] + g) * ROWS
            sent_ref[first : first + ROWS, :] = own_ref[rows_at(block), :]
    lane = lax.broadcasted_iota(jnp.int32, (4, LANES), 1)
    row = lax.broadcasted_iota(jnp.int32, (4, LANES), 0)
    for c in range(wall_ref.shape[1] // LANES):
        block = wall_ref[:, c * LANES : (c + 1) * LANES]
        kept = (row < 3) | (lane < count_ref[c])
        live_ref[4 * c : 4 * c + 4, :] = jnp.where(kept, block, 0.0)
    first = live_ref[: edge0_ref.shape[0], :]
    last = live_ref[live_ref.shape[0] - edge0_ref.shape[0] :, :]
    along = along_ref[0]
    edge0_ref[...] = jnp.where(along % 2 == 0, last, first)
    end = row_length - row_length % 2 - 1
    inside = jnp.where((along == 0) | (along == end), 0.0, 1.0)
    edge1_ref[...] = jnp.where(along % 2 == 0, first, last) * inside


def outgoing_pass(own, ghost_list, place, wall_state, wall_count, along):
    walls = wall_state.shape[1] // LANES
    rows = [8 * ghost_list.shape[1] * ROWS, walls * 4, EB * 4, EB * 4]
    return pl.pallas_call(
        functools.partial(outgoing_kernel, lax.axis_size("wall")),
        out_shape=[jax.ShapeDtypeStruct((row, LANES), jnp.float32) for row in rows],
        in_specs=[VMEM, SMEM, SMEM, VMEM, SMEM, SMEM],
        out_specs=[VMEM] * len(rows),
        name="outgoing_pass",
    )(own, ghost_list, place, wall_state, wall_count, along)


def swapped(shard, axis, mask):
    count = math.prod(lax.axis_size(name) for name in axis)
    return lax.ppermute(shard, axis, [(i, i ^ mask) for i in range(count)])


def largest(peak, outer, inner):
    count, width = lax.axis_size(outer), lax.axis_size(inner)
    other = 1 if width > 1 else 0
    masks = [other] if other else []
    masks += [1 << bit | other for bit in range(1, (width - 1).bit_length())]
    masks += [width << bit | other for bit in range((count - 1).bit_length())]
    for mask in masks:
        peak = jnp.maximum(peak, swapped(peak, (outer, inner), mask))
    return peak


def facing(edges, axis):
    count = lax.axis_size(axis)
    landed = []
    for start, sent in enumerate(edges):
        pairs = [(i, (i + 1) % count) for i in range(start, count - count % 2, 2)]
        landed.append(lax.ppermute(sent, axis, pairs + [(j, i) for i, j in pairs]))
    return landed


def per_device(fluid_state, ghost_list, pair_list, wall_state, wall_count, wall_pairs):
    block_total = fluid_state.shape[1] // LANES
    own = jnp.transpose(fluid_state.reshape(8, block_total, LANES), (1, 0, 2)).reshape(-1, LANES)
    place = (lax.axis_index("orb") % 8).reshape(1)
    along = lax.axis_index("wall").reshape(1)
    sent, walls, *edges = outgoing_pass(own, ghost_list, place, wall_state, wall_count, along)
    edges = facing(edges, "wall")
    groups = [list(range(g, g + 8)) for g in range(0, lax.axis_size("orb"), 8)]
    landed = lax.all_to_all(
        sent.reshape(8, -1, LANES),
        "orb",
        0,
        0,
        axis_index_groups=groups if len(groups) > 1 else None,
    )
    own_results = own_pass(own, walls, edges, wall_pairs, along)
    rate, acceleration, local_peak = fluid_pass(
        own, landed.reshape(-1, LANES), pair_list, place, own_results
    )
    peak = largest(local_peak, "orb", "wall")[0, 0]
    time_step = courant * jnp.sqrt(smoothing / (peak + 1e-06))
    return (rate.reshape(-1), acceleration, time_step)


def solution(mesh):
    return jax.shard_map(
        per_device,
        mesh=mesh,
        in_specs=(
            P(None, ("orb", "wall")),
            P(None, ("orb", "wall")),
            P(("orb", "wall"), None),
            P(None, ("orb", "wall")),
            P(("orb", "wall")),
            P(("orb", "wall"), None),
        ),
        out_specs=(P(("orb", "wall")), P(None, ("orb", "wall")), P()),
        check_vma=False,
    )
```
